32 devices in a mesh: dx: 2 (over y), dy: 16 (over z, x, core).
Axes of the slice: x: 2, y: 2, z: 4, core: 2. Of those that a mesh axis runs over, the one named last changes fastest.
Arguments:
- vectors: bfloat16 [2, 16, 256, 16, 128], P(None, 'dx', 'dy'), may hold values from -6 to 6
- resident: bfloat16 [16, 256, 16, 512], P('dx', 'dy'), may hold values from -6 to 6
- inv_mass: float32 [16, 256, 16], P('dx', 'dy'), may hold values from 0.26 to 1.3
- potential: float32 [16, 256, 16], P('dx', 'dy'), may hold values from -0.4 to 0.4
- cell_matrix: bfloat16 [729, 729], replicated, may hold values from -1 to 1.3, as said below
- connectivity: int32 [2, 16, 4, 729], P('dx', 'dy'), may hold values from 0 to 2447, as said below
Outputs:
- filtered: float32 [2, 16, 256, 16, 128], P(None, 'dx', 'dy')
- margin: float32 [512, 256], P('dy')
The draws below stay inside these ranges and needn't reach their ends.
Inputs may be any that keep to these rules, and one draw needn't show every extreme that they name: `connectivity`: cell c of a device, with c = (cx * 2 + cy) * 2 + cz, covers the extended nodes with i from cx * 8 to cx * 8 + 8, j from cy * 8 to cy * 8 + 8, and k from cz * 8 to cz * 8 + 8 taken modulo 2 * 8; its 729 entries name each of these nodes once, in an order that may differ from cell to cell. `cell_matrix`: Symmetric.
All inputs are finite; a program needn't handle non-finite values.
Results may differ from the reference program's by a relative error of at most 0.0055.
Values may be sent and summed in bfloat16 or wider, within the bound.
No kernel may reach another device: no remote copies, remote signals or barrier semaphores. Data moves between devices by JAX's collectives and lax.ppermute only.
A program may use at most 64 MiB of HBM per device.

```python
import jax
import jax.numpy as jnp
from jax import lax

P_SIZE = 8
NC = 729
CELL_X = 1
CELL_Y = 2
CELL_Z = 2
CELLS_DEV = 4
V = 128
BLOCKS = 2
RES = 512
DEGREE = 3
NX = 16
NY = 256
NZ = 16
N_DX = 2
N_DY = 16


def draw_connectivity(key, part):
    orders = jnp.array([[0, 1, 2], [0, 2, 1], [1, 0, 2], [1, 2, 0], [2, 0, 1], [2, 1, 0]], jnp.int32)
    key_order, key_flip = jax.random.split(jax.random.fold_in(key, 11))
    shape = (N_DX, N_DY, CELLS_DEV)
    which = jax.random.randint(key_order, shape, 0, 6)
    flips = jax.random.randint(key_flip, shape + (3,), 0, 2)
    local = jnp.arange(NC, dtype=jnp.int32)
    coords = jnp.stack([local // ((P_SIZE + 1) * (P_SIZE + 1)), local // (P_SIZE + 1) % (P_SIZE + 1), local % (P_SIZE + 1)], axis=-1)
    chosen = orders[which]
    onehot = (chosen[..., :, None] == jnp.arange(3, dtype=jnp.int32)).astype(jnp.int32)
    moved = jnp.sum(coords[None, None, None, :, None, :] * onehot[..., None, :, :], axis=-1)
    moved = jnp.where(flips[..., None, :] == 1, P_SIZE - moved, moved)
    cell = jnp.arange(CELLS_DEV, dtype=jnp.int32)
    cell_x = cell // (CELL_Y * CELL_Z)
    cell_y = cell // CELL_Z % CELL_Y
    cell_z = cell % CELL_Z
    index_i = cell_x[:, None] * P_SIZE + moved[..., 0]
    index_j = cell_y[:, None] * P_SIZE + moved[..., 1]
    index_k = (cell_z[:, None] * P_SIZE + moved[..., 2]) % (CELL_Z * P_SIZE)
    return ((index_i * (CELL_Y * P_SIZE + 1) + index_j) * (CELL_Z * P_SIZE) + index_k).astype(jnp.int32)


def draw_inv_mass(key, part):
    key = jax.random.fold_in(key, 23)
    edge_x = (jnp.arange(NX) % P_SIZE == 0).astype(jnp.float32)
    edge_y = (jnp.arange(NY) % P_SIZE == 0).astype(jnp.float32)
    edge_z = (jnp.arange(NZ) % P_SIZE == 0).astype(jnp.float32)
    shared = edge_x[:, None, None] + edge_y[None, :, None] + edge_z[None, None, :]
    multiple = jnp.exp2(shared)
    factor = jnp.exp(jax.random.uniform(key, (NX, NY, NZ), jnp.float32, jnp.log(0.75), jnp.log(1.3)))
    return (factor / jnp.sqrt(multiple)).astype(jnp.float32)


def draw_cell_matrix(key, part):
    key_off, key_diag = jax.random.split(jax.random.fold_in(key, 37))
    raw = jax.random.normal(key_off, (NC, NC), jnp.float32)
    offdiag = (raw + raw.T) * (0.6 / jnp.sqrt(2.0 * NC))
    offdiag = jnp.clip(offdiag, -0.3, 0.3)
    diagonal = jax.random.uniform(key_diag, (NC,), jnp.float32, 0.8, 1.2)
    whole = offdiag * (1.0 - jnp.eye(NC, dtype=jnp.float32)) + jnp.diag(diagonal)
    return whole.astype(jnp.bfloat16)


def with_spikes(drawn, stream_key, source, target, shards_of, factor):
    owner, partner = [(jnp.arange(drawn.shape[dim]) // (drawn.shape[dim] // shards_of)).reshape([-1 if axis == dim else 1 for axis in range(drawn.ndim)]) for dim in (source, target)]
    chosen = jax.random.permutation(stream_key, shards_of)[partner]
    strong = (owner == chosen) | (owner == (partner + shards_of // 2) % shards_of)
    return jnp.where(strong, factor * drawn, drawn)


def level_of(own_key, dims, shards, low, high):
    level, own = 1.0, jax.random.fold_in(own_key, 6)
    for position, parts in shards:
        steps = jnp.exp(jax.random.uniform(jax.random.fold_in(own, position), (parts,), jnp.float32, low / len(shards), high / len(shards)))
        level = level * jnp.repeat(steps, dims[position] // parts).reshape([-1 if axis == position else 1 for axis in range(len(dims))])
    return level


def normal_values(own_key, shape, width, bound, cuts=(), kind=jnp.bfloat16):
    values = width * jax.random.normal(own_key, shape, jnp.float32)
    if cuts:
        values = values * level_of(own_key, shape, cuts, -0.22, 0.18)
    return jnp.clip(values, -bound, bound).astype(kind)


def heavy_noise(rng, shape, deviation, limit, shards, heavy, held_as=jnp.bfloat16):
    result = deviation * jax.random.normal(rng, shape, jnp.float32)
    if shards:
        result = result * level_of(rng, shape, shards, -0.22, 0.18)
    return jnp.clip(with_spikes(result, jax.random.fold_in(rng, 3), *heavy), -limit, limit).astype(held_as)


def setup_inputs(seed: int = 0) -> dict:
    splits = jax.random.split(jax.random.key(seed), 7)
    vectors = normal_values(splits[0], (BLOCKS, NX, NY, NZ, V), 1.0, 6.0, ((1, 2), (2, 16)))
    resident = heavy_noise(splits[1], (NX, NY, NZ, RES), 1.0, 6.0, ((0, 2), (1, 16)), (1, 3, 16, 2.0))
    inv_mass = draw_inv_mass(jax.random.fold_in(splits[6], 71), 0)
    potential = jnp.clip(jax.random.uniform(splits[3], (NX, NY, NZ), jnp.float32, -0.4, 0.4) * level_of(splits[3], (NX, NY, NZ), ((0, 2), (1, 16)), -0.4, 0.0), -0.4, 0.4)
    cell_matrix = draw_cell_matrix(jax.random.fold_in(splits[6], 71), 0)
    connectivity = draw_connectivity(jax.random.fold_in(splits[6], 71), 0)
    return {"vectors": vectors, "resident": resident, "inv_mass": inv_mass, "potential": potential, "cell_matrix": cell_matrix, "connectivity": connectivity}


center_shift = 1.2
half_width = 2.0

def node_table(connectivity):
    count_x, count_y, cell_count, node_count = connectivity.shape
    ext_y = CELL_Y * P_SIZE + 1
    ext_z = CELL_Z * P_SIZE
    index_i = connectivity // (ext_y * ext_z)
    index_j = connectivity // ext_z % ext_y
    index_k = connectivity % ext_z
    place_x = jnp.arange(count_x, dtype=jnp.int32)[:, None, None, None]
    place_y = jnp.arange(count_y, dtype=jnp.int32)[None, :, None, None]
    global_x = (place_x * (CELL_X * P_SIZE) + index_i) % NX
    global_y = (place_y * (CELL_Y * P_SIZE) + index_j) % NY
    flat = (global_x * NY + global_y) * NZ + index_k
    return flat.reshape(count_x * count_y, cell_count * node_count).astype(jnp.int32)

def apply_hamiltonian(values, inv_mass, potential, cell_matrix, table):
    vec_width = values.shape[-1]
    scaled = (values * inv_mass[..., None]).astype(jnp.bfloat16).reshape(-1, vec_width)
    kinetic = cell_matrix.astype(jnp.float32)

    def add_domain(total, indices):
        picked = scaled[indices].astype(jnp.float32).reshape(CELLS_DEV, NC, vec_width)
        product = jnp.einsum('il,clw->ciw', kinetic, picked, precision=lax.Precision.HIGHEST)
        return (total.at[indices].add(product.reshape(-1, vec_width)), None)
    start = jnp.zeros((NX * NY * NZ, vec_width), jnp.float32)
    total, unused = lax.scan(add_domain, start, table)
    assembled = total.reshape(values.shape)
    return inv_mass[..., None] * assembled + potential[..., None] * values

def reference(vectors, resident, inv_mass, potential, cell_matrix, connectivity):
    table = node_table(connectivity)
    resident_rows = resident.reshape(-1, RES)
    norm_scale = 1.0 / jnp.sqrt(jnp.float32(NX * NY * NZ))
    results = []
    margins = []
    for block_id in range(BLOCKS):
        start = vectors[block_id].astype(jnp.float32)
        image = apply_hamiltonian(start, inv_mass, potential, cell_matrix, table)
        older = start
        current = (image - center_shift * start) / half_width
        for degree_id in range(1, DEGREE):
            image = apply_hamiltonian(current, inv_mass, potential, cell_matrix, table)
            newer = 2.0 * (image - center_shift * current) / half_width - older
            older = current
            current = newer
        results.append(current)
        rounded = current.astype(jnp.bfloat16).reshape(-1, V)
        inner = lax.dot_general(resident_rows, rounded, (((0,), (0,)), ((), ())), preferred_element_type=jnp.float32)
        margins.append(inner * norm_scale)
    return (jnp.stack(results), jnp.concatenate(margins, axis=1))
```

```python
import functools
import math

import jax
import jax.numpy as jnp
from jax import lax
from jax.experimental import pallas as pl
from jax.experimental.pallas import tpu as pltpu
from jax.sharding import PartitionSpec as P

DEGREE = 3
LANES = 128
SUB = 16
VMEM_LIMIT = 40 * 1024 * 1024

center_shift = 1.2
half_width = 2.0


def round_up(value, step):
    return -(-value // step) * step


class Sizes:
    def __init__(self, vectors, inv_mass, connectivity):
        self.blocks = vectors.shape[0]
        self.width = vectors.shape[-1]
        self.ex, self.ey, self.ez = inv_mass.shape
        self.cells, self.nodes = connectivity.shape[2:]
        self.n1 = round(self.nodes ** (1.0 / 3.0))
        self.p = self.n1 - 1
        self.cx, self.cy, self.cz = self.ex // self.p, self.ey // self.p, self.ez // self.p
        self.gx, self.gy, self.gz = self.ex + 1, self.ey + 1, self.ez
        self.main = self.n1 * self.n1 * self.p
        self.rows = round_up(self.nodes, SUB)
        self.depth = round_up(self.nodes, LANES)
        self.ext = (self.gx, self.gy, self.gz, self.width)
        self.own = (self.ex, self.ey, self.ez, self.width)

    def cell_origins(self):
        for a in range(self.cx):
            for b in range(self.cy):
                for c in range(self.cz):
                    yield a * self.p, b * self.p, c * self.p


def send(value, steps_x, steps_y):
    nx, ny = lax.axis_size("dx"), lax.axis_size("dy")
    pairs = [
        (a * ny + b, ((a + steps_x) % nx) * ny + (b + steps_y) % ny)
        for a in range(nx)
        for b in range(ny)
    ]
    return lax.ppermute(value, ("dx", "dy"), pairs)


def swap_pair(value, steps_y):
    if lax.axis_size("dx") == 2:
        return send(value, 1, steps_y)
    return jnp.stack([send(value[0], -1, steps_y), send(value[1], 1, steps_y)])


def order_kernel(index_ref, matrix_ref, out_ref):
    depth = matrix_ref.shape[0]
    rows = out_ref.shape[1]
    place = lax.broadcasted_iota(jnp.int32, (depth, depth), 0)
    pick = (place == index_ref[0]).astype(jnp.float32).astype(jnp.bfloat16)
    half = jnp.dot(pick[:rows], matrix_ref[...], preferred_element_type=jnp.float32)
    whole = lax.dot_general(
        half.astype(jnp.bfloat16), pick, (((1,), (1,)), ((), ())),
        preferred_element_type=jnp.float32,
    )
    out_ref[0] = whole.astype(jnp.bfloat16)


def ordered_matrices(sz, cell_matrix, connectivity):
    conn = connectivity.reshape(sz.cells, sz.nodes)
    origin = jnp.array(list(sz.cell_origins()), jnp.int32)
    li = conn // (sz.gy * sz.gz) - origin[:, :1]
    lj = conn // sz.gz % sz.gy - origin[:, 1:2]
    lk = (conn % sz.gz - origin[:, 2:] + sz.gz) % sz.gz
    column = li * sz.n1 + lj
    index = jnp.where(lk < sz.p, column * sz.p + lk, sz.main + column)
    pad = sz.depth - sz.nodes
    index = jnp.pad(index, ((0, 0), (0, pad)), constant_values=-1)
    index = index.reshape(sz.cells, 1, sz.depth)
    matrix = jnp.pad(cell_matrix, ((0, pad), (0, pad)))
    return pl.pallas_call(
        order_kernel,
        grid=(sz.cells,),
        in_specs=[
            pl.BlockSpec((1, 1, sz.depth), lambda c: (c, 0, 0)),
            pl.BlockSpec((sz.depth, sz.depth), lambda c: (0, 0)),
        ],
        out_specs=pl.BlockSpec((1, sz.rows, sz.depth), lambda c: (c, 0, 0)),
        out_shape=jax.ShapeDtypeStruct((sz.cells, sz.rows, sz.depth), jnp.bfloat16),
        compiler_params=pltpu.CompilerParams(vmem_limit_bytes=VMEM_LIMIT),
        cost_estimate=pl.CostEstimate(
            flops=4 * sz.cells * sz.depth**3, bytes_accessed=6 * sz.depth**2 * 2, transcendentals=0
        ),
        name="order_cells",
    )(index, matrix)


def cell_products(sz, u_ref, mat_ref, rhs_ref, edge_ref, acc_ref):
    n1, p, width = sz.n1, sz.p, sz.width
    flat = sz.gx * sz.gy * sz.gz
    u_flat, acc_flat = u_ref.reshape(flat, width), acc_ref.reshape(flat, width)
    acc_ref[...] = jnp.zeros_like(acc_ref)
    tail = sz.nodes // 8 * 8
    rhs_ref[tail:, :] = jnp.zeros((sz.depth - tail, width), jnp.float32)
    for cell, (x0, y0, z0) in enumerate(sz.cell_origins()):
        x1, y1, z1 = x0 + n1, y0 + n1, z0 + p
        wrap = z1 % sz.gz
        rhs_ref[: sz.main] = u_ref[x0:x1, y0:y1, z0:z1].reshape(sz.main, width)
        for i in range(n1):
            start = ((x0 + i) * sz.gy + y0) * sz.gz + wrap
            rhs_ref[sz.main + i * n1 : sz.main + (i + 1) * n1] = u_flat[
                pl.ds(start, n1, stride=sz.gz)
            ]
        product = jnp.dot(
            mat_ref[cell], rhs_ref[...].astype(jnp.bfloat16), preferred_element_type=jnp.float32
        )
        acc_ref[x0:x1, y0:y1, z0:z1] += product[: sz.main].reshape(n1, n1, p, width)
        edge_ref[...] = product[sz.main :]
        for i in range(n1):
            start = ((x0 + i) * sz.gy + y0) * sz.gz + wrap
            rows = pl.ds(start, n1, stride=sz.gz)
            acc_flat[rows] = acc_flat[rows] + edge_ref[i * n1 : (i + 1) * n1]


def write_messages(sz, acc_ref, face_x, low_y, high_y, low_d, high_d):
    last_x, last_y = sz.gx - 1, sz.gy - 1
    face_x[0] = acc_ref[0].astype(face_x.dtype)
    face_x[1] = acc_ref[last_x].astype(face_x.dtype)
    low_y[...] = acc_ref[:, 0].astype(low_y.dtype)
    high_y[...] = acc_ref[:, last_y].astype(high_y.dtype)
    low_d[0] = acc_ref[0, 0].astype(low_d.dtype)
    low_d[1] = acc_ref[last_x, 0].astype(low_d.dtype)
    high_d[0] = acc_ref[0, last_y].astype(high_d.dtype)
    high_d[1] = acc_ref[last_x, last_y].astype(high_d.dtype)


def summed_at(sz, i, j, acc_ref, face_x, low_y, high_y, low_d, high_d):
    total = acc_ref[i, j]
    end_x, end_y = sz.gx - 1, sz.gy - 1
    side = 1 if i == 0 else 0 if i == end_x else None
    if side is not None:
        total = total + face_x[side, j].astype(jnp.float32)
    if j == 0:
        total = total + high_y[i].astype(jnp.float32)
        if side is not None:
            total = total + high_d[side].astype(jnp.float32)
    if j == end_y:
        total = total + low_y[i].astype(jnp.float32)
        if side is not None:
            total = total + low_d[side].astype(jnp.float32)
    return total


def first_kernel(
    sz, block, vec_ref, gx_ref, gy_ref, gd_ref, inv_ref, mat_ref,
    x_ref, acc_ref, face_x, low_y, high_y, low_d, high_d, u_ref, rhs_ref, edge_ref,
):
    x_ref[: sz.ex, : sz.ey] = vec_ref[block]
    x_ref[sz.ex, : sz.ey] = gx_ref[block]
    x_ref[: sz.ex, sz.ey] = gy_ref[block]
    x_ref[sz.ex, sz.ey] = gd_ref[block]
    u_ref[...] = x_ref[...].astype(jnp.float32) * inv_ref[...]
    cell_products(sz, u_ref, mat_ref, rhs_ref, edge_ref, acc_ref)
    write_messages(sz, acc_ref, face_x, low_y, high_y, low_d, high_d)


def second_kernel(
    sz, x_ref, sum_ref, face_x_in, low_y_in, high_y_in, low_d_in, high_d_in, inv_ref, pot_ref, mat_ref,
    y_ref, acc_ref, face_x, low_y, high_y, low_d, high_d, u_ref, rhs_ref, edge_ref,
):
    for i in range(sz.gx):
        for j in range(sz.gy):
            total = summed_at(
                sz, i, j, sum_ref, face_x_in, low_y_in, high_y_in, low_d_in, high_d_in
            )
            old = x_ref[i, j].astype(jnp.float32)
            inv = inv_ref[i, j]
            image = inv * total + pot_ref[i, j] * old
            new = (image - center_shift * old) / half_width
            y_ref[i, j] = new
            u_ref[i, j] = inv * new
    cell_products(sz, u_ref, mat_ref, rhs_ref, edge_ref, acc_ref)
    write_messages(sz, acc_ref, face_x, low_y, high_y, low_d, high_d)


def third_kernel(
    sz, x_ref, y_ref, sum_ref, face_x_in, low_y_in, high_y_in, low_d_in, high_d_in,
    inv_ref, pot_ref, mat_ref,
    part_ref, face_x, high_y, high_d, new_ref, acc_ref, u_ref, rhs_ref, edge_ref,
):
    for i in range(sz.gx):
        for j in range(sz.gy):
            total = summed_at(
                sz, i, j, sum_ref, face_x_in, low_y_in, high_y_in, low_d_in, high_d_in
            )
            old = y_ref[i, j]
            inv = inv_ref[i, j]
            image = inv * total + pot_ref[i, j] * old
            new = 2.0 * (image - center_shift * old) / half_width - x_ref[i, j].astype(jnp.float32)
            new_ref[i, j] = new
            u_ref[i, j] = inv * new
    cell_products(sz, u_ref, mat_ref, rhs_ref, edge_ref, acc_ref)
    face_x[...] = acc_ref[sz.ex, : sz.ey].astype(face_x.dtype)
    high_y[...] = acc_ref[: sz.ex, sz.ey].astype(high_y.dtype)
    high_d[...] = acc_ref[sz.ex, sz.ey].astype(high_d.dtype)
    for i in range(sz.ex):
        for j in range(sz.ey):
            new = new_ref[i, j]
            image = inv_ref[i, j] * acc_ref[i, j] + pot_ref[i, j] * new
            part_ref[i, j] = 2.0 * (image - center_shift * new) / half_width - y_ref[i, j]


def last_kernel(sz, block, part_ref, face_x, high_y, high_d, inv_ref, *refs):
    out_ref, rounded_ref, value_ref, sem = refs[-4:]
    gain = 2.0 / half_width
    for i in range(sz.ex):
        for j in range(sz.ey):
            value = part_ref[i, j]
            more = None
            if i == 0:
                more = face_x[j].astype(jnp.float32)
            if j == 0:
                term = high_y[i].astype(jnp.float32)
                more = term if more is None else more + term
                if i == 0:
                    more = more + high_d[...].astype(jnp.float32)
            if more is not None:
                value = value + gain * (inv_ref[i, j] * more)
            value_ref[i, j] = value
            rounded_ref[i, j] = value.astype(jnp.bfloat16)
    copy = pltpu.make_async_copy(value_ref, out_ref.at[block], sem)
    copy.start()
    copy.wait()


def call(kernel, name, flops, out_shape, scratch, operands, specs=None, out_specs=None, aliases=None):
    size = sum(math.prod(s.shape) * jnp.dtype(s.dtype).itemsize for s in (*operands, *out_shape))
    whole = pl.BlockSpec(memory_space=pltpu.VMEM)
    return pl.pallas_call(
        kernel,
        in_specs=[whole] * len(operands) if specs is None else specs,
        out_specs=[whole] * len(out_shape) if out_specs is None else out_specs,
        out_shape=out_shape,
        scratch_shapes=scratch,
        input_output_aliases=aliases or {},
        compiler_params=pltpu.CompilerParams(vmem_limit_bytes=VMEM_LIMIT),
        cost_estimate=pl.CostEstimate(flops=flops, bytes_accessed=size, transcendentals=0),
        name=name,
    )(*operands)


def grow(own, from_x, from_y, from_d):
    wide = jnp.concatenate([own, from_x[..., None, :, :]], axis=-3)
    side = jnp.concatenate([from_y, from_d[..., None, :]], axis=-2)
    return jnp.concatenate([wide, side[..., None, :]], axis=-2)


def body(vectors, resident, inv_mass, potential, cell_matrix, connectivity):
    sz = Sizes(vectors, inv_mass, connectivity)
    bf16, f32 = jnp.bfloat16, jnp.float32
    nx, ny = lax.axis_size("dx"), lax.axis_size("dy")
    norm_scale = 1.0 / math.sqrt(sz.ex * sz.ey * sz.ez * nx * ny)
    ext, own, width = sz.ext, sz.own, sz.width

    fields = jnp.stack([inv_mass, potential])
    ghost_fields = (
        send(fields[:, 0], -1, 0), send(fields[:, :, 0], 0, -1), send(fields[:, 0, 0], -1, -1)
    )
    ghosts = (
        send(vectors[:, 0], -1, 0), send(vectors[:, :, 0], 0, -1), send(vectors[:, 0, 0], -1, -1)
    )
    matrices = ordered_matrices(sz, cell_matrix, connectivity)
    fields = grow(fields, *ghost_fields)
    inv_b = jnp.broadcast_to(fields[0][..., None], ext)
    pot_b = jnp.broadcast_to(fields[1][..., None], ext)

    def like(shape, dtype):
        return jax.ShapeDtypeStruct(shape, dtype)

    messages = [
        like((2,) + ext[1:], bf16),
        like((ext[0],) + ext[2:], bf16),
        like((ext[0],) + ext[2:], bf16),
        like((2,) + ext[2:], bf16),
        like((2,) + ext[2:], bf16),
    ]
    scratch = [
        pltpu.VMEM(ext, f32),
        pltpu.VMEM((sz.depth, width), f32),
        pltpu.VMEM((sz.rows - sz.main, width), f32),
    ]
    flops = 2 * sz.cells * sz.rows * sz.depth * width

    def exchange(face_x, low_y, high_y, low_d, high_d):
        return (
            swap_pair(face_x, 0), send(low_y, 0, -1), send(high_y, 0, 1),
            swap_pair(low_d, -1), swap_pair(high_d, 1),
        )

    whole = pl.BlockSpec(memory_space=pltpu.VMEM)
    filtered = None
    margins = []
    states = []
    for block in range(sz.blocks):
        x_ext, part, *sent = call(
            functools.partial(first_kernel, sz, block), "first", flops,
            [like(ext, bf16), like(ext, f32)] + messages, scratch,
            [vectors, *ghosts, inv_b, matrices],
        )
        states.append((x_ext, part, exchange(*sent)))
    for block in range(sz.blocks):
        x_ext, part, got = states[block]
        y1, part, *sent = call(
            functools.partial(second_kernel, sz), "second", flops,
            [like(ext, f32), like(ext, f32)] + messages, scratch,
            [x_ext, part, *got, inv_b, pot_b, matrices],
        )
        states[block] = (x_ext, y1, part, exchange(*sent))
    for block in range(sz.blocks):
        x_ext, y1, part, got = states[block]
        part, face_x, high_y, high_d = call(
            functools.partial(third_kernel, sz), "third", flops,
            [like(own, f32), like(own[1:], bf16), like((sz.ex,) + own[2:], bf16), like(own[2:], bf16)],
            [pltpu.VMEM(ext, f32), pltpu.VMEM(ext, f32)] + scratch,
            [x_ext, y1, part, *got, inv_b, pot_b, matrices],
        )
        states[block] = (part, send(face_x, 1, 0), send(high_y, 0, 1), send(high_d, 1, 1))
    for block in range(sz.blocks):
        part, face_x, high_y, high_d = states[block]
        operands = [part, face_x, high_y, high_d, inv_b]
        specs = [whole] * 5
        aliases = {}
        if filtered is not None:
            aliases = {5: 0}
            operands.append(filtered)
            specs.append(pl.BlockSpec(memory_space=pl.ANY))
        filtered, rounded = call(
            functools.partial(last_kernel, sz, block), "last", 0,
            [like((sz.blocks,) + own, f32), like(own, bf16)],
            [pltpu.VMEM(own, f32), pltpu.SemaphoreType.DMA], operands, specs,
            [pl.BlockSpec(memory_space=pl.ANY), whole], aliases,
        )
        local = lax.dot_general(
            resident.reshape(-1, resident.shape[-1]), rounded.reshape(-1, width),
            (((0,), (0,)), ((), ())), preferred_element_type=f32,
        )
        local = (local * norm_scale).astype(bf16).reshape(ny, -1, width)
        pieces = lax.all_to_all(local, "dy", 0, 0)
        mine = jnp.sum(pieces.astype(f32), axis=0)
        total = mine
        for step in range(1, nx):
            total = total + send(mine, step, 0)
        margins.append(total)
    return (filtered, jnp.concatenate(margins, axis=-1))


def solution(mesh):
    return jax.shard_map(
        body,
        mesh=mesh,
        in_specs=(
            P(None, "dx", "dy", None, None),
            P("dx", "dy", None, None),
            P("dx", "dy", None),
            P("dx", "dy", None),
            P(),
            P("dx", "dy", None, None),
        ),
        out_specs=(P(None, "dx", "dy", None, None), P("dy", None)),
        check_vma=False,
    )
```

```python
import functools
import math

import jax
import jax.numpy as jnp
from jax import lax
from jax.experimental import pallas as pl
from jax.experimental.pallas import tpu as pltpu
from jax.sharding import PartitionSpec as P

LANES = 128
SUB = 16
VMEM_LIMIT = 40 * 1024 * 1024

center_shift = 1.2
half_width = 2.0


def round_up(value, step):
    return -(-value // step) * step


class Sizes:
    def __init__(self, vectors, inv_mass, connectivity):
        self.blocks = vectors.shape[0]
        self.width = vectors.shape[-1]
        self.full = self.blocks * self.width
        self.ex, self.ey, self.ez = inv_mass.shape
        self.cells, self.nodes = connectivity.shape[2:]
        self.n1 = round(self.nodes ** (1.0 / 3.0))
        self.p = self.n1 - 1
        self.cx, self.cy, self.cz = self.ex // self.p, self.ey // self.p, self.ez // self.p
        self.gx, self.gy, self.gz = self.ex + 1, self.ey + 1, self.ez
        self.main = self.n1 * self.n1 * self.p
        self.rows = round_up(self.nodes, SUB)
        self.depth = round_up(self.nodes, LANES)
        self.ext = (self.blocks, self.gx, self.gy, self.gz, self.width)
        self.own = (self.blocks, self.ex, self.ey, self.ez, self.width)

    def cell_origins(self):
        for a in range(self.cx):
            for b in range(self.cy):
                for c in range(self.cz):
                    yield a * self.p, b * self.p, c * self.p


def send(value, steps_x, steps_y):
    nx, ny = lax.axis_size("dx"), lax.axis_size("dy")
    pairs = [
        (a * ny + b, ((a + steps_x) % nx) * ny + (b + steps_y) % ny)
        for a in range(nx)
        for b in range(ny)
    ]
    return lax.ppermute(value, ("dx", "dy"), pairs)


def swap_x(value):
    if lax.axis_size("dx") == 2:
        return send(value, 1, 0)
    return jnp.stack([send(value[0], -1, 0), send(value[1], 1, 0)])


def swap_y(near, far):
    ny = lax.axis_size("dy")
    near_pairs = [(b, b + 1 if b % 2 == 0 else b - 1) for b in range(ny)]
    far_pairs = [(b, (b - 1 if b % 2 == 0 else b + 1) % ny) for b in range(ny)]
    far = lax.ppermute(far, "dy", far_pairs)
    near = lax.ppermute(near, "dy", near_pairs)
    return near, far


def order_kernel(sz, origins, conn_ref, matrix_ref, out_ref):
    f32, bf16 = jnp.float32, jnp.bfloat16
    for cell, (x0, y0, z0) in enumerate(origins):
        conn = conn_ref[cell].astype(f32)
        li = jnp.floor((conn + 0.5) * (1.0 / (sz.gy * sz.gz)))
        rest = conn - li * (sz.gy * sz.gz)
        lj = jnp.floor((rest + 0.5) * (1.0 / sz.gz))
        lk = rest - lj * sz.gz - z0
        lk = jnp.where(lk < 0, lk + sz.gz, lk)
        column = (li - x0) * sz.n1 + (lj - y0)
        index = jnp.where(lk < sz.p, column * sz.p + lk, sz.main + column).astype(jnp.int32)
        place = lax.broadcasted_iota(jnp.int32, (sz.depth, sz.nodes), 0)
        pick = (place == index).astype(f32).astype(bf16)
        half = jnp.dot(pick[: sz.rows], matrix_ref[...], preferred_element_type=f32)
        whole = lax.dot_general(
            half.astype(bf16), pick, (((1,), (1,)), ((), ())), preferred_element_type=f32
        )
        out_ref[cell] = whole.astype(bf16)


def cell_products(sz, u_ref, mat_refs, rhs_ref, edge_ref, acc_ref):
    n1, p, width = sz.n1, sz.p, sz.width
    flat = sz.gx * sz.gy * sz.gz
    u_flat = u_ref.reshape(sz.blocks * flat, width)
    acc_flat = acc_ref.reshape(sz.blocks * flat, width)
    acc_ref[...] = jnp.zeros_like(acc_ref)
    tail = sz.nodes // 8 * 8
    rhs_ref[tail:, :] = jnp.zeros((sz.depth - tail, sz.full), jnp.float32)
    matrices = [ref.at[c] for ref in mat_refs for c in range(ref.shape[0])]
    for matrix, (x0, y0, z0) in zip(matrices, sz.cell_origins()):
        x1, y1, z1 = x0 + n1, y0 + n1, z0 + p
        wrap = z1 % sz.gz
        edges = []
        for b in range(sz.blocks):
            lanes = slice(b * width, (b + 1) * width)
            rhs_ref[: sz.main, lanes] = u_ref[b, x0:x1, y0:y1, z0:z1].reshape(sz.main, width)
            for i in range(n1):
                start = b * flat + ((x0 + i) * sz.gy + y0) * sz.gz + wrap
                edge = slice(i * n1, (i + 1) * n1)
                edges.append((pl.ds(start, n1, stride=sz.gz), edge, lanes))
        for rows, edge, lanes in edges:
            rhs_ref[sz.main + edge.start : sz.main + edge.stop, lanes] = u_flat[rows]
        product = jnp.dot(
            matrix[...], rhs_ref[...].astype(jnp.bfloat16), preferred_element_type=jnp.float32
        )
        for b in range(sz.blocks):
            lanes = slice(b * width, (b + 1) * width)
            acc_ref[b, x0:x1, y0:y1, z0:z1] += product[: sz.main, lanes].reshape(n1, n1, p, width)
        edge_ref[...] = product[sz.main :]
        for rows, edge, lanes in edges:
            acc_flat[rows] = acc_flat[rows] + edge_ref[edge, lanes]


def write_messages(sz, even, acc_ref, corner, face, side):
    end_x, end_y = sz.gx - 1, sz.gy - 1
    near = jnp.where(even, end_y, 0)
    for slot, j in enumerate((near, end_y - near)):
        for b in range(sz.blocks):
            corner[0, slot, b] = acc_ref[b, 0, j].astype(corner.dtype)
            corner[1, slot, b] = acc_ref[b, end_x, j].astype(corner.dtype)
            side[slot, b] = acc_ref[b, :, j]
    for b in range(sz.blocks):
        face[0, b] = acc_ref[b, 0, 1:end_y].astype(face.dtype)
        face[1, b] = acc_ref[b, end_x, 1:end_y].astype(face.dtype)


def side_kernel(sz, side_ref, corner_ref, near_ref, far_ref):
    for slot, out in enumerate((near_ref, far_ref)):
        for i in range(sz.gx):
            value = side_ref[slot, :, i]
            if i == 0:
                value = value + corner_ref[1, slot].astype(jnp.float32)
            if i == sz.gx - 1:
                value = value + corner_ref[0, slot].astype(jnp.float32)
            out[:, i] = value.astype(out.dtype)


def summed_at(sz, even, i, j, acc_ref, corner, face, near, far):
    f32 = jnp.float32
    total = acc_ref[:, i, j]
    end_x, end_y = sz.gx - 1, sz.gy - 1
    side = 1 if i == 0 else 0 if i == end_x else None
    if j in (0, end_y):
        is_near = even if j == end_y else jnp.logical_not(even)
        if side is not None:
            total = total + jnp.where(
                is_near, corner[side, 0].astype(f32), corner[side, 1].astype(f32)
            )
        total = total + jnp.where(is_near, near[:, i].astype(f32), far[:, i].astype(f32))
    elif side is not None:
        total = total + face[side, :, j - 1].astype(f32)
    return total


def first_kernel(
    sz, n_mat, even_ref, vec_ref, from_x, from_y, own_inv, own_pot, *refs
):
    mats = refs[:n_mat]
    x_ref, inv_ref, pot_ref, acc_ref, corner, face, side, u_ref, rhs_ref, edge_ref = refs[n_mat:]
    even = even_ref[0] == 0
    inv_ref[: sz.ex, : sz.ey] = own_inv[...]
    pot_ref[: sz.ex, : sz.ey] = own_pot[...]

    def fields(parts):
        parts = parts.astype(jnp.float32)
        for at, ref in enumerate((inv_ref, pot_ref)):
            total = sum(parts[..., 3 * at + k : 3 * at + k + 1] for k in range(3))
            yield ref, jnp.broadcast_to(total, parts.shape)

    for j in range(sz.ey):
        for ref, value in fields(from_x[sz.blocks, j]):
            ref[sz.ex, j] = value
    for i in range(sz.gx):
        for ref, value in fields(from_y[sz.blocks, i]):
            ref[i, sz.ey] = value
    x_ref[:, : sz.ex, : sz.ey] = vec_ref[...]
    x_ref[:, sz.ex, : sz.ey] = from_x[: sz.blocks]
    x_ref[:, :, sz.ey] = from_y[: sz.blocks]
    for i in range(sz.gx):
        for j in range(sz.gy):
            u_ref[:, i, j] = x_ref[:, i, j].astype(jnp.float32) * inv_ref[i, j]
    cell_products(sz, u_ref, mats, rhs_ref, edge_ref, acc_ref)
    write_messages(sz, even, acc_ref, corner, face, side)


def second_kernel(
    sz, n_mat, even_ref, x_ref, sum_ref, corner_in, face_in, near_in, far_in, inv_ref, pot_ref, *refs
):
    mats = refs[:n_mat]
    y_ref, acc_ref, corner, face, side, u_ref, rhs_ref, edge_ref = refs[n_mat:]
    even = even_ref[0] == 0
    for i in range(sz.gx):
        for j in range(sz.gy):
            total = summed_at(sz, even, i, j, sum_ref, corner_in, face_in, near_in, far_in)
            old = x_ref[:, i, j].astype(jnp.float32)
            inv = inv_ref[i, j]
            image = inv * total + pot_ref[i, j] * old
            new = (image - center_shift * old) / half_width
            y_ref[:, i, j] = new
            u_ref[:, i, j] = inv * new
    cell_products(sz, u_ref, mats, rhs_ref, edge_ref, acc_ref)
    write_messages(sz, even, acc_ref, corner, face, side)


def third_kernel(
    sz, n_mat, even_ref, x_ref, y_ref, sum_ref, corner_in, face_in, near_in, far_in, inv_ref, pot_ref,
    *refs,
):
    mats = refs[:n_mat]
    part_ref, corner, face, side, new_ref, acc_ref, u_ref, rhs_ref, edge_ref = refs[n_mat:]
    even = even_ref[0] == 0
    for i in range(sz.gx):
        for j in range(sz.gy):
            total = summed_at(sz, even, i, j, sum_ref, corner_in, face_in, near_in, far_in)
            old = y_ref[:, i, j]
            inv = inv_ref[i, j]
            image = inv * total + pot_ref[i, j] * old
            new = 2.0 * (image - center_shift * old) / half_width - x_ref[:, i, j].astype(jnp.float32)
            new_ref[:, i, j] = new
            u_ref[:, i, j] = inv * new
    cell_products(sz, u_ref, mats, rhs_ref, edge_ref, acc_ref)
    corner[...] = acc_ref[:, sz.ex, sz.ey].astype(corner.dtype)
    face[...] = acc_ref[:, sz.ex, : sz.ey].astype(face.dtype)
    side[...] = acc_ref[:, : sz.ex, sz.ey].astype(side.dtype)
    for i in range(sz.ex):
        for j in range(sz.ey):
            new = new_ref[:, i, j]
            image = inv_ref[i, j] * acc_ref[:, i, j] + pot_ref[i, j] * new
            part_ref[:, i, j] = 2.0 * (image - center_shift * new) / half_width - y_ref[:, i, j]


def last_side_kernel(sz, side_ref, corner_ref, out_ref):
    for i in range(sz.ex):
        value = side_ref[:, i]
        if i == 0:
            value = value + corner_ref[...].astype(jnp.float32)
        out_ref[:, i] = value.astype(out_ref.dtype)


def last_kernel(sz, part_ref, face, side, inv_ref, out_ref, rounded_ref):
    gain = 2.0 / half_width
    for i in range(sz.ex):
        for j in range(sz.ey):
            value = part_ref[:, i, j]
            more = None
            if i == 0:
                more = face[:, j].astype(jnp.float32)
            if j == 0:
                term = side[:, i].astype(jnp.float32)
                more = term if more is None else more + term
            if more is not None:
                value = value + gain * (inv_ref[i, j] * more)
            for b in range(sz.blocks):
                lanes = slice(b * sz.width, (b + 1) * sz.width)
                rounded_ref[i, j, :, lanes] = value[b].astype(jnp.bfloat16)
            out_ref[:, i, j] = value


def call(kernel, name, flops, out_shape, scratch, operands, scalar_first=False):
    size = sum(math.prod(s.shape) * jnp.dtype(s.dtype).itemsize for s in (*operands, *out_shape))
    whole = pl.BlockSpec(memory_space=pltpu.VMEM)
    specs = [whole] * len(operands)
    if scalar_first:
        specs[0] = pl.BlockSpec(memory_space=pltpu.SMEM)
    return pl.pallas_call(
        kernel,
        in_specs=specs,
        out_specs=[whole] * len(out_shape),
        out_shape=out_shape,
        scratch_shapes=scratch,
        compiler_params=pltpu.CompilerParams(vmem_limit_bytes=VMEM_LIMIT),
        cost_estimate=pl.CostEstimate(flops=flops, bytes_accessed=size, transcendentals=0),
        name=name,
    )(*operands)


def field_parts(fields, width):
    parts = []
    for at in range(fields.shape[0]):
        rest = fields[at]
        for _ in range(3):
            part = lax.reduce_precision(rest, 8, 7)
            rest = rest - part
            parts.append(part.astype(jnp.bfloat16))
    stacked = jnp.stack(parts, axis=-1)
    pads = [(0, 0)] * (stacked.ndim - 1) + [(0, width - len(parts))]
    return jnp.pad(stacked, pads)[None]


def body(vectors, resident, inv_mass, potential, cell_matrix, connectivity):
    sz = Sizes(vectors, inv_mass, connectivity)
    bf16, f32 = jnp.bfloat16, jnp.float32
    nx, ny = lax.axis_size("dx"), lax.axis_size("dy")
    norm_scale = 1.0 / math.sqrt(sz.ex * sz.ey * sz.ez * nx * ny)
    ext, own, full, width = sz.ext, sz.own, sz.full, sz.width

    def like(shape, dtype):
        return jax.ShapeDtypeStruct(shape, dtype)

    fields = jnp.stack([inv_mass, potential])
    to_x = jnp.concatenate([vectors[:, 0], field_parts(fields[:, 0], width)])
    from_x = send(to_x, -1, 0)
    to_y = jnp.concatenate([vectors[:, :, 0], field_parts(fields[:, :, 0], width)])
    to_y = jnp.concatenate([to_y, from_x[:, None, 0]], axis=1)
    from_y = send(to_y, 0, -1)

    conn = connectivity.reshape(sz.cells, 1, sz.nodes)
    origins = list(sz.cell_origins())
    halves = 2 if sz.cells % 2 == 0 else 1
    step = sz.cells // halves
    matrices = []
    for at in range(0, sz.cells, step):
        matrices += call(
            functools.partial(order_kernel, sz, origins[at : at + step]), "order_cells",
            4 * step * sz.depth**3, [like((step, sz.rows, sz.depth), bf16)], [],
            [conn[at : at + step], cell_matrix],
        )
    own_inv = jnp.broadcast_to(inv_mass[..., None], inv_mass.shape + (width,))
    own_pot = jnp.broadcast_to(potential[..., None], inv_mass.shape + (width,))
    parity = jnp.reshape(lax.axis_index("dy") % 2, (1,)).astype(jnp.int32)

    messages = [
        like((2, 2, sz.blocks, sz.ez, width), bf16),
        like((2, sz.blocks, sz.gy - 2, sz.ez, width), bf16),
        like((2, sz.blocks, sz.gx, sz.ez, width), f32),
    ]
    scratch = [
        pltpu.VMEM(ext, f32),
        pltpu.VMEM((sz.depth, full), f32),
        pltpu.VMEM((sz.rows - sz.main, full), f32),
    ]
    flops = 2 * sz.cells * sz.rows * sz.depth * full
    field_ext = like(ext[1:], f32)

    def exchange(corner, face, side):
        corner = swap_x(corner)
        face = swap_x(face)
        near, far = call(
            functools.partial(side_kernel, sz), "sides", 0,
            [like((sz.blocks, sz.gx, sz.ez, width), bf16)] * 2, [], [side, corner],
        )
        return (corner, face, *swap_y(near, far))

    x_ext, inv_b, pot_b, part, *sent = call(
        functools.partial(first_kernel, sz, len(matrices)), "first", flops,
        [like(ext, bf16), field_ext, field_ext, like(ext, f32)] + messages, scratch,
        [parity, vectors, from_x, from_y, own_inv, own_pot, *matrices], True,
    )
    y1, part, *sent = call(
        functools.partial(second_kernel, sz, len(matrices)), "second", flops,
        [like(ext, f32), like(ext, f32)] + messages, scratch,
        [parity, x_ext, part, *exchange(*sent), inv_b, pot_b, *matrices], True,
    )
    part, corner, face, side = call(
        functools.partial(third_kernel, sz, len(matrices)), "third", flops,
        [
            like(own, f32), like((sz.blocks, sz.ez, width), bf16),
            like((sz.blocks, sz.ey, sz.ez, width), bf16), like((sz.blocks, sz.ex, sz.ez, width), f32),
        ],
        [pltpu.VMEM(ext, f32), pltpu.VMEM(ext, f32)] + scratch,
        [parity, x_ext, y1, part, *exchange(*sent), inv_b, pot_b, *matrices], True,
    )
    corner = send(corner, 1, 0)
    face = send(face, 1, 0)
    (side,) = call(
        functools.partial(last_side_kernel, sz), "last_side", 0,
        [like((sz.blocks, sz.ex, sz.ez, width), bf16)], [], [side, corner],
    )
    side = send(side, 0, 1)
    filtered, rounded = call(
        functools.partial(last_kernel, sz), "last", 0,
        [like(own, f32), like(own[1:4] + (full,), bf16)], [],
        [part, face, side, inv_b],
    )
    local = lax.dot_general(
        resident.reshape(-1, resident.shape[-1]), rounded.reshape(-1, full),
        (((0,), (0,)), ((), ())), preferred_element_type=f32,
    )
    local = (local * norm_scale).astype(bf16).reshape(ny, -1, full)
    pieces = lax.all_to_all(local, "dy", 0, 0)
    mine = jnp.sum(pieces.astype(f32), axis=0)
    total = mine
    for steps in range(1, nx):
        total = total + send(mine, steps, 0)
    return (filtered, total)


def solution(mesh):
    return jax.shard_map(
        body,
        mesh=mesh,
        in_specs=(
            P(None, "dx", "dy", None, None),
            P("dx", "dy", None, None),
            P("dx", "dy", None),
            P("dx", "dy", None),
            P(),
            P("dx", "dy", None, None),
        ),
        out_specs=(P(None, "dx", "dy", None, None), P("dy", None)),
        check_vma=False,
    )
```

```python
import functools
import math

import jax
import jax.numpy as jnp
from jax import lax
from jax.experimental import pallas as pl
from jax.experimental.pallas import tpu as pltpu
from jax.sharding import PartitionSpec as P

LANES = 128
SUB = 16
VMEM_LIMIT = 28 * 1024 * 1024

center_shift = 1.2
half_width = 2.0


def round_up(value, step):
    return -(-value // step) * step


class Sizes:
    def __init__(self, vectors, inv_mass, connectivity):
        self.blocks = vectors.shape[0]
        self.width = vectors.shape[-1]
        self.full = self.blocks * self.width
        self.ex, self.ey, self.ez = inv_mass.shape
        self.cells, self.nodes = connectivity.shape[2:]
        self.n1 = round(self.nodes ** (1.0 / 3.0))
        self.p = self.n1 - 1
        self.cx, self.cy, self.cz = self.ex // self.p, self.ey // self.p, self.ez // self.p
        self.gx, self.gy, self.gz = self.ex + 1, self.ey + 1, self.ez
        self.main = self.n1 * self.n1 * self.p
        self.rows = round_up(self.nodes, SUB)
        self.depth = round_up(self.nodes, LANES)
        self.ext = (self.blocks, self.gx, self.gy, self.gz, self.width)
        self.own = (self.blocks, self.ex, self.ey, self.ez, self.width)

    def cell_origins(self):
        for a in range(self.cx):
            for b in range(self.cy):
                for c in range(self.cz):
                    yield a * self.p, b * self.p, c * self.p


def send(value, steps_x, steps_y):
    nx, ny = lax.axis_size("dx"), lax.axis_size("dy")
    pairs = [
        (a * ny + b, ((a + steps_x) % nx) * ny + (b + steps_y) % ny)
        for a in range(nx)
        for b in range(ny)
    ]
    return lax.ppermute(value, ("dx", "dy"), pairs)


def swap_x(value):
    if lax.axis_size("dx") == 2:
        return send(value, 1, 0)
    return jnp.stack([send(value[0], -1, 0), send(value[1], 1, 0)])


def swap_y(near, far):
    ny = lax.axis_size("dy")
    near_pairs = [(b, b + 1 if b % 2 == 0 else b - 1) for b in range(ny)]
    far_pairs = [(b, (b - 1 if b % 2 == 0 else b + 1) % ny) for b in range(ny)]
    far = lax.ppermute(far, "dy", far_pairs)
    near = lax.ppermute(near, "dy", near_pairs)
    return near, far


def order_kernel(sz, first, count, conn_ref, matrix_ref, out_ref):
    f32, bf16 = jnp.float32, jnp.bfloat16
    for slot in range(count):
        cell = first + slot
        x0, y0, z0 = list(sz.cell_origins())[cell]
        conn = conn_ref[cell : cell + 1, :].astype(f32)
        li = jnp.floor((conn + 0.5) * (1.0 / (sz.gy * sz.gz)))
        rest = conn - li * (sz.gy * sz.gz)
        lj = jnp.floor((rest + 0.5) * (1.0 / sz.gz))
        lk = rest - lj * sz.gz - z0
        lk = jnp.where(lk < 0, lk + sz.gz, lk)
        column = (li - x0) * sz.n1 + (lj - y0)
        index = jnp.where(lk < sz.p, column * sz.p + lk, sz.main + column).astype(jnp.int32)
        place = lax.broadcasted_iota(jnp.int32, (sz.depth, sz.nodes), 0)
        pick = (place == index).astype(f32).astype(bf16)
        half = jnp.dot(pick[: sz.rows], matrix_ref[...], preferred_element_type=f32)
        whole = lax.dot_general(
            half.astype(bf16), pick, (((1,), (1,)), ((), ())), preferred_element_type=f32
        )
        out_ref[slot] = whole.astype(bf16)


def cell_products(sz, u_ref, mat_refs, rhs_ref, edge_ref, acc_ref):
    n1, p, width = sz.n1, sz.p, sz.width
    flat = sz.gx * sz.gy * sz.gz
    u_flat = u_ref.reshape(sz.blocks * flat, width)
    acc_flat = acc_ref.reshape(sz.blocks * flat, width)
    acc_ref[...] = jnp.zeros_like(acc_ref)
    tail = sz.nodes // 8 * 8
    rhs_ref[tail:, :] = jnp.zeros((sz.depth - tail, sz.full), jnp.float32)
    matrices = [ref.at[c] for ref in mat_refs for c in range(ref.shape[0])]
    for matrix, (x0, y0, z0) in zip(matrices, sz.cell_origins()):
        x1, y1, z1 = x0 + n1, y0 + n1, z0 + p
        wrap = z1 % sz.gz
        edges = []
        for b in range(sz.blocks):
            lanes = slice(b * width, (b + 1) * width)
            rhs_ref[: sz.main, lanes] = u_ref[b, x0:x1, y0:y1, z0:z1].reshape(sz.main, width)
            for i in range(n1):
                start = b * flat + ((x0 + i) * sz.gy + y0) * sz.gz + wrap
                edge = slice(i * n1, (i + 1) * n1)
                edges.append((pl.ds(start, n1, stride=sz.gz), edge, lanes))
        for rows, edge, lanes in edges:
            rhs_ref[sz.main + edge.start : sz.main + edge.stop, lanes] = u_flat[rows]
        product = jnp.dot(
            matrix[...], rhs_ref[...].astype(jnp.bfloat16), preferred_element_type=jnp.float32
        )
        for b in range(sz.blocks):
            lanes = slice(b * width, (b + 1) * width)
            acc_ref[b, x0:x1, y0:y1, z0:z1] += product[: sz.main, lanes].reshape(n1, n1, p, width)
        edge_ref[...] = product[sz.main :]
        for rows, edge, lanes in edges:
            acc_flat[rows] = acc_flat[rows] + edge_ref[edge, lanes]


def write_messages(sz, even, acc_ref, corner, face, side):
    end_x, end_y = sz.gx - 1, sz.gy - 1
    near = jnp.where(even, end_y, 0)
    for slot, j in enumerate((near, end_y - near)):
        for b in range(sz.blocks):
            corner[0, slot, b] = acc_ref[b, 0, j].astype(corner.dtype)
            corner[1, slot, b] = acc_ref[b, end_x, j].astype(corner.dtype)
            side[slot, b] = acc_ref[b, :, j]
    for b in range(sz.blocks):
        face[0, b] = acc_ref[b, 0, 1:end_y].astype(face.dtype)
        face[1, b] = acc_ref[b, end_x, 1:end_y].astype(face.dtype)


def side_kernel(sz, side_ref, corner_ref, face_in, near_ref, far_ref, face_out):
    del face_in, face_out
    for slot, out in enumerate((near_ref, far_ref)):
        for i in range(sz.gx):
            value = side_ref[slot, :, i]
            if i == 0:
                value = value + corner_ref[1, slot].astype(jnp.float32)
            if i == sz.gx - 1:
                value = value + corner_ref[0, slot].astype(jnp.float32)
            out[:, i] = value.astype(out.dtype)


def summed_at(sz, even, i, j, acc_ref, corner, face, near, far):
    f32 = jnp.float32
    total = acc_ref[:, i, j]
    end_x, end_y = sz.gx - 1, sz.gy - 1
    side = 1 if i == 0 else 0 if i == end_x else None
    if j in (0, end_y):
        is_near = even if j == end_y else jnp.logical_not(even)
        if side is not None:
            total = total + jnp.where(
                is_near, corner[side, 0].astype(f32), corner[side, 1].astype(f32)
            )
        total = total + jnp.where(is_near, near[:, i].astype(f32), far[:, i].astype(f32))
    elif side is not None:
        total = total + face[side, :, j - 1].astype(f32)
    return total


def field_row(inv, pot):
    lane = lax.broadcasted_iota(jnp.int32, inv.shape, inv.ndim - 1)
    row = jnp.zeros_like(inv)
    for at, rest in enumerate((inv, pot)):
        for k in range(3):
            part = rest.astype(jnp.bfloat16).astype(jnp.float32)
            rest = rest - part
            row = jnp.where(lane == 3 * at + k, part, row)
    return row.astype(jnp.bfloat16)


def pack_x_kernel(sz, vec_ref, inv_ref, pot_ref, out_ref):
    out_ref[: sz.blocks] = vec_ref[...]
    out_ref[sz.blocks] = field_row(inv_ref[...], pot_ref[...])


def pack_y_kernel(sz, vec_ref, inv_ref, pot_ref, from_x, out_ref):
    out_ref[: sz.blocks, : sz.ex] = vec_ref[:, :, 0]
    out_ref[sz.blocks, : sz.ex] = field_row(inv_ref[:, 0], pot_ref[:, 0])
    out_ref[:, sz.ex] = from_x[:, 0]


def first_kernel(
    sz, n_mat, even_ref, vec_ref, from_x, from_y, own_inv, own_pot, *refs
):
    mats = refs[:n_mat]
    x_ref, inv_ref, pot_ref, acc_ref, corner, face, side, u_ref, rhs_ref, edge_ref = refs[n_mat:]
    even = even_ref[0] == 0
    inv_ref[: sz.ex, : sz.ey] = own_inv[...]
    pot_ref[: sz.ex, : sz.ey] = own_pot[...]

    def fields(parts):
        parts = parts.astype(jnp.float32)
        for at, ref in enumerate((inv_ref, pot_ref)):
            total = sum(parts[..., 3 * at + k : 3 * at + k + 1] for k in range(3))
            yield ref, jnp.broadcast_to(total, parts.shape)

    for j in range(sz.ey):
        for ref, value in fields(from_x[sz.blocks, j]):
            ref[sz.ex, j] = value
    for i in range(sz.gx):
        for ref, value in fields(from_y[sz.blocks, i]):
            ref[i, sz.ey] = value
    x_ref[:, : sz.ex, : sz.ey] = vec_ref[...]
    x_ref[:, sz.ex, : sz.ey] = from_x[: sz.blocks]
    x_ref[:, :, sz.ey] = from_y[: sz.blocks]
    for i in range(sz.gx):
        for j in range(sz.gy):
            u_ref[:, i, j] = x_ref[:, i, j].astype(jnp.float32) * inv_ref[i, j]
    cell_products(sz, u_ref, mats, rhs_ref, edge_ref, acc_ref)
    write_messages(sz, even, acc_ref, corner, face, side)


def second_kernel(
    sz, n_mat, even_ref, x_ref, sum_ref, corner_in, face_in, near_in, far_in, inv_ref, pot_ref, *refs
):
    mats = refs[:n_mat]
    y_ref, acc_ref, corner, face, side, u_ref, rhs_ref, edge_ref = refs[n_mat:]
    even = even_ref[0] == 0
    for i in range(sz.gx):
        for j in range(sz.gy):
            total = summed_at(sz, even, i, j, sum_ref, corner_in, face_in, near_in, far_in)
            old = x_ref[:, i, j].astype(jnp.float32)
            inv = inv_ref[i, j]
            image = inv * total + pot_ref[i, j] * old
            new = (image - center_shift * old) / half_width
            y_ref[:, i, j] = new
            u_ref[:, i, j] = inv * new
    cell_products(sz, u_ref, mats, rhs_ref, edge_ref, acc_ref)
    write_messages(sz, even, acc_ref, corner, face, side)


def third_kernel(
    sz, n_mat, even_ref, x_ref, y_ref, sum_ref, corner_in, face_in, near_in, far_in, inv_ref, pot_ref,
    *refs,
):
    mats = refs[:n_mat]
    part_ref, corner, face, side, new_ref, acc_ref, u_ref, rhs_ref, edge_ref = refs[n_mat:]
    even = even_ref[0] == 0
    for i in range(sz.gx):
        for j in range(sz.gy):
            total = summed_at(sz, even, i, j, sum_ref, corner_in, face_in, near_in, far_in)
            old = y_ref[:, i, j]
            inv = inv_ref[i, j]
            image = inv * total + pot_ref[i, j] * old
            new = 2.0 * (image - center_shift * old) / half_width - x_ref[:, i, j].astype(jnp.float32)
            new_ref[:, i, j] = new
            u_ref[:, i, j] = inv * new
    cell_products(sz, u_ref, mats, rhs_ref, edge_ref, acc_ref)
    corner[...] = acc_ref[:, sz.ex, sz.ey].astype(corner.dtype)
    face[...] = acc_ref[:, sz.ex, : sz.ey].astype(face.dtype)
    side[...] = acc_ref[:, : sz.ex, sz.ey].astype(side.dtype)
    for i in range(sz.ex):
        for j in range(sz.ey):
            new = new_ref[:, i, j]
            image = inv_ref[i, j] * acc_ref[:, i, j] + pot_ref[i, j] * new
            part_ref[:, i, j] = 2.0 * (image - center_shift * new) / half_width - y_ref[:, i, j]


def last_side_kernel(sz, side_ref, corner_ref, face_in, out_ref, face_out):
    del face_in, face_out
    for i in range(sz.ex):
        value = side_ref[:, i]
        if i == 0:
            value = value + corner_ref[...].astype(jnp.float32)
        out_ref[:, i] = value.astype(out_ref.dtype)


def last_kernel(sz, part_ref, face, side, inv_ref, out_ref, rounded_ref):
    gain = 2.0 / half_width
    for i in range(sz.ex):
        for j in range(sz.ey):
            value = part_ref[:, i, j]
            more = None
            if i == 0:
                more = face[:, j].astype(jnp.float32)
            if j == 0:
                term = side[:, i].astype(jnp.float32)
                more = term if more is None else more + term
            if more is not None:
                value = value + gain * (inv_ref[i, j] * more)
            for b in range(sz.blocks):
                lanes = slice(b * sz.width, (b + 1) * sz.width)
                rounded_ref[i, j, :, lanes] = value[b].astype(jnp.bfloat16)
            out_ref[:, i, j] = value


def call(kernel, name, flops, out_shape, scratch, operands, scalar_first=False, aliases=None):
    out_shape = [jax.ShapeDtypeStruct(s.shape, s.dtype) for s in out_shape]
    size = sum(math.prod(s.shape) * jnp.dtype(s.dtype).itemsize for s in (*operands, *out_shape))
    whole = pl.BlockSpec(memory_space=pltpu.VMEM)
    specs = [whole] * len(operands)
    if scalar_first:
        specs[0] = pl.BlockSpec(memory_space=pltpu.SMEM)
    return pl.pallas_call(
        kernel,
        in_specs=specs,
        out_specs=[whole] * len(out_shape),
        out_shape=out_shape,
        scratch_shapes=scratch,
        input_output_aliases=aliases or {},
        compiler_params=pltpu.CompilerParams(vmem_limit_bytes=VMEM_LIMIT),
        cost_estimate=pl.CostEstimate(flops=flops, bytes_accessed=size, transcendentals=0),
        name=name,
    )(*operands)


def body(vectors, resident, inv_mass, potential, cell_matrix, connectivity):
    sz = Sizes(vectors, inv_mass, connectivity)
    bf16, f32 = jnp.bfloat16, jnp.float32
    nx, ny = lax.axis_size("dx"), lax.axis_size("dy")
    norm_scale = 1.0 / math.sqrt(sz.ex * sz.ey * sz.ez * nx * ny)
    ext, own, full, width = sz.ext, sz.own, sz.full, sz.width

    def like(shape, dtype):
        return jax.ShapeDtypeStruct(shape, dtype)

    own_inv = jnp.broadcast_to(inv_mass[..., None], inv_mass.shape + (width,))
    own_pot = jnp.broadcast_to(potential[..., None], inv_mass.shape + (width,))
    (to_x,) = call(
        functools.partial(pack_x_kernel, sz), "pack_x", 0,
        [like((sz.blocks + 1, sz.ey, sz.ez, width), bf16)], [],
        [vectors[:, 0], own_inv[0], own_pot[0]],
    )
    from_x = send(to_x, -1, 0)
    (to_y,) = call(
        functools.partial(pack_y_kernel, sz), "pack_y", 0,
        [like((sz.blocks + 1, sz.gx, sz.ez, width), bf16)], [], [vectors, own_inv, own_pot, from_x],
    )
    from_y = send(to_y, 0, -1)

    conn = connectivity.reshape(sz.cells, sz.nodes)
    halves = 2 if sz.cells % 2 == 0 else 1
    step = sz.cells // halves
    matrices = []
    for at in range(0, sz.cells, step):
        matrices += call(
            functools.partial(order_kernel, sz, at, step), "order_cells",
            4 * step * sz.depth**3, [like((step, sz.rows, sz.depth), bf16)], [],
            [conn, cell_matrix],
        )
    parity = jnp.reshape(lax.axis_index("dy") % 2, (1,)).astype(jnp.int32)

    messages = [
        like((2, 2, sz.blocks, sz.ez, width), bf16),
        like((2, sz.blocks, sz.gy - 2, sz.ez, width), bf16),
        like((2, sz.blocks, sz.gx, sz.ez, width), f32),
    ]
    scratch = [
        pltpu.VMEM(ext, f32),
        pltpu.VMEM((sz.depth, full), f32),
        pltpu.VMEM((sz.rows - sz.main, full), f32),
    ]
    flops = 2 * sz.cells * sz.rows * sz.depth * full
    field_ext = like(ext[1:], f32)

    def exchange(corner, face, side):
        corner = swap_x(corner)
        near, far, face = call(
            functools.partial(side_kernel, sz), "sides", 0,
            [like((sz.blocks, sz.gx, sz.ez, width), bf16)] * 2 + [face], [], [side, corner, face],
            aliases={2: 2},
        )
        face = swap_x(face)
        return (corner, face, *swap_y(near, far))

    x_ext, inv_b, pot_b, part, *sent = call(
        functools.partial(first_kernel, sz, len(matrices)), "first", flops,
        [like(ext, bf16), field_ext, field_ext, like(ext, f32)] + messages, scratch,
        [parity, vectors, from_x, from_y, own_inv, own_pot, *matrices], True,
    )
    y1, part, *sent = call(
        functools.partial(second_kernel, sz, len(matrices)), "second", flops,
        [like(ext, f32), like(ext, f32)] + messages, scratch,
        [parity, x_ext, part, *exchange(*sent), inv_b, pot_b, *matrices], True,
    )
    part, corner, face, side = call(
        functools.partial(third_kernel, sz, len(matrices)), "third", flops,
        [
            like(own, f32), like((sz.blocks, sz.ez, width), bf16),
            like((sz.blocks, sz.ey, sz.ez, width), bf16), like((sz.blocks, sz.ex, sz.ez, width), f32),
        ],
        [pltpu.VMEM(ext, f32), pltpu.VMEM(ext, f32)] + scratch,
        [parity, x_ext, y1, part, *exchange(*sent), inv_b, pot_b, *matrices], True,
    )
    corner = send(corner, 1, 0)
    side, face = call(
        functools.partial(last_side_kernel, sz), "last_side", 0,
        [like((sz.blocks, sz.ex, sz.ez, width), bf16), face], [], [side, corner, face],
        aliases={2: 1},
    )
    face = send(face, 1, 0)
    side = send(side, 0, 1)
    filtered, rounded = call(
        functools.partial(last_kernel, sz), "last", 0,
        [like(own, f32), like(own[1:4] + (full,), bf16)], [],
        [part, face, side, inv_b],
    )
    local = lax.dot_general(
        resident.reshape(-1, resident.shape[-1]), rounded.reshape(-1, full),
        (((0,), (0,)), ((), ())), preferred_element_type=f32,
    )
    local = (local * norm_scale).astype(bf16).reshape(ny, -1, full)
    pieces = lax.all_to_all(local, "dy", 0, 0)
    mine = jnp.sum(pieces.astype(f32), axis=0)
    total = mine
    for steps in range(1, nx):
        total = total + send(mine, steps, 0)
    return (filtered, total)


def solution(mesh):
    return jax.shard_map(
        body,
        mesh=mesh,
        in_specs=(
            P(None, "dx", "dy", None, None),
            P("dx", "dy", None, None),
            P("dx", "dy", None),
            P("dx", "dy", None),
            P(),
            P("dx", "dy", None, None),
        ),
        out_specs=(P(None, "dx", "dy", None, None), P("dy", None)),
        check_vma=False,
    )
```

```python
import functools
import math

import jax
import jax.numpy as jnp
from jax import lax
from jax.experimental import pallas as pl
from jax.experimental.pallas import tpu as pltpu
from jax.sharding import PartitionSpec as P

LANES = 128
SUB = 16
VMEM_LIMIT = 16 * 1024 * 1024

center_shift = 1.2
half_width = 2.0


def round_up(value, step):
    return -(-value // step) * step


class Sizes:
    def __init__(self, vectors, resident, inv_mass, connectivity):
        self.blocks = vectors.shape[0]
        self.width = vectors.shape[-1]
        self.full = self.blocks * self.width
        self.groups = resident.shape[-1] // LANES
        self.ex, self.ey, self.ez = inv_mass.shape
        self.cells, self.nodes = connectivity.shape[2:]
        self.n1 = round(self.nodes ** (1.0 / 3.0))
        self.p = self.n1 - 1
        self.cx, self.cy, self.cz = self.ex // self.p, self.ey // self.p, self.ez // self.p
        self.gx, self.gy, self.gz = self.ex + 1, self.ey + 1, self.ez
        self.main = self.n1 * self.n1 * self.p
        self.rows = round_up(self.nodes, SUB)
        self.depth = round_up(self.nodes, LANES)
        self.ext = (self.blocks, self.gx, self.gy, self.gz, self.width)
        self.own = (self.blocks, self.ex, self.ey, self.ez, self.width)

    def cell_origins(self):
        for a in range(self.cx):
            for b in range(self.cy):
                for c in range(self.cz):
                    yield a * self.p, b * self.p, c * self.p


def send(value, steps_x, steps_y):
    nx, ny = lax.axis_size("dx"), lax.axis_size("dy")
    pairs = [
        (a * ny + b, ((a + steps_x) % nx) * ny + (b + steps_y) % ny)
        for a in range(nx)
        for b in range(ny)
    ]
    return lax.ppermute(value, ("dx", "dy"), pairs)


def swap_x(value):
    if lax.axis_size("dx") == 2:
        return send(value, 1, 0)
    return jnp.stack([send(value[0], -1, 0), send(value[1], 1, 0)])


def swap_y(near, far):
    ny = lax.axis_size("dy")
    near_pairs = [(b, b + 1 if b % 2 == 0 else b - 1) for b in range(ny)]
    far_pairs = [(b, (b - 1 if b % 2 == 0 else b + 1) % ny) for b in range(ny)]
    far = lax.ppermute(far, "dy", far_pairs)
    near = lax.ppermute(near, "dy", near_pairs)
    return near, far


def order_kernel(sz, first, count, conn_ref, matrix_ref, out_ref):
    f32, bf16 = jnp.float32, jnp.bfloat16
    for slot in range(count):
        cell = first + slot
        x0, y0, z0 = list(sz.cell_origins())[cell]
        conn = conn_ref[cell : cell + 1, :].astype(f32)
        li = jnp.floor((conn + 0.5) * (1.0 / (sz.gy * sz.gz)))
        rest = conn - li * (sz.gy * sz.gz)
        lj = jnp.floor((rest + 0.5) * (1.0 / sz.gz))
        lk = rest - lj * sz.gz - z0
        lk = jnp.where(lk < 0, lk + sz.gz, lk)
        column = (li - x0) * sz.n1 + (lj - y0)
        index = jnp.where(lk < sz.p, column * sz.p + lk, sz.main + column).astype(jnp.int32)
        place = lax.broadcasted_iota(jnp.int32, (sz.depth, sz.nodes), 0)
        pick = (place == index).astype(f32).astype(bf16)
        half = jnp.dot(pick[: sz.rows], matrix_ref[...], preferred_element_type=f32)
        whole = lax.dot_general(
            half.astype(bf16), pick, (((1,), (1,)), ((), ())), preferred_element_type=f32
        )
        out_ref[slot] = whole.astype(bf16)


def cell_products(sz, u_ref, mat_refs, rhs_ref, edge_ref, acc_ref):
    n1, p, width = sz.n1, sz.p, sz.width
    flat = sz.gx * sz.gy * sz.gz
    u_flat = u_ref.reshape(sz.blocks * flat, width)
    acc_flat = acc_ref.reshape(sz.blocks * flat, width)
    acc_ref[...] = jnp.zeros_like(acc_ref)
    tail = sz.nodes // 8 * 8
    rhs_ref[tail:, :] = jnp.zeros((sz.depth - tail, sz.full), jnp.float32)
    matrices = [ref.at[c] for ref in mat_refs for c in range(ref.shape[0])]
    for matrix, (x0, y0, z0) in zip(matrices, sz.cell_origins()):
        x1, y1, z1 = x0 + n1, y0 + n1, z0 + p
        wrap = z1 % sz.gz
        edges = []
        for b in range(sz.blocks):
            lanes = slice(b * width, (b + 1) * width)
            rhs_ref[: sz.main, lanes] = u_ref[b, x0:x1, y0:y1, z0:z1].reshape(sz.main, width)
            for i in range(n1):
                start = b * flat + ((x0 + i) * sz.gy + y0) * sz.gz + wrap
                edge = slice(i * n1, (i + 1) * n1)
                edges.append((pl.ds(start, n1, stride=sz.gz), edge, lanes))
        for rows, edge, lanes in edges:
            rhs_ref[sz.main + edge.start : sz.main + edge.stop, lanes] = u_flat[rows]
        product = jnp.dot(
            matrix[...], rhs_ref[...].astype(jnp.bfloat16), preferred_element_type=jnp.float32
        )
        for b in range(sz.blocks):
            lanes = slice(b * width, (b + 1) * width)
            acc_ref[b, x0:x1, y0:y1, z0:z1] += product[: sz.main, lanes].reshape(n1, n1, p, width)
        edge_ref[...] = product[sz.main :]
        for rows, edge, lanes in edges:
            acc_flat[rows] = acc_flat[rows] + edge_ref[edge, lanes]


def write_messages(sz, even, acc_ref, corner, face, side):
    end_x, end_y = sz.gx - 1, sz.gy - 1
    near = jnp.where(even, end_y, 0)
    for slot, j in enumerate((near, end_y - near)):
        for b in range(sz.blocks):
            corner[0, slot * sz.blocks + b] = acc_ref[b, 0, j].astype(corner.dtype)
            corner[1, slot * sz.blocks + b] = acc_ref[b, end_x, j].astype(corner.dtype)
            side[slot, b] = acc_ref[b, :, j]
    for b in range(sz.blocks):
        face[0, b] = acc_ref[b, 0, 1:end_y].astype(face.dtype)
        face[1, b] = acc_ref[b, end_x, 1:end_y].astype(face.dtype)


def side_kernel(sz, side_ref, corner_ref, face_in, near_ref, far_ref, face_out):
    del face_in, face_out
    for slot, out in enumerate((near_ref, far_ref)):
        pair = slice(slot * sz.blocks, (slot + 1) * sz.blocks)
        for i in range(sz.gx):
            value = side_ref[slot, :, i]
            if i == 0:
                value = value + corner_ref[1, pair].astype(jnp.float32)
            if i == sz.gx - 1:
                value = value + corner_ref[0, pair].astype(jnp.float32)
            out[:, i] = value.astype(out.dtype)


def summed_at(sz, even, i, j, acc_ref, corner, face, near, far):
    f32 = jnp.float32
    total = acc_ref[:, i, j]
    end_x, end_y = sz.gx - 1, sz.gy - 1
    side = 1 if i == 0 else 0 if i == end_x else None
    if j in (0, end_y):
        is_near = even if j == end_y else jnp.logical_not(even)
        if side is not None:
            total = total + jnp.where(
                is_near, corner[side, : sz.blocks].astype(f32),
                corner[side, sz.blocks : 2 * sz.blocks].astype(f32),
            )
        total = total + jnp.where(is_near, near[:, i].astype(f32), far[:, i].astype(f32))
    elif side is not None:
        total = total + face[side, :, j - 1].astype(f32)
    return total


def field_row(inv, pot):
    lane = lax.broadcasted_iota(jnp.int32, inv.shape, inv.ndim - 1)
    row = jnp.zeros_like(inv)
    for at, rest in enumerate((inv, pot)):
        for k in range(3):
            part = rest.astype(jnp.bfloat16).astype(jnp.float32)
            rest = rest - part
            row = jnp.where(lane == 3 * at + k, part, row)
    return row.astype(jnp.bfloat16)


def field_rows(sz, inv, pot, count):
    inv, pot = inv.T, pot.T
    shape = (sz.ez, sz.width)
    for at in range(count):
        yield at, field_row(
            jnp.broadcast_to(inv[:, at : at + 1], shape), jnp.broadcast_to(pot[:, at : at + 1], shape)
        )


def pack_x_kernel(
    sz, vec_hbm, inv_hbm, pot_hbm, mat_hbm, conn_hbm, out_ref, mat_ref, conn_ref, field_ref, sems
):
    loads = [
        pltpu.make_async_copy(mat_hbm, mat_ref, sems.at[2 + sz.blocks]),
        pltpu.make_async_copy(conn_hbm, conn_ref, sems.at[3 + sz.blocks]),
    ]
    copies = [
        pltpu.make_async_copy(inv_hbm.at[0], field_ref.at[0], sems.at[0]),
        pltpu.make_async_copy(pot_hbm.at[0], field_ref.at[1], sems.at[1]),
    ]
    for b in range(sz.blocks):
        copies.append(pltpu.make_async_copy(vec_hbm.at[b, 0], out_ref.at[b], sems.at[2 + b]))
    copies += loads
    for copy in copies:
        copy.start()
    for copy in copies[:2]:
        copy.wait()
    for j, row in field_rows(sz, field_ref[0], field_ref[1], sz.ey):
        out_ref[sz.blocks, j] = row
    for copy in copies[2:]:
        copy.wait()


def pack_y_kernel(sz, vec_hbm, res_hbm, inv_hbm, pot_hbm, from_x, out_ref, res_ref, field_ref, sems):
    base = (sz.blocks + 1) * sz.gx
    copies = [
        pltpu.make_async_copy(inv_hbm.at[:, 0], field_ref.at[0], sems.at[0]),
        pltpu.make_async_copy(pot_hbm.at[:, 0], field_ref.at[1], sems.at[1]),
        pltpu.make_async_copy(res_hbm.at[0], res_ref, sems.at[2]),
    ]
    for b in range(sz.blocks):
        rows = pl.ds(b * sz.gx, sz.ex)
        copies.append(pltpu.make_async_copy(vec_hbm.at[b, :, 0], out_ref.at[rows], sems.at[3 + b]))
    for g in range(sz.groups):
        rows = pl.ds(base + g * sz.ex, sz.ex)
        lanes = pl.ds(g * LANES, LANES)
        copies.append(
            pltpu.make_async_copy(
                res_hbm.at[:, 0, :, lanes], out_ref.at[rows], sems.at[3 + sz.blocks + g]
            )
        )
    for copy in copies:
        copy.start()
    for copy in copies[:2]:
        copy.wait()
    for i, row in field_rows(sz, field_ref[0], field_ref[1], sz.ex):
        out_ref[sz.blocks * sz.gx + i] = row
    for b in range(sz.blocks + 1):
        out_ref[b * sz.gx + sz.ex] = from_x[b, 0]
    for copy in copies[2:]:
        copy.wait()


def resident_rows_kernel(sz, from_y, corner, out_ref):
    base = (sz.blocks + 1) * sz.gx
    for g in range(sz.groups):
        lanes = slice(g * LANES, (g + 1) * LANES)
        for i in range(sz.ex):
            out_ref[i, :, lanes] = from_y[base + g * sz.ex + i]
        out_ref[sz.ex, :, lanes] = corner[0, 2 * sz.blocks + g]


def first_kernel(
    sz, n_mat, even_ref, vec_ref, from_x, from_y, own_inv, own_pot, res_in, *refs
):
    del res_in
    mats = refs[:n_mat]
    res_out, x_ref, inv_ref, pot_ref, acc_ref, corner, face, side = refs[n_mat : n_mat + 8]
    u_ref, rhs_ref, edge_ref = refs[n_mat + 8 :]
    del res_out
    even = even_ref[0] == 0
    inv_ref[: sz.ex, : sz.ey] = own_inv[...]
    pot_ref[: sz.ex, : sz.ey] = own_pot[...]

    def fields(parts):
        parts = parts.astype(jnp.float32)
        for at, ref in enumerate((inv_ref, pot_ref)):
            total = sum(parts[..., 3 * at + k : 3 * at + k + 1] for k in range(3))
            yield ref, jnp.broadcast_to(total, parts.shape)

    for j in range(sz.ey):
        for ref, value in fields(from_x[sz.blocks, j]):
            ref[sz.ex, j] = value
    for i in range(sz.gx):
        for ref, value in fields(from_y[sz.blocks * sz.gx + i]):
            ref[i, sz.ey] = value
    x_ref[:, : sz.ex, : sz.ey] = vec_ref[...]
    x_ref[:, sz.ex, : sz.ey] = from_x[: sz.blocks]
    for b in range(sz.blocks):
        x_ref[b, :, sz.ey] = from_y[b * sz.gx : (b + 1) * sz.gx]
    for i in range(sz.gx):
        for j in range(sz.gy):
            u_ref[:, i, j] = x_ref[:, i, j].astype(jnp.float32) * inv_ref[i, j]
    cell_products(sz, u_ref, mats, rhs_ref, edge_ref, acc_ref)
    write_messages(sz, even, acc_ref, corner, face, side)
    base = (sz.blocks + 1) * sz.gx
    for g in range(sz.groups):
        corner[0, 2 * sz.blocks + g] = from_y[base + g * sz.ex]
        corner[1, 2 * sz.blocks + g] = jnp.zeros((sz.ez, sz.width), corner.dtype)


def second_kernel(
    sz, n_mat, even_ref, x_ref, sum_ref, corner_in, face_in, near_in, far_in, inv_ref, pot_ref, *refs
):
    mats = refs[:n_mat]
    y_ref, acc_ref, corner, face, side, u_ref, rhs_ref, edge_ref = refs[n_mat:]
    even = even_ref[0] == 0
    for i in range(sz.gx):
        for j in range(sz.gy):
            total = summed_at(sz, even, i, j, sum_ref, corner_in, face_in, near_in, far_in)
            old = x_ref[:, i, j].astype(jnp.float32)
            inv = inv_ref[i, j]
            image = inv * total + pot_ref[i, j] * old
            new = (image - center_shift * old) / half_width
            y_ref[:, i, j] = new
            u_ref[:, i, j] = inv * new
    cell_products(sz, u_ref, mats, rhs_ref, edge_ref, acc_ref)
    write_messages(sz, even, acc_ref, corner, face, side)


def put_lanes(sz, ref, at, value):
    for b in range(sz.blocks):
        ref[at, :, b * sz.width : (b + 1) * sz.width] = value[b]


def third_kernel(
    sz, n_mat, even_ref, x_ref, y_ref, sum_ref, corner_in, face_in, near_in, far_in, inv_ref, pot_ref,
    *refs,
):
    mats = refs[:n_mat]
    part_ref, corner, face, side, own_rows, face_rows, side_rows = refs[n_mat : n_mat + 7]
    new_ref, acc_ref, u_ref, rhs_ref, edge_ref = refs[n_mat + 7 :]
    even = even_ref[0] == 0
    for i in range(sz.gx):
        for j in range(sz.gy):
            total = summed_at(sz, even, i, j, sum_ref, corner_in, face_in, near_in, far_in)
            old = y_ref[:, i, j]
            inv = inv_ref[i, j]
            image = inv * total + pot_ref[i, j] * old
            new = 2.0 * (image - center_shift * old) / half_width - x_ref[:, i, j].astype(jnp.float32)
            new_ref[:, i, j] = new
            u_ref[:, i, j] = inv * new
    cell_products(sz, u_ref, mats, rhs_ref, edge_ref, acc_ref)
    gain = 2.0 / half_width
    for i in range(sz.gx):
        for j in range(sz.gy):
            if i == sz.ex or j == sz.ey:
                value = gain * (inv_ref[i, j] * acc_ref[:, i, j])
                rounded = value.astype(face.dtype)
                if j == sz.ey:
                    put_lanes(sz, side_rows, i, rounded)
                    if i == sz.ex:
                        corner[...] = rounded
                    else:
                        side[:, i] = value
                else:
                    put_lanes(sz, face_rows, j, rounded)
                    face[:, j] = rounded
            else:
                new = new_ref[:, i, j]
                image = inv_ref[i, j] * acc_ref[:, i, j] + pot_ref[i, j] * new
                value = 2.0 * (image - center_shift * new) / half_width - y_ref[:, i, j]
                part_ref[:, i, j] = value
                put_lanes(sz, own_rows, i * sz.ey + j, value.astype(face.dtype))


def last_side_kernel(sz, side_ref, corner_ref, face_in, out_ref, face_out):
    del face_in, face_out
    for i in range(sz.ex):
        value = side_ref[:, i]
        if i == 0:
            value = value + corner_ref[...].astype(jnp.float32)
        out_ref[:, i] = value.astype(out_ref.dtype)


def last_kernel(sz, part_ref, face, side, out_ref):
    for i in range(sz.ex):
        for j in range(sz.ey):
            value = part_ref[:, i, j]
            more = None
            if i == 0:
                more = face[:, j].astype(jnp.float32)
            if j == 0:
                term = side[:, i].astype(jnp.float32)
                more = term if more is None else more + term
            if more is not None:
                value = value + more
            out_ref[:, i, j] = value


def call(kernel, name, flops, out_shape, scratch, operands, scalar_first=False, aliases=None,
         hbm=0):
    out_shape = [jax.ShapeDtypeStruct(s.shape, s.dtype) for s in out_shape]
    size = sum(math.prod(s.shape) * jnp.dtype(s.dtype).itemsize for s in (*operands, *out_shape))
    whole = pl.BlockSpec(memory_space=pltpu.VMEM)
    specs = [pl.BlockSpec(memory_space=pltpu.HBM)] * hbm + [whole] * (len(operands) - hbm)
    if scalar_first:
        specs[0] = pl.BlockSpec(memory_space=pltpu.SMEM)
    operands = [pltpu.with_memory_space_constraint(a, pltpu.HBM) for a in operands[:hbm]] + list(
        operands[hbm:]
    )
    return pl.pallas_call(
        kernel,
        in_specs=specs,
        out_specs=[whole] * len(out_shape),
        out_shape=out_shape,
        scratch_shapes=scratch,
        input_output_aliases=aliases or {},
        compiler_params=pltpu.CompilerParams(vmem_limit_bytes=VMEM_LIMIT),
        cost_estimate=pl.CostEstimate(flops=flops, bytes_accessed=size, transcendentals=0),
        name=name,
    )(*operands)


def body(vectors, resident, inv_mass, potential, cell_matrix, connectivity):
    sz = Sizes(vectors, resident, inv_mass, connectivity)
    bf16, f32 = jnp.bfloat16, jnp.float32
    nx, ny = lax.axis_size("dx"), lax.axis_size("dy")
    norm_scale = 1.0 / math.sqrt(sz.ex * sz.ey * sz.ez * nx * ny)
    ext, own, full, width = sz.ext, sz.own, sz.full, sz.width

    def like(shape, dtype):
        return jax.ShapeDtypeStruct(shape, dtype)

    own_inv = jnp.broadcast_to(inv_mass[..., None], inv_mass.shape + (width,))
    own_pot = jnp.broadcast_to(potential[..., None], inv_mass.shape + (width,))
    conn = connectivity.reshape(sz.cells, sz.nodes)
    to_x, cell_matrix, conn = call(
        functools.partial(pack_x_kernel, sz), "pack_x", 0,
        [like((sz.blocks + 1, sz.ey, sz.ez, width), bf16), cell_matrix, conn],
        [pltpu.VMEM((2, sz.ey, sz.ez), f32), pltpu.SemaphoreType.DMA((4 + sz.blocks,))],
        [vectors, inv_mass, potential, cell_matrix, conn], hbm=5,
    )
    from_x = send(to_x, -1, 0)
    to_y, res_face = call(
        functools.partial(pack_y_kernel, sz), "pack_y", 0,
        [
            like(((sz.blocks + 1) * sz.gx + sz.groups * sz.ex, sz.ez, width), bf16),
            like(resident.shape[1:], bf16),
        ],
        [
            pltpu.VMEM((2, sz.ex, sz.ez), f32),
            pltpu.SemaphoreType.DMA((3 + sz.blocks + sz.groups,)),
        ],
        [vectors, resident, inv_mass, potential, from_x], hbm=4,
    )
    from_y = send(to_y, 0, -1)
    res_x = send(res_face, -1, 0)

    halves = 2 if sz.cells % 2 == 0 else 1
    step = sz.cells // halves
    matrices = []
    for at in range(0, sz.cells, step):
        matrices += call(
            functools.partial(order_kernel, sz, at, step), "order_cells",
            4 * step * sz.depth**3, [like((step, sz.rows, sz.depth), bf16)], [],
            [conn, cell_matrix],
        )
    parity = jnp.reshape(lax.axis_index("dy") % 2, (1,)).astype(jnp.int32)

    messages = [
        like((2, 2 * sz.blocks, sz.ez, width), bf16),
        like((2, sz.blocks, sz.gy - 2, sz.ez, width), bf16),
        like((2, sz.blocks, sz.gx, sz.ez, width), f32),
    ]
    scratch = [
        pltpu.VMEM(ext, f32),
        pltpu.VMEM((sz.depth, full), f32),
        pltpu.VMEM((sz.rows - sz.main, full), f32),
    ]
    flops = 2 * sz.cells * sz.rows * sz.depth * full
    field_ext = like(ext[1:], f32)

    def exchange(corner, face, side):
        corner = swap_x(corner)
        near, far, face = call(
            functools.partial(side_kernel, sz), "sides", 0,
            [like((sz.blocks, sz.gx, sz.ez, width), bf16)] * 2 + [face], [], [side, corner, face],
            aliases={2: 2},
        )
        face = swap_x(face)
        return (corner, face, *swap_y(near, far))

    first_corner = like((2, 2 * sz.blocks + sz.groups, sz.ez, width), bf16)
    res_x, x_ext, inv_b, pot_b, part, *sent = call(
        functools.partial(first_kernel, sz, len(matrices)), "first", flops,
        [res_x, like(ext, bf16), field_ext, field_ext, like(ext, f32), first_corner] + messages[1:],
        scratch, [parity, vectors, from_x, from_y, own_inv, own_pot, res_x, *matrices], True,
        aliases={6: 0},
    )
    got = exchange(*sent)
    (res_y,) = call(
        functools.partial(resident_rows_kernel, sz), "resident_rows", 0,
        [like((sz.gx,) + resident.shape[2:], bf16)], [], [from_y, got[0]],
    )
    y1, part, *sent = call(
        functools.partial(second_kernel, sz, len(matrices)), "second", flops,
        [like(ext, f32), like(ext, f32)] + messages, scratch,
        [parity, x_ext, part, *got, inv_b, pot_b, *matrices], True,
    )
    part, corner, face, side, *rows = call(
        functools.partial(third_kernel, sz, len(matrices)), "third", flops,
        [
            like(own, f32), like((sz.blocks, sz.ez, width), bf16),
            like((sz.blocks, sz.ey, sz.ez, width), bf16), like((sz.blocks, sz.ex, sz.ez, width), f32),
            like((sz.ex * sz.ey, sz.ez, full), bf16), like((sz.ey, sz.ez, full), bf16),
            like((sz.gx, sz.ez, full), bf16),
        ],
        [pltpu.VMEM(ext, f32), pltpu.VMEM(ext, f32)] + scratch,
        [parity, x_ext, y1, part, *exchange(*sent), inv_b, pot_b, *matrices], True,
    )
    local = sum(
        lax.dot_general(
            many.reshape(-1, many.shape[-1]), few.reshape(-1, full), (((0,), (0,)), ((), ())),
            preferred_element_type=f32,
        )
        for many, few in zip((resident, res_x, res_y), rows)
    )
    local = (local * norm_scale).astype(bf16).reshape(ny, -1, full)
    pieces = lax.all_to_all(local, "dy", 0, 0)
    mine = jnp.sum(pieces.astype(f32), axis=0)
    total = mine
    for steps in range(1, nx):
        total = total + send(mine, steps, 0)
    corner = send(corner, 1, 0)
    side, face = call(
        functools.partial(last_side_kernel, sz), "last_side", 0,
        [like((sz.blocks, sz.ex, sz.ez, width), bf16), face], [], [side, corner, face],
        aliases={2: 1},
    )
    face = send(face, 1, 0)
    side = send(side, 0, 1)
    (filtered,) = call(
        functools.partial(last_kernel, sz), "last", 0, [like(own, f32)], [], [part, face, side]
    )
    return (filtered, total)


def solution(mesh):
    return jax.shard_map(
        body,
        mesh=mesh,
        in_specs=(
            P(None, "dx", "dy", None, None),
            P("dx", "dy", None, None),
            P("dx", "dy", None),
            P("dx", "dy", None),
            P(),
            P("dx", "dy", None, None),
        ),
        out_specs=(P(None, "dx", "dy", None, None), P("dy", None)),
        check_vma=False,
    )
```

```python
import functools
import math

import jax
import jax.numpy as jnp
from jax import lax
from jax.experimental import pallas as pl
from jax.experimental.pallas import tpu as pltpu
from jax.sharding import PartitionSpec as P

LANES = 128
SUB = 16
VMEM_LIMIT = 16 * 1024 * 1024

center_shift = 1.2
half_width = 2.0
gain = 2.0 / half_width

f32, bf16 = jnp.float32, jnp.bfloat16


def round_up(value, step):
    return -(-value // step) * step


class Sizes:
    def __init__(self, vectors, resident, inv_mass, connectivity):
        self.blocks = vectors.shape[0]
        self.width = vectors.shape[-1]
        self.full = self.blocks * self.width
        self.groups = resident.shape[-1] // LANES
        self.ex, self.ey, self.ez = inv_mass.shape
        self.cells, self.nodes = connectivity.shape[2:]
        self.n1 = round(self.nodes ** (1.0 / 3.0))
        self.p = self.n1 - 1
        self.cx, self.cy, self.cz = self.ex // self.p, self.ey // self.p, self.ez // self.p
        self.gx, self.gy, self.gz = self.ex + 1, self.ey + 1, self.ez
        self.edge = (self.blocks, self.ez, self.width)
        self.origins = [
            (a * self.p, b * self.p, c * self.p)
            for a in range(self.cx)
            for b in range(self.cy)
            for c in range(self.cz)
        ]
        self.most = max(len(self.cell_corners(cell)) for cell in range(self.cells))
        self.base = round_up(self.most * self.n1, 8)
        plain = self.n1 * self.n1 - min(len(self.cell_corners(cell)) for cell in range(self.cells))
        self.tail = self.base + plain * self.p
        self.rows = round_up(self.tail + plain, SUB)
        self.depth = round_up(self.rows, LANES)
        self.own_edges = self.ex * self.ey
        self.edges = round_up(self.own_edges + self.ey + self.gx, LANES // self.ez)

    def corner(self, i, j):
        if i in (0, self.ex) and j in (0, self.ey):
            return 2 * (i // self.ex) + j // self.ey
        return None

    def cell_corners(self, cell):
        x0, y0, _ = self.origins[cell]
        return [
            (i, j)
            for i in range(self.n1)
            for j in range(self.n1)
            if self.corner(x0 + i, y0 + j) is not None
        ]

    def runs(self, cell):
        corners = self.cell_corners(cell)
        place = 0
        for i in range(self.n1):
            js = [j for j in range(self.n1) if (i, j) not in corners]
            while js:
                count = 1
                while count < len(js) and js[count] == js[0] + count:
                    count += 1
                yield place, i, js[0], count
                place += count
                js = js[count:]


def send(value, steps_x, steps_y):
    nx, ny = lax.axis_size("dx"), lax.axis_size("dy")
    pairs = [
        (a * ny + b, ((a + steps_x) % nx) * ny + (b + steps_y) % ny)
        for a in range(nx)
        for b in range(ny)
    ]
    return lax.ppermute(value, ("dx", "dy"), pairs)


def swap_x(value):
    if lax.axis_size("dx") == 2:
        return send(value, 1, 0)
    return jnp.stack([send(value[0], -1, 0), send(value[1], 1, 0)])


def swap_y(near, far):
    ny = lax.axis_size("dy")
    near_pairs = [(b, b + 1 if b % 2 == 0 else b - 1) for b in range(ny)]
    far_pairs = [(b, (b - 1 if b % 2 == 0 else b + 1) % ny) for b in range(ny)]
    far = lax.ppermute(far, "dy", far_pairs)
    near = lax.ppermute(near, "dy", near_pairs)
    return near, far


def order_kernel(sz, first, count, conn_ref, matrix_ref, out_ref):
    for slot in range(count):
        cell = first + slot
        x0, y0, z0 = sz.origins[cell]
        conn = conn_ref[cell : cell + 1, :].astype(f32)
        li = jnp.floor((conn + 0.5) * (1.0 / (sz.gy * sz.gz)))
        rest = conn - li * (sz.gy * sz.gz)
        lj = jnp.floor((rest + 0.5) * (1.0 / sz.gz))
        lk = rest - lj * sz.gz - z0
        lk = jnp.where(lk < 0, lk + sz.gz, lk)
        column = (li - x0) * sz.n1 + (lj - y0)
        corners = [i * sz.n1 + j for i, j in sz.cell_corners(cell)]
        place = column
        for at in corners:
            place = place - jnp.where(column > at, 1.0, 0.0)
        index = jnp.where(lk < sz.p, sz.base + place * sz.p + lk, sz.tail + place)
        for rank, at in enumerate(corners):
            special = jnp.where(lk < sz.p, rank * sz.p + lk, len(corners) * sz.p + rank)
            index = jnp.where(column == at, special, index)
        index = index.astype(jnp.int32)
        row = lax.broadcasted_iota(jnp.int32, (sz.depth, sz.nodes), 0)
        pick = (row == index).astype(f32).astype(bf16)
        half = jnp.dot(pick[: sz.rows], matrix_ref[...], preferred_element_type=f32)
        whole = lax.dot_general(
            half.astype(bf16), pick, (((1,), (1,)), ((), ())), preferred_element_type=f32
        )
        out_ref[slot] = whole.astype(bf16)


def field_row(inv, pot):
    lane = lax.broadcasted_iota(jnp.int32, inv.shape, inv.ndim - 1)
    row = jnp.zeros_like(inv)
    for at, rest in enumerate((inv, pot)):
        for k in range(3):
            part = rest.astype(bf16).astype(f32)
            rest = rest - part
            row = jnp.where(lane == 3 * at + k, part, row)
    return row.astype(bf16)


def field_rows(sz, inv, pot, count):
    inv, pot = inv.T, pot.T
    shape = (sz.ez, sz.width)
    for at in range(count):
        yield at, field_row(
            jnp.broadcast_to(inv[:, at : at + 1], shape), jnp.broadcast_to(pot[:, at : at + 1], shape)
        )


def fields_of(row):
    row = row.astype(f32)
    return [
        jnp.broadcast_to(sum(row[:, 3 * at + k : 3 * at + k + 1] for k in range(3)), row.shape)
        for at in range(2)
    ]


def pack_kernel(
    sz, vec_hbm, res_hbm, inv_hbm, pot_hbm, mat_hbm, conn_hbm,
    to_x, to_y, mat_ref, conn_ref, at_x, at_y, sems,
):
    slabs = sz.blocks + 1
    pairs = [
        (inv_hbm.at[0], at_x.at[0]), (pot_hbm.at[0], at_x.at[1]),
        (inv_hbm.at[:, 0], at_y.at[0]), (pot_hbm.at[:, 0], at_y.at[1]),
    ]
    for b in range(sz.blocks):
        pairs.append((vec_hbm.at[b, 0], to_x.at[pl.ds(b * sz.ey, sz.ey)]))
        pairs.append((vec_hbm.at[b, :, 0], to_y.at[pl.ds(b * sz.ex, sz.ex)]))
    for g in range(sz.groups):
        lanes = pl.ds(g * LANES, LANES)
        pairs.append((res_hbm.at[0, :, :, lanes], to_x.at[pl.ds((slabs + g) * sz.ey, sz.ey)]))
        pairs.append((res_hbm.at[:, 0, :, lanes], to_y.at[pl.ds((slabs + g) * sz.ex, sz.ex)]))
    pairs += [(mat_hbm, mat_ref), (conn_hbm, conn_ref)]
    copies = [pltpu.make_async_copy(a, b, sems.at[k]) for k, (a, b) in enumerate(pairs)]
    for copy in copies:
        copy.start()
    for copy in copies[:4]:
        copy.wait()
    for j, row in field_rows(sz, at_x[0], at_x[1], sz.ey):
        to_x[sz.blocks * sz.ey + j] = row
    for i, row in field_rows(sz, at_y[0], at_y[1], sz.ex):
        to_y[sz.blocks * sz.ex + i] = row
    for copy in copies[4:]:
        copy.wait()


def ghost_corner_kernel(sz, from_y, out_ref):
    for part in range(out_ref.shape[0]):
        out_ref[part] = from_y[part * sz.ex]


def turn_kernel(sz, res_ref, from_x, from_y, corner, out_ref):
    slabs = sz.blocks + 1
    own = sz.own_edges * sz.ez
    for g in range(sz.groups):
        lanes = slice(g * LANES, (g + 1) * LANES)
        out_ref[lanes, :own] = res_ref[:, lanes].T
        ghost_x = from_x[(slabs + g) * sz.ey : (slabs + g + 1) * sz.ey]
        ghost_y = from_y[(slabs + g) * sz.ex : (slabs + g + 1) * sz.ex]
        rest = sz.edges - sz.own_edges - sz.ey - sz.gx
        parts = [ghost_x, ghost_y, corner[slabs + g : slabs + g + 1]]
        if rest:
            parts.append(jnp.zeros((rest, sz.ez, LANES), bf16))
        ghosts = jnp.concatenate(parts, axis=0)
        out_ref[lanes, own:] = ghosts.reshape(-1, LANES).T


class Nodes:
    def __init__(self, sz, vec, from_x, from_y, own_inv, own_pot, ghost_x, ghost_y, corners=None):
        self.sz, self.vec, self.from_x, self.from_y = sz, vec, from_x, from_y
        self.own, self.ghost_x, self.ghost_y, self.corners = (own_inv, own_pot), ghost_x, ghost_y, corners

    def x(self, i, j):
        sz = self.sz
        if i < sz.ex and j < sz.ey:
            return self.vec[:, i, j].astype(f32)
        if i == sz.ex:
            parts = [self.from_x[b * sz.ey + j] for b in range(sz.blocks)]
        else:
            parts = [self.from_y[b * sz.ex + i] for b in range(sz.blocks)]
        return jnp.stack(parts).astype(f32)

    def field(self, at, i, j):
        sz = self.sz
        if i < sz.ex and j < sz.ey:
            return self.own[at][i, j]
        if i < sz.ex:
            return self.ghost_y[at, i]
        if j < sz.ey:
            return self.ghost_x[at, j]
        return self.corners[at]

    def inv(self, i, j):
        return self.field(0, i, j)

    def pot(self, i, j):
        return self.field(1, i, j)


class Sums:
    def __init__(self, sz, even, acc, face, near, far, corner=None):
        self.sz, self.even, self.acc, self.face = sz, even, acc, face
        self.near, self.far, self.corner = near, far, corner

    def at(self, i, j):
        sz = self.sz
        total = self.acc[:, i, j]
        side = 1 if i == 0 else 0 if i == sz.ex else None
        if side is not None:
            total = total + self.face[side, :, j].astype(f32)
        if j in (0, sz.ey):
            is_near = self.even if j == sz.ey else jnp.logical_not(self.even)
            total = total + jnp.where(is_near, self.near[:, i].astype(f32), self.far[:, i].astype(f32))
            if side is not None:
                total = total + jnp.where(
                    is_near, self.corner[side, 0].astype(f32), self.corner[side, 1].astype(f32)
                )
        return total


def plain_edges(sz):
    return [(i, j) for i in range(sz.gx) for j in range(sz.gy) if sz.corner(i, j) is None]


def corner_edges(sz):
    return [(i, j) for i in (0, sz.ex) for j in (0, sz.ey)]


def main_products(sz, u_ref, mat_refs, rhs_ref, out_ref):
    width = sz.width
    flat = sz.gx * sz.gy * sz.gz
    u_flat = u_ref.reshape(sz.blocks * flat, width)
    matrices = [ref.at[c] for ref in mat_refs for c in range(ref.shape[0])]
    rhs_ref[: sz.base] = jnp.zeros((sz.base, sz.full), f32)
    last = sz.nodes // 8 * 8
    rhs_ref[last:] = jnp.zeros((sz.depth - last, sz.full), f32)
    for cell, (x0, y0, z0) in enumerate(sz.origins):
        z1 = z0 + sz.p
        wrap = z1 % sz.gz
        for b in range(sz.blocks):
            lanes = slice(b * width, (b + 1) * width)
            for place, i, j, count in sz.runs(cell):
                row = sz.base + place * sz.p
                rhs_ref[row : row + count * sz.p, lanes] = u_ref[
                    b, x0 + i, y0 + j : y0 + j + count, z0:z1
                ].reshape(count * sz.p, width)
        for b in range(sz.blocks):
            lanes = slice(b * width, (b + 1) * width)
            for place, i, j, count in sz.runs(cell):
                start = b * flat + ((x0 + i) * sz.gy + y0 + j) * sz.gz + wrap
                rhs_ref[sz.tail + place : sz.tail + place + count, lanes] = u_flat[
                    pl.ds(start, count, stride=sz.gz)
                ]
        out_ref[cell] = jnp.dot(
            matrices[cell][...], rhs_ref[...].astype(bf16), preferred_element_type=f32
        )


def corner_products(sz, u_corner, prod_ref, mat_refs, small_ref, tail_ref, acc_ref):
    width = sz.width
    flat = sz.gx * sz.gy * sz.gz
    acc_flat = acc_ref.reshape(sz.blocks * flat, width)
    matrices = [ref.at[c] for ref in mat_refs for c in range(ref.shape[0])]
    small_ref[...] = jnp.zeros_like(small_ref)
    touched = set()
    for cell, (x0, y0, z0) in enumerate(sz.origins):
        z1 = z0 + sz.p
        wrap = z1 % sz.gz
        corners = sz.cell_corners(cell)
        for rank, (i, j) in enumerate(corners):
            value = u_corner[sz.corner(x0 + i, y0 + j)]
            last = len(corners) * sz.p + rank
            for b in range(sz.blocks):
                lanes = slice(b * width, (b + 1) * width)
                small_ref[rank * sz.p : (rank + 1) * sz.p, lanes] = value[b, z0:z1]
                small_ref[last : last + 1, lanes] = value[b, wrap : wrap + 1]
        total = prod_ref[cell] + jnp.dot(
            matrices[cell][:, : small_ref.shape[0]], small_ref[...].astype(bf16),
            preferred_element_type=f32,
        )
        tail_ref[cell, : sz.base] = total[: sz.base]
        tail_ref[cell, sz.base :] = total[sz.tail :]
        spans = [(rank * sz.p, i, j, 1) for rank, (i, j) in enumerate(corners)]
        spans += [(sz.base + place * sz.p, i, j, count) for place, i, j, count in sz.runs(cell)]
        for row, i, j, count in spans:
            for at in range(count):
                part = total[row + at * sz.p : row + (at + 1) * sz.p]
                key = (x0 + i, y0 + j + at, z0)
                for b in range(sz.blocks):
                    value = part[:, b * width : (b + 1) * width]
                    if key in touched:
                        value = acc_ref[b, key[0], key[1], z0:z1] + value
                    acc_ref[b, key[0], key[1], z0:z1] = value
                touched.add(key)
    for cell, (x0, y0, z0) in enumerate(sz.origins):
        wrap = (z0 + sz.p) % sz.gz
        corners = sz.cell_corners(cell)
        spans = [(len(corners) * sz.p + rank, i, j, 1) for rank, (i, j) in enumerate(corners)]
        spans += [(sz.base + place, i, j, count) for place, i, j, count in sz.runs(cell)]
        for row, i, j, count in spans:
            for b in range(sz.blocks):
                start = b * flat + ((x0 + i) * sz.gy + y0 + j) * sz.gz + wrap
                rows = pl.ds(start, count, stride=sz.gz) if count > 1 else pl.ds(start, 1)
                lanes = slice(b * width, (b + 1) * width)
                acc_flat[rows] = acc_flat[rows] + tail_ref[cell, row : row + count, lanes]


def write_messages(sz, even, acc_ref, face, near, far):
    at_near = jnp.where(even, sz.ey, 0)
    for b in range(sz.blocks):
        face[0, b] = acc_ref[b, 0].astype(bf16)
        face[1, b] = acc_ref[b, sz.ex].astype(bf16)
        near[b] = acc_ref[b, :, at_near].astype(bf16)
        far[b] = acc_ref[b, :, sz.ey - at_near].astype(bf16)


def corner_pack_kernel(sz, near, far, out_ref):
    for side, i in enumerate((0, sz.ex)):
        for slot, ref in enumerate((near, far)):
            out_ref[side, slot] = ref[:, i]


def first_main(sz, n_mat, vec, from_x, from_y, own_inv, own_pot, *refs):
    mats = refs[:n_mat]
    prod_ref, ghost_x, ghost_y, u_ref, rhs_ref = refs[n_mat:]
    for j in range(sz.ey):
        ghost_x[0, j], ghost_x[1, j] = fields_of(from_x[sz.blocks * sz.ey + j])
    for i in range(sz.ex):
        ghost_y[0, i], ghost_y[1, i] = fields_of(from_y[sz.blocks * sz.ex + i])
    nodes = Nodes(sz, vec, from_x, from_y, own_inv, own_pot, ghost_x, ghost_y)
    for i, j in plain_edges(sz):
        u_ref[:, i, j] = nodes.x(i, j) * nodes.inv(i, j)
    main_products(sz, u_ref, mats, rhs_ref, prod_ref)


def first_corner(sz, n_mat, even_ref, vec, from_x, from_y, corner, own_inv, own_pot, ghost_x, ghost_y,
                 prod_ref, *refs):
    mats = refs[:n_mat]
    acc_ref, face, near, far, last_x, last_field, small_ref, tail_ref = refs[n_mat:]
    last_field[0], last_field[1] = fields_of(corner[sz.blocks])
    for b in range(sz.blocks):
        last_x[b] = corner[b].astype(f32)
    nodes = Nodes(sz, vec, from_x, from_y, own_inv, own_pot, ghost_x, ghost_y, last_field)
    u_corner = []
    for i, j in corner_edges(sz):
        x = last_x[...] if (i, j) == (sz.ex, sz.ey) else nodes.x(i, j)
        u_corner.append(x * nodes.inv(i, j))
    corner_products(sz, u_corner, prod_ref, mats, small_ref, tail_ref, acc_ref)
    write_messages(sz, even_ref[0] == 0, acc_ref, face, near, far)


def second_main(sz, n_mat, even_ref, vec, from_x, from_y, own_inv, own_pot, ghost_x, ghost_y,
                acc_in, face_in, near_in, far_in, *refs):
    mats = refs[:n_mat]
    prod_ref, y_ref, u_ref, rhs_ref = refs[n_mat:]
    nodes = Nodes(sz, vec, from_x, from_y, own_inv, own_pot, ghost_x, ghost_y)
    sums = Sums(sz, even_ref[0] == 0, acc_in, face_in, near_in, far_in)
    for i, j in plain_edges(sz):
        old, inv = nodes.x(i, j), nodes.inv(i, j)
        image = inv * sums.at(i, j) + nodes.pot(i, j) * old
        new = (image - center_shift * old) / half_width
        y_ref[:, i, j] = new
        u_ref[:, i, j] = inv * new
    main_products(sz, u_ref, mats, rhs_ref, prod_ref)


def second_corner(sz, n_mat, even_ref, vec, from_x, from_y, own_inv, own_pot, ghost_x, ghost_y, last_x,
                  last_field, acc_in, face_in, near_in, far_in, corner_in, prod_ref, *refs):
    mats = refs[:n_mat]
    acc_ref, face, near, far, y_corner, small_ref, tail_ref = refs[n_mat:]
    even = even_ref[0] == 0
    nodes = Nodes(sz, vec, from_x, from_y, own_inv, own_pot, ghost_x, ghost_y, last_field)
    sums = Sums(sz, even, acc_in, face_in, near_in, far_in, corner_in)
    u_corner = []
    for at, (i, j) in enumerate(corner_edges(sz)):
        old = last_x[...] if (i, j) == (sz.ex, sz.ey) else nodes.x(i, j)
        inv = nodes.inv(i, j)
        image = inv * sums.at(i, j) + nodes.pot(i, j) * old
        new = (image - center_shift * old) / half_width
        y_corner[at] = new
        u_corner.append(inv * new)
    corner_products(sz, u_corner, prod_ref, mats, small_ref, tail_ref, acc_ref)
    write_messages(sz, even, acc_ref, face, near, far)


def third_main(sz, n_mat, even_ref, vec, from_x, from_y, own_inv, own_pot, ghost_x, ghost_y,
               acc_in, face_in, near_in, far_in, y_ref, *refs):
    mats = refs[:n_mat]
    prod_ref, new_ref, u_ref, rhs_ref = refs[n_mat:]
    nodes = Nodes(sz, vec, from_x, from_y, own_inv, own_pot, ghost_x, ghost_y)
    sums = Sums(sz, even_ref[0] == 0, acc_in, face_in, near_in, far_in)
    for i, j in plain_edges(sz):
        old, inv = y_ref[:, i, j], nodes.inv(i, j)
        image = inv * sums.at(i, j) + nodes.pot(i, j) * old
        new = 2.0 * (image - center_shift * old) / half_width - nodes.x(i, j)
        new_ref[:, i, j] = new
        u_ref[:, i, j] = inv * new
    main_products(sz, u_ref, mats, rhs_ref, prod_ref)


def third_corner(sz, n_mat, norm_scale, even_ref, vec, from_x, from_y, own_inv, own_pot, ghost_x, ghost_y,
                 last_x, last_field, acc_in, face_in, near_in, far_in, corner_in, prod_ref, y_ref,
                 y_corner, new_ref, turned, *refs):
    mats = refs[:n_mat]
    part_ref, face, side, corner, margin = refs[n_mat : n_mat + 5]
    acc_ref, rows_ref, small_ref, tail_ref = refs[n_mat + 5 :]
    nodes = Nodes(sz, vec, from_x, from_y, own_inv, own_pot, ghost_x, ghost_y, last_field)
    sums = Sums(sz, even_ref[0] == 0, acc_in, face_in, near_in, far_in, corner_in)
    u_corner, new_corner = [], []
    for at, (i, j) in enumerate(corner_edges(sz)):
        x = last_x[...] if (i, j) == (sz.ex, sz.ey) else nodes.x(i, j)
        old, inv = y_corner[at], nodes.inv(i, j)
        image = inv * sums.at(i, j) + nodes.pot(i, j) * old
        new_corner.append(2.0 * (image - center_shift * old) / half_width - x)
        u_corner.append(inv * new_corner[-1])
    corner_products(sz, u_corner, prod_ref, mats, small_ref, tail_ref, acc_ref)

    def put_row(at, value):
        for b in range(sz.blocks):
            rows_ref[at, :, b * sz.width : (b + 1) * sz.width] = value[b]

    for i in range(sz.gx):
        for j in range(sz.gy):
            acc, inv = acc_ref[:, i, j], nodes.inv(i, j)
            if i == sz.ex or j == sz.ey:
                value = gain * (inv * acc)
                rounded = value.astype(bf16)
                if j < sz.ey:
                    put_row(sz.own_edges + j, rounded)
                    face[:, j] = rounded
                else:
                    put_row(sz.own_edges + sz.ey + i, rounded)
                    if i < sz.ex:
                        side[:, i] = value
                    else:
                        corner[...] = rounded
                continue
            at = sz.corner(i, j)
            old = y_ref[:, i, j] if at is None else y_corner[at]
            new = new_ref[:, i, j] if at is None else new_corner[at]
            image = inv * acc + nodes.pot(i, j) * new
            value = 2.0 * (image - center_shift * new) / half_width - old
            part_ref[:, i, j] = value
            put_row(i * sz.ey + j, value.astype(bf16))
    for at in range(sz.own_edges + sz.ey + sz.gx, sz.edges):
        rows_ref[at] = jnp.zeros((sz.ez, sz.full), bf16)
    local = jnp.dot(
        turned[...], rows_ref[...].reshape(sz.edges * sz.ez, sz.full), preferred_element_type=f32
    )
    margin[...] = (local * norm_scale).astype(bf16)


def last_side_kernel(sz, side_ref, corner_ref, face_in, out_ref, face_out):
    del face_in, face_out
    for i in range(sz.ex):
        value = side_ref[:, i]
        if i == 0:
            value = value + corner_ref[...].astype(f32)
        out_ref[:, i] = value.astype(out_ref.dtype)


def last_kernel(sz, part_ref, face, side, out_ref):
    for i in range(sz.ex):
        for j in range(sz.ey):
            value = part_ref[:, i, j]
            if i == 0:
                value = value + face[:, j].astype(f32)
            if j == 0:
                value = value + side[:, i].astype(f32)
            out_ref[:, i, j] = value


def like(shape, dtype):
    return jax.ShapeDtypeStruct(shape, dtype)


def call(kernel, name, flops, out_shape, scratch, operands, hbm=0, scalar_first=False, aliases=None):
    out_shape = [like(s.shape, s.dtype) for s in out_shape]
    size = sum(math.prod(s.shape) * jnp.dtype(s.dtype).itemsize for s in (*operands, *out_shape))
    whole = pl.BlockSpec(memory_space=pltpu.VMEM)
    specs = [pl.BlockSpec(memory_space=pltpu.HBM)] * hbm + [whole] * (len(operands) - hbm)
    if scalar_first:
        specs[0] = pl.BlockSpec(memory_space=pltpu.SMEM)
    operands = [pltpu.with_memory_space_constraint(a, pltpu.HBM) for a in operands[:hbm]] + list(
        operands[hbm:]
    )
    return pl.pallas_call(
        kernel,
        in_specs=specs,
        out_specs=[whole] * len(out_shape),
        out_shape=out_shape,
        scratch_shapes=scratch,
        input_output_aliases=aliases or {},
        compiler_params=pltpu.CompilerParams(vmem_limit_bytes=VMEM_LIMIT),
        cost_estimate=pl.CostEstimate(flops=flops, bytes_accessed=size, transcendentals=0),
        name=name,
    )(*operands)


def body(vectors, resident, inv_mass, potential, cell_matrix, connectivity):
    sz = Sizes(vectors, resident, inv_mass, connectivity)
    nx, ny = lax.axis_size("dx"), lax.axis_size("dy")
    norm_scale = 1.0 / math.sqrt(sz.ex * sz.ey * sz.ez * nx * ny)
    blocks, ez, width, full = sz.blocks, sz.ez, sz.width, sz.full
    res_count = resident.shape[-1]
    tile = (ez, width)
    parts = blocks + 1 + sz.groups

    conn = connectivity.reshape(sz.cells, sz.nodes)
    to_x, to_y, cell_matrix, conn = call(
        functools.partial(pack_kernel, sz), "pack", 0,
        [like((parts * sz.ey,) + tile, bf16), like((parts * sz.ex,) + tile, bf16), cell_matrix, conn],
        [
            pltpu.VMEM((2, sz.ey, ez), f32), pltpu.VMEM((2, sz.ex, ez), f32),
            pltpu.SemaphoreType.DMA((6 + 2 * blocks + 2 * sz.groups,)),
        ],
        [vectors, resident, inv_mass, potential, cell_matrix, conn], hbm=6,
    )
    from_x = send(to_x, -1, 0)
    from_y = send(to_y, 0, -1)

    halves = 2 if sz.cells % 2 == 0 else 1
    step = sz.cells // halves
    mats = []
    for at in range(0, sz.cells, step):
        mats += call(
            functools.partial(order_kernel, sz, at, step), "order_cells",
            4 * step * sz.depth**3, [like((step, sz.rows, sz.depth), bf16)], [], [conn, cell_matrix],
        )
    own_inv = jnp.broadcast_to(inv_mass[..., None], inv_mass.shape + (width,))
    own_pot = jnp.broadcast_to(potential[..., None], inv_mass.shape + (width,))
    parity = jnp.reshape(lax.axis_index("dy") % 2, (1,)).astype(jnp.int32)
    (ghost_corner,) = call(
        functools.partial(ghost_corner_kernel, sz), "ghost_corner", 0,
        [like((parts,) + tile, bf16)], [], [from_y],
    )
    ghost_corner = send(ghost_corner, -1, 0)

    grid = (blocks, sz.gx, sz.gy) + tile
    own = (blocks, sz.ex, sz.ey) + tile
    products = like((sz.cells, sz.rows, full), f32)
    messages = [
        like((2, blocks, sz.gy) + tile, bf16),
        like((blocks, sz.gx) + tile, bf16),
        like((blocks, sz.gx) + tile, bf16),
    ]
    main_scratch = [pltpu.VMEM(grid, f32), pltpu.VMEM((sz.depth, full), f32)]
    corner_scratch = [
        pltpu.VMEM((LANES, full), f32),
        pltpu.VMEM((sz.cells, sz.base + sz.rows - sz.tail, full), f32),
    ]
    n_mat = len(mats)
    flops = 2 * sz.cells * sz.rows * sz.depth * full
    small_flops = 2 * sz.cells * sz.rows * LANES * full

    def exchange(face, near, far):
        face = swap_x(face)
        near, far = swap_y(near, far)
        (corner,) = call(
            functools.partial(corner_pack_kernel, sz), "corner_pack", 0,
            [like((2, 2) + sz.edge, bf16)], [], [near, far],
        )
        return [face, near, far], swap_x(corner)

    prod, ghost_x, ghost_y = call(
        functools.partial(first_main, sz, n_mat), "first_main", flops,
        [products, like((2, sz.ey) + tile, f32), like((2, sz.ex) + tile, f32)], main_scratch,
        [vectors, from_x, from_y, own_inv, own_pot, *mats],
    )
    acc, face, near, far, last_x, last_field = call(
        functools.partial(first_corner, sz, n_mat), "first_corner", small_flops,
        [like(grid, f32), *messages, like(sz.edge, f32), like((2,) + tile, f32)], corner_scratch,
        [
            parity, vectors, from_x, from_y, ghost_corner, own_inv, own_pot, ghost_x, ghost_y, prod, *mats,
        ],
        scalar_first=True,
    )
    (turned,) = call(
        functools.partial(turn_kernel, sz), "turn_residents", flops // 2,
        [like((res_count, sz.edges * ez), bf16)], [],
        [resident.reshape(-1, res_count), from_x, from_y, ghost_corner],
    )
    got, corner = exchange(face, near, far)
    state = [vectors, from_x, from_y, own_inv, own_pot, ghost_x, ghost_y]
    ends = [last_x, last_field]
    prod, y1 = call(
        functools.partial(second_main, sz, n_mat), "second_main", flops,
        [products, like(grid, f32)], main_scratch,
        [parity, *state, acc, *got, *mats], scalar_first=True,
    )
    acc, face, near, far, y1_corner = call(
        functools.partial(second_corner, sz, n_mat), "second_corner", small_flops,
        [like(grid, f32), *messages, like((4,) + sz.edge, f32)], corner_scratch,
        [parity, *state, *ends, acc, *got, corner, prod, *mats], scalar_first=True,
    )
    got, corner = exchange(face, near, far)
    prod, y2 = call(
        functools.partial(third_main, sz, n_mat), "third_main", flops,
        [products, like(grid, f32)], main_scratch,
        [parity, *state, acc, *got, y1, *mats], scalar_first=True,
    )
    part, face, side, corner, local = call(
        functools.partial(third_corner, sz, n_mat, norm_scale), "third_corner",
        small_flops + 2 * res_count * sz.edges * ez * full,
        [
            like(own, f32), like((blocks, sz.ey) + tile, bf16), like((blocks, sz.ex) + tile, f32),
            like(sz.edge, bf16), like((res_count, full), bf16),
        ],
        [pltpu.VMEM(grid, f32), pltpu.VMEM((sz.edges, ez, full), bf16)] + corner_scratch,
        [parity, *state, *ends, acc, *got, corner, prod, y1, y1_corner, y2, turned, *mats],
        scalar_first=True,
    )

    pieces = lax.all_to_all(local.reshape(ny, -1, full), "dy", 0, 0)
    mine = jnp.sum(pieces.astype(f32), axis=0)
    margin = mine
    for steps in range(1, nx):
        margin = margin + send(mine, steps, 0)

    corner = send(corner, 1, 0)
    side, face = call(
        functools.partial(last_side_kernel, sz), "last_side", 0,
        [like((blocks, sz.ex) + tile, bf16), face], [], [side, corner, face], aliases={2: 1},
    )
    face = send(face, 1, 0)
    side = send(side, 0, 1)
    (filtered,) = call(
        functools.partial(last_kernel, sz), "last", 0, [like(own, f32)], [], [part, face, side]
    )
    return (filtered, margin)


def solution(mesh):
    return jax.shard_map(
        body,
        mesh=mesh,
        in_specs=(
            P(None, "dx", "dy", None, None),
            P("dx", "dy", None, None),
            P("dx", "dy", None),
            P("dx", "dy", None),
            P(),
            P("dx", "dy", None, None),
        ),
        out_specs=(P(None, "dx", "dy", None, None), P("dy", None)),
        check_vma=False,
    )
```

```python
import functools
import math

import jax
import jax.numpy as jnp
from jax import lax
from jax.experimental import pallas as pl
from jax.experimental.pallas import tpu as pltpu
from jax.sharding import PartitionSpec as P

LANES = 128
TILE = 256
SUB = 16
VMEM_LIMIT = 16 * 1024 * 1024

center_shift = 1.2
half_width = 2.0
gain = 2.0 / half_width

f32, bf16 = jnp.float32, jnp.bfloat16


def round_up(value, step):
    return -(-value // step) * step


class Sizes:
    def __init__(self, vectors, resident, inv_mass, connectivity):
        self.blocks = vectors.shape[0]
        self.width = vectors.shape[-1]
        self.full = self.blocks * self.width
        self.res = resident.shape[-1]
        self.wide = self.res + self.full + self.width
        self.ex, self.ey, self.ez = inv_mass.shape
        self.cells, self.nodes = connectivity.shape[2:]
        self.n1 = round(self.nodes ** (1.0 / 3.0))
        self.p = self.n1 - 1
        self.cx, self.cy, self.cz = self.ex // self.p, self.ey // self.p, self.ez // self.p
        self.gx, self.gy, self.gz = self.ex + 1, self.ey + 1, self.ez
        self.edge = (self.blocks, self.ez, self.width)
        self.origins = [
            (a * self.p, b * self.p, c * self.p)
            for a in range(self.cx)
            for b in range(self.cy)
            for c in range(self.cz)
        ]
        self.most = max(len(self.cell_corners(cell)) for cell in range(self.cells))
        self.base = round_up(self.most * self.n1, 8)
        plain = self.n1 * self.n1 - min(len(self.cell_corners(cell)) for cell in range(self.cells))
        self.tail = self.base + plain * self.p
        self.rows = round_up(self.tail + plain, SUB)
        self.depth = round_up(self.rows, LANES)
        self.own_edges = self.ex * self.ey
        self.edges = round_up(self.own_edges + self.ey + self.gx, LANES // self.ez)

    def corner(self, i, j):
        if i in (0, self.ex) and j in (0, self.ey):
            return 2 * (i // self.ex) + j // self.ey
        return None

    def cell_corners(self, cell):
        x0, y0, _ = self.origins[cell]
        return [
            (i, j)
            for i in range(self.n1)
            for j in range(self.n1)
            if self.corner(x0 + i, y0 + j) is not None
        ]

    def runs(self, cell):
        corners = self.cell_corners(cell)
        place = 0
        for i in range(self.n1):
            js = [j for j in range(self.n1) if (i, j) not in corners]
            while js:
                count = 1
                while count < len(js) and js[count] == js[0] + count:
                    count += 1
                yield place, i, js[0], count
                place += count
                js = js[count:]


def send(value, steps_x, steps_y):
    nx, ny = lax.axis_size("dx"), lax.axis_size("dy")
    pairs = [
        (a * ny + b, ((a + steps_x) % nx) * ny + (b + steps_y) % ny)
        for a in range(nx)
        for b in range(ny)
    ]
    return lax.ppermute(value, ("dx", "dy"), pairs)


def swap_x(value):
    if lax.axis_size("dx") == 2:
        return send(value, 1, 0)
    return jnp.stack([send(value[0], -1, 0), send(value[1], 1, 0)])


def swap_y(near, far):
    ny = lax.axis_size("dy")
    near_pairs = [(b, b + 1 if b % 2 == 0 else b - 1) for b in range(ny)]
    far_pairs = [(b, (b - 1 if b % 2 == 0 else b + 1) % ny) for b in range(ny)]
    far = lax.ppermute(far, "dy", far_pairs)
    near = lax.ppermute(near, "dy", near_pairs)
    return near, far


def order_kernel(sz, conn_ref, matrix_ref, out_ref):
    for cell in range(sz.cells):
        x0, y0, z0 = sz.origins[cell]
        conn = conn_ref[cell : cell + 1, :].astype(f32)
        li = jnp.floor((conn + 0.5) * (1.0 / (sz.gy * sz.gz)))
        rest = conn - li * (sz.gy * sz.gz)
        lj = jnp.floor((rest + 0.5) * (1.0 / sz.gz))
        lk = rest - lj * sz.gz - z0
        lk = jnp.where(lk < 0, lk + sz.gz, lk)
        column = (li - x0) * sz.n1 + (lj - y0)
        corners = [i * sz.n1 + j for i, j in sz.cell_corners(cell)]
        place = column
        for at in corners:
            place = place - jnp.where(column > at, 1.0, 0.0)
        index = jnp.where(lk < sz.p, sz.base + place * sz.p + lk, sz.tail + place)
        for rank, at in enumerate(corners):
            special = jnp.where(lk < sz.p, rank * sz.p + lk, len(corners) * sz.p + rank)
            index = jnp.where(column == at, special, index)
        index = index.astype(jnp.int32)
        row = lax.broadcasted_iota(jnp.int32, (sz.depth, sz.nodes), 0)
        pick = (row == index).astype(f32).astype(bf16)
        half = jnp.dot(pick[: sz.rows], matrix_ref[...], preferred_element_type=f32)
        half = half.astype(bf16)
        cuts = list(range(0, sz.depth, TILE)) + [sz.depth]
        for r0, r1 in zip(cuts[:-1], cuts[1:]):
            r1 = min(r1, sz.rows)
            block = lax.dot_general(
                half[r0:r1], pick[r0:], (((1,), (1,)), ((), ())), preferred_element_type=f32
            ).astype(bf16)
            out_ref[cell, r0:r1, r0:] = block
            for c0, c1 in zip(cuts[:-1], cuts[1:]):
                if c0 > r0:
                    mirror = block[:, c0 - r0 : c1 - r0].T
                    c1 = min(c1, sz.rows)
                    out_ref[cell, c0:c1, r0:r1] = mirror[: c1 - c0]


def field_row(inv, pot):
    lane = lax.broadcasted_iota(jnp.int32, inv.shape, inv.ndim - 1)
    row = jnp.zeros_like(inv)
    for at, rest in enumerate((inv, pot)):
        for k in range(3):
            part = rest.astype(bf16).astype(f32)
            rest = rest - part
            row = jnp.where(lane == 3 * at + k, part, row)
    return row.astype(bf16)


def field_rows(sz, inv, pot, count):
    inv, pot = inv.T, pot.T
    shape = (sz.ez, sz.width)
    for at in range(count):
        yield at, field_row(
            jnp.broadcast_to(inv[:, at : at + 1], shape), jnp.broadcast_to(pot[:, at : at + 1], shape)
        )


def fields_of(row):
    row = row.astype(f32)
    return [
        jnp.broadcast_to(sum(row[:, 3 * at + k : 3 * at + k + 1] for k in range(3)), row.shape)
        for at in range(2)
    ]


def pack_kernel(
    sz, vec_hbm, res_hbm, inv_hbm, pot_hbm, mat_hbm, conn_hbm,
    to_x, to_y, mat_ref, conn_ref, at_x, at_y, sems,
):
    pairs = [
        (inv_hbm.at[0], at_x.at[0]), (pot_hbm.at[0], at_x.at[1]),
        (inv_hbm.at[:, 0], at_y.at[0]), (pot_hbm.at[:, 0], at_y.at[1]),
        (res_hbm.at[0], to_x.at[:, :, pl.ds(0, sz.res)]),
        (res_hbm.at[:, 0], to_y.at[:, :, pl.ds(0, sz.res)]),
    ]
    for b in range(sz.blocks):
        lanes = pl.ds(sz.res + b * sz.width, sz.width)
        pairs.append((vec_hbm.at[b, 0], to_x.at[:, :, lanes]))
        pairs.append((vec_hbm.at[b, :, 0], to_y.at[:, :, lanes]))
    pairs += [(mat_hbm, mat_ref), (conn_hbm, conn_ref)]
    copies = [pltpu.make_async_copy(a, b, sems.at[k]) for k, (a, b) in enumerate(pairs)]
    for copy in copies:
        copy.start()
    for copy in copies[:4]:
        copy.wait()
    for j, row in field_rows(sz, at_x[0], at_x[1], sz.ey):
        to_x[j, :, sz.res + sz.full :] = row
    for i, row in field_rows(sz, at_y[0], at_y[1], sz.ex):
        to_y[i, :, sz.res + sz.full :] = row
    for copy in copies[4:]:
        copy.wait()


def turn_kernel(sz, res_ref, from_x, from_y, corner, out_ref):
    own = sz.own_edges * sz.ez
    for g in range(0, sz.res, LANES):
        lanes = slice(g, g + LANES)
        out_ref[lanes, :own] = res_ref[:, lanes].T
        rest = sz.edges - sz.own_edges - sz.ey - sz.gx
        parts = [from_x[:, :, lanes], from_y[:, :, lanes], corner[:, :, lanes]]
        if rest:
            parts.append(jnp.zeros((rest, sz.ez, LANES), bf16))
        ghosts = jnp.concatenate(parts, axis=0)
        out_ref[lanes, own:] = ghosts.reshape(-1, LANES).T


def vectors_of(sz, edge):
    lanes = [slice(sz.res + b * sz.width, sz.res + (b + 1) * sz.width) for b in range(sz.blocks)]
    return jnp.stack([edge[:, at] for at in lanes]).astype(f32)


class Nodes:
    def __init__(self, sz, vec, from_x, from_y, own_inv, own_pot, ghost_x, ghost_y, corners=None):
        self.sz, self.vec, self.from_x, self.from_y = sz, vec, from_x, from_y
        self.own, self.ghost_x, self.ghost_y, self.corners = (own_inv, own_pot), ghost_x, ghost_y, corners

    def x(self, i, j):
        sz = self.sz
        if i < sz.ex and j < sz.ey:
            return self.vec[:, i, j].astype(f32)
        return vectors_of(sz, self.from_x[j] if i == sz.ex else self.from_y[i])

    def field(self, at, i, j):
        sz = self.sz
        if i < sz.ex and j < sz.ey:
            return self.own[at][i, j]
        if i < sz.ex:
            return self.ghost_y[at, i]
        if j < sz.ey:
            return self.ghost_x[at, j]
        return self.corners[at]

    def inv(self, i, j):
        return self.field(0, i, j)

    def pot(self, i, j):
        return self.field(1, i, j)


class Sums:
    def __init__(self, sz, even, acc, face, near, far, corner=None):
        self.sz, self.even, self.acc, self.face = sz, even, acc, face
        self.near, self.far, self.corner = near, far, corner

    def at(self, i, j):
        sz = self.sz
        total = self.acc[:, i, j]
        side = 1 if i == 0 else 0 if i == sz.ex else None
        if side is not None:
            total = total + self.face[side, :, j].astype(f32)
        if j in (0, sz.ey):
            is_near = self.even if j == sz.ey else jnp.logical_not(self.even)
            total = total + jnp.where(is_near, self.near[:, i].astype(f32), self.far[:, i].astype(f32))
            if side is not None:
                total = total + jnp.where(
                    is_near, self.corner[side, 0].astype(f32), self.corner[side, 1].astype(f32)
                )
        return total


def corner_edges(sz):
    return [(i, j) for i in (0, sz.ex) for j in (0, sz.ey)]


def main_products(sz, prepare, u_ref, mat_refs, rhs_ref, out_ref):
    width = sz.width
    flat = sz.gx * sz.gy * sz.gz
    u_flat = u_ref.reshape(sz.blocks * flat, width)
    matrices = [ref.at[c] for ref in mat_refs for c in range(ref.shape[0])]
    last = sz.nodes // 8 * 8
    ready = set()
    for cell, (x0, y0, z0) in enumerate(sz.origins):
        slot = cell % 2
        if cell < 2:
            rhs_ref[slot, : sz.base] = jnp.zeros((sz.base, sz.full), f32)
            rhs_ref[slot, last:] = jnp.zeros((sz.depth - last, sz.full), f32)
        for place, i, j, count in sz.runs(cell):
            for at in range(j, j + count):
                if (x0 + i, y0 + at) not in ready:
                    prepare(x0 + i, y0 + at)
                    ready.add((x0 + i, y0 + at))
        z1 = z0 + sz.p
        wrap = z1 % sz.gz
        for b in range(sz.blocks):
            lanes = slice(b * width, (b + 1) * width)
            for place, i, j, count in sz.runs(cell):
                row = sz.base + place * sz.p
                rhs_ref[slot, row : row + count * sz.p, lanes] = u_ref[
                    b, x0 + i, y0 + j : y0 + j + count, z0:z1
                ].reshape(count * sz.p, width)
        for b in range(sz.blocks):
            lanes = slice(b * width, (b + 1) * width)
            for place, i, j, count in sz.runs(cell):
                start = b * flat + ((x0 + i) * sz.gy + y0 + j) * sz.gz + wrap
                rhs_ref[slot, sz.tail + place : sz.tail + place + count, lanes] = u_flat[
                    pl.ds(start, count, stride=sz.gz)
                ]
        out_ref[cell] = jnp.dot(
            matrices[cell][...], rhs_ref[slot].astype(bf16), preferred_element_type=f32
        )


def corner_products(sz, u_corner, prod_ref, mat_refs, small_ref, tail_ref, acc_ref):
    width = sz.width
    flat = sz.gx * sz.gy * sz.gz
    acc_flat = acc_ref.reshape(sz.blocks * flat, width)
    matrices = [ref.at[c] for ref in mat_refs for c in range(ref.shape[0])]
    small_ref[...] = jnp.zeros_like(small_ref)
    touched = set()
    for cell, (x0, y0, z0) in enumerate(sz.origins):
        z1 = z0 + sz.p
        wrap = z1 % sz.gz
        corners = sz.cell_corners(cell)
        for rank, (i, j) in enumerate(corners):
            value = u_corner[sz.corner(x0 + i, y0 + j)]
            last = len(corners) * sz.p + rank
            for b in range(sz.blocks):
                lanes = slice(b * width, (b + 1) * width)
                small_ref[rank * sz.p : (rank + 1) * sz.p, lanes] = value[b, z0:z1]
                small_ref[last : last + 1, lanes] = value[b, wrap : wrap + 1]
        total = prod_ref[cell] + jnp.dot(
            matrices[cell][:, : small_ref.shape[0]], small_ref[...].astype(bf16),
            preferred_element_type=f32,
        )
        tail_ref[cell, : sz.base] = total[: sz.base]
        tail_ref[cell, sz.base :] = total[sz.tail :]
        spans = [(rank * sz.p, i, j, 1) for rank, (i, j) in enumerate(corners)]
        spans += [(sz.base + place * sz.p, i, j, count) for place, i, j, count in sz.runs(cell)]
        for row, i, j, count in spans:
            for at in range(count):
                part = total[row + at * sz.p : row + (at + 1) * sz.p]
                key = (x0 + i, y0 + j + at, z0)
                for b in range(sz.blocks):
                    value = part[:, b * width : (b + 1) * width]
                    if key in touched:
                        value = acc_ref[b, key[0], key[1], z0:z1] + value
                    acc_ref[b, key[0], key[1], z0:z1] = value
                touched.add(key)
    for cell, (x0, y0, z0) in enumerate(sz.origins):
        wrap = (z0 + sz.p) % sz.gz
        corners = sz.cell_corners(cell)
        spans = [(len(corners) * sz.p + rank, i, j, 1) for rank, (i, j) in enumerate(corners)]
        spans += [(sz.base + place, i, j, count) for place, i, j, count in sz.runs(cell)]
        for row, i, j, count in spans:
            for b in range(sz.blocks):
                start = b * flat + ((x0 + i) * sz.gy + y0 + j) * sz.gz + wrap
                rows = pl.ds(start, count, stride=sz.gz) if count > 1 else pl.ds(start, 1)
                lanes = slice(b * width, (b + 1) * width)
                acc_flat[rows] = acc_flat[rows] + tail_ref[cell, row : row + count, lanes]


def write_messages(sz, even, acc_ref, face, near, far):
    at_near = jnp.where(even, sz.ey, 0)
    for b in range(sz.blocks):
        face[0, b] = acc_ref[b, 0].astype(bf16)
        face[1, b] = acc_ref[b, sz.ex].astype(bf16)
        near[b] = acc_ref[b, :, at_near].astype(bf16)
        far[b] = acc_ref[b, :, sz.ey - at_near].astype(bf16)


def corner_pack_kernel(sz, near, far, out_ref):
    for side, i in enumerate((0, sz.ex)):
        for slot, ref in enumerate((near, far)):
            out_ref[side, slot] = ref[:, i]


def first_main(sz, n_mat, vec, from_x, from_y, own_inv, own_pot, *refs):
    mats = refs[:n_mat]
    prod_ref, ghost_x, ghost_y, u_ref, rhs_ref = refs[n_mat:]
    for j in range(sz.ey):
        ghost_x[0, j], ghost_x[1, j] = fields_of(from_x[j, :, sz.res + sz.full :])
    for i in range(sz.ex):
        ghost_y[0, i], ghost_y[1, i] = fields_of(from_y[i, :, sz.res + sz.full :])
    nodes = Nodes(sz, vec, from_x, from_y, own_inv, own_pot, ghost_x, ghost_y)

    def prepare(i, j):
        u_ref[:, i, j] = nodes.x(i, j) * nodes.inv(i, j)

    main_products(sz, prepare, u_ref, mats, rhs_ref, prod_ref)


def first_corner(sz, n_mat, even_ref, vec, from_x, from_y, corner, own_inv, own_pot, ghost_x, ghost_y,
                 prod_ref, *refs):
    mats = refs[:n_mat]
    acc_ref, face, near, far, last_x, last_field, small_ref, tail_ref = refs[n_mat:]
    last_field[0], last_field[1] = fields_of(corner[0, :, sz.res + sz.full :])
    last_x[...] = vectors_of(sz, corner[0])
    nodes = Nodes(sz, vec, from_x, from_y, own_inv, own_pot, ghost_x, ghost_y, last_field)
    u_corner = []
    for i, j in corner_edges(sz):
        x = last_x[...] if (i, j) == (sz.ex, sz.ey) else nodes.x(i, j)
        u_corner.append(x * nodes.inv(i, j))
    corner_products(sz, u_corner, prod_ref, mats, small_ref, tail_ref, acc_ref)
    write_messages(sz, even_ref[0] == 0, acc_ref, face, near, far)


def second_main(sz, n_mat, even_ref, vec, from_x, from_y, own_inv, own_pot, ghost_x, ghost_y,
                acc_in, face_in, near_in, far_in, *refs):
    mats = refs[:n_mat]
    prod_ref, y_ref, u_ref, rhs_ref = refs[n_mat:]
    nodes = Nodes(sz, vec, from_x, from_y, own_inv, own_pot, ghost_x, ghost_y)
    sums = Sums(sz, even_ref[0] == 0, acc_in, face_in, near_in, far_in)

    def prepare(i, j):
        old, inv = nodes.x(i, j), nodes.inv(i, j)
        image = inv * sums.at(i, j) + nodes.pot(i, j) * old
        new = (image - center_shift * old) / half_width
        y_ref[:, i, j] = new
        u_ref[:, i, j] = inv * new

    main_products(sz, prepare, u_ref, mats, rhs_ref, prod_ref)


def second_corner(sz, n_mat, even_ref, vec, from_x, from_y, own_inv, own_pot, ghost_x, ghost_y, last_x,
                  last_field, acc_in, face_in, near_in, far_in, corner_in, prod_ref, *refs):
    mats = refs[:n_mat]
    acc_ref, face, near, far, y_corner, small_ref, tail_ref = refs[n_mat:]
    even = even_ref[0] == 0
    nodes = Nodes(sz, vec, from_x, from_y, own_inv, own_pot, ghost_x, ghost_y, last_field)
    sums = Sums(sz, even, acc_in, face_in, near_in, far_in, corner_in)
    u_corner = []
    for at, (i, j) in enumerate(corner_edges(sz)):
        old = last_x[...] if (i, j) == (sz.ex, sz.ey) else nodes.x(i, j)
        inv = nodes.inv(i, j)
        image = inv * sums.at(i, j) + nodes.pot(i, j) * old
        new = (image - center_shift * old) / half_width
        y_corner[at] = new
        u_corner.append(inv * new)
    corner_products(sz, u_corner, prod_ref, mats, small_ref, tail_ref, acc_ref)
    write_messages(sz, even, acc_ref, face, near, far)


def third_main(sz, n_mat, even_ref, vec, from_x, from_y, own_inv, own_pot, ghost_x, ghost_y,
               acc_in, face_in, near_in, far_in, y_ref, *refs):
    mats = refs[:n_mat]
    prod_ref, new_ref, u_ref, rhs_ref = refs[n_mat:]
    nodes = Nodes(sz, vec, from_x, from_y, own_inv, own_pot, ghost_x, ghost_y)
    sums = Sums(sz, even_ref[0] == 0, acc_in, face_in, near_in, far_in)

    def prepare(i, j):
        old, inv = y_ref[:, i, j], nodes.inv(i, j)
        image = inv * sums.at(i, j) + nodes.pot(i, j) * old
        new = 2.0 * (image - center_shift * old) / half_width - nodes.x(i, j)
        new_ref[:, i, j] = new
        u_ref[:, i, j] = inv * new

    main_products(sz, prepare, u_ref, mats, rhs_ref, prod_ref)


def third_corner(sz, n_mat, norm_scale, even_ref, vec, from_x, from_y, own_inv, own_pot, ghost_x, ghost_y,
                 last_x, last_field, acc_in, face_in, near_in, far_in, corner_in, prod_ref, y_ref,
                 y_corner, new_ref, turned, *refs):
    mats = refs[:n_mat]
    out_hbm, edge_x, edge_y, face, side, corner, margin = refs[n_mat : n_mat + 7]
    part_ref, sem, acc_ref, rows_ref, small_ref, tail_ref = refs[n_mat + 7 :]
    nodes = Nodes(sz, vec, from_x, from_y, own_inv, own_pot, ghost_x, ghost_y, last_field)
    sums = Sums(sz, even_ref[0] == 0, acc_in, face_in, near_in, far_in, corner_in)
    u_corner, new_corner = [], []
    for at, (i, j) in enumerate(corner_edges(sz)):
        x = last_x[...] if (i, j) == (sz.ex, sz.ey) else nodes.x(i, j)
        old, inv = y_corner[at], nodes.inv(i, j)
        image = inv * sums.at(i, j) + nodes.pot(i, j) * old
        new_corner.append(2.0 * (image - center_shift * old) / half_width - x)
        u_corner.append(inv * new_corner[-1])
    corner_products(sz, u_corner, prod_ref, mats, small_ref, tail_ref, acc_ref)

    def put_row(at, value):
        for b in range(sz.blocks):
            rows_ref[at, :, b * sz.width : (b + 1) * sz.width] = value[b]

    for i in range(sz.gx):
        for j in range(sz.gy):
            acc, inv = acc_ref[:, i, j], nodes.inv(i, j)
            if i == sz.ex or j == sz.ey:
                value = gain * (inv * acc)
                rounded = value.astype(bf16)
                if j < sz.ey:
                    put_row(sz.own_edges + j, rounded)
                    face[:, j] = rounded
                else:
                    put_row(sz.own_edges + sz.ey + i, rounded)
                    if i < sz.ex:
                        side[:, i] = value
                    else:
                        corner[...] = rounded
                continue
            at = sz.corner(i, j)
            old = y_ref[:, i, j] if at is None else y_corner[at]
            new = new_ref[:, i, j] if at is None else new_corner[at]
            image = inv * acc + nodes.pot(i, j) * new
            value = 2.0 * (image - center_shift * new) / half_width - old
            part_ref[:, i, j] = value
            if i == 0:
                edge_x[:, j] = value
            elif j == 0:
                edge_y[:, i - 1] = value
            put_row(i * sz.ey + j, value.astype(bf16))
    copy = pltpu.make_async_copy(part_ref, out_hbm, sem)
    copy.start()
    for at in range(sz.own_edges + sz.ey + sz.gx, sz.edges):
        rows_ref[at] = jnp.zeros((sz.ez, sz.full), bf16)
    local = jnp.dot(
        turned[...], rows_ref[...].reshape(sz.edges * sz.ez, sz.full), preferred_element_type=f32
    )
    margin[...] = (local * norm_scale).astype(bf16)
    copy.wait()


def last_side_kernel(sz, side_ref, corner_ref, face_in, out_ref, face_out):
    del face_in, face_out
    for i in range(sz.ex):
        value = side_ref[:, i]
        if i == 0:
            value = value + corner_ref[...].astype(f32)
        out_ref[:, i] = value.astype(out_ref.dtype)


def last_kernel(sz, old_hbm, edge_x, edge_y, face, side, out_hbm, at_x, at_y, sems):
    del old_hbm
    for j in range(sz.ey):
        value = edge_x[:, j] + face[:, j].astype(f32)
        if j == 0:
            value = value + side[:, 0].astype(f32)
        at_x[:, j] = value
    for i in range(1, sz.ex):
        at_y[:, i - 1] = edge_y[:, i - 1] + side[:, i].astype(f32)
    copies = [
        pltpu.make_async_copy(at_x, out_hbm.at[:, 0], sems.at[0]),
        pltpu.make_async_copy(at_y, out_hbm.at[:, pl.ds(1, sz.ex - 1), 0], sems.at[1]),
    ]
    for copy in copies:
        copy.start()
    for copy in copies:
        copy.wait()


def like(shape, dtype):
    return jax.ShapeDtypeStruct(shape, dtype)


def call(kernel, name, flops, out_shape, scratch, operands, hbm=0, scalar_first=False, aliases=None,
         out_hbm=0):
    out_shape = [like(s.shape, s.dtype) for s in out_shape]
    size = sum(math.prod(s.shape) * jnp.dtype(s.dtype).itemsize for s in (*operands, *out_shape))
    whole = pl.BlockSpec(memory_space=pltpu.VMEM)
    specs = [pl.BlockSpec(memory_space=pltpu.HBM)] * hbm + [whole] * (len(operands) - hbm)
    if scalar_first:
        specs[0] = pl.BlockSpec(memory_space=pltpu.SMEM)
    out_specs = [pl.BlockSpec(memory_space=pltpu.HBM)] * out_hbm + [whole] * (len(out_shape) - out_hbm)
    out_shape = [pltpu.HBM(s.shape, s.dtype) for s in out_shape[:out_hbm]] + out_shape[out_hbm:]
    operands = [pltpu.with_memory_space_constraint(a, pltpu.HBM) for a in operands[:hbm]] + list(
        operands[hbm:]
    )
    return pl.pallas_call(
        kernel,
        in_specs=specs,
        out_specs=out_specs,
        out_shape=out_shape,
        scratch_shapes=scratch,
        input_output_aliases=aliases or {},
        compiler_params=pltpu.CompilerParams(vmem_limit_bytes=VMEM_LIMIT),
        cost_estimate=pl.CostEstimate(flops=flops, bytes_accessed=size, transcendentals=0),
        name=name,
    )(*operands)


def body(vectors, resident, inv_mass, potential, cell_matrix, connectivity):
    sz = Sizes(vectors, resident, inv_mass, connectivity)
    nx, ny = lax.axis_size("dx"), lax.axis_size("dy")
    norm_scale = 1.0 / math.sqrt(sz.ex * sz.ey * sz.ez * nx * ny)
    blocks, ez, width, full = sz.blocks, sz.ez, sz.width, sz.full
    res_count = resident.shape[-1]
    tile = (ez, width)

    conn = connectivity.reshape(sz.cells, sz.nodes)
    to_x, to_y, cell_matrix, conn = call(
        functools.partial(pack_kernel, sz), "pack", 0,
        [like((sz.ey, ez, sz.wide), bf16), like((sz.ex, ez, sz.wide), bf16), cell_matrix, conn],
        [
            pltpu.VMEM((2, sz.ey, ez), f32), pltpu.VMEM((2, sz.ex, ez), f32),
            pltpu.SemaphoreType.DMA((8 + 2 * blocks,)),
        ],
        [vectors, resident, inv_mass, potential, cell_matrix, conn], hbm=6,
    )
    from_x = send(to_x, -1, 0)
    from_y = send(to_y, 0, -1)

    mats = call(
        functools.partial(order_kernel, sz), "order_cells", 4 * sz.cells * sz.depth**3,
        [like((sz.cells, sz.rows, sz.depth), bf16)], [], [conn, cell_matrix],
    )
    own_inv = jnp.broadcast_to(inv_mass[..., None], inv_mass.shape + (width,))
    own_pot = jnp.broadcast_to(potential[..., None], inv_mass.shape + (width,))
    parity = jnp.reshape(lax.axis_index("dy") % 2, (1,)).astype(jnp.int32)
    ghost_corner = send(from_y[:1], -1, 0)

    grid = (blocks, sz.gx, sz.gy) + tile
    own = (blocks, sz.ex, sz.ey) + tile
    products = like((sz.cells, sz.rows, full), f32)
    messages = [
        like((2, blocks, sz.gy) + tile, bf16),
        like((blocks, sz.gx) + tile, bf16),
        like((blocks, sz.gx) + tile, bf16),
    ]
    main_scratch = [pltpu.VMEM(grid, f32), pltpu.VMEM((2, sz.depth, full), f32)]
    corner_scratch = [
        pltpu.VMEM((LANES, full), f32),
        pltpu.VMEM((sz.cells, sz.base + sz.rows - sz.tail, full), f32),
    ]
    n_mat = len(mats)
    flops = 2 * sz.cells * sz.rows * sz.depth * full
    small_flops = 2 * sz.cells * sz.rows * LANES * full

    def exchange(face, near, far):
        face = swap_x(face)
        near, far = swap_y(near, far)
        (corner,) = call(
            functools.partial(corner_pack_kernel, sz), "corner_pack", 0,
            [like((2, 2) + sz.edge, bf16)], [], [near, far],
        )
        return [face, near, far], swap_x(corner)

    prod, ghost_x, ghost_y = call(
        functools.partial(first_main, sz, n_mat), "first_main", flops,
        [products, like((2, sz.ey) + tile, f32), like((2, sz.ex) + tile, f32)], main_scratch,
        [vectors, from_x, from_y, own_inv, own_pot, *mats],
    )
    acc, face, near, far, last_x, last_field = call(
        functools.partial(first_corner, sz, n_mat), "first_corner", small_flops,
        [like(grid, f32), *messages, like(sz.edge, f32), like((2,) + tile, f32)], corner_scratch,
        [
            parity, vectors, from_x, from_y, ghost_corner, own_inv, own_pot, ghost_x, ghost_y, prod, *mats,
        ],
        scalar_first=True,
    )
    (turned,) = call(
        functools.partial(turn_kernel, sz), "turn_residents", flops // 2,
        [like((res_count, sz.edges * ez), bf16)], [],
        [resident.reshape(-1, res_count), from_x, from_y, ghost_corner],
    )
    got, corner = exchange(face, near, far)
    state = [vectors, from_x, from_y, own_inv, own_pot, ghost_x, ghost_y]
    ends = [last_x, last_field]
    prod, y1 = call(
        functools.partial(second_main, sz, n_mat), "second_main", flops,
        [products, like(grid, f32)], main_scratch,
        [parity, *state, acc, *got, *mats], scalar_first=True,
    )
    acc, face, near, far, y1_corner = call(
        functools.partial(second_corner, sz, n_mat), "second_corner", small_flops,
        [like(grid, f32), *messages, like((4,) + sz.edge, f32)], corner_scratch,
        [parity, *state, *ends, acc, *got, corner, prod, *mats], scalar_first=True,
    )
    got, corner = exchange(face, near, far)
    prod, y2 = call(
        functools.partial(third_main, sz, n_mat), "third_main", flops,
        [products, like(grid, f32)], main_scratch,
        [parity, *state, acc, *got, y1, *mats], scalar_first=True,
    )
    filtered, edge_x, edge_y, face, side, corner, local = call(
        functools.partial(third_corner, sz, n_mat, norm_scale), "third_corner",
        small_flops + 2 * res_count * sz.edges * ez * full,
        [
            like(own, f32), like((blocks, sz.ey) + tile, f32), like((blocks, sz.ex - 1) + tile, f32),
            like((blocks, sz.ey) + tile, bf16), like((blocks, sz.ex) + tile, f32),
            like(sz.edge, bf16), like((res_count, full), bf16),
        ],
        [pltpu.VMEM(own, f32), pltpu.SemaphoreType.DMA, pltpu.VMEM(grid, f32), pltpu.VMEM((sz.edges, ez, full), bf16)] + corner_scratch,
        [parity, *state, *ends, acc, *got, corner, prod, y1, y1_corner, y2, turned, *mats],
        scalar_first=True, out_hbm=1,
    )

    pieces = lax.all_to_all(local.reshape(ny, -1, full), "dy", 0, 0)
    mine = jnp.sum(pieces.astype(f32), axis=0)
    margin = mine
    for steps in range(1, nx):
        margin = margin + send(mine, steps, 0)

    corner = send(corner, 1, 0)
    side, face = call(
        functools.partial(last_side_kernel, sz), "last_side", 0,
        [like((blocks, sz.ex) + tile, bf16), face], [], [side, corner, face], aliases={2: 1},
    )
    face = send(face, 1, 0)
    side = send(side, 0, 1)
    (filtered,) = call(
        functools.partial(last_kernel, sz), "last", 0, [like(own, f32)],
        [
            pltpu.VMEM((blocks, sz.ey) + tile, f32), pltpu.VMEM((blocks, sz.ex - 1) + tile, f32),
            pltpu.SemaphoreType.DMA((2,)),
        ],
        [filtered, edge_x, edge_y, face, side], hbm=1, out_hbm=1, aliases={0: 0},
    )
    return (filtered, margin)


def solution(mesh):
    return jax.shard_map(
        body,
        mesh=mesh,
        in_specs=(
            P(None, "dx", "dy", None, None),
            P("dx", "dy", None, None),
            P("dx", "dy", None),
            P("dx", "dy", None),
            P(),
            P("dx", "dy", None, None),
        ),
        out_specs=(P(None, "dx", "dy", None, None), P("dy", None)),
        check_vma=False,
    )
```

```python
import functools
import math

import jax
import jax.numpy as jnp
from jax import lax
from jax.experimental import pallas as pl
from jax.experimental.pallas import tpu as pltpu
from jax.sharding import PartitionSpec as P

LANES = 128
TILE = 256
SUB = 16
VMEM_LIMIT = 16 * 1024 * 1024

center_shift = 1.2
half_width = 2.0
gain = 2.0 / half_width

f32, bf16 = jnp.float32, jnp.bfloat16


def round_up(value, step):
    return -(-value // step) * step


class Sizes:
    def __init__(self, vectors, resident, inv_mass, connectivity):
        self.blocks = vectors.shape[0]
        self.width = vectors.shape[-1]
        self.full = self.blocks * self.width
        self.res = resident.shape[-1]
        self.wide = self.res + self.full + self.width
        self.ex, self.ey, self.ez = inv_mass.shape
        self.cells, self.nodes = connectivity.shape[2:]
        self.n1 = round(self.nodes ** (1.0 / 3.0))
        self.p = self.n1 - 1
        self.cx, self.cy, self.cz = self.ex // self.p, self.ey // self.p, self.ez // self.p
        self.gx, self.gy, self.gz = self.ex + 1, self.ey + 1, self.ez
        self.edge = (self.blocks, self.ez, self.width)
        self.origins = [
            (a * self.p, b * self.p, c * self.p)
            for a in range(self.cx)
            for b in range(self.cy)
            for c in range(self.cz)
        ]
        self.most = max(len(self.cell_corners(cell)) for cell in range(self.cells))
        self.base = round_up(self.most * self.n1, 8)
        plain = self.n1 * self.n1 - min(len(self.cell_corners(cell)) for cell in range(self.cells))
        self.tail = self.base + plain * self.p
        self.rows = round_up(self.tail + plain, SUB)
        self.depth = round_up(self.rows, LANES)
        self.own_edges = self.ex * self.ey
        self.edges = round_up(self.own_edges + self.ey + self.gx, LANES // self.ez)

    def corner(self, i, j):
        if i in (0, self.ex) and j in (0, self.ey):
            return 2 * (i // self.ex) + j // self.ey
        return None

    def cell_corners(self, cell):
        x0, y0, _ = self.origins[cell]
        return [
            (i, j)
            for i in range(self.n1)
            for j in range(self.n1)
            if self.corner(x0 + i, y0 + j) is not None
        ]

    def runs(self, cell):
        corners = self.cell_corners(cell)
        place = 0
        for i in range(self.n1):
            js = [j for j in range(self.n1) if (i, j) not in corners]
            while js:
                count = 1
                while count < len(js) and js[count] == js[0] + count:
                    count += 1
                yield place, i, js[0], count
                place += count
                js = js[count:]


def send(value, steps_x, steps_y):
    nx, ny = lax.axis_size("dx"), lax.axis_size("dy")
    pairs = [
        (a * ny + b, ((a + steps_x) % nx) * ny + (b + steps_y) % ny)
        for a in range(nx)
        for b in range(ny)
    ]
    return lax.ppermute(value, ("dx", "dy"), pairs)


def swap_x(value):
    if lax.axis_size("dx") == 2:
        return send(value, 1, 0)
    return jnp.stack([send(value[0], -1, 0), send(value[1], 1, 0)])


def send_near(value):
    pairs = [(b, b + 1 if b % 2 == 0 else b - 1) for b in range(lax.axis_size("dy"))]
    return lax.ppermute(value, "dy", pairs)


def swap_y(near, far):
    ny = lax.axis_size("dy")
    far_pairs = [(b, (b - 1 if b % 2 == 0 else b + 1) % ny) for b in range(ny)]
    far = lax.ppermute(far, "dy", far_pairs)
    return send_near(near), far


def order_kernel(sz, conn_ref, matrix_ref, out_ref):
    for cell in range(sz.cells):
        x0, y0, z0 = sz.origins[cell]
        conn = conn_ref[cell : cell + 1, :].astype(f32)
        li = jnp.floor((conn + 0.5) * (1.0 / (sz.gy * sz.gz)))
        rest = conn - li * (sz.gy * sz.gz)
        lj = jnp.floor((rest + 0.5) * (1.0 / sz.gz))
        lk = rest - lj * sz.gz - z0
        lk = jnp.where(lk < 0, lk + sz.gz, lk)
        column = (li - x0) * sz.n1 + (lj - y0)
        corners = [i * sz.n1 + j for i, j in sz.cell_corners(cell)]
        place = column
        for at in corners:
            place = place - jnp.where(column > at, 1.0, 0.0)
        index = jnp.where(lk < sz.p, sz.base + place * sz.p + lk, sz.tail + place)
        for rank, at in enumerate(corners):
            special = jnp.where(lk < sz.p, rank * sz.p + lk, len(corners) * sz.p + rank)
            index = jnp.where(column == at, special, index)
        index = index.astype(jnp.int32)
        row = lax.broadcasted_iota(jnp.int32, (sz.depth, sz.nodes), 0)
        pick = (row == index).astype(f32).astype(bf16)
        half = jnp.dot(pick[: sz.rows], matrix_ref[...], preferred_element_type=f32)
        half = half.astype(bf16)
        cuts = list(range(0, sz.depth, TILE)) + [sz.depth]
        for r0, r1 in zip(cuts[:-1], cuts[1:]):
            r1 = min(r1, sz.rows)
            block = lax.dot_general(
                half[r0:r1], pick[r0:], (((1,), (1,)), ((), ())), preferred_element_type=f32
            ).astype(bf16)
            out_ref[cell, r0:r1, r0:] = block
            for c0, c1 in zip(cuts[:-1], cuts[1:]):
                if c0 > r0:
                    mirror = block[:, c0 - r0 : c1 - r0].T
                    c1 = min(c1, sz.rows)
                    out_ref[cell, c0:c1, r0:r1] = mirror[: c1 - c0]


def field_row(inv, pot):
    lane = lax.broadcasted_iota(jnp.int32, inv.shape, inv.ndim - 1)
    row = jnp.zeros_like(inv)
    for at, rest in enumerate((inv, pot)):
        for k in range(3):
            part = rest.astype(bf16).astype(f32)
            rest = rest - part
            row = jnp.where(lane == 3 * at + k, part, row)
    return row.astype(bf16)


def field_rows(sz, inv, pot, count):
    inv, pot = inv.T, pot.T
    shape = (sz.ez, sz.width)
    for at in range(count):
        yield at, field_row(
            jnp.broadcast_to(inv[:, at : at + 1], shape), jnp.broadcast_to(pot[:, at : at + 1], shape)
        )


def fields_of(row):
    row = row.astype(f32)
    return [
        jnp.broadcast_to(sum(row[:, 3 * at + k : 3 * at + k + 1] for k in range(3)), row.shape)
        for at in range(2)
    ]


def pack_kernel(
    sz, vec_hbm, res_hbm, inv_hbm, pot_hbm, mat_hbm, conn_hbm,
    to_x, to_y, mat_ref, conn_ref, at_x, at_y, sems,
):
    pairs = [
        (inv_hbm.at[0], at_x.at[0]), (pot_hbm.at[0], at_x.at[1]),
        (inv_hbm.at[:, 0], at_y.at[0]), (pot_hbm.at[:, 0], at_y.at[1]),
        (res_hbm.at[0], to_x.at[:, :, pl.ds(0, sz.res)]),
        (res_hbm.at[:, 0], to_y.at[:, :, pl.ds(0, sz.res)]),
    ]
    for b in range(sz.blocks):
        lanes = pl.ds(sz.res + b * sz.width, sz.width)
        pairs.append((vec_hbm.at[b, 0], to_x.at[:, :, lanes]))
        pairs.append((vec_hbm.at[b, :, 0], to_y.at[:, :, lanes]))
    pairs += [(mat_hbm, mat_ref), (conn_hbm, conn_ref)]
    copies = [pltpu.make_async_copy(a, b, sems.at[k]) for k, (a, b) in enumerate(pairs)]
    for copy in copies:
        copy.start()
    for copy in copies[:4]:
        copy.wait()
    for j, row in field_rows(sz, at_x[0], at_x[1], sz.ey):
        to_x[j, :, sz.res + sz.full :] = row
    for i, row in field_rows(sz, at_y[0], at_y[1], sz.ex):
        to_y[i, :, sz.res + sz.full :] = row
    for copy in copies[4:]:
        copy.wait()


def turn_kernel(sz, pieces, res_ref, from_x, from_y, corner, out_ref):
    own = sz.own_edges * sz.ez
    share = sz.res // out_ref.shape[0] // pieces

    def put(g, columns, value):
        for at in range(0, LANES, share):
            owner = (g + at) // share
            row = owner // 2 * share
            out_ref[owner % 2, row : row + share, columns] = value[at : at + share]

    for g in range(0, sz.res, LANES):
        lanes = slice(g, g + LANES)
        put(g, slice(0, own), res_ref[:, lanes].T)
        rest = sz.edges - sz.own_edges - sz.ey - sz.gx
        parts = [from_x[:, :, lanes], from_y[:, :, lanes], corner[:, :, lanes]]
        if rest:
            parts.append(jnp.zeros((rest, sz.ez, LANES), bf16))
        ghosts = jnp.concatenate(parts, axis=0)
        put(g, slice(own, sz.edges * sz.ez), ghosts.reshape(-1, LANES).T)


def vectors_of(sz, edge):
    lanes = [slice(sz.res + b * sz.width, sz.res + (b + 1) * sz.width) for b in range(sz.blocks)]
    return jnp.stack([edge[:, at] for at in lanes]).astype(f32)


class Nodes:
    def __init__(self, sz, vec, from_x, from_y, own_inv, own_pot, ghost_x, ghost_y, corners=None):
        self.sz, self.vec, self.from_x, self.from_y = sz, vec, from_x, from_y
        self.own, self.ghost_x, self.ghost_y, self.corners = (own_inv, own_pot), ghost_x, ghost_y, corners

    def x(self, i, j):
        sz = self.sz
        if i < sz.ex and j < sz.ey:
            return self.vec[:, i, j].astype(f32)
        return vectors_of(sz, self.from_x[j] if i == sz.ex else self.from_y[i])

    def field(self, at, i, j):
        sz = self.sz
        if i < sz.ex and j < sz.ey:
            return self.own[at][i, j]
        if i < sz.ex:
            return self.ghost_y[at, i]
        if j < sz.ey:
            return self.ghost_x[at, j]
        return self.corners[at]

    def inv(self, i, j):
        return self.field(0, i, j)

    def pot(self, i, j):
        return self.field(1, i, j)


class Sums:
    def __init__(self, sz, even, acc, face, near, far, corner=None):
        self.sz, self.even, self.acc, self.face = sz, even, acc, face
        self.near, self.far, self.corner = near, far, corner

    def at(self, i, j):
        sz = self.sz
        total = self.acc[:, i, j]
        side = 1 if i == 0 else 0 if i == sz.ex else None
        if side is not None:
            total = total + self.face[side, :, j].astype(f32)
        if j in (0, sz.ey):
            is_near = self.even if j == sz.ey else jnp.logical_not(self.even)
            total = total + jnp.where(is_near, self.near[:, i].astype(f32), self.far[:, i].astype(f32))
            if side is not None:
                total = total + jnp.where(
                    is_near, self.corner[side, 0].astype(f32), self.corner[side, 1].astype(f32)
                )
        return total


def corner_edges(sz):
    return [(i, j) for i in (0, sz.ex) for j in (0, sz.ey)]


def main_products(sz, prepare, u_ref, mat_refs, rhs_ref, out_ref):
    width = sz.width
    flat = sz.gx * sz.gy * sz.gz
    u_flat = u_ref.reshape(sz.blocks * flat, width)
    matrices = [ref.at[c] for ref in mat_refs for c in range(ref.shape[0])]
    last = sz.nodes // 8 * 8
    ready = set()
    for cell, (x0, y0, z0) in enumerate(sz.origins):
        slot = cell % 2
        if cell < 2:
            rhs_ref[slot, : sz.base] = jnp.zeros((sz.base, sz.full), f32)
            rhs_ref[slot, last:] = jnp.zeros((sz.depth - last, sz.full), f32)
        for place, i, j, count in sz.runs(cell):
            for at in range(j, j + count):
                if (x0 + i, y0 + at) not in ready:
                    prepare(x0 + i, y0 + at)
                    ready.add((x0 + i, y0 + at))
        z1 = z0 + sz.p
        wrap = z1 % sz.gz
        for b in range(sz.blocks):
            lanes = slice(b * width, (b + 1) * width)
            for place, i, j, count in sz.runs(cell):
                row = sz.base + place * sz.p
                rhs_ref[slot, row : row + count * sz.p, lanes] = u_ref[
                    b, x0 + i, y0 + j : y0 + j + count, z0:z1
                ].reshape(count * sz.p, width)
        for b in range(sz.blocks):
            lanes = slice(b * width, (b + 1) * width)
            for place, i, j, count in sz.runs(cell):
                start = b * flat + ((x0 + i) * sz.gy + y0 + j) * sz.gz + wrap
                rhs_ref[slot, sz.tail + place : sz.tail + place + count, lanes] = u_flat[
                    pl.ds(start, count, stride=sz.gz)
                ]
        out_ref[cell] = jnp.dot(
            matrices[cell][...], rhs_ref[slot].astype(bf16), preferred_element_type=f32
        )


def corner_products(sz, u_corner, prod_ref, mat_refs, small_ref, tail_ref, acc_ref):
    width = sz.width
    flat = sz.gx * sz.gy * sz.gz
    acc_flat = acc_ref.reshape(sz.blocks * flat, width)
    matrices = [ref.at[c] for ref in mat_refs for c in range(ref.shape[0])]
    small_ref[...] = jnp.zeros_like(small_ref)
    touched = set()
    for cell, (x0, y0, z0) in enumerate(sz.origins):
        z1 = z0 + sz.p
        wrap = z1 % sz.gz
        corners = sz.cell_corners(cell)
        for rank, (i, j) in enumerate(corners):
            value = u_corner[sz.corner(x0 + i, y0 + j)]
            last = len(corners) * sz.p + rank
            for b in range(sz.blocks):
                lanes = slice(b * width, (b + 1) * width)
                small_ref[rank * sz.p : (rank + 1) * sz.p, lanes] = value[b, z0:z1]
                small_ref[last : last + 1, lanes] = value[b, wrap : wrap + 1]
        total = prod_ref[cell] + jnp.dot(
            matrices[cell][:, : small_ref.shape[0]], small_ref[...].astype(bf16),
            preferred_element_type=f32,
        )
        tail_ref[cell, : sz.base] = total[: sz.base]
        tail_ref[cell, sz.base :] = total[sz.tail :]
        spans = [(rank * sz.p, i, j, 1) for rank, (i, j) in enumerate(corners)]
        spans += [(sz.base + place * sz.p, i, j, count) for place, i, j, count in sz.runs(cell)]
        for row, i, j, count in spans:
            for at in range(count):
                part = total[row + at * sz.p : row + (at + 1) * sz.p]
                key = (x0 + i, y0 + j + at, z0)
                for b in range(sz.blocks):
                    value = part[:, b * width : (b + 1) * width]
                    if key in touched:
                        value = acc_ref[b, key[0], key[1], z0:z1] + value
                    acc_ref[b, key[0], key[1], z0:z1] = value
                touched.add(key)
    for cell, (x0, y0, z0) in enumerate(sz.origins):
        wrap = (z0 + sz.p) % sz.gz
        corners = sz.cell_corners(cell)
        spans = [(len(corners) * sz.p + rank, i, j, 1) for rank, (i, j) in enumerate(corners)]
        spans += [(sz.base + place, i, j, count) for place, i, j, count in sz.runs(cell)]
        for row, i, j, count in spans:
            for b in range(sz.blocks):
                start = b * flat + ((x0 + i) * sz.gy + y0 + j) * sz.gz + wrap
                rows = pl.ds(start, count, stride=sz.gz) if count > 1 else pl.ds(start, 1)
                lanes = slice(b * width, (b + 1) * width)
                acc_flat[rows] = acc_flat[rows] + tail_ref[cell, row : row + count, lanes]


def write_messages(sz, even, acc_ref, face, near, far):
    at_near = jnp.where(even, sz.ey, 0)
    for b in range(sz.blocks):
        face[0, b] = acc_ref[b, 0].astype(bf16)
        face[1, b] = acc_ref[b, sz.ex].astype(bf16)
        near[b] = acc_ref[b, :, at_near].astype(bf16)
        far[b] = acc_ref[b, :, sz.ey - at_near].astype(bf16)


def corner_pack_kernel(sz, near, far, out_ref):
    for side, i in enumerate((0, sz.ex)):
        for slot, ref in enumerate((near, far)):
            out_ref[side, slot] = ref[:, i]


def first_main(sz, n_mat, vec, from_x, from_y, own_inv, own_pot, *refs):
    mats = refs[:n_mat]
    prod_ref, ghost_x, ghost_y, u_ref, rhs_ref = refs[n_mat:]
    for j in range(sz.ey):
        ghost_x[0, j], ghost_x[1, j] = fields_of(from_x[j, :, sz.res + sz.full :])
    for i in range(sz.ex):
        ghost_y[0, i], ghost_y[1, i] = fields_of(from_y[i, :, sz.res + sz.full :])
    nodes = Nodes(sz, vec, from_x, from_y, own_inv, own_pot, ghost_x, ghost_y)

    def prepare(i, j):
        u_ref[:, i, j] = nodes.x(i, j) * nodes.inv(i, j)

    main_products(sz, prepare, u_ref, mats, rhs_ref, prod_ref)


def first_corner(sz, n_mat, even_ref, vec, from_x, from_y, corner, own_inv, own_pot, ghost_x, ghost_y,
                 prod_ref, *refs):
    mats = refs[:n_mat]
    acc_ref, face, near, far, last_x, last_field, small_ref, tail_ref = refs[n_mat:]
    last_field[0], last_field[1] = fields_of(corner[0, :, sz.res + sz.full :])
    last_x[...] = vectors_of(sz, corner[0])
    nodes = Nodes(sz, vec, from_x, from_y, own_inv, own_pot, ghost_x, ghost_y, last_field)
    u_corner = []
    for i, j in corner_edges(sz):
        x = last_x[...] if (i, j) == (sz.ex, sz.ey) else nodes.x(i, j)
        u_corner.append(x * nodes.inv(i, j))
    corner_products(sz, u_corner, prod_ref, mats, small_ref, tail_ref, acc_ref)
    write_messages(sz, even_ref[0] == 0, acc_ref, face, near, far)


def second_main(sz, n_mat, even_ref, vec, from_x, from_y, own_inv, own_pot, ghost_x, ghost_y,
                acc_in, face_in, near_in, far_in, *refs):
    mats = refs[:n_mat]
    prod_ref, y_ref, u_ref, rhs_ref = refs[n_mat:]
    nodes = Nodes(sz, vec, from_x, from_y, own_inv, own_pot, ghost_x, ghost_y)
    sums = Sums(sz, even_ref[0] == 0, acc_in, face_in, near_in, far_in)

    def prepare(i, j):
        old, inv = nodes.x(i, j), nodes.inv(i, j)
        image = inv * sums.at(i, j) + nodes.pot(i, j) * old
        new = (image - center_shift * old) / half_width
        y_ref[:, i, j] = new
        u_ref[:, i, j] = inv * new

    main_products(sz, prepare, u_ref, mats, rhs_ref, prod_ref)


def second_corner(sz, n_mat, even_ref, vec, from_x, from_y, own_inv, own_pot, ghost_x, ghost_y, last_x,
                  last_field, acc_in, face_in, near_in, far_in, corner_in, prod_ref, *refs):
    mats = refs[:n_mat]
    acc_ref, face, near, far, y_corner, small_ref, tail_ref = refs[n_mat:]
    even = even_ref[0] == 0
    nodes = Nodes(sz, vec, from_x, from_y, own_inv, own_pot, ghost_x, ghost_y, last_field)
    sums = Sums(sz, even, acc_in, face_in, near_in, far_in, corner_in)
    u_corner = []
    for at, (i, j) in enumerate(corner_edges(sz)):
        old = last_x[...] if (i, j) == (sz.ex, sz.ey) else nodes.x(i, j)
        inv = nodes.inv(i, j)
        image = inv * sums.at(i, j) + nodes.pot(i, j) * old
        new = (image - center_shift * old) / half_width
        y_corner[at] = new
        u_corner.append(inv * new)
    corner_products(sz, u_corner, prod_ref, mats, small_ref, tail_ref, acc_ref)
    write_messages(sz, even, acc_ref, face, near, far)


def third_main(sz, n_mat, even_ref, vec, from_x, from_y, own_inv, own_pot, ghost_x, ghost_y,
               acc_in, face_in, near_in, far_in, y_ref, *refs):
    mats = refs[:n_mat]
    prod_ref, new_ref, u_ref, rhs_ref = refs[n_mat:]
    nodes = Nodes(sz, vec, from_x, from_y, own_inv, own_pot, ghost_x, ghost_y)
    sums = Sums(sz, even_ref[0] == 0, acc_in, face_in, near_in, far_in)

    def prepare(i, j):
        old, inv = y_ref[:, i, j], nodes.inv(i, j)
        image = inv * sums.at(i, j) + nodes.pot(i, j) * old
        new = 2.0 * (image - center_shift * old) / half_width - nodes.x(i, j)
        new_ref[:, i, j] = new
        u_ref[:, i, j] = inv * new

    main_products(sz, prepare, u_ref, mats, rhs_ref, prod_ref)


def third_corner(sz, n_mat, norm_scale, even_ref, vec, from_x, from_y, own_inv, own_pot, ghost_x, ghost_y,
                 last_x, last_field, acc_in, face_in, near_in, far_in, corner_in, prod_ref, y_ref,
                 y_corner, new_ref, turned, *refs):
    mats = refs[:n_mat]
    out_hbm, edge_x, edge_y, face, side, corner, give, keep = refs[n_mat : n_mat + 8]
    part_ref, sem, acc_ref, rows_ref, small_ref, tail_ref = refs[n_mat + 8 :]
    nodes = Nodes(sz, vec, from_x, from_y, own_inv, own_pot, ghost_x, ghost_y, last_field)
    sums = Sums(sz, even_ref[0] == 0, acc_in, face_in, near_in, far_in, corner_in)
    u_corner, new_corner = [], []
    for at, (i, j) in enumerate(corner_edges(sz)):
        x = last_x[...] if (i, j) == (sz.ex, sz.ey) else nodes.x(i, j)
        old, inv = y_corner[at], nodes.inv(i, j)
        image = inv * sums.at(i, j) + nodes.pot(i, j) * old
        new_corner.append(2.0 * (image - center_shift * old) / half_width - x)
        u_corner.append(inv * new_corner[-1])
    corner_products(sz, u_corner, prod_ref, mats, small_ref, tail_ref, acc_ref)

    def put_row(at, value):
        for b in range(sz.blocks):
            rows_ref[at, :, b * sz.width : (b + 1) * sz.width] = value[b]

    copies = []
    for i in range(sz.gx):
        for j in range(sz.gy):
            acc, inv = acc_ref[:, i, j], nodes.inv(i, j)
            if i == sz.ex or j == sz.ey:
                value = gain * (inv * acc)
                rounded = value.astype(bf16)
                if j < sz.ey:
                    put_row(sz.own_edges + j, rounded)
                    face[:, j] = rounded
                else:
                    put_row(sz.own_edges + sz.ey + i, rounded)
                    if i < sz.ex:
                        side[:, i] = value
                    else:
                        corner[...] = rounded
                continue
            at = sz.corner(i, j)
            old = y_ref[:, i, j] if at is None else y_corner[at]
            new = new_ref[:, i, j] if at is None else new_corner[at]
            image = inv * acc + nodes.pot(i, j) * new
            value = 2.0 * (image - center_shift * new) / half_width - old
            part_ref[:, i, j] = value
            if i == 0:
                edge_x[:, j] = value
            elif j == 0:
                edge_y[:, i - 1] = value
            put_row(i * sz.ey + j, value.astype(bf16))
        if i < sz.ex:
            copies.append(pltpu.make_async_copy(part_ref.at[:, i], out_hbm.at[:, i], sem.at[i]))
            copies[-1].start()
    for at in range(sz.own_edges + sz.ey + sz.gx, sz.edges):
        rows_ref[at] = jnp.zeros((sz.ez, sz.full), bf16)
    rows = rows_ref[...].reshape(sz.edges * sz.ez, sz.full)
    mine = even_ref[0]
    for half, out in ((1 - mine, give), (mine, keep)):
        local = jnp.dot(turned[half], rows, preferred_element_type=f32)
        out[...] = (local * norm_scale).astype(out.dtype)
    for copy in copies:
        copy.wait()


def last_side_kernel(sz, side_ref, corner_ref, face_in, out_ref, face_out):
    del face_in, face_out
    for i in range(sz.ex):
        value = side_ref[:, i]
        if i == 0:
            value = value + corner_ref[...].astype(f32)
        out_ref[:, i] = value.astype(out_ref.dtype)


def last_kernel(sz, old_hbm, edge_x, edge_y, face, side, out_hbm, at_x, at_y, sems):
    del old_hbm
    for j in range(sz.ey):
        value = edge_x[:, j] + face[:, j].astype(f32)
        if j == 0:
            value = value + side[:, 0].astype(f32)
        at_x[:, j] = value
    for i in range(1, sz.ex):
        at_y[:, i - 1] = edge_y[:, i - 1] + side[:, i].astype(f32)
    copies = [
        pltpu.make_async_copy(at_x, out_hbm.at[:, 0], sems.at[0]),
        pltpu.make_async_copy(at_y, out_hbm.at[:, pl.ds(1, sz.ex - 1), 0], sems.at[1]),
    ]
    for copy in copies:
        copy.start()
    for copy in copies:
        copy.wait()


def like(shape, dtype):
    return jax.ShapeDtypeStruct(shape, dtype)


class Pinned:
    def __init__(self, value):
        self.value, self.shape, self.dtype = value, value.shape, value.dtype


def call(kernel, name, flops, out_shape, scratch, operands, hbm=0, scalar_first=False, aliases=None,
         out_hbm=0):
    pinned = [isinstance(s, Pinned) for s in out_shape]
    out_shape = [like(s.shape, s.dtype) for s in out_shape]
    size = sum(math.prod(s.shape) * jnp.dtype(s.dtype).itemsize for s in (*operands, *out_shape))
    whole = pl.BlockSpec(memory_space=pltpu.VMEM)
    specs = [pl.BlockSpec(memory_space=pltpu.HBM)] * hbm + [whole] * (len(operands) - hbm)
    if scalar_first:
        specs[0] = pl.BlockSpec(memory_space=pltpu.SMEM)
    out_specs = [pl.BlockSpec(memory_space=pltpu.HBM)] * out_hbm + [whole] * (len(out_shape) - out_hbm)
    out_shape = [pltpu.HBM(s.shape, s.dtype) for s in out_shape[:out_hbm]] + out_shape[out_hbm:]
    out_shape = [pltpu.VMEM(s.shape, s.dtype) if p else s for s, p in zip(out_shape, pinned)]
    operands = [pltpu.with_memory_space_constraint(a, pltpu.HBM) for a in operands[:hbm]] + list(
        pltpu.with_memory_space_constraint(a.value, pltpu.VMEM) if isinstance(a, Pinned) else a
        for a in operands[hbm:]
    )
    results = pl.pallas_call(
        kernel,
        in_specs=specs,
        out_specs=out_specs,
        out_shape=out_shape,
        scratch_shapes=scratch,
        input_output_aliases=aliases or {},
        compiler_params=pltpu.CompilerParams(vmem_limit_bytes=VMEM_LIMIT),
        cost_estimate=pl.CostEstimate(flops=flops, bytes_accessed=size, transcendentals=0),
        name=name,
    )(*operands)
    return [Pinned(r) if p else r for r, p in zip(results, pinned)]


def body(vectors, resident, inv_mass, potential, cell_matrix, connectivity):
    sz = Sizes(vectors, resident, inv_mass, connectivity)
    nx, ny = lax.axis_size("dx"), lax.axis_size("dy")
    norm_scale = 1.0 / math.sqrt(sz.ex * sz.ey * sz.ez * nx * ny)
    blocks, ez, width, full = sz.blocks, sz.ez, sz.width, sz.full
    res_count = resident.shape[-1]
    tile = (ez, width)

    conn = connectivity.reshape(sz.cells, sz.nodes)
    to_x, to_y, cell_matrix, conn = call(
        functools.partial(pack_kernel, sz), "pack", 0,
        [like((sz.ey, ez, sz.wide), bf16), like((sz.ex, ez, sz.wide), bf16), Pinned(cell_matrix), conn],
        [
            pltpu.VMEM((2, sz.ey, ez), f32), pltpu.VMEM((2, sz.ex, ez), f32),
            pltpu.SemaphoreType.DMA((8 + 2 * blocks,)),
        ],
        [vectors, resident, inv_mass, potential, cell_matrix, conn], hbm=6,
    )
    from_x = send(to_x, -1, 0)
    from_y = send(to_y, 0, -1)

    mats = call(
        functools.partial(order_kernel, sz), "order_cells", 4 * sz.cells * sz.depth**3,
        [Pinned(like((sz.cells, sz.rows, sz.depth), bf16))], [], [conn, cell_matrix],
    )
    own_inv = jnp.broadcast_to(inv_mass[..., None], inv_mass.shape + (width,))
    own_pot = jnp.broadcast_to(potential[..., None], inv_mass.shape + (width,))
    parity = jnp.reshape(lax.axis_index("dy") % 2, (1,)).astype(jnp.int32)
    ghost_corner = send(from_y[:1], -1, 0)

    grid = (blocks, sz.gx, sz.gy) + tile
    own = (blocks, sz.ex, sz.ey) + tile
    products = Pinned(like((sz.cells, sz.rows, full), f32))
    state_grid = Pinned(like(grid, f32))
    messages = [
        like((2, blocks, sz.gy) + tile, bf16),
        like((blocks, sz.gx) + tile, bf16),
        like((blocks, sz.gx) + tile, bf16),
    ]
    main_scratch = [pltpu.VMEM(grid, f32), pltpu.VMEM((2, sz.depth, full), f32)]
    corner_scratch = [
        pltpu.VMEM((LANES, full), f32),
        pltpu.VMEM((sz.cells, sz.base + sz.rows - sz.tail, full), f32),
    ]
    n_mat = len(mats)
    flops = 2 * sz.cells * sz.rows * sz.depth * full
    small_flops = 2 * sz.cells * sz.rows * LANES * full

    def exchange(face, near, far):
        face = swap_x(face)
        near, far = swap_y(near, far)
        (corner,) = call(
            functools.partial(corner_pack_kernel, sz), "corner_pack", 0,
            [like((2, 2) + sz.edge, bf16)], [], [near, far],
        )
        return [face, near, far], swap_x(corner)

    prod, ghost_x, ghost_y = call(
        functools.partial(first_main, sz, n_mat), "first_main", flops,
        [products, like((2, sz.ey) + tile, f32), like((2, sz.ex) + tile, f32)], main_scratch,
        [vectors, from_x, from_y, own_inv, own_pot, *mats],
    )
    acc, face, near, far, last_x, last_field = call(
        functools.partial(first_corner, sz, n_mat), "first_corner", small_flops,
        [state_grid, *messages, like(sz.edge, f32), like((2,) + tile, f32)], corner_scratch,
        [
            parity, vectors, from_x, from_y, ghost_corner, own_inv, own_pot, ghost_x, ghost_y, prod, *mats,
        ],
        scalar_first=True,
    )
    (turned,) = call(
        functools.partial(turn_kernel, sz, ny // 2), "turn_residents", flops // 2,
        [like((2, res_count // 2, sz.edges * ez), bf16)], [],
        [resident.reshape(-1, res_count), from_x, from_y, ghost_corner],
    )
    got, corner = exchange(face, near, far)
    state = [vectors, from_x, from_y, own_inv, own_pot, ghost_x, ghost_y]
    ends = [last_x, last_field]
    prod, y1 = call(
        functools.partial(second_main, sz, n_mat), "second_main", flops,
        [products, state_grid], main_scratch,
        [parity, *state, acc, *got, *mats], scalar_first=True,
    )
    acc, face, near, far, y1_corner = call(
        functools.partial(second_corner, sz, n_mat), "second_corner", small_flops,
        [state_grid, *messages, like((4,) + sz.edge, f32)], corner_scratch,
        [parity, *state, *ends, acc, *got, corner, prod, *mats], scalar_first=True,
    )
    got, corner = exchange(face, near, far)
    prod, y2 = call(
        functools.partial(third_main, sz, n_mat), "third_main", flops,
        [products, state_grid], main_scratch,
        [parity, *state, acc, *got, y1, *mats], scalar_first=True,
    )
    filtered, edge_x, edge_y, face, side, corner, give, keep = call(
        functools.partial(third_corner, sz, n_mat, norm_scale), "third_corner",
        small_flops + 2 * res_count * sz.edges * ez * full,
        [
            like(own, f32), like((blocks, sz.ey) + tile, f32), like((blocks, sz.ex - 1) + tile, f32),
            like((blocks, sz.ey) + tile, bf16), like((blocks, sz.ex) + tile, f32),
            like(sz.edge, bf16), like((res_count // 2, full), bf16), like((res_count // 2, full), f32),
        ],
        [pltpu.VMEM(own, f32), pltpu.SemaphoreType.DMA((sz.ex,)), pltpu.VMEM(grid, f32), pltpu.VMEM((sz.edges, ez, full), bf16)] + corner_scratch,
        [parity, *state, *ends, acc, *got, corner, prod, y1, y1_corner, y2, turned, *mats],
        scalar_first=True, out_hbm=1,
    )

    mine = (keep + send_near(give).astype(f32)).astype(bf16).reshape(1, ny // 2, -1, full)
    mine = jnp.broadcast_to(mine, (nx,) + mine.shape[1:]).reshape(nx * ny // 2, -1, full)
    groups = [[a * ny + b for a in range(nx) for b in range(c, ny, 2)] for c in range(2)]
    pieces = lax.all_to_all(mine, ("dx", "dy"), 0, 0, axis_index_groups=groups)
    margin = jnp.sum(pieces.astype(f32), axis=0)

    corner = send(corner, 1, 0)
    side, face = call(
        functools.partial(last_side_kernel, sz), "last_side", 0,
        [like((blocks, sz.ex) + tile, bf16), face], [], [side, corner, face], aliases={2: 1},
    )
    face = send(face, 1, 0)
    side = send(side, 0, 1)
    (filtered,) = call(
        functools.partial(last_kernel, sz), "last", 0, [like(own, f32)],
        [
            pltpu.VMEM((blocks, sz.ey) + tile, f32), pltpu.VMEM((blocks, sz.ex - 1) + tile, f32),
            pltpu.SemaphoreType.DMA((2,)),
        ],
        [filtered, edge_x, edge_y, face, side], hbm=1, out_hbm=1, aliases={0: 0},
    )
    return (filtered, margin)


def solution(mesh):
    return jax.shard_map(
        body,
        mesh=mesh,
        in_specs=(
            P(None, "dx", "dy", None, None),
            P("dx", "dy", None, None),
            P("dx", "dy", None),
            P("dx", "dy", None),
            P(),
            P("dx", "dy", None, None),
        ),
        out_specs=(P(None, "dx", "dy", None, None), P("dy", None)),
        check_vma=False,
    )
```

```python
import functools
import math

import jax
import jax.numpy as jnp
from jax import lax
from jax.experimental import pallas as pl
from jax.experimental.pallas import tpu as pltpu
from jax.sharding import PartitionSpec as P

LANES = 128
TILE = 256
SUB = 16
VMEM_LIMIT = 12 * 1024 * 1024

center_shift = 1.2
half_width = 2.0
gain = 2.0 / half_width

f32, bf16 = jnp.float32, jnp.bfloat16


def round_up(value, step):
    return -(-value // step) * step


class Sizes:
    def __init__(self, vectors, resident, inv_mass, connectivity):
        self.blocks = vectors.shape[0]
        self.width = vectors.shape[-1]
        self.full = self.blocks * self.width
        self.res = resident.shape[-1]
        self.wide = self.res + self.full + self.width
        self.ex, self.ey, self.ez = inv_mass.shape
        self.cells, self.nodes = connectivity.shape[2:]
        self.n1 = round(self.nodes ** (1.0 / 3.0))
        self.p = self.n1 - 1
        self.cx, self.cy, self.cz = self.ex // self.p, self.ey // self.p, self.ez // self.p
        self.gx, self.gy, self.gz = self.ex + 1, self.ey + 1, self.ez
        self.edge = (self.blocks, self.ez, self.width)
        self.origins = [
            (a * self.p, b * self.p, c * self.p)
            for a in range(self.cx)
            for b in range(self.cy)
            for c in range(self.cz)
        ]
        self.most = max(len(self.cell_corners(cell)) for cell in range(self.cells))
        self.base = round_up(self.most * self.n1, 8)
        plain = self.n1 * self.n1 - min(len(self.cell_corners(cell)) for cell in range(self.cells))
        self.tail = self.base + plain * self.p
        self.rows = round_up(self.tail + plain, SUB)
        self.depth = round_up(self.rows, LANES)
        self.own_edges = self.ex * self.ey
        self.edges = round_up(self.own_edges + self.ey + self.gx, LANES // self.ez)

    def corner(self, i, j):
        if i in (0, self.ex) and j in (0, self.ey):
            return 2 * (i // self.ex) + j // self.ey
        return None

    def cell_corners(self, cell):
        x0, y0, _ = self.origins[cell]
        return [
            (i, j)
            for i in range(self.n1)
            for j in range(self.n1)
            if self.corner(x0 + i, y0 + j) is not None
        ]

    def runs(self, cell):
        corners = self.cell_corners(cell)
        place = 0
        for i in range(self.n1):
            js = [j for j in range(self.n1) if (i, j) not in corners]
            while js:
                count = 1
                while count < len(js) and js[count] == js[0] + count:
                    count += 1
                yield place, i, js[0], count
                place += count
                js = js[count:]


def send(value, steps_x, steps_y):
    nx, ny = lax.axis_size("dx"), lax.axis_size("dy")
    pairs = [
        (a * ny + b, ((a + steps_x) % nx) * ny + (b + steps_y) % ny)
        for a in range(nx)
        for b in range(ny)
    ]
    return lax.ppermute(value, ("dx", "dy"), pairs)


def swap_x(value):
    if lax.axis_size("dx") == 2:
        return send(value, 1, 0)
    return jnp.stack([send(value[0], -1, 0), send(value[1], 1, 0)])


def send_near(value):
    pairs = [(b, b + 1 if b % 2 == 0 else b - 1) for b in range(lax.axis_size("dy"))]
    return lax.ppermute(value, "dy", pairs)


def swap_y(near, far):
    ny = lax.axis_size("dy")
    far_pairs = [(b, (b - 1 if b % 2 == 0 else b + 1) % ny) for b in range(ny)]
    far = lax.ppermute(far, "dy", far_pairs)
    return send_near(near), far


def order_kernel(sz, conn_ref, matrix_ref, *out_refs):
    for cell in range(sz.cells):
        x0, y0, z0 = sz.origins[cell]
        conn = conn_ref[cell : cell + 1, :].astype(f32)
        li = jnp.floor((conn + 0.5) * (1.0 / (sz.gy * sz.gz)))
        rest = conn - li * (sz.gy * sz.gz)
        lj = jnp.floor((rest + 0.5) * (1.0 / sz.gz))
        lk = rest - lj * sz.gz - z0
        lk = jnp.where(lk < 0, lk + sz.gz, lk)
        column = (li - x0) * sz.n1 + (lj - y0)
        corners = [i * sz.n1 + j for i, j in sz.cell_corners(cell)]
        place = column
        for at in corners:
            place = place - jnp.where(column > at, 1.0, 0.0)
        index = jnp.where(lk < sz.p, sz.base + place * sz.p + lk, sz.tail + place)
        for rank, at in enumerate(corners):
            special = jnp.where(lk < sz.p, rank * sz.p + lk, len(corners) * sz.p + rank)
            index = jnp.where(column == at, special, index)
        index = index.astype(jnp.int32)
        row = lax.broadcasted_iota(jnp.int32, (sz.depth, sz.nodes), 0)
        pick = (row == index).astype(f32).astype(bf16)
        half = jnp.dot(pick[: sz.rows], matrix_ref[...], preferred_element_type=f32)
        half = half.astype(bf16)
        cuts = list(range(0, sz.depth, TILE)) + [sz.depth]
        for r0, r1 in zip(cuts[:-1], cuts[1:]):
            r1 = min(r1, sz.rows)
            block = lax.dot_general(
                half[r0:r1], pick[r0:], (((1,), (1,)), ((), ())), preferred_element_type=f32
            ).astype(bf16)
            out_refs[cell][r0:r1, r0:] = block
            for c0, c1 in zip(cuts[:-1], cuts[1:]):
                if c0 > r0:
                    mirror = block[:, c0 - r0 : c1 - r0].T
                    c1 = min(c1, sz.rows)
                    out_refs[cell][c0:c1, r0:r1] = mirror[: c1 - c0]


def field_row(inv, pot):
    lane = lax.broadcasted_iota(jnp.int32, inv.shape, inv.ndim - 1)
    row = jnp.zeros_like(inv)
    for at, rest in enumerate((inv, pot)):
        for k in range(3):
            part = rest.astype(bf16).astype(f32)
            rest = rest - part
            row = jnp.where(lane == 3 * at + k, part, row)
    return row.astype(bf16)


def field_rows(sz, inv, pot, count):
    inv, pot = inv.T, pot.T
    shape = (sz.ez, sz.width)
    for at in range(count):
        yield at, field_row(
            jnp.broadcast_to(inv[:, at : at + 1], shape), jnp.broadcast_to(pot[:, at : at + 1], shape)
        )


def fields_of(row):
    row = row.astype(f32)
    return [
        jnp.broadcast_to(sum(row[:, 3 * at + k : 3 * at + k + 1] for k in range(3)), row.shape)
        for at in range(2)
    ]


def pack_kernel(
    sz, vec_hbm, res_hbm, inv_hbm, pot_hbm, mat_hbm, conn_hbm,
    to_x, to_y, mat_ref, conn_ref, at_x, at_y, sems,
):
    pairs = [
        (inv_hbm.at[0], at_x.at[0]), (pot_hbm.at[0], at_x.at[1]),
        (inv_hbm.at[:, 0], at_y.at[0]), (pot_hbm.at[:, 0], at_y.at[1]),
        (res_hbm.at[0], to_x.at[:, :, pl.ds(0, sz.res)]),
        (res_hbm.at[:, 0], to_y.at[:, :, pl.ds(0, sz.res)]),
    ]
    for b in range(sz.blocks):
        lanes = pl.ds(sz.res + b * sz.width, sz.width)
        pairs.append((vec_hbm.at[b, 0], to_x.at[:, :, lanes]))
        pairs.append((vec_hbm.at[b, :, 0], to_y.at[:, :, lanes]))
    pairs += [(mat_hbm, mat_ref), (conn_hbm, conn_ref)]
    copies = [pltpu.make_async_copy(a, b, sems.at[k]) for k, (a, b) in enumerate(pairs)]
    for copy in copies:
        copy.start()
    for copy in copies[:4]:
        copy.wait()
    for j, row in field_rows(sz, at_x[0], at_x[1], sz.ey):
        to_x[j, :, sz.res + sz.full :] = row
    for i, row in field_rows(sz, at_y[0], at_y[1], sz.ex):
        to_y[i, :, sz.res + sz.full :] = row
    for copy in copies[4:]:
        copy.wait()


def turn_kernel(sz, pieces, res_ref, from_x, from_y, corner, out_ref):
    own = sz.own_edges * sz.ez
    share = sz.res // out_ref.shape[0] // pieces

    def put(g, columns, value):
        for at in range(0, LANES, share):
            owner = (g + at) // share
            row = owner // 2 * share
            out_ref[owner % 2, row : row + share, columns] = value[at : at + share]

    for g in range(0, sz.res, LANES):
        lanes = slice(g, g + LANES)
        put(g, slice(0, own), res_ref[:, lanes].T)
        rest = sz.edges - sz.own_edges - sz.ey - sz.gx
        parts = [from_x[:, :, lanes], from_y[:, :, lanes], corner[:, :, lanes]]
        if rest:
            parts.append(jnp.zeros((rest, sz.ez, LANES), bf16))
        ghosts = jnp.concatenate(parts, axis=0)
        put(g, slice(own, sz.edges * sz.ez), ghosts.reshape(-1, LANES).T)


def vectors_of(sz, edge):
    lanes = [slice(sz.res + b * sz.width, sz.res + (b + 1) * sz.width) for b in range(sz.blocks)]
    return jnp.stack([edge[:, at] for at in lanes]).astype(f32)


class Nodes:
    def __init__(self, sz, vec, from_x, from_y, own_inv, own_pot, ghost_x, ghost_y, corners=None):
        self.sz, self.vec, self.from_x, self.from_y = sz, vec, from_x, from_y
        self.own, self.ghost_x, self.ghost_y, self.corners = (own_inv, own_pot), ghost_x, ghost_y, corners

    def x(self, i, j):
        sz = self.sz
        if i < sz.ex and j < sz.ey:
            return self.vec[:, i, j].astype(f32)
        return vectors_of(sz, self.from_x[j] if i == sz.ex else self.from_y[i])

    def field(self, at, i, j):
        sz = self.sz
        if i < sz.ex and j < sz.ey:
            return self.own[at][i, j]
        if i < sz.ex:
            return self.ghost_y[at, i]
        if j < sz.ey:
            return self.ghost_x[at, j]
        return self.corners[at]

    def inv(self, i, j):
        return self.field(0, i, j)

    def pot(self, i, j):
        return self.field(1, i, j)


class Sums:
    def __init__(self, sz, even, acc, face, near, far, corner=None):
        self.sz, self.even, self.acc, self.face = sz, even, acc, face
        self.near, self.far, self.corner = near, far, corner

    def at(self, i, j):
        sz = self.sz
        total = self.acc[:, i, j]
        side = 1 if i == 0 else 0 if i == sz.ex else None
        if side is not None:
            total = total + self.face[side, :, j].astype(f32)
        if j in (0, sz.ey):
            is_near = self.even if j == sz.ey else jnp.logical_not(self.even)
            total = total + jnp.where(is_near, self.near[:, i].astype(f32), self.far[:, i].astype(f32))
            if side is not None:
                total = total + jnp.where(
                    is_near, self.corner[side, 0].astype(f32), self.corner[side, 1].astype(f32)
                )
        return total


def corner_edges(sz):
    return [(i, j) for i in (0, sz.ex) for j in (0, sz.ey)]


def main_products(sz, prepare, u_ref, mat_refs, rhs_ref, out_ref):
    width = sz.width
    flat = sz.gx * sz.gy * sz.gz
    u_flat = u_ref.reshape(sz.blocks * flat, width)
    last = sz.nodes // 8 * 8
    ready = set()
    for cell, (x0, y0, z0) in enumerate(sz.origins):
        slot = cell % 2
        if cell < 2:
            rhs_ref[slot, : sz.base] = jnp.zeros((sz.base, sz.full), f32)
            rhs_ref[slot, last:] = jnp.zeros((sz.depth - last, sz.full), f32)
        for place, i, j, count in sz.runs(cell):
            for at in range(j, j + count):
                if (x0 + i, y0 + at) not in ready:
                    prepare(x0 + i, y0 + at)
                    ready.add((x0 + i, y0 + at))
        z1 = z0 + sz.p
        wrap = z1 % sz.gz
        for b in range(sz.blocks):
            lanes = slice(b * width, (b + 1) * width)
            for place, i, j, count in sz.runs(cell):
                row = sz.base + place * sz.p
                rhs_ref[slot, row : row + count * sz.p, lanes] = u_ref[
                    b, x0 + i, y0 + j : y0 + j + count, z0:z1
                ].reshape(count * sz.p, width)
        for b in range(sz.blocks):
            lanes = slice(b * width, (b + 1) * width)
            for place, i, j, count in sz.runs(cell):
                start = b * flat + ((x0 + i) * sz.gy + y0 + j) * sz.gz + wrap
                rhs_ref[slot, sz.tail + place : sz.tail + place + count, lanes] = u_flat[
                    pl.ds(start, count, stride=sz.gz)
                ]
        out_ref[cell] = jnp.dot(
            mat_refs[cell][...], rhs_ref[slot].astype(bf16), preferred_element_type=f32
        )


def corner_products(sz, u_corner, prod_ref, mat_refs, small_ref, tail_ref, acc_ref):
    width = sz.width
    flat = sz.gx * sz.gy * sz.gz
    acc_flat = acc_ref.reshape(sz.blocks * flat, width)
    small_ref[...] = jnp.zeros_like(small_ref)
    touched = set()
    for cell, (x0, y0, z0) in enumerate(sz.origins):
        z1 = z0 + sz.p
        wrap = z1 % sz.gz
        corners = sz.cell_corners(cell)
        for rank, (i, j) in enumerate(corners):
            value = u_corner[sz.corner(x0 + i, y0 + j)]
            last = len(corners) * sz.p + rank
            for b in range(sz.blocks):
                lanes = slice(b * width, (b + 1) * width)
                small_ref[rank * sz.p : (rank + 1) * sz.p, lanes] = value[b, z0:z1]
                small_ref[last : last + 1, lanes] = value[b, wrap : wrap + 1]
        total = prod_ref[cell] + jnp.dot(
            mat_refs[cell][:, : small_ref.shape[0]], small_ref[...].astype(bf16),
            preferred_element_type=f32,
        )
        tail_ref[cell, : sz.base] = total[: sz.base]
        tail_ref[cell, sz.base :] = total[sz.tail :]
        spans = [(rank * sz.p, i, j, 1) for rank, (i, j) in enumerate(corners)]
        spans += [(sz.base + place * sz.p, i, j, count) for place, i, j, count in sz.runs(cell)]
        for row, i, j, count in spans:
            for at in range(count):
                part = total[row + at * sz.p : row + (at + 1) * sz.p]
                key = (x0 + i, y0 + j + at, z0)
                for b in range(sz.blocks):
                    value = part[:, b * width : (b + 1) * width]
                    if key in touched:
                        value = acc_ref[b, key[0], key[1], z0:z1] + value
                    acc_ref[b, key[0], key[1], z0:z1] = value
                touched.add(key)
    for cell, (x0, y0, z0) in enumerate(sz.origins):
        wrap = (z0 + sz.p) % sz.gz
        corners = sz.cell_corners(cell)
        spans = [(len(corners) * sz.p + rank, i, j, 1) for rank, (i, j) in enumerate(corners)]
        spans += [(sz.base + place, i, j, count) for place, i, j, count in sz.runs(cell)]
        for row, i, j, count in spans:
            for b in range(sz.blocks):
                start = b * flat + ((x0 + i) * sz.gy + y0 + j) * sz.gz + wrap
                rows = pl.ds(start, count, stride=sz.gz) if count > 1 else pl.ds(start, 1)
                lanes = slice(b * width, (b + 1) * width)
                acc_flat[rows] = acc_flat[rows] + tail_ref[cell, row : row + count, lanes]


def write_messages(sz, even, acc_ref, face, near, far):
    at_near = jnp.where(even, sz.ey, 0)
    for b in range(sz.blocks):
        face[0, b] = acc_ref[b, 0].astype(bf16)
        face[1, b] = acc_ref[b, sz.ex].astype(bf16)
        near[b] = acc_ref[b, :, at_near].astype(bf16)
        far[b] = acc_ref[b, :, sz.ey - at_near].astype(bf16)


def corner_pack_kernel(sz, near, far, out_ref):
    for side, i in enumerate((0, sz.ex)):
        for slot, ref in enumerate((near, far)):
            out_ref[side, slot] = ref[:, i]


def first_main(sz, n_mat, vec, from_x, from_y, own_inv, own_pot, *refs):
    mats = refs[:n_mat]
    prod_ref, ghost_x, ghost_y, u_ref, rhs_ref = refs[n_mat:]
    for j in range(sz.ey):
        ghost_x[0, j], ghost_x[1, j] = fields_of(from_x[j, :, sz.res + sz.full :])
    for i in range(sz.ex):
        ghost_y[0, i], ghost_y[1, i] = fields_of(from_y[i, :, sz.res + sz.full :])
    nodes = Nodes(sz, vec, from_x, from_y, own_inv, own_pot, ghost_x, ghost_y)

    def prepare(i, j):
        u_ref[:, i, j] = nodes.x(i, j) * nodes.inv(i, j)

    main_products(sz, prepare, u_ref, mats, rhs_ref, prod_ref)


def first_corner(sz, n_mat, even_ref, vec, from_x, from_y, corner, own_inv, own_pot, ghost_x, ghost_y,
                 prod_ref, *refs):
    mats = refs[:n_mat]
    acc_ref, face, near, far, last_x, last_field, small_ref, tail_ref = refs[n_mat:]
    last_field[0], last_field[1] = fields_of(corner[0, :, sz.res + sz.full :])
    last_x[...] = vectors_of(sz, corner[0])
    nodes = Nodes(sz, vec, from_x, from_y, own_inv, own_pot, ghost_x, ghost_y, last_field)
    u_corner = []
    for i, j in corner_edges(sz):
        x = last_x[...] if (i, j) == (sz.ex, sz.ey) else nodes.x(i, j)
        u_corner.append(x * nodes.inv(i, j))
    corner_products(sz, u_corner, prod_ref, mats, small_ref, tail_ref, acc_ref)
    write_messages(sz, even_ref[0] == 0, acc_ref, face, near, far)


def second_main(sz, n_mat, even_ref, vec, from_x, from_y, own_inv, own_pot, ghost_x, ghost_y,
                acc_in, face_in, near_in, far_in, *refs):
    mats = refs[:n_mat]
    prod_ref, y_ref, u_ref, rhs_ref = refs[n_mat:]
    nodes = Nodes(sz, vec, from_x, from_y, own_inv, own_pot, ghost_x, ghost_y)
    sums = Sums(sz, even_ref[0] == 0, acc_in, face_in, near_in, far_in)

    def prepare(i, j):
        old, inv = nodes.x(i, j), nodes.inv(i, j)
        image = inv * sums.at(i, j) + nodes.pot(i, j) * old
        new = (image - center_shift * old) / half_width
        y_ref[:, i, j] = new
        u_ref[:, i, j] = inv * new

    main_products(sz, prepare, u_ref, mats, rhs_ref, prod_ref)


def second_corner(sz, n_mat, even_ref, vec, from_x, from_y, own_inv, own_pot, ghost_x, ghost_y, last_x,
                  last_field, acc_in, face_in, near_in, far_in, corner_in, prod_ref, *refs):
    mats = refs[:n_mat]
    acc_ref, face, near, far, y_corner, small_ref, tail_ref = refs[n_mat:]
    even = even_ref[0] == 0
    nodes = Nodes(sz, vec, from_x, from_y, own_inv, own_pot, ghost_x, ghost_y, last_field)
    sums = Sums(sz, even, acc_in, face_in, near_in, far_in, corner_in)
    u_corner = []
    for at, (i, j) in enumerate(corner_edges(sz)):
        old = last_x[...] if (i, j) == (sz.ex, sz.ey) else nodes.x(i, j)
        inv = nodes.inv(i, j)
        image = inv * sums.at(i, j) + nodes.pot(i, j) * old
        new = (image - center_shift * old) / half_width
        y_corner[at] = new
        u_corner.append(inv * new)
    corner_products(sz, u_corner, prod_ref, mats, small_ref, tail_ref, acc_ref)
    write_messages(sz, even, acc_ref, face, near, far)


def third_main(sz, n_mat, even_ref, vec, from_x, from_y, own_inv, own_pot, ghost_x, ghost_y,
               acc_in, face_in, near_in, far_in, y_ref, *refs):
    mats = refs[:n_mat]
    prod_ref, new_ref, u_ref, rhs_ref = refs[n_mat:]
    nodes = Nodes(sz, vec, from_x, from_y, own_inv, own_pot, ghost_x, ghost_y)
    sums = Sums(sz, even_ref[0] == 0, acc_in, face_in, near_in, far_in)

    def prepare(i, j):
        old, inv = y_ref[:, i, j], nodes.inv(i, j)
        image = inv * sums.at(i, j) + nodes.pot(i, j) * old
        new = 2.0 * (image - center_shift * old) / half_width - nodes.x(i, j)
        new_ref[:, i, j] = new
        u_ref[:, i, j] = inv * new

    main_products(sz, prepare, u_ref, mats, rhs_ref, prod_ref)


def third_corner(sz, n_mat, even_ref, vec, from_x, from_y, own_inv, own_pot, ghost_x, ghost_y,
                 last_x, last_field, acc_in, face_in, near_in, far_in, corner_in, prod_ref, y_corner, *refs):
    mats = refs[:n_mat]
    acc_ref, new_corner, face, small_ref, tail_ref = refs[n_mat:]
    nodes = Nodes(sz, vec, from_x, from_y, own_inv, own_pot, ghost_x, ghost_y, last_field)
    sums = Sums(sz, even_ref[0] == 0, acc_in, face_in, near_in, far_in, corner_in)
    u_corner = []
    for at, (i, j) in enumerate(corner_edges(sz)):
        x = last_x[...] if (i, j) == (sz.ex, sz.ey) else nodes.x(i, j)
        old, inv = y_corner[at], nodes.inv(i, j)
        image = inv * sums.at(i, j) + nodes.pot(i, j) * old
        new = 2.0 * (image - center_shift * old) / half_width - x
        new_corner[at] = new
        u_corner.append(inv * new)
    corner_products(sz, u_corner, prod_ref, mats, small_ref, tail_ref, acc_ref)
    for j in range(sz.gy):
        face[:, j] = (gain * (nodes.inv(sz.ex, j) * acc_ref[:, sz.ex, j])).astype(bf16)


def third_end(sz, norm_scale, even_ref, own_inv, own_pot, ghost_x, ghost_y, last_field, acc_ref, y_ref,
              y_corner, new_ref, new_corner, turned, *refs):
    out_hbm, edge_x, edge_y, side, give, keep, part_ref, sem, rows_ref = refs
    nodes = Nodes(sz, None, None, None, own_inv, own_pot, ghost_x, ghost_y, last_field)

    def put_row(at, value):
        for b in range(sz.blocks):
            rows_ref[at, :, b * sz.width : (b + 1) * sz.width] = value[b]

    copies = []
    for i in range(sz.gx):
        for j in range(sz.gy):
            acc, inv = acc_ref[:, i, j], nodes.inv(i, j)
            if i == sz.ex or j == sz.ey:
                value = gain * (inv * acc)
                rounded = value.astype(bf16)
                if j < sz.ey:
                    put_row(sz.own_edges + j, rounded)
                else:
                    put_row(sz.own_edges + sz.ey + i, rounded)
                    if i < sz.ex:
                        side[:, i] = value
                continue
            at = sz.corner(i, j)
            old = y_ref[:, i, j] if at is None else y_corner[at]
            new = new_ref[:, i, j] if at is None else new_corner[at]
            image = inv * acc + nodes.pot(i, j) * new
            value = 2.0 * (image - center_shift * new) / half_width - old
            part_ref[:, i, j] = value
            if i == 0:
                edge_x[:, j] = value
            elif j == 0:
                edge_y[:, i - 1] = value
            put_row(i * sz.ey + j, value.astype(bf16))
        if i < sz.ex:
            copies.append(pltpu.make_async_copy(part_ref.at[:, i], out_hbm.at[:, i], sem.at[i]))
            copies[-1].start()
    for at in range(sz.own_edges + sz.ey + sz.gx, sz.edges):
        rows_ref[at] = jnp.zeros((sz.ez, sz.full), bf16)
    rows = rows_ref[...].reshape(sz.edges * sz.ez, sz.full)
    mine = even_ref[0]
    for half, out in ((1 - mine, give), (mine, keep)):
        local = jnp.dot(turned[half], rows, preferred_element_type=f32)
        out[...] = (local * norm_scale).astype(out.dtype)
    for copy in copies:
        copy.wait()


def ready_kernel(sz, keep, taken, side_ref, face, pieces, out_ref):
    for i in range(sz.ex):
        value = side_ref[:, i]
        if i == 0:
            value = value + face[:, sz.ey].astype(f32)
        out_ref[:, i] = value.astype(out_ref.dtype)
    rows = pieces.shape[2]
    for at in range(pieces.shape[1]):
        span = slice(at * rows, (at + 1) * rows)
        value = (keep[span] + taken[span].astype(f32)).astype(pieces.dtype)
        for copy in range(pieces.shape[0]):
            pieces[copy, at] = value


def last_kernel(sz, old_hbm, edge_x, edge_y, face, side, out_hbm, at_x, at_y, sems):
    del old_hbm
    for j in range(sz.ey):
        value = edge_x[:, j] + face[:, j].astype(f32)
        if j == 0:
            value = value + side[:, 0].astype(f32)
        at_x[:, j] = value
    for i in range(1, sz.ex):
        at_y[:, i - 1] = edge_y[:, i - 1] + side[:, i].astype(f32)
    copies = [
        pltpu.make_async_copy(at_x, out_hbm.at[:, 0], sems.at[0]),
        pltpu.make_async_copy(at_y, out_hbm.at[:, pl.ds(1, sz.ex - 1), 0], sems.at[1]),
    ]
    for copy in copies:
        copy.start()
    for copy in copies:
        copy.wait()


def like(shape, dtype):
    return jax.ShapeDtypeStruct(shape, dtype)


class Pinned:
    def __init__(self, value):
        self.value, self.shape, self.dtype = value, value.shape, value.dtype


def call(kernel, name, flops, out_shape, scratch, operands, hbm=0, scalar_first=False, aliases=None,
         out_hbm=0):
    pinned = [isinstance(s, Pinned) for s in out_shape]
    out_shape = [like(s.shape, s.dtype) for s in out_shape]
    size = sum(math.prod(s.shape) * jnp.dtype(s.dtype).itemsize for s in (*operands, *out_shape))
    whole = pl.BlockSpec(memory_space=pltpu.VMEM)
    specs = [pl.BlockSpec(memory_space=pltpu.HBM)] * hbm + [whole] * (len(operands) - hbm)
    if scalar_first:
        specs[0] = pl.BlockSpec(memory_space=pltpu.SMEM)
    out_specs = [pl.BlockSpec(memory_space=pltpu.HBM)] * out_hbm + [whole] * (len(out_shape) - out_hbm)
    out_shape = [pltpu.HBM(s.shape, s.dtype) for s in out_shape[:out_hbm]] + out_shape[out_hbm:]
    out_shape = [pltpu.VMEM(s.shape, s.dtype) if p else s for s, p in zip(out_shape, pinned)]
    operands = [pltpu.with_memory_space_constraint(a, pltpu.HBM) for a in operands[:hbm]] + list(
        pltpu.with_memory_space_constraint(a.value, pltpu.VMEM) if isinstance(a, Pinned) else a
        for a in operands[hbm:]
    )
    results = pl.pallas_call(
        kernel,
        in_specs=specs,
        out_specs=out_specs,
        out_shape=out_shape,
        scratch_shapes=scratch,
        input_output_aliases=aliases or {},
        compiler_params=pltpu.CompilerParams(vmem_limit_bytes=VMEM_LIMIT),
        cost_estimate=pl.CostEstimate(flops=flops, bytes_accessed=size, transcendentals=0),
        name=name,
    )(*operands)
    return [Pinned(r) if p else r for r, p in zip(results, pinned)]


def body(vectors, resident, inv_mass, potential, cell_matrix, connectivity):
    sz = Sizes(vectors, resident, inv_mass, connectivity)
    nx, ny = lax.axis_size("dx"), lax.axis_size("dy")
    norm_scale = 1.0 / math.sqrt(sz.ex * sz.ey * sz.ez * nx * ny)
    blocks, ez, width, full = sz.blocks, sz.ez, sz.width, sz.full
    res_count = resident.shape[-1]
    tile = (ez, width)

    conn = connectivity.reshape(sz.cells, sz.nodes)
    to_x, to_y, cell_matrix, conn = call(
        functools.partial(pack_kernel, sz), "pack", 0,
        [like((sz.ey, ez, sz.wide), bf16), like((sz.ex, ez, sz.wide), bf16), Pinned(cell_matrix), conn],
        [
            pltpu.VMEM((2, sz.ey, ez), f32), pltpu.VMEM((2, sz.ex, ez), f32),
            pltpu.SemaphoreType.DMA((8 + 2 * blocks,)),
        ],
        [vectors, resident, inv_mass, potential, cell_matrix, conn], hbm=6,
    )
    from_x = send(to_x, -1, 0)
    from_y = send(to_y, 0, -1)

    mats = call(
        functools.partial(order_kernel, sz), "order_cells", 4 * sz.cells * sz.depth**3,
        [Pinned(like((sz.rows, sz.depth), bf16))] * sz.cells, [], [conn, cell_matrix],
    )
    own_inv = jnp.broadcast_to(inv_mass[..., None], inv_mass.shape + (width,))
    own_pot = jnp.broadcast_to(potential[..., None], inv_mass.shape + (width,))
    parity = jnp.reshape(lax.axis_index("dy") % 2, (1,)).astype(jnp.int32)
    ghost_corner = send(from_y[:1], -1, 0)

    grid = (blocks, sz.gx, sz.gy) + tile
    own = (blocks, sz.ex, sz.ey) + tile
    products = Pinned(like((sz.cells, sz.rows, full), f32))
    state_grid = Pinned(like(grid, f32))
    messages = [
        like((2, blocks, sz.gy) + tile, bf16),
        like((blocks, sz.gx) + tile, bf16),
        like((blocks, sz.gx) + tile, bf16),
    ]
    main_scratch = [pltpu.VMEM(grid, f32), pltpu.VMEM((2, sz.depth, full), f32)]
    corner_scratch = [
        pltpu.VMEM((LANES, full), f32),
        pltpu.VMEM((sz.cells, sz.base + sz.rows - sz.tail, full), f32),
    ]
    n_mat = len(mats)
    flops = 2 * sz.cells * sz.rows * sz.depth * full
    small_flops = 2 * sz.cells * sz.rows * LANES * full

    def exchange(face, near, far):
        face = swap_x(face)
        near, far = swap_y(near, far)
        (corner,) = call(
            functools.partial(corner_pack_kernel, sz), "corner_pack", 0,
            [like((2, 2) + sz.edge, bf16)], [], [near, far],
        )
        return [face, near, far], swap_x(corner)

    prod, ghost_x, ghost_y = call(
        functools.partial(first_main, sz, n_mat), "first_main", flops,
        [products, like((2, sz.ey) + tile, f32), like((2, sz.ex) + tile, f32)], main_scratch,
        [vectors, from_x, from_y, own_inv, own_pot, *mats],
    )
    acc, face, near, far, last_x, last_field = call(
        functools.partial(first_corner, sz, n_mat), "first_corner", small_flops,
        [state_grid, *messages, like(sz.edge, f32), like((2,) + tile, f32)], corner_scratch,
        [
            parity, vectors, from_x, from_y, ghost_corner, own_inv, own_pot, ghost_x, ghost_y, prod, *mats,
        ],
        scalar_first=True,
    )
    (turned,) = call(
        functools.partial(turn_kernel, sz, ny // 2), "turn_residents", flops // 2,
        [like((2, res_count // 2, sz.edges * ez), bf16)], [],
        [resident.reshape(-1, res_count), from_x, from_y, ghost_corner],
    )
    got, corner = exchange(face, near, far)
    state = [vectors, from_x, from_y, own_inv, own_pot, ghost_x, ghost_y]
    ends = [last_x, last_field]
    prod, y1 = call(
        functools.partial(second_main, sz, n_mat), "second_main", flops,
        [products, state_grid], main_scratch,
        [parity, *state, acc, *got, *mats], scalar_first=True,
    )
    acc, face, near, far, y1_corner = call(
        functools.partial(second_corner, sz, n_mat), "second_corner", small_flops,
        [state_grid, *messages, like((4,) + sz.edge, f32)], corner_scratch,
        [parity, *state, *ends, acc, *got, corner, prod, *mats], scalar_first=True,
    )
    got, corner = exchange(face, near, far)
    prod, y2 = call(
        functools.partial(third_main, sz, n_mat), "third_main", flops,
        [products, state_grid], main_scratch,
        [parity, *state, acc, *got, y1, *mats], scalar_first=True,
    )
    acc, new_corner, face = call(
        functools.partial(third_corner, sz, n_mat), "third_corner", small_flops,
        [state_grid, like((4,) + sz.edge, f32), like((blocks, sz.gy) + tile, bf16)], corner_scratch,
        [parity, *state, *ends, acc, *got, corner, prod, y1_corner, *mats], scalar_first=True,
    )
    face = send(face, 1, 0)
    filtered, edge_x, edge_y, side, give, keep = call(
        functools.partial(third_end, sz, norm_scale), "third_end", 2 * res_count * sz.edges * ez * full,
        [
            like(own, f32), like((blocks, sz.ey) + tile, f32), like((blocks, sz.ex - 1) + tile, f32),
            like((blocks, sz.ex) + tile, f32), like((res_count // 2, full), bf16), like((res_count // 2, full), f32),
        ],
        [
            pltpu.VMEM(own, f32), pltpu.SemaphoreType.DMA((sz.ex,)),
            pltpu.VMEM((sz.edges, ez, full), bf16),
        ],
        [
            parity, own_inv, own_pot, ghost_x, ghost_y, last_field, acc, y1, y1_corner, y2, new_corner, turned,
        ],
        scalar_first=True, out_hbm=1,
    )

    pieces, side = call(
        functools.partial(ready_kernel, sz), "ready", 0,
        [like((nx, ny // 2, res_count // ny, full), bf16), like((blocks, sz.ex) + tile, bf16)],
        [], [keep, send_near(give), side, face],
    )
    pieces = pieces.reshape(nx * ny // 2, -1, full)
    groups = [[a * ny + b for a in range(nx) for b in range(c, ny, 2)] for c in range(2)]
    pieces = lax.all_to_all(pieces, ("dx", "dy"), 0, 0, axis_index_groups=groups)
    margin = jnp.sum(pieces.astype(f32), axis=0)

    side = send(side, 0, 1)
    (filtered,) = call(
        functools.partial(last_kernel, sz), "last", 0, [like(own, f32)],
        [
            pltpu.VMEM((blocks, sz.ey) + tile, f32), pltpu.VMEM((blocks, sz.ex - 1) + tile, f32),
            pltpu.SemaphoreType.DMA((2,)),
        ],
        [filtered, edge_x, edge_y, face, side], hbm=1, out_hbm=1, aliases={0: 0},
    )
    return (filtered, margin)


def solution(mesh):
    return jax.shard_map(
        body,
        mesh=mesh,
        in_specs=(
            P(None, "dx", "dy", None, None),
            P("dx", "dy", None, None),
            P("dx", "dy", None),
            P("dx", "dy", None),
            P(),
            P("dx", "dy", None, None),
        ),
        out_specs=(P(None, "dx", "dy", None, None), P("dy", None)),
        check_vma=False,
    )
```

```python
import functools
import math

import jax
import jax.numpy as jnp
from jax import lax
from jax.experimental import pallas as pl
from jax.experimental.pallas import tpu as pltpu
from jax.sharding import PartitionSpec as P

LANES = 128
TILE = 256
SUB = 16
VMEM_LIMIT = 16 * 1024 * 1024

center_shift = 1.2
half_width = 2.0
gain = 2.0 / half_width

f32, bf16 = jnp.float32, jnp.bfloat16


def round_up(value, step):
    return -(-value // step) * step


class Sizes:
    def __init__(self, vectors, resident, inv_mass, connectivity):
        self.blocks = vectors.shape[0]
        self.width = vectors.shape[-1]
        self.full = self.blocks * self.width
        self.res = resident.shape[-1]
        self.wide = self.res + self.full + self.width
        self.ex, self.ey, self.ez = inv_mass.shape
        self.cells, self.nodes = connectivity.shape[2:]
        self.n1 = round(self.nodes ** (1.0 / 3.0))
        self.p = self.n1 - 1
        self.cx, self.cy, self.cz = self.ex // self.p, self.ey // self.p, self.ez // self.p
        self.gx, self.gy, self.gz = self.ex + 1, self.ey + 1, self.ez
        self.edge = (self.blocks, self.ez, self.width)
        self.origins = [
            (a * self.p, b * self.p, c * self.p)
            for a in range(self.cx)
            for b in range(self.cy)
            for c in range(self.cz)
        ]
        self.most = max(len(self.cell_corners(cell)) for cell in range(self.cells))
        self.base = round_up(self.most * self.n1, 8)
        plain = self.n1 * self.n1 - min(len(self.cell_corners(cell)) for cell in range(self.cells))
        self.tail = self.base + plain * self.p
        self.rows = round_up(self.tail + plain, SUB)
        self.depth = round_up(self.rows, LANES)
        self.own_edges = self.ex * self.ey
        self.edges = round_up(self.own_edges + self.ey + self.gx, LANES // self.ez)

    def corner(self, i, j):
        if i in (0, self.ex) and j in (0, self.ey):
            return 2 * (i // self.ex) + j // self.ey
        return None

    def cell_corners(self, cell):
        x0, y0, _ = self.origins[cell]
        return [
            (i, j)
            for i in range(self.n1)
            for j in range(self.n1)
            if self.corner(x0 + i, y0 + j) is not None
        ]

    def runs(self, cell):
        corners = self.cell_corners(cell)
        place = 0
        for i in range(self.n1):
            js = [j for j in range(self.n1) if (i, j) not in corners]
            while js:
                count = 1
                while count < len(js) and js[count] == js[0] + count:
                    count += 1
                yield place, i, js[0], count
                place += count
                js = js[count:]


def send(value, steps_x, steps_y):
    nx, ny = lax.axis_size("dx"), lax.axis_size("dy")
    pairs = [
        (a * ny + b, ((a + steps_x) % nx) * ny + (b + steps_y) % ny)
        for a in range(nx)
        for b in range(ny)
    ]
    return lax.ppermute(value, ("dx", "dy"), pairs)


def swap_x(value):
    if lax.axis_size("dx") == 2:
        return send(value, 1, 0)
    return jnp.stack([send(value[0], -1, 0), send(value[1], 1, 0)])


def send_near(value):
    pairs = [(b, b + 1 if b % 2 == 0 else b - 1) for b in range(lax.axis_size("dy"))]
    return lax.ppermute(value, "dy", pairs)


def swap_y(near, far):
    ny = lax.axis_size("dy")
    far_pairs = [(b, (b - 1 if b % 2 == 0 else b + 1) % ny) for b in range(ny)]
    far = lax.ppermute(far, "dy", far_pairs)
    return send_near(near), far


def cell_matrices(refs):
    return [ref.at[at] for ref in refs for at in range(ref.shape[0])]


def order_kernel(sz, conn_ref, matrix_ref, *out_refs):
    matrices = cell_matrices(out_refs)
    for cell in range(sz.cells):
        x0, y0, z0 = sz.origins[cell]
        conn = conn_ref[cell : cell + 1, :].astype(f32)
        li = jnp.floor((conn + 0.5) * (1.0 / (sz.gy * sz.gz)))
        rest = conn - li * (sz.gy * sz.gz)
        lj = jnp.floor((rest + 0.5) * (1.0 / sz.gz))
        lk = rest - lj * sz.gz - z0
        lk = jnp.where(lk < 0, lk + sz.gz, lk)
        column = (li - x0) * sz.n1 + (lj - y0)
        corners = [i * sz.n1 + j for i, j in sz.cell_corners(cell)]
        place = column
        for at in corners:
            place = place - jnp.where(column > at, 1.0, 0.0)
        index = jnp.where(lk < sz.p, sz.base + place * sz.p + lk, sz.tail + place)
        for rank, at in enumerate(corners):
            special = jnp.where(lk < sz.p, rank * sz.p + lk, len(corners) * sz.p + rank)
            index = jnp.where(column == at, special, index)
        index = index.astype(jnp.int32)
        row = lax.broadcasted_iota(jnp.int32, (sz.depth, sz.nodes), 0)
        pick = (row == index).astype(f32).astype(bf16)
        half = jnp.dot(pick[: sz.rows], matrix_ref[...], preferred_element_type=f32)
        half = half.astype(bf16)
        cuts = list(range(0, sz.depth, TILE)) + [sz.depth]
        for r0, r1 in zip(cuts[:-1], cuts[1:]):
            r1 = min(r1, sz.rows)
            block = lax.dot_general(
                half[r0:r1], pick[r0:], (((1,), (1,)), ((), ())), preferred_element_type=f32
            ).astype(bf16)
            matrices[cell][r0:r1, r0:] = block
            for c0, c1 in zip(cuts[:-1], cuts[1:]):
                if c0 > r0:
                    mirror = block[:, c0 - r0 : c1 - r0].T
                    c1 = min(c1, sz.rows)
                    matrices[cell][c0:c1, r0:r1] = mirror[: c1 - c0]


def field_row(inv, pot):
    lane = lax.broadcasted_iota(jnp.int32, inv.shape, inv.ndim - 1)
    row = jnp.zeros_like(inv)
    for at, rest in enumerate((inv, pot)):
        for k in range(3):
            part = rest.astype(bf16).astype(f32)
            rest = rest - part
            row = jnp.where(lane == 3 * at + k, part, row)
    return row.astype(bf16)


def field_rows(sz, inv, pot, count):
    inv, pot = inv.T, pot.T
    shape = (sz.ez, sz.width)
    for at in range(count):
        yield at, field_row(
            jnp.broadcast_to(inv[:, at : at + 1], shape), jnp.broadcast_to(pot[:, at : at + 1], shape)
        )


def fields_of(row):
    row = row.astype(f32)
    return [
        jnp.broadcast_to(sum(row[:, 3 * at + k : 3 * at + k + 1] for k in range(3)), row.shape)
        for at in range(2)
    ]


def pack_kernel(
    sz, vec_hbm, res_hbm, inv_hbm, pot_hbm, mat_hbm, conn_hbm,
    to_x, to_y, mat_ref, conn_ref, at_x, at_y, sems,
):
    pairs = [
        (inv_hbm.at[0], at_x.at[0]), (pot_hbm.at[0], at_x.at[1]),
        (inv_hbm.at[:, 0], at_y.at[0]), (pot_hbm.at[:, 0], at_y.at[1]),
        (res_hbm.at[0], to_x.at[:, :, pl.ds(0, sz.res)]),
        (res_hbm.at[:, 0], to_y.at[:, :, pl.ds(0, sz.res)]),
    ]
    for b in range(sz.blocks):
        lanes = pl.ds(sz.res + b * sz.width, sz.width)
        pairs.append((vec_hbm.at[b, 0], to_x.at[:, :, lanes]))
        pairs.append((vec_hbm.at[b, :, 0], to_y.at[:, :, lanes]))
    pairs += [(mat_hbm, mat_ref), (conn_hbm, conn_ref)]
    copies = [pltpu.make_async_copy(a, b, sems.at[k]) for k, (a, b) in enumerate(pairs)]
    for copy in copies:
        copy.start()
    for copy in copies[:4]:
        copy.wait()
    for j, row in field_rows(sz, at_x[0], at_x[1], sz.ey):
        to_x[j, :, sz.res + sz.full :] = row
    for i, row in field_rows(sz, at_y[0], at_y[1], sz.ex):
        to_y[i, :, sz.res + sz.full :] = row
    for copy in copies[4:]:
        copy.wait()


def turn_kernel(sz, pieces, res_hbm, from_x, from_y, corner, out_ref, res_ref, sems):
    own = sz.own_edges * sz.ez
    share = sz.res // out_ref.shape[0] // pieces
    copies = [
        pltpu.make_async_copy(res_hbm.at[:, pl.ds(g, LANES)], res_ref.at[:, pl.ds(g, LANES)], sems.at[at])
        for at, g in enumerate(range(0, sz.res, LANES))
    ]
    for copy in copies:
        copy.start()

    def put(g, columns, value):
        for at in range(0, LANES, share):
            owner = (g + at) // share
            row = owner // 2 * share
            out_ref[owner % 2, row : row + share, columns] = value[at : at + share]

    for g in range(0, sz.res, LANES):
        lanes = slice(g, g + LANES)
        copies[g // LANES].wait()
        put(g, slice(0, own), res_ref[:, lanes].T)
        rest = sz.edges - sz.own_edges - sz.ey - sz.gx
        parts = [from_x[:, :, lanes], from_y[:, :, lanes], corner[:, :, lanes]]
        if rest:
            parts.append(jnp.zeros((rest, sz.ez, LANES), bf16))
        ghosts = jnp.concatenate(parts, axis=0)
        put(g, slice(own, sz.edges * sz.ez), ghosts.reshape(-1, LANES).T)


def vectors_of(sz, edge):
    lanes = [slice(sz.res + b * sz.width, sz.res + (b + 1) * sz.width) for b in range(sz.blocks)]
    return jnp.stack([edge[:, at] for at in lanes]).astype(f32)


class Nodes:
    def __init__(self, sz, vec, from_x, from_y, own_inv, own_pot, ghost_x, ghost_y, corners=None):
        self.sz, self.vec, self.from_x, self.from_y = sz, vec, from_x, from_y
        self.own, self.ghost_x, self.ghost_y, self.corners = (own_inv, own_pot), ghost_x, ghost_y, corners

    def x(self, i, j):
        sz = self.sz
        if i < sz.ex and j < sz.ey:
            return self.vec[:, i, j].astype(f32)
        return vectors_of(sz, self.from_x[j] if i == sz.ex else self.from_y[i])

    def field(self, at, i, j):
        sz = self.sz
        if i < sz.ex and j < sz.ey:
            return self.own[at][i, j]
        if i < sz.ex:
            return self.ghost_y[at, i]
        if j < sz.ey:
            return self.ghost_x[at, j]
        return self.corners[at]

    def inv(self, i, j):
        return self.field(0, i, j)

    def pot(self, i, j):
        return self.field(1, i, j)


class Sums:
    def __init__(self, sz, even, acc, face, near, far, corner=None):
        self.sz, self.even, self.acc, self.face = sz, even, acc, face
        self.near, self.far, self.corner = near, far, corner

    def at(self, i, j):
        sz = self.sz
        total = self.acc[:, i, j]
        side = 1 if i == 0 else 0 if i == sz.ex else None
        if side is not None:
            total = total + self.face[side, :, j].astype(f32)
        if j in (0, sz.ey):
            is_near = self.even if j == sz.ey else jnp.logical_not(self.even)
            total = total + jnp.where(is_near, self.near[:, i].astype(f32), self.far[:, i].astype(f32))
            if side is not None:
                total = total + jnp.where(
                    is_near, self.corner[side, 0].astype(f32), self.corner[side, 1].astype(f32)
                )
        return total


def corner_edges(sz):
    return [(i, j) for i in (0, sz.ex) for j in (0, sz.ey)]


def main_products(sz, prepare, u_ref, mat_refs, rhs_ref, out_ref):
    width = sz.width
    flat = sz.gx * sz.gy * sz.gz
    u_flat = u_ref.reshape(sz.blocks * flat, width)
    last = sz.nodes // 8 * 8
    matrices = cell_matrices(mat_refs)
    ready = set()
    for cell, (x0, y0, z0) in enumerate(sz.origins):
        slot = cell % 2
        if cell < 2:
            rhs_ref[slot, : sz.base] = jnp.zeros((sz.base, sz.full), f32)
            rhs_ref[slot, last:] = jnp.zeros((sz.depth - last, sz.full), f32)
        for place, i, j, count in sz.runs(cell):
            for at in range(j, j + count):
                if (x0 + i, y0 + at) not in ready:
                    prepare(x0 + i, y0 + at)
                    ready.add((x0 + i, y0 + at))
        z1 = z0 + sz.p
        wrap = z1 % sz.gz
        for b in range(sz.blocks):
            lanes = slice(b * width, (b + 1) * width)
            for place, i, j, count in sz.runs(cell):
                row = sz.base + place * sz.p
                rhs_ref[slot, row : row + count * sz.p, lanes] = u_ref[
                    b, x0 + i, y0 + j : y0 + j + count, z0:z1
                ].reshape(count * sz.p, width)
        for b in range(sz.blocks):
            lanes = slice(b * width, (b + 1) * width)
            for place, i, j, count in sz.runs(cell):
                start = b * flat + ((x0 + i) * sz.gy + y0 + j) * sz.gz + wrap
                rhs_ref[slot, sz.tail + place : sz.tail + place + count, lanes] = u_flat[
                    pl.ds(start, count, stride=sz.gz)
                ]
        out_ref[cell] = jnp.dot(
            matrices[cell][...], rhs_ref[slot].astype(bf16), preferred_element_type=f32
        )


def corner_products(sz, u_corner, prod_ref, mat_refs, small_ref, tail_ref, acc_ref):
    width = sz.width
    flat = sz.gx * sz.gy * sz.gz
    acc_flat = acc_ref.reshape(sz.blocks * flat, width)
    small_ref[...] = jnp.zeros_like(small_ref)
    matrices = cell_matrices(mat_refs)
    touched = set()
    for cell, (x0, y0, z0) in enumerate(sz.origins):
        z1 = z0 + sz.p
        wrap = z1 % sz.gz
        corners = sz.cell_corners(cell)
        for rank, (i, j) in enumerate(corners):
            value = u_corner[sz.corner(x0 + i, y0 + j)]
            last = len(corners) * sz.p + rank
            for b in range(sz.blocks):
                lanes = slice(b * width, (b + 1) * width)
                small_ref[rank * sz.p : (rank + 1) * sz.p, lanes] = value[b, z0:z1]
                small_ref[last : last + 1, lanes] = value[b, wrap : wrap + 1]
        total = prod_ref[cell] + jnp.dot(
            matrices[cell][:, : small_ref.shape[0]], small_ref[...].astype(bf16),
            preferred_element_type=f32,
        )
        tail_ref[cell, : sz.base] = total[: sz.base]
        tail_ref[cell, sz.base :] = total[sz.tail :]
        spans = [(rank * sz.p, i, j, 1) for rank, (i, j) in enumerate(corners)]
        spans += [(sz.base + place * sz.p, i, j, count) for place, i, j, count in sz.runs(cell)]
        for row, i, j, count in spans:
            for at in range(count):
                part = total[row + at * sz.p : row + (at + 1) * sz.p]
                key = (x0 + i, y0 + j + at, z0)
                for b in range(sz.blocks):
                    value = part[:, b * width : (b + 1) * width]
                    if key in touched:
                        value = acc_ref[b, key[0], key[1], z0:z1] + value
                    acc_ref[b, key[0], key[1], z0:z1] = value
                touched.add(key)
    for cell, (x0, y0, z0) in enumerate(sz.origins):
        wrap = (z0 + sz.p) % sz.gz
        corners = sz.cell_corners(cell)
        spans = [(len(corners) * sz.p + rank, i, j, 1) for rank, (i, j) in enumerate(corners)]
        spans += [(sz.base + place, i, j, count) for place, i, j, count in sz.runs(cell)]
        for row, i, j, count in spans:
            for b in range(sz.blocks):
                start = b * flat + ((x0 + i) * sz.gy + y0 + j) * sz.gz + wrap
                rows = pl.ds(start, count, stride=sz.gz) if count > 1 else pl.ds(start, 1)
                lanes = slice(b * width, (b + 1) * width)
                acc_flat[rows] = acc_flat[rows] + tail_ref[cell, row : row + count, lanes]


def write_messages(sz, even, acc_ref, face, near, far):
    at_near = jnp.where(even, sz.ey, 0)
    for b in range(sz.blocks):
        face[0, b] = acc_ref[b, 0].astype(bf16)
        face[1, b] = acc_ref[b, sz.ex].astype(bf16)
        near[b] = acc_ref[b, :, at_near].astype(bf16)
        far[b] = acc_ref[b, :, sz.ey - at_near].astype(bf16)


def corner_pack_kernel(sz, near, far, out_ref):
    for side, i in enumerate((0, sz.ex)):
        for slot, ref in enumerate((near, far)):
            out_ref[side, slot] = ref[:, i]


def first_main(sz, n_mat, vec, from_x, from_y, own_inv, own_pot, *refs):
    mats = refs[:n_mat]
    prod_ref, ghost_x, ghost_y, u_ref, rhs_ref = refs[n_mat:]
    for j in range(sz.ey):
        ghost_x[0, j], ghost_x[1, j] = fields_of(from_x[j, :, sz.res + sz.full :])
    for i in range(sz.ex):
        ghost_y[0, i], ghost_y[1, i] = fields_of(from_y[i, :, sz.res + sz.full :])
    nodes = Nodes(sz, vec, from_x, from_y, own_inv, own_pot, ghost_x, ghost_y)

    def prepare(i, j):
        u_ref[:, i, j] = nodes.x(i, j) * nodes.inv(i, j)

    main_products(sz, prepare, u_ref, mats, rhs_ref, prod_ref)


def first_corner(sz, n_mat, even_ref, vec, from_x, from_y, corner, own_inv, own_pot, ghost_x, ghost_y,
                 prod_ref, *refs):
    mats = refs[:n_mat]
    acc_ref, face, near, far, last_x, last_field, small_ref, tail_ref = refs[n_mat:]
    last_field[0], last_field[1] = fields_of(corner[0, :, sz.res + sz.full :])
    last_x[...] = vectors_of(sz, corner[0])
    nodes = Nodes(sz, vec, from_x, from_y, own_inv, own_pot, ghost_x, ghost_y, last_field)
    u_corner = []
    for i, j in corner_edges(sz):
        x = last_x[...] if (i, j) == (sz.ex, sz.ey) else nodes.x(i, j)
        u_corner.append(x * nodes.inv(i, j))
    corner_products(sz, u_corner, prod_ref, mats, small_ref, tail_ref, acc_ref)
    write_messages(sz, even_ref[0] == 0, acc_ref, face, near, far)


def second_main(sz, n_mat, even_ref, vec, from_x, from_y, own_inv, own_pot, ghost_x, ghost_y,
                acc_in, face_in, near_in, far_in, *refs):
    mats = refs[:n_mat]
    prod_ref, y_ref, u_ref, rhs_ref = refs[n_mat:]
    nodes = Nodes(sz, vec, from_x, from_y, own_inv, own_pot, ghost_x, ghost_y)
    sums = Sums(sz, even_ref[0] == 0, acc_in, face_in, near_in, far_in)

    def prepare(i, j):
        old, inv = nodes.x(i, j), nodes.inv(i, j)
        image = inv * sums.at(i, j) + nodes.pot(i, j) * old
        new = (image - center_shift * old) / half_width
        y_ref[:, i, j] = new
        u_ref[:, i, j] = inv * new

    main_products(sz, prepare, u_ref, mats, rhs_ref, prod_ref)


def second_corner(sz, n_mat, even_ref, vec, from_x, from_y, own_inv, own_pot, ghost_x, ghost_y, last_x,
                  last_field, acc_in, face_in, near_in, far_in, corner_in, prod_ref, *refs):
    mats = refs[:n_mat]
    acc_ref, face, near, far, y_corner, small_ref, tail_ref = refs[n_mat:]
    even = even_ref[0] == 0
    nodes = Nodes(sz, vec, from_x, from_y, own_inv, own_pot, ghost_x, ghost_y, last_field)
    sums = Sums(sz, even, acc_in, face_in, near_in, far_in, corner_in)
    u_corner = []
    for at, (i, j) in enumerate(corner_edges(sz)):
        old = last_x[...] if (i, j) == (sz.ex, sz.ey) else nodes.x(i, j)
        inv = nodes.inv(i, j)
        image = inv * sums.at(i, j) + nodes.pot(i, j) * old
        new = (image - center_shift * old) / half_width
        y_corner[at] = new
        u_corner.append(inv * new)
    corner_products(sz, u_corner, prod_ref, mats, small_ref, tail_ref, acc_ref)
    write_messages(sz, even, acc_ref, face, near, far)


def third_main(sz, n_mat, even_ref, vec, from_x, from_y, own_inv, own_pot, ghost_x, ghost_y,
               acc_in, face_in, near_in, far_in, y_ref, *refs):
    mats = refs[:n_mat]
    prod_ref, new_ref, u_ref, rhs_ref = refs[n_mat:]
    nodes = Nodes(sz, vec, from_x, from_y, own_inv, own_pot, ghost_x, ghost_y)
    sums = Sums(sz, even_ref[0] == 0, acc_in, face_in, near_in, far_in)

    def prepare(i, j):
        old, inv = y_ref[:, i, j], nodes.inv(i, j)
        image = inv * sums.at(i, j) + nodes.pot(i, j) * old
        new = 2.0 * (image - center_shift * old) / half_width - nodes.x(i, j)
        new_ref[:, i, j] = new
        u_ref[:, i, j] = inv * new

    main_products(sz, prepare, u_ref, mats, rhs_ref, prod_ref)


def third_corner(sz, n_mat, even_ref, vec, from_x, from_y, own_inv, own_pot, ghost_x, ghost_y,
                 last_x, last_field, acc_in, face_in, near_in, far_in, corner_in, prod_ref, y_corner, *refs):
    mats = refs[:n_mat]
    acc_ref, new_corner, face, small_ref, tail_ref = refs[n_mat:]
    nodes = Nodes(sz, vec, from_x, from_y, own_inv, own_pot, ghost_x, ghost_y, last_field)
    sums = Sums(sz, even_ref[0] == 0, acc_in, face_in, near_in, far_in, corner_in)
    u_corner = []
    for at, (i, j) in enumerate(corner_edges(sz)):
        x = last_x[...] if (i, j) == (sz.ex, sz.ey) else nodes.x(i, j)
        old, inv = y_corner[at], nodes.inv(i, j)
        image = inv * sums.at(i, j) + nodes.pot(i, j) * old
        new = 2.0 * (image - center_shift * old) / half_width - x
        new_corner[at] = new
        u_corner.append(inv * new)
    corner_products(sz, u_corner, prod_ref, mats, small_ref, tail_ref, acc_ref)
    for j in range(sz.gy):
        face[:, j] = (gain * (nodes.inv(sz.ex, j) * acc_ref[:, sz.ex, j])).astype(bf16)


def third_end(sz, norm_scale, even_ref, own_inv, own_pot, ghost_x, ghost_y, last_field, acc_ref, y_ref,
              y_corner, new_ref, new_corner, turned, *refs):
    out_hbm, edge_x, edge_y, side, give, keep, part_ref, sem, rows_ref = refs
    nodes = Nodes(sz, None, None, None, own_inv, own_pot, ghost_x, ghost_y, last_field)

    def put_row(at, value):
        for b in range(sz.blocks):
            rows_ref[at, :, b * sz.width : (b + 1) * sz.width] = value[b]

    copies = []
    for i in range(sz.gx):
        for j in range(sz.gy):
            acc, inv = acc_ref[:, i, j], nodes.inv(i, j)
            if i == sz.ex or j == sz.ey:
                value = gain * (inv * acc)
                rounded = value.astype(bf16)
                if j < sz.ey:
                    put_row(sz.own_edges + j, rounded)
                else:
                    put_row(sz.own_edges + sz.ey + i, rounded)
                    if i < sz.ex:
                        side[:, i] = value
                continue
            at = sz.corner(i, j)
            old = y_ref[:, i, j] if at is None else y_corner[at]
            new = new_ref[:, i, j] if at is None else new_corner[at]
            image = inv * acc + nodes.pot(i, j) * new
            value = 2.0 * (image - center_shift * new) / half_width - old
            part_ref[:, i, j] = value
            if i == 0:
                edge_x[:, j] = value
            elif j == 0:
                edge_y[:, i - 1] = value
            put_row(i * sz.ey + j, value.astype(bf16))
        if i < sz.ex:
            copies.append(pltpu.make_async_copy(part_ref.at[:, i], out_hbm.at[:, i], sem.at[i]))
            copies[-1].start()
    for at in range(sz.own_edges + sz.ey + sz.gx, sz.edges):
        rows_ref[at] = jnp.zeros((sz.ez, sz.full), bf16)
    rows = rows_ref[...].reshape(sz.edges * sz.ez, sz.full)
    mine = even_ref[0]
    for half, out in ((1 - mine, give), (mine, keep)):
        local = jnp.dot(turned[half], rows, preferred_element_type=f32)
        out[...] = (local * norm_scale).astype(out.dtype)
    for copy in copies:
        copy.wait()


def ready_kernel(sz, keep, taken, side_ref, face, pieces, out_ref):
    for i in range(sz.ex):
        value = side_ref[:, i]
        if i == 0:
            value = value + face[:, sz.ey].astype(f32)
        out_ref[:, i] = value.astype(out_ref.dtype)
    rows = pieces.shape[2]
    for at in range(pieces.shape[1]):
        span = slice(at * rows, (at + 1) * rows)
        value = (keep[span] + taken[span].astype(f32)).astype(pieces.dtype)
        for copy in range(pieces.shape[0]):
            pieces[copy, at] = value


def last_kernel(sz, old_hbm, edge_x, edge_y, face, side, out_hbm, at_x, at_y, sems):
    del old_hbm
    for j in range(sz.ey):
        value = edge_x[:, j] + face[:, j].astype(f32)
        if j == 0:
            value = value + side[:, 0].astype(f32)
        at_x[:, j] = value
    for i in range(1, sz.ex):
        at_y[:, i - 1] = edge_y[:, i - 1] + side[:, i].astype(f32)
    copies = [
        pltpu.make_async_copy(at_x, out_hbm.at[:, 0], sems.at[0]),
        pltpu.make_async_copy(at_y, out_hbm.at[:, pl.ds(1, sz.ex - 1), 0], sems.at[1]),
    ]
    for copy in copies:
        copy.start()
    for copy in copies:
        copy.wait()


def like(shape, dtype):
    return jax.ShapeDtypeStruct(shape, dtype)


class Pinned:
    def __init__(self, value):
        self.value, self.shape, self.dtype = value, value.shape, value.dtype


def call(kernel, name, flops, out_shape, scratch, operands, hbm=0, scalar_first=False, aliases=None,
         out_hbm=0):
    pinned = [isinstance(s, Pinned) for s in out_shape]
    out_shape = [like(s.shape, s.dtype) for s in out_shape]
    size = sum(math.prod(s.shape) * jnp.dtype(s.dtype).itemsize for s in (*operands, *out_shape))
    whole = pl.BlockSpec(memory_space=pltpu.VMEM)
    specs = [pl.BlockSpec(memory_space=pltpu.HBM)] * hbm + [whole] * (len(operands) - hbm)
    if scalar_first:
        specs[0] = pl.BlockSpec(memory_space=pltpu.SMEM)
    out_specs = [pl.BlockSpec(memory_space=pltpu.HBM)] * out_hbm + [whole] * (len(out_shape) - out_hbm)
    out_shape = [pltpu.HBM(s.shape, s.dtype) for s in out_shape[:out_hbm]] + out_shape[out_hbm:]
    out_shape = [pltpu.VMEM(s.shape, s.dtype) if p else s for s, p in zip(out_shape, pinned)]
    operands = [pltpu.with_memory_space_constraint(a, pltpu.HBM) for a in operands[:hbm]] + list(
        pltpu.with_memory_space_constraint(a.value, pltpu.VMEM) if isinstance(a, Pinned) else a
        for a in operands[hbm:]
    )
    results = pl.pallas_call(
        kernel,
        in_specs=specs,
        out_specs=out_specs,
        out_shape=out_shape,
        scratch_shapes=scratch,
        input_output_aliases=aliases or {},
        compiler_params=pltpu.CompilerParams(vmem_limit_bytes=VMEM_LIMIT),
        cost_estimate=pl.CostEstimate(flops=flops, bytes_accessed=size, transcendentals=0),
        name=name,
    )(*operands)
    return [Pinned(r) if p else r for r, p in zip(results, pinned)]


def body(vectors, resident, inv_mass, potential, cell_matrix, connectivity):
    sz = Sizes(vectors, resident, inv_mass, connectivity)
    nx, ny = lax.axis_size("dx"), lax.axis_size("dy")
    norm_scale = 1.0 / math.sqrt(sz.ex * sz.ey * sz.ez * nx * ny)
    blocks, ez, width, full = sz.blocks, sz.ez, sz.width, sz.full
    res_count = resident.shape[-1]
    tile = (ez, width)

    conn = connectivity.reshape(sz.cells, sz.nodes)
    to_x, to_y, cell_matrix, conn = call(
        functools.partial(pack_kernel, sz), "pack", 0,
        [like((sz.ey, ez, sz.wide), bf16), like((sz.ex, ez, sz.wide), bf16), Pinned(cell_matrix), conn],
        [
            pltpu.VMEM((2, sz.ey, ez), f32), pltpu.VMEM((2, sz.ex, ez), f32),
            pltpu.SemaphoreType.DMA((8 + 2 * blocks,)),
        ],
        [vectors, resident, inv_mass, potential, cell_matrix, conn], hbm=6,
    )
    from_x = send(to_x, -1, 0)
    from_y = send(to_y, 0, -1)

    halves = 2 if sz.cells % 2 == 0 else 1
    mats = call(
        functools.partial(order_kernel, sz), "order_cells", 4 * sz.cells * sz.depth**3,
        [Pinned(like((sz.cells // halves, sz.rows, sz.depth), bf16))] * halves, [], [conn, cell_matrix],
    )
    own_inv = jnp.broadcast_to(inv_mass[..., None], inv_mass.shape + (width,))
    own_pot = jnp.broadcast_to(potential[..., None], inv_mass.shape + (width,))
    parity = jnp.reshape(lax.axis_index("dy") % 2, (1,)).astype(jnp.int32)
    ghost_corner = send(from_y[:1], -1, 0)

    grid = (blocks, sz.gx, sz.gy) + tile
    own = (blocks, sz.ex, sz.ey) + tile
    products = Pinned(like((sz.cells, sz.rows, full), f32))
    state_grid = Pinned(like(grid, f32))
    messages = [
        like((2, blocks, sz.gy) + tile, bf16),
        like((blocks, sz.gx) + tile, bf16),
        like((blocks, sz.gx) + tile, bf16),
    ]
    main_scratch = [pltpu.VMEM(grid, f32), pltpu.VMEM((2, sz.depth, full), f32)]
    corner_scratch = [
        pltpu.VMEM((LANES, full), f32),
        pltpu.VMEM((sz.cells, sz.base + sz.rows - sz.tail, full), f32),
    ]
    n_mat = len(mats)
    flops = 2 * sz.cells * sz.rows * sz.depth * full
    small_flops = 2 * sz.cells * sz.rows * LANES * full

    def exchange(face, near, far):
        face = swap_x(face)
        near, far = swap_y(near, far)
        (corner,) = call(
            functools.partial(corner_pack_kernel, sz), "corner_pack", 0,
            [like((2, 2) + sz.edge, bf16)], [], [near, far],
        )
        return [face, near, far], swap_x(corner)

    prod, ghost_x, ghost_y = call(
        functools.partial(first_main, sz, n_mat), "first_main", flops,
        [products, like((2, sz.ey) + tile, f32), like((2, sz.ex) + tile, f32)], main_scratch,
        [vectors, from_x, from_y, own_inv, own_pot, *mats],
    )
    acc, face, near, far, last_x, last_field = call(
        functools.partial(first_corner, sz, n_mat), "first_corner", small_flops,
        [state_grid, *messages, like(sz.edge, f32), like((2,) + tile, f32)], corner_scratch,
        [
            parity, vectors, from_x, from_y, ghost_corner, own_inv, own_pot, ghost_x, ghost_y, prod, *mats,
        ],
        scalar_first=True,
    )
    (turned,) = call(
        functools.partial(turn_kernel, sz, ny // 2), "turn_residents", flops // 2,
        [like((2, res_count // 2, sz.edges * ez), bf16)],
        [
            pltpu.VMEM((sz.own_edges * ez, res_count), bf16),
            pltpu.SemaphoreType.DMA((res_count // LANES,)),
        ],
        [resident.reshape(-1, res_count), from_x, from_y, ghost_corner], hbm=1,
    )
    got, corner = exchange(face, near, far)
    state = [vectors, from_x, from_y, own_inv, own_pot, ghost_x, ghost_y]
    ends = [last_x, last_field]
    prod, y1 = call(
        functools.partial(second_main, sz, n_mat), "second_main", flops,
        [products, state_grid], main_scratch,
        [parity, *state, acc, *got, *mats], scalar_first=True,
    )
    acc, face, near, far, y1_corner = call(
        functools.partial(second_corner, sz, n_mat), "second_corner", small_flops,
        [state_grid, *messages, like((4,) + sz.edge, f32)], corner_scratch,
        [parity, *state, *ends, acc, *got, corner, prod, *mats], scalar_first=True,
    )
    got, corner = exchange(face, near, far)
    prod, y2 = call(
        functools.partial(third_main, sz, n_mat), "third_main", flops,
        [products, state_grid], main_scratch,
        [parity, *state, acc, *got, y1, *mats], scalar_first=True,
    )
    acc, new_corner, face = call(
        functools.partial(third_corner, sz, n_mat), "third_corner", small_flops,
        [state_grid, like((4,) + sz.edge, f32), like((blocks, sz.gy) + tile, bf16)], corner_scratch,
        [parity, *state, *ends, acc, *got, corner, prod, y1_corner, *mats], scalar_first=True,
    )
    face = send(face, 1, 0)
    filtered, edge_x, edge_y, side, give, keep = call(
        functools.partial(third_end, sz, norm_scale), "third_end", 2 * res_count * sz.edges * ez * full,
        [
            like(own, f32), like((blocks, sz.ey) + tile, f32), like((blocks, sz.ex - 1) + tile, f32),
            like((blocks, sz.ex) + tile, f32), like((res_count // 2, full), bf16), like((res_count // 2, full), f32),
        ],
        [
            pltpu.VMEM(own, f32), pltpu.SemaphoreType.DMA((sz.ex,)),
            pltpu.VMEM((sz.edges, ez, full), bf16),
        ],
        [
            parity, own_inv, own_pot, ghost_x, ghost_y, last_field, acc, y1, y1_corner, y2, new_corner, turned,
        ],
        scalar_first=True, out_hbm=1,
    )

    pieces, side = call(
        functools.partial(ready_kernel, sz), "ready", 0,
        [like((nx, ny // 2, res_count // ny, full), bf16), like((blocks, sz.ex) + tile, bf16)],
        [], [keep, send_near(give), side, face],
    )
    pieces = pieces.reshape(nx * ny // 2, -1, full)
    groups = [[a * ny + b for a in range(nx) for b in range(c, ny, 2)] for c in range(2)]
    pieces = lax.all_to_all(pieces, ("dx", "dy"), 0, 0, axis_index_groups=groups)
    margin = jnp.sum(pieces.astype(f32), axis=0)

    side = send(side, 0, 1)
    (filtered,) = call(
        functools.partial(last_kernel, sz), "last", 0, [like(own, f32)],
        [
            pltpu.VMEM((blocks, sz.ey) + tile, f32), pltpu.VMEM((blocks, sz.ex - 1) + tile, f32),
            pltpu.SemaphoreType.DMA((2,)),
        ],
        [filtered, edge_x, edge_y, face, side], hbm=1, out_hbm=1, aliases={0: 0},
    )
    return (filtered, margin)


def solution(mesh):
    return jax.shard_map(
        body,
        mesh=mesh,
        in_specs=(
            P(None, "dx", "dy", None, None),
            P("dx", "dy", None, None),
            P("dx", "dy", None),
            P("dx", "dy", None),
            P(),
            P("dx", "dy", None, None),
        ),
        out_specs=(P(None, "dx", "dy", None, None), P("dy", None)),
        check_vma=False,
    )
```

```python
import functools
import math

import jax
import jax.numpy as jnp
from jax import lax
from jax.experimental import pallas as pl
from jax.experimental.pallas import tpu as pltpu
from jax.sharding import PartitionSpec as P

LANES = 128
TILE = 256
SUB = 16
VMEM_LIMIT = 16 * 1024 * 1024

center_shift = 1.2
half_width = 2.0
gain = 2.0 / half_width

f32, bf16 = jnp.float32, jnp.bfloat16


def round_up(value, step):
    return -(-value // step) * step


class Sizes:
    def __init__(self, vectors, resident, inv_mass, connectivity):
        self.blocks = vectors.shape[0]
        self.width = vectors.shape[-1]
        self.full = self.blocks * self.width
        self.res = resident.shape[-1]
        self.wide = self.res + self.full + self.width
        self.ex, self.ey, self.ez = inv_mass.shape
        self.cells, self.nodes = connectivity.shape[2:]
        self.n1 = round(self.nodes ** (1.0 / 3.0))
        self.p = self.n1 - 1
        self.cx, self.cy, self.cz = self.ex // self.p, self.ey // self.p, self.ez // self.p
        self.gx, self.gy, self.gz = self.ex + 1, self.ey + 1, self.ez
        self.edge = (self.blocks, self.ez, self.width)
        self.origins = [
            (a * self.p, b * self.p, c * self.p)
            for a in range(self.cx)
            for b in range(self.cy)
            for c in range(self.cz)
        ]
        self.most = max(len(self.cell_corners(cell)) for cell in range(self.cells))
        self.base = round_up(self.most * self.n1, 8)
        plain = self.n1 * self.n1 - min(len(self.cell_corners(cell)) for cell in range(self.cells))
        self.tail = self.base + plain * self.p
        self.rows = round_up(self.tail + plain, SUB)
        self.depth = round_up(self.rows, LANES)
        self.own_edges = self.ex * self.ey
        self.edges = round_up(self.own_edges + self.ey + self.gx, LANES // self.ez)

    def corner(self, i, j):
        if i in (0, self.ex) and j in (0, self.ey):
            return 2 * (i // self.ex) + j // self.ey
        return None

    def cell_corners(self, cell):
        x0, y0, _ = self.origins[cell]
        return [
            (i, j)
            for i in range(self.n1)
            for j in range(self.n1)
            if self.corner(x0 + i, y0 + j) is not None
        ]

    def runs(self, cell):
        corners = self.cell_corners(cell)
        place = 0
        for i in range(self.n1):
            js = [j for j in range(self.n1) if (i, j) not in corners]
            while js:
                count = 1
                while count < len(js) and js[count] == js[0] + count:
                    count += 1
                yield place, i, js[0], count
                place += count
                js = js[count:]


def send(value, steps_x, steps_y):
    nx, ny = lax.axis_size("dx"), lax.axis_size("dy")
    pairs = [
        (a * ny + b, ((a + steps_x) % nx) * ny + (b + steps_y) % ny)
        for a in range(nx)
        for b in range(ny)
    ]
    return lax.ppermute(value, ("dx", "dy"), pairs)


def swap_x(value):
    if lax.axis_size("dx") == 2:
        return send(value, 1, 0)
    return jnp.stack([send(value[0], -1, 0), send(value[1], 1, 0)])


def send_near(value):
    pairs = [(b, b + 1 if b % 2 == 0 else b - 1) for b in range(lax.axis_size("dy"))]
    return lax.ppermute(value, "dy", pairs)


def swap_y(near, far):
    ny = lax.axis_size("dy")
    far_pairs = [(b, (b - 1 if b % 2 == 0 else b + 1) % ny) for b in range(ny)]
    far = lax.ppermute(far, "dy", far_pairs)
    return send_near(near), far


def cell_matrices(refs):
    return [ref.at[at] for ref in refs for at in range(ref.shape[0])]


def order_kernel(sz, conn_ref, matrix_ref, *out_refs):
    matrices = cell_matrices(out_refs)
    for cell in range(sz.cells):
        x0, y0, z0 = sz.origins[cell]
        conn = conn_ref[cell : cell + 1, :].astype(f32)
        li = jnp.floor((conn + 0.5) * (1.0 / (sz.gy * sz.gz)))
        rest = conn - li * (sz.gy * sz.gz)
        lj = jnp.floor((rest + 0.5) * (1.0 / sz.gz))
        lk = rest - lj * sz.gz - z0
        lk = jnp.where(lk < 0, lk + sz.gz, lk)
        column = (li - x0) * sz.n1 + (lj - y0)
        corners = [i * sz.n1 + j for i, j in sz.cell_corners(cell)]
        place = column
        for at in corners:
            place = place - jnp.where(column > at, 1.0, 0.0)
        index = jnp.where(lk < sz.p, sz.base + place * sz.p + lk, sz.tail + place)
        for rank, at in enumerate(corners):
            special = jnp.where(lk < sz.p, rank * sz.p + lk, len(corners) * sz.p + rank)
            index = jnp.where(column == at, special, index)
        index = index.astype(jnp.int32)
        row = lax.broadcasted_iota(jnp.int32, (sz.depth, sz.nodes), 0)
        pick = (row == index).astype(f32).astype(bf16)
        half = jnp.dot(pick[: sz.rows], matrix_ref[...], preferred_element_type=f32)
        half = half.astype(bf16)
        cuts = list(range(0, sz.depth, TILE)) + [sz.depth]
        for r0, r1 in zip(cuts[:-1], cuts[1:]):
            r1 = min(r1, sz.rows)
            block = lax.dot_general(
                half[r0:r1], pick[r0:], (((1,), (1,)), ((), ())), preferred_element_type=f32
            ).astype(bf16)
            matrices[cell][r0:r1, r0:] = block
            for c0, c1 in zip(cuts[:-1], cuts[1:]):
                if c0 > r0:
                    mirror = block[:, c0 - r0 : c1 - r0].T
                    c1 = min(c1, sz.rows)
                    matrices[cell][c0:c1, r0:r1] = mirror[: c1 - c0]


def field_row(inv, pot):
    lane = lax.broadcasted_iota(jnp.int32, inv.shape, inv.ndim - 1)
    row = jnp.zeros_like(inv)
    for at, rest in enumerate((inv, pot)):
        for k in range(3):
            part = rest.astype(bf16).astype(f32)
            rest = rest - part
            row = jnp.where(lane == 3 * at + k, part, row)
    return row.astype(bf16)


def field_rows(sz, inv, pot, count):
    inv, pot = inv.T, pot.T
    shape = (sz.ez, sz.width)
    for at in range(count):
        yield at, field_row(
            jnp.broadcast_to(inv[:, at : at + 1], shape), jnp.broadcast_to(pot[:, at : at + 1], shape)
        )


def fields_of(row):
    row = row.astype(f32)
    return [
        jnp.broadcast_to(sum(row[:, 3 * at + k : 3 * at + k + 1] for k in range(3)), row.shape)
        for at in range(2)
    ]


def pack_kernel(
    sz, vec_hbm, res_hbm, inv_hbm, pot_hbm, mat_hbm, conn_hbm,
    to_x, to_y, mat_ref, conn_ref, at_x, at_y, sems,
):
    pairs = [
        (inv_hbm.at[0], at_x.at[0]), (pot_hbm.at[0], at_x.at[1]),
        (inv_hbm.at[:, 0], at_y.at[0]), (pot_hbm.at[:, 0], at_y.at[1]),
        (res_hbm.at[0], to_x.at[:, :, pl.ds(0, sz.res)]),
        (res_hbm.at[:, 0], to_y.at[:, :, pl.ds(0, sz.res)]),
    ]
    for b in range(sz.blocks):
        lanes = pl.ds(sz.res + b * sz.width, sz.width)
        pairs.append((vec_hbm.at[b, 0], to_x.at[:, :, lanes]))
        pairs.append((vec_hbm.at[b, :, 0], to_y.at[:, :, lanes]))
    pairs += [(mat_hbm, mat_ref), (conn_hbm, conn_ref)]
    copies = [pltpu.make_async_copy(a, b, sems.at[k]) for k, (a, b) in enumerate(pairs)]
    for copy in copies:
        copy.start()
    for copy in copies[:4]:
        copy.wait()
    for j, row in field_rows(sz, at_x[0], at_x[1], sz.ey):
        to_x[j, :, sz.res + sz.full :] = row
    for i, row in field_rows(sz, at_y[0], at_y[1], sz.ex):
        to_y[i, :, sz.res + sz.full :] = row
    for copy in copies[4:]:
        copy.wait()


def turn_kernel(sz, pieces, res_ref, from_x, from_y, corner, out_ref):
    own = sz.own_edges * sz.ez
    share = sz.res // out_ref.shape[0] // pieces

    def put(g, columns, value):
        for at in range(0, LANES, share):
            owner = (g + at) // share
            row = owner // 2 * share
            out_ref[owner % 2, row : row + share, columns] = value[at : at + share]

    for g in range(0, sz.res, LANES):
        lanes = slice(g, g + LANES)
        put(g, slice(0, own), res_ref[:, lanes].T)
        rest = sz.edges - sz.own_edges - sz.ey - sz.gx
        parts = [from_x[:, :, lanes], from_y[:, :, lanes], corner[:, :, lanes]]
        if rest:
            parts.append(jnp.zeros((rest, sz.ez, LANES), bf16))
        ghosts = jnp.concatenate(parts, axis=0)
        put(g, slice(own, sz.edges * sz.ez), ghosts.reshape(-1, LANES).T)


def vectors_of(sz, edge):
    lanes = [slice(sz.res + b * sz.width, sz.res + (b + 1) * sz.width) for b in range(sz.blocks)]
    return jnp.stack([edge[:, at] for at in lanes]).astype(f32)


class Nodes:
    def __init__(self, sz, vec, from_x, from_y, own_inv, own_pot, ghost_x, ghost_y, corners=None):
        self.sz, self.vec, self.from_x, self.from_y = sz, vec, from_x, from_y
        self.own, self.ghost_x, self.ghost_y, self.corners = (own_inv, own_pot), ghost_x, ghost_y, corners

    def x(self, i, j):
        sz = self.sz
        if i < sz.ex and j < sz.ey:
            return self.vec[:, i, j].astype(f32)
        return vectors_of(sz, self.from_x[j] if i == sz.ex else self.from_y[i])

    def field(self, at, i, j):
        sz = self.sz
        if i < sz.ex and j < sz.ey:
            return self.own[at][i, j]
        if i < sz.ex:
            return self.ghost_y[at, i]
        if j < sz.ey:
            return self.ghost_x[at, j]
        return self.corners[at]

    def inv(self, i, j):
        return self.field(0, i, j)

    def pot(self, i, j):
        return self.field(1, i, j)


class Sums:
    def __init__(self, sz, even, acc, face, near, far, corner=None):
        self.sz, self.even, self.acc, self.face = sz, even, acc, face
        self.near, self.far, self.corner = near, far, corner

    def at(self, i, j):
        sz = self.sz
        total = self.acc[:, i, j]
        side = 1 if i == 0 else 0 if i == sz.ex else None
        if side is not None:
            total = total + self.face[side, :, j].astype(f32)
        if j in (0, sz.ey):
            is_near = self.even if j == sz.ey else jnp.logical_not(self.even)
            total = total + jnp.where(is_near, self.near[:, i].astype(f32), self.far[:, i].astype(f32))
            if side is not None:
                total = total + jnp.where(
                    is_near, self.corner[side, 0].astype(f32), self.corner[side, 1].astype(f32)
                )
        return total


def corner_edges(sz):
    return [(i, j) for i in (0, sz.ex) for j in (0, sz.ey)]


def main_products(sz, prepare, u_ref, mat_refs, rhs_ref, out_ref):
    width = sz.width
    flat = sz.gx * sz.gy * sz.gz
    u_flat = u_ref.reshape(sz.blocks * flat, width)
    last = sz.nodes // 8 * 8
    matrices = cell_matrices(mat_refs)
    ready = set()
    for cell, (x0, y0, z0) in enumerate(sz.origins):
        slot = cell % 2
        if cell < 2:
            rhs_ref[slot, : sz.base] = jnp.zeros((sz.base, sz.full), f32)
            rhs_ref[slot, last:] = jnp.zeros((sz.depth - last, sz.full), f32)
        for place, i, j, count in sz.runs(cell):
            for at in range(j, j + count):
                if (x0 + i, y0 + at) not in ready:
                    prepare(x0 + i, y0 + at)
                    ready.add((x0 + i, y0 + at))
        z1 = z0 + sz.p
        wrap = z1 % sz.gz
        for b in range(sz.blocks):
            lanes = slice(b * width, (b + 1) * width)
            for place, i, j, count in sz.runs(cell):
                row = sz.base + place * sz.p
                rhs_ref[slot, row : row + count * sz.p, lanes] = u_ref[
                    b, x0 + i, y0 + j : y0 + j + count, z0:z1
                ].reshape(count * sz.p, width)
        for b in range(sz.blocks):
            lanes = slice(b * width, (b + 1) * width)
            for place, i, j, count in sz.runs(cell):
                start = b * flat + ((x0 + i) * sz.gy + y0 + j) * sz.gz + wrap
                rhs_ref[slot, sz.tail + place : sz.tail + place + count, lanes] = u_flat[
                    pl.ds(start, count, stride=sz.gz)
                ]
        out_ref[cell] = jnp.dot(
            matrices[cell][...], rhs_ref[slot].astype(bf16), preferred_element_type=f32
        )


def corner_products(sz, u_corner, prod_ref, mat_refs, small_ref, tail_ref, acc_ref):
    width = sz.width
    flat = sz.gx * sz.gy * sz.gz
    acc_flat = acc_ref.reshape(sz.blocks * flat, width)
    small_ref[...] = jnp.zeros_like(small_ref)
    matrices = cell_matrices(mat_refs)
    touched = set()
    for cell, (x0, y0, z0) in enumerate(sz.origins):
        z1 = z0 + sz.p
        wrap = z1 % sz.gz
        corners = sz.cell_corners(cell)
        for rank, (i, j) in enumerate(corners):
            value = u_corner[sz.corner(x0 + i, y0 + j)]
            last = len(corners) * sz.p + rank
            for b in range(sz.blocks):
                lanes = slice(b * width, (b + 1) * width)
                small_ref[rank * sz.p : (rank + 1) * sz.p, lanes] = value[b, z0:z1]
                small_ref[last : last + 1, lanes] = value[b, wrap : wrap + 1]
        total = prod_ref[cell] + jnp.dot(
            matrices[cell][:, : small_ref.shape[0]], small_ref[...].astype(bf16),
            preferred_element_type=f32,
        )
        tail_ref[cell, : sz.base] = total[: sz.base]
        tail_ref[cell, sz.base :] = total[sz.tail :]
        spans = [(rank * sz.p, i, j, 1) for rank, (i, j) in enumerate(corners)]
        spans += [(sz.base + place * sz.p, i, j, count) for place, i, j, count in sz.runs(cell)]
        for row, i, j, count in spans:
            for at in range(count):
                part = total[row + at * sz.p : row + (at + 1) * sz.p]
                key = (x0 + i, y0 + j + at, z0)
                for b in range(sz.blocks):
                    value = part[:, b * width : (b + 1) * width]
                    if key in touched:
                        value = acc_ref[b, key[0], key[1], z0:z1] + value
                    acc_ref[b, key[0], key[1], z0:z1] = value
                touched.add(key)
    for cell, (x0, y0, z0) in enumerate(sz.origins):
        wrap = (z0 + sz.p) % sz.gz
        corners = sz.cell_corners(cell)
        spans = [(len(corners) * sz.p + rank, i, j, 1) for rank, (i, j) in enumerate(corners)]
        spans += [(sz.base + place, i, j, count) for place, i, j, count in sz.runs(cell)]
        for row, i, j, count in spans:
            for b in range(sz.blocks):
                start = b * flat + ((x0 + i) * sz.gy + y0 + j) * sz.gz + wrap
                rows = pl.ds(start, count, stride=sz.gz) if count > 1 else pl.ds(start, 1)
                lanes = slice(b * width, (b + 1) * width)
                acc_flat[rows] = acc_flat[rows] + tail_ref[cell, row : row + count, lanes]


def write_messages(sz, even, acc_ref, face, near, far):
    at_near = jnp.where(even, sz.ey, 0)
    for b in range(sz.blocks):
        face[0, b] = acc_ref[b, 0].astype(bf16)
        face[1, b] = acc_ref[b, sz.ex].astype(bf16)
        near[b] = acc_ref[b, :, at_near].astype(bf16)
        far[b] = acc_ref[b, :, sz.ey - at_near].astype(bf16)


def corner_pack_kernel(sz, near, far, out_ref):
    for side, i in enumerate((0, sz.ex)):
        for slot, ref in enumerate((near, far)):
            out_ref[side, slot] = ref[:, i]


def first_main(sz, n_mat, vec, from_x, from_y, own_inv, own_pot, *refs):
    mats = refs[:n_mat]
    prod_ref, ghost_x, ghost_y, u_ref, rhs_ref = refs[n_mat:]
    for j in range(sz.ey):
        ghost_x[0, j], ghost_x[1, j] = fields_of(from_x[j, :, sz.res + sz.full :])
    for i in range(sz.ex):
        ghost_y[0, i], ghost_y[1, i] = fields_of(from_y[i, :, sz.res + sz.full :])
    nodes = Nodes(sz, vec, from_x, from_y, own_inv, own_pot, ghost_x, ghost_y)

    def prepare(i, j):
        u_ref[:, i, j] = nodes.x(i, j) * nodes.inv(i, j)

    main_products(sz, prepare, u_ref, mats, rhs_ref, prod_ref)


def first_corner(sz, n_mat, even_ref, vec, from_x, from_y, corner, own_inv, own_pot, ghost_x, ghost_y,
                 prod_ref, *refs):
    mats = refs[:n_mat]
    acc_ref, face, near, far, last_x, last_field, small_ref, tail_ref = refs[n_mat:]
    last_field[0], last_field[1] = fields_of(corner[0, :, sz.res + sz.full :])
    last_x[...] = vectors_of(sz, corner[0])
    nodes = Nodes(sz, vec, from_x, from_y, own_inv, own_pot, ghost_x, ghost_y, last_field)
    u_corner = []
    for i, j in corner_edges(sz):
        x = last_x[...] if (i, j) == (sz.ex, sz.ey) else nodes.x(i, j)
        u_corner.append(x * nodes.inv(i, j))
    corner_products(sz, u_corner, prod_ref, mats, small_ref, tail_ref, acc_ref)
    write_messages(sz, even_ref[0] == 0, acc_ref, face, near, far)


def second_main(sz, n_mat, even_ref, vec, from_x, from_y, own_inv, own_pot, ghost_x, ghost_y,
                acc_in, face_in, near_in, far_in, *refs):
    mats = refs[:n_mat]
    prod_ref, y_ref, u_ref, rhs_ref = refs[n_mat:]
    nodes = Nodes(sz, vec, from_x, from_y, own_inv, own_pot, ghost_x, ghost_y)
    sums = Sums(sz, even_ref[0] == 0, acc_in, face_in, near_in, far_in)

    def prepare(i, j):
        old, inv = nodes.x(i, j), nodes.inv(i, j)
        image = inv * sums.at(i, j) + nodes.pot(i, j) * old
        new = (image - center_shift * old) / half_width
        y_ref[:, i, j] = new
        u_ref[:, i, j] = inv * new

    main_products(sz, prepare, u_ref, mats, rhs_ref, prod_ref)


def second_corner(sz, n_mat, even_ref, vec, from_x, from_y, own_inv, own_pot, ghost_x, ghost_y, last_x,
                  last_field, acc_in, face_in, near_in, far_in, corner_in, prod_ref, *refs):
    mats = refs[:n_mat]
    acc_ref, face, near, far, y_corner, small_ref, tail_ref = refs[n_mat:]
    even = even_ref[0] == 0
    nodes = Nodes(sz, vec, from_x, from_y, own_inv, own_pot, ghost_x, ghost_y, last_field)
    sums = Sums(sz, even, acc_in, face_in, near_in, far_in, corner_in)
    u_corner = []
    for at, (i, j) in enumerate(corner_edges(sz)):
        old = last_x[...] if (i, j) == (sz.ex, sz.ey) else nodes.x(i, j)
        inv = nodes.inv(i, j)
        image = inv * sums.at(i, j) + nodes.pot(i, j) * old
        new = (image - center_shift * old) / half_width
        y_corner[at] = new
        u_corner.append(inv * new)
    corner_products(sz, u_corner, prod_ref, mats, small_ref, tail_ref, acc_ref)
    write_messages(sz, even, acc_ref, face, near, far)


def third_main(sz, n_mat, even_ref, vec, from_x, from_y, own_inv, own_pot, ghost_x, ghost_y,
               acc_in, face_in, near_in, far_in, y_ref, *refs):
    mats = refs[:n_mat]
    prod_ref, new_ref, u_ref, rhs_ref = refs[n_mat:]
    nodes = Nodes(sz, vec, from_x, from_y, own_inv, own_pot, ghost_x, ghost_y)
    sums = Sums(sz, even_ref[0] == 0, acc_in, face_in, near_in, far_in)

    def prepare(i, j):
        old, inv = y_ref[:, i, j], nodes.inv(i, j)
        image = inv * sums.at(i, j) + nodes.pot(i, j) * old
        new = 2.0 * (image - center_shift * old) / half_width - nodes.x(i, j)
        new_ref[:, i, j] = new
        u_ref[:, i, j] = inv * new

    main_products(sz, prepare, u_ref, mats, rhs_ref, prod_ref)


def third_corner(sz, n_mat, even_ref, vec, from_x, from_y, own_inv, own_pot, ghost_x, ghost_y,
                 last_x, last_field, acc_in, face_in, near_in, far_in, corner_in, prod_ref, y_corner, *refs):
    mats = refs[:n_mat]
    acc_ref, new_corner, face, small_ref, tail_ref = refs[n_mat:]
    nodes = Nodes(sz, vec, from_x, from_y, own_inv, own_pot, ghost_x, ghost_y, last_field)
    sums = Sums(sz, even_ref[0] == 0, acc_in, face_in, near_in, far_in, corner_in)
    u_corner = []
    for at, (i, j) in enumerate(corner_edges(sz)):
        x = last_x[...] if (i, j) == (sz.ex, sz.ey) else nodes.x(i, j)
        old, inv = y_corner[at], nodes.inv(i, j)
        image = inv * sums.at(i, j) + nodes.pot(i, j) * old
        new = 2.0 * (image - center_shift * old) / half_width - x
        new_corner[at] = new
        u_corner.append(inv * new)
    corner_products(sz, u_corner, prod_ref, mats, small_ref, tail_ref, acc_ref)
    for j in range(sz.gy):
        face[:, j] = (gain * (nodes.inv(sz.ex, j) * acc_ref[:, sz.ex, j])).astype(bf16)


def third_end(sz, norm_scale, even_ref, own_inv, own_pot, ghost_x, ghost_y, last_field, acc_ref, y_ref,
              y_corner, new_ref, new_corner, turned, *refs):
    out_hbm, edge_x, edge_y, side, give, keep, part_ref, sem, rows_ref = refs
    nodes = Nodes(sz, None, None, None, own_inv, own_pot, ghost_x, ghost_y, last_field)

    def put_row(at, value):
        for b in range(sz.blocks):
            rows_ref[at, :, b * sz.width : (b + 1) * sz.width] = value[b]

    copies = []
    for i in range(sz.gx):
        for j in range(sz.gy):
            acc, inv = acc_ref[:, i, j], nodes.inv(i, j)
            if i == sz.ex or j == sz.ey:
                value = gain * (inv * acc)
                rounded = value.astype(bf16)
                if j < sz.ey:
                    put_row(sz.own_edges + j, rounded)
                else:
                    put_row(sz.own_edges + sz.ey + i, rounded)
                    if i < sz.ex:
                        side[:, i] = value
                continue
            at = sz.corner(i, j)
            old = y_ref[:, i, j] if at is None else y_corner[at]
            new = new_ref[:, i, j] if at is None else new_corner[at]
            image = inv * acc + nodes.pot(i, j) * new
            value = 2.0 * (image - center_shift * new) / half_width - old
            part_ref[:, i, j] = value
            if i == 0:
                edge_x[:, j] = value
            elif j == 0:
                edge_y[:, i - 1] = value
            put_row(i * sz.ey + j, value.astype(bf16))
        if i < sz.ex:
            copies.append(pltpu.make_async_copy(part_ref.at[:, i], out_hbm.at[:, i], sem.at[i]))
            copies[-1].start()
    for at in range(sz.own_edges + sz.ey + sz.gx, sz.edges):
        rows_ref[at] = jnp.zeros((sz.ez, sz.full), bf16)
    rows = rows_ref[...].reshape(sz.edges * sz.ez, sz.full)
    mine = even_ref[0]
    for half, out in ((1 - mine, give), (mine, keep)):
        local = jnp.dot(turned[half], rows, preferred_element_type=f32)
        out[...] = (local * norm_scale).astype(out.dtype)
    for copy in copies:
        copy.wait()


def ready_kernel(sz, keep, taken, side_ref, face, pieces, out_ref):
    for i in range(sz.ex):
        value = side_ref[:, i]
        if i == 0:
            value = value + face[:, sz.ey].astype(f32)
        out_ref[:, i] = value.astype(out_ref.dtype)
    rows = pieces.shape[2]
    for at in range(pieces.shape[1]):
        span = slice(at * rows, (at + 1) * rows)
        value = (keep[span] + taken[span].astype(f32)).astype(pieces.dtype)
        for copy in range(pieces.shape[0]):
            pieces[copy, at] = value


def last_kernel(sz, old_hbm, edge_x, edge_y, face, side, out_hbm, at_x, at_y, sems):
    del old_hbm
    for j in range(sz.ey):
        value = edge_x[:, j] + face[:, j].astype(f32)
        if j == 0:
            value = value + side[:, 0].astype(f32)
        at_x[:, j] = value
    for i in range(1, sz.ex):
        at_y[:, i - 1] = edge_y[:, i - 1] + side[:, i].astype(f32)
    copies = [
        pltpu.make_async_copy(at_x, out_hbm.at[:, 0], sems.at[0]),
        pltpu.make_async_copy(at_y, out_hbm.at[:, pl.ds(1, sz.ex - 1), 0], sems.at[1]),
    ]
    for copy in copies:
        copy.start()
    for copy in copies:
        copy.wait()


def like(shape, dtype):
    return jax.ShapeDtypeStruct(shape, dtype)


def call(kernel, name, flops, out_shape, scratch, operands, hbm=0, scalar_first=False, aliases=None,
         out_hbm=0):
    out_shape = [like(s.shape, s.dtype) for s in out_shape]
    size = sum(math.prod(s.shape) * jnp.dtype(s.dtype).itemsize for s in (*operands, *out_shape))
    whole = pl.BlockSpec(memory_space=pltpu.VMEM)
    specs = [pl.BlockSpec(memory_space=pltpu.HBM)] * hbm + [whole] * (len(operands) - hbm)
    if scalar_first:
        specs[0] = pl.BlockSpec(memory_space=pltpu.SMEM)
    out_specs = [pl.BlockSpec(memory_space=pltpu.HBM)] * out_hbm + [whole] * (len(out_shape) - out_hbm)
    out_shape = [pltpu.HBM(s.shape, s.dtype) for s in out_shape[:out_hbm]] + out_shape[out_hbm:]
    operands = [pltpu.with_memory_space_constraint(a, pltpu.HBM) for a in operands[:hbm]] + list(
        operands[hbm:]
    )
    return pl.pallas_call(
        kernel,
        in_specs=specs,
        out_specs=out_specs,
        out_shape=out_shape,
        scratch_shapes=scratch,
        input_output_aliases=aliases or {},
        compiler_params=pltpu.CompilerParams(vmem_limit_bytes=VMEM_LIMIT),
        cost_estimate=pl.CostEstimate(flops=flops, bytes_accessed=size, transcendentals=0),
        name=name,
    )(*operands)


def body(vectors, resident, inv_mass, potential, cell_matrix, connectivity):
    sz = Sizes(vectors, resident, inv_mass, connectivity)
    nx, ny = lax.axis_size("dx"), lax.axis_size("dy")
    norm_scale = 1.0 / math.sqrt(sz.ex * sz.ey * sz.ez * nx * ny)
    blocks, ez, width, full = sz.blocks, sz.ez, sz.width, sz.full
    res_count = resident.shape[-1]
    tile = (ez, width)

    conn = connectivity.reshape(sz.cells, sz.nodes)
    to_x, to_y, cell_matrix, conn = call(
        functools.partial(pack_kernel, sz), "pack", 0,
        [like((sz.ey, ez, sz.wide), bf16), like((sz.ex, ez, sz.wide), bf16), cell_matrix, conn],
        [
            pltpu.VMEM((2, sz.ey, ez), f32), pltpu.VMEM((2, sz.ex, ez), f32),
            pltpu.SemaphoreType.DMA((8 + 2 * blocks,)),
        ],
        [vectors, resident, inv_mass, potential, cell_matrix, conn], hbm=6,
    )
    from_x = send(to_x, -1, 0)
    from_y = send(to_y, 0, -1)

    halves = 2 if sz.cells % 2 == 0 else 1
    mats = call(
        functools.partial(order_kernel, sz), "order_cells", 4 * sz.cells * sz.depth**3,
        [like((sz.cells // halves, sz.rows, sz.depth), bf16)] * halves, [], [conn, cell_matrix],
    )
    own_inv = jnp.broadcast_to(inv_mass[..., None], inv_mass.shape + (width,))
    own_pot = jnp.broadcast_to(potential[..., None], inv_mass.shape + (width,))
    parity = jnp.reshape(lax.axis_index("dy") % 2, (1,)).astype(jnp.int32)
    ghost_corner = send(from_y[:1], -1, 0)

    grid = (blocks, sz.gx, sz.gy) + tile
    own = (blocks, sz.ex, sz.ey) + tile
    products = like((sz.cells, sz.rows, full), f32)
    state_grid = like(grid, f32)
    messages = [
        like((2, blocks, sz.gy) + tile, bf16),
        like((blocks, sz.gx) + tile, bf16),
        like((blocks, sz.gx) + tile, bf16),
    ]
    main_scratch = [pltpu.VMEM(grid, f32), pltpu.VMEM((2, sz.depth, full), f32)]
    corner_scratch = [
        pltpu.VMEM((LANES, full), f32),
        pltpu.VMEM((sz.cells, sz.base + sz.rows - sz.tail, full), f32),
    ]
    n_mat = len(mats)
    flops = 2 * sz.cells * sz.rows * sz.depth * full
    small_flops = 2 * sz.cells * sz.rows * LANES * full

    def exchange(face, near, far):
        face = swap_x(face)
        near, far = swap_y(near, far)
        (corner,) = call(
            functools.partial(corner_pack_kernel, sz), "corner_pack", 0,
            [like((2, 2) + sz.edge, bf16)], [], [near, far],
        )
        return [face, near, far], swap_x(corner)

    prod, ghost_x, ghost_y = call(
        functools.partial(first_main, sz, n_mat), "first_main", flops,
        [products, like((2, sz.ey) + tile, f32), like((2, sz.ex) + tile, f32)], main_scratch,
        [vectors, from_x, from_y, own_inv, own_pot, *mats],
    )
    acc, face, near, far, last_x, last_field = call(
        functools.partial(first_corner, sz, n_mat), "first_corner", small_flops,
        [state_grid, *messages, like(sz.edge, f32), like((2,) + tile, f32)], corner_scratch,
        [
            parity, vectors, from_x, from_y, ghost_corner, own_inv, own_pot, ghost_x, ghost_y, prod, *mats,
        ],
        scalar_first=True,
    )
    (turned,) = call(
        functools.partial(turn_kernel, sz, ny // 2), "turn_residents", flops // 2,
        [like((2, res_count // 2, sz.edges * ez), bf16)], [],
        [resident.reshape(-1, res_count), from_x, from_y, ghost_corner],
    )
    got, corner = exchange(face, near, far)
    state = [vectors, from_x, from_y, own_inv, own_pot, ghost_x, ghost_y]
    ends = [last_x, last_field]
    prod, y1 = call(
        functools.partial(second_main, sz, n_mat), "second_main", flops,
        [products, state_grid], main_scratch,
        [parity, *state, acc, *got, *mats], scalar_first=True,
    )
    acc, face, near, far, y1_corner = call(
        functools.partial(second_corner, sz, n_mat), "second_corner", small_flops,
        [state_grid, *messages, like((4,) + sz.edge, f32)], corner_scratch,
        [parity, *state, *ends, acc, *got, corner, prod, *mats], scalar_first=True,
    )
    got, corner = exchange(face, near, far)
    prod, y2 = call(
        functools.partial(third_main, sz, n_mat), "third_main", flops,
        [products, state_grid], main_scratch,
        [parity, *state, acc, *got, y1, *mats], scalar_first=True,
    )
    acc, new_corner, face = call(
        functools.partial(third_corner, sz, n_mat), "third_corner", small_flops,
        [state_grid, like((4,) + sz.edge, f32), like((blocks, sz.gy) + tile, bf16)], corner_scratch,
        [parity, *state, *ends, acc, *got, corner, prod, y1_corner, *mats], scalar_first=True,
    )
    face = send(face, 1, 0)
    filtered, edge_x, edge_y, side, give, keep = call(
        functools.partial(third_end, sz, norm_scale), "third_end", 2 * res_count * sz.edges * ez * full,
        [
            like(own, f32), like((blocks, sz.ey) + tile, f32), like((blocks, sz.ex - 1) + tile, f32),
            like((blocks, sz.ex) + tile, f32), like((res_count // 2, full), bf16), like((res_count // 2, full), f32),
        ],
        [
            pltpu.VMEM(own, f32), pltpu.SemaphoreType.DMA((sz.ex,)),
            pltpu.VMEM((sz.edges, ez, full), bf16),
        ],
        [
            parity, own_inv, own_pot, ghost_x, ghost_y, last_field, acc, y1, y1_corner, y2, new_corner, turned,
        ],
        scalar_first=True, out_hbm=1,
    )

    pieces, side = call(
        functools.partial(ready_kernel, sz), "ready", 0,
        [like((nx, ny // 2, res_count // ny, full), bf16), like((blocks, sz.ex) + tile, bf16)],
        [], [keep, send_near(give), side, face],
    )
    pieces = pieces.reshape(nx * ny // 2, -1, full)
    groups = [[a * ny + b for a in range(nx) for b in range(c, ny, 2)] for c in range(2)]
    pieces = lax.all_to_all(pieces, ("dx", "dy"), 0, 0, axis_index_groups=groups)
    margin = jnp.sum(pieces.astype(f32), axis=0)

    side = send(side, 0, 1)
    (filtered,) = call(
        functools.partial(last_kernel, sz), "last", 0, [like(own, f32)],
        [
            pltpu.VMEM((blocks, sz.ey) + tile, f32), pltpu.VMEM((blocks, sz.ex - 1) + tile, f32),
            pltpu.SemaphoreType.DMA((2,)),
        ],
        [filtered, edge_x, edge_y, face, side], hbm=1, out_hbm=1, aliases={0: 0},
    )
    return (filtered, margin)


def solution(mesh):
    return jax.shard_map(
        body,
        mesh=mesh,
        in_specs=(
            P(None, "dx", "dy", None, None),
            P("dx", "dy", None, None),
            P("dx", "dy", None),
            P("dx", "dy", None),
            P(),
            P("dx", "dy", None, None),
        ),
        out_specs=(P(None, "dx", "dy", None, None), P("dy", None)),
        check_vma=False,
    )
```

```python
import functools
import math

import jax
import jax.numpy as jnp
from jax import lax
from jax.experimental import pallas as pl
from jax.experimental.pallas import tpu as pltpu
from jax.sharding import PartitionSpec as P

LANES = 128
TILE = 256
SUB = 16
VMEM_LIMIT = 16 * 1024 * 1024

center_shift = 1.2
half_width = 2.0
gain = 2.0 / half_width

f32, bf16 = jnp.float32, jnp.bfloat16


def round_up(value, step):
    return -(-value // step) * step


class Sizes:
    def __init__(self, vectors, resident, inv_mass, connectivity):
        self.blocks = vectors.shape[0]
        self.width = vectors.shape[-1]
        self.full = self.blocks * self.width
        self.res = resident.shape[-1]
        self.wide = self.res + self.full + self.width
        self.ex, self.ey, self.ez = inv_mass.shape
        self.cells, self.nodes = connectivity.shape[2:]
        self.n1 = round(self.nodes ** (1.0 / 3.0))
        self.p = self.n1 - 1
        self.cx, self.cy, self.cz = self.ex // self.p, self.ey // self.p, self.ez // self.p
        self.gx, self.gy, self.gz = self.ex + 1, self.ey + 1, self.ez
        self.edge = (self.blocks, self.ez, self.width)
        self.origins = [
            (a * self.p, b * self.p, c * self.p)
            for a in range(self.cx)
            for b in range(self.cy)
            for c in range(self.cz)
        ]
        self.most = max(len(self.cell_corners(cell)) for cell in range(self.cells))
        self.base = round_up(self.most * self.n1, 8)
        plain = self.n1 * self.n1 - min(len(self.cell_corners(cell)) for cell in range(self.cells))
        self.tail = self.base + plain * self.p
        self.rows = round_up(self.tail + plain, SUB)
        self.depth = round_up(self.rows, LANES)
        self.own_edges = self.ex * self.ey
        self.edges = round_up(self.own_edges + self.ey + self.gx, LANES // self.ez)

    def corner(self, i, j):
        if i in (0, self.ex) and j in (0, self.ey):
            return 2 * (i // self.ex) + j // self.ey
        return None

    def cell_corners(self, cell):
        x0, y0, _ = self.origins[cell]
        return [
            (i, j)
            for i in range(self.n1)
            for j in range(self.n1)
            if self.corner(x0 + i, y0 + j) is not None
        ]

    def runs(self, cell):
        corners = self.cell_corners(cell)
        place = 0
        for i in range(self.n1):
            js = [j for j in range(self.n1) if (i, j) not in corners]
            while js:
                count = 1
                while count < len(js) and js[count] == js[0] + count:
                    count += 1
                yield place, i, js[0], count
                place += count
                js = js[count:]


def send(value, steps_x, steps_y):
    nx, ny = lax.axis_size("dx"), lax.axis_size("dy")
    pairs = [
        (a * ny + b, ((a + steps_x) % nx) * ny + (b + steps_y) % ny)
        for a in range(nx)
        for b in range(ny)
    ]
    return lax.ppermute(value, ("dx", "dy"), pairs)


def swap_x(value):
    if lax.axis_size("dx") == 2:
        return send(value, 1, 0)
    return jnp.stack([send(value[0], -1, 0), send(value[1], 1, 0)])


def send_near(value):
    pairs = [(b, b + 1 if b % 2 == 0 else b - 1) for b in range(lax.axis_size("dy"))]
    return lax.ppermute(value, "dy", pairs)


def swap_y(near, far):
    ny = lax.axis_size("dy")
    far_pairs = [(b, (b - 1 if b % 2 == 0 else b + 1) % ny) for b in range(ny)]
    far = lax.ppermute(far, "dy", far_pairs)
    return send_near(near), far


def order_kernel(sz, first, conn_ref, matrix_ref, out_ref):
    for slot in range(out_ref.shape[0]):
        cell = first + slot
        x0, y0, z0 = sz.origins[cell]
        conn = conn_ref[cell : cell + 1, :].astype(f32)
        li = jnp.floor((conn + 0.5) * (1.0 / (sz.gy * sz.gz)))
        rest = conn - li * (sz.gy * sz.gz)
        lj = jnp.floor((rest + 0.5) * (1.0 / sz.gz))
        lk = rest - lj * sz.gz - z0
        lk = jnp.where(lk < 0, lk + sz.gz, lk)
        column = (li - x0) * sz.n1 + (lj - y0)
        corners = [i * sz.n1 + j for i, j in sz.cell_corners(cell)]
        place = column
        for at in corners:
            place = place - jnp.where(column > at, 1.0, 0.0)
        index = jnp.where(lk < sz.p, sz.base + place * sz.p + lk, sz.tail + place)
        for rank, at in enumerate(corners):
            special = jnp.where(lk < sz.p, rank * sz.p + lk, len(corners) * sz.p + rank)
            index = jnp.where(column == at, special, index)
        index = index.astype(jnp.int32)
        row = lax.broadcasted_iota(jnp.int32, (sz.depth, sz.nodes), 0)
        pick = (row == index).astype(f32).astype(bf16)
        half = jnp.dot(pick[: sz.rows], matrix_ref[...], preferred_element_type=f32)
        half = half.astype(bf16)
        cuts = list(range(0, sz.depth, TILE)) + [sz.depth]
        for r0, r1 in zip(cuts[:-1], cuts[1:]):
            r1 = min(r1, sz.rows)
            block = lax.dot_general(
                half[r0:r1], pick[r0:], (((1,), (1,)), ((), ())), preferred_element_type=f32
            ).astype(bf16)
            out_ref[slot, r0:r1, r0:] = block
            for c0, c1 in zip(cuts[:-1], cuts[1:]):
                if c0 > r0:
                    mirror = block[:, c0 - r0 : c1 - r0].T
                    c1 = min(c1, sz.rows)
                    out_ref[slot, c0:c1, r0:r1] = mirror[: c1 - c0]


def field_row(inv, pot):
    lane = lax.broadcasted_iota(jnp.int32, inv.shape, inv.ndim - 1)
    row = jnp.zeros_like(inv)
    for at, rest in enumerate((inv, pot)):
        for k in range(3):
            part = rest.astype(bf16).astype(f32)
            rest = rest - part
            row = jnp.where(lane == 3 * at + k, part, row)
    return row.astype(bf16)


def field_rows(sz, inv, pot, count):
    inv, pot = inv.T, pot.T
    shape = (sz.ez, sz.width)
    for at in range(count):
        yield at, field_row(
            jnp.broadcast_to(inv[:, at : at + 1], shape), jnp.broadcast_to(pot[:, at : at + 1], shape)
        )


def fields_of(row):
    row = row.astype(f32)
    return [
        jnp.broadcast_to(sum(row[:, 3 * at + k : 3 * at + k + 1] for k in range(3)), row.shape)
        for at in range(2)
    ]


def pack_kernel(
    sz, vec_hbm, res_hbm, inv_hbm, pot_hbm, mat_hbm, conn_hbm,
    to_x, to_y, mat_ref, conn_ref, at_x, at_y, sems,
):
    pairs = [
        (inv_hbm.at[0], at_x.at[0]), (pot_hbm.at[0], at_x.at[1]),
        (inv_hbm.at[:, 0], at_y.at[0]), (pot_hbm.at[:, 0], at_y.at[1]),
        (res_hbm.at[0], to_x.at[:, :, pl.ds(0, sz.res)]),
        (res_hbm.at[:, 0], to_y.at[:, :, pl.ds(0, sz.res)]),
    ]
    for b in range(sz.blocks):
        lanes = pl.ds(sz.res + b * sz.width, sz.width)
        pairs.append((vec_hbm.at[b, 0], to_x.at[:, :, lanes]))
        pairs.append((vec_hbm.at[b, :, 0], to_y.at[:, :, lanes]))
    pairs += [(mat_hbm, mat_ref), (conn_hbm, conn_ref)]
    copies = [pltpu.make_async_copy(a, b, sems.at[k]) for k, (a, b) in enumerate(pairs)]
    for copy in copies:
        copy.start()
    for copy in copies[:4]:
        copy.wait()
    for j, row in field_rows(sz, at_x[0], at_x[1], sz.ey):
        to_x[j, :, sz.res + sz.full :] = row
    for i, row in field_rows(sz, at_y[0], at_y[1], sz.ex):
        to_y[i, :, sz.res + sz.full :] = row
    for copy in copies[4:]:
        copy.wait()


def turn_kernel(sz, pieces, res_ref, from_x, from_y, corner, out_ref):
    own = sz.own_edges * sz.ez
    share = sz.res // out_ref.shape[0] // pieces

    def put(g, columns, value):
        for at in range(0, LANES, share):
            owner = (g + at) // share
            row = owner // 2 * share
            out_ref[owner % 2, row : row + share, columns] = value[at : at + share]

    for g in range(0, sz.res, LANES):
        lanes = slice(g, g + LANES)
        put(g, slice(0, own), res_ref[:, lanes].T)
        rest = sz.edges - sz.own_edges - sz.ey - sz.gx
        parts = [from_x[:, :, lanes], from_y[:, :, lanes], corner[:, :, lanes]]
        if rest:
            parts.append(jnp.zeros((rest, sz.ez, LANES), bf16))
        ghosts = jnp.concatenate(parts, axis=0)
        put(g, slice(own, sz.edges * sz.ez), ghosts.reshape(-1, LANES).T)


def vectors_of(sz, edge):
    lanes = [slice(sz.res + b * sz.width, sz.res + (b + 1) * sz.width) for b in range(sz.blocks)]
    return jnp.stack([edge[:, at] for at in lanes]).astype(f32)


class Nodes:
    def __init__(self, sz, vec, from_x, from_y, own_inv, own_pot, ghost_x, ghost_y, corners=None):
        self.sz, self.vec, self.from_x, self.from_y = sz, vec, from_x, from_y
        self.own, self.ghost_x, self.ghost_y, self.corners = (own_inv, own_pot), ghost_x, ghost_y, corners

    def x(self, i, j):
        sz = self.sz
        if i < sz.ex and j < sz.ey:
            return self.vec[:, i, j].astype(f32)
        return vectors_of(sz, self.from_x[j] if i == sz.ex else self.from_y[i])

    def field(self, at, i, j):
        sz = self.sz
        if i < sz.ex and j < sz.ey:
            return self.own[at][i, j]
        if i < sz.ex:
            return self.ghost_y[at, i]
        if j < sz.ey:
            return self.ghost_x[at, j]
        return self.corners[at]

    def inv(self, i, j):
        return self.field(0, i, j)

    def pot(self, i, j):
        return self.field(1, i, j)


class Sums:
    def __init__(self, sz, even, acc, face, near, far, corner=None):
        self.sz, self.even, self.acc, self.face = sz, even, acc, face
        self.near, self.far, self.corner = near, far, corner

    def at(self, i, j):
        sz = self.sz
        total = self.acc[:, i, j]
        side = 1 if i == 0 else 0 if i == sz.ex else None
        if side is not None:
            total = total + self.face[side, :, j].astype(f32)
        if j in (0, sz.ey):
            is_near = self.even if j == sz.ey else jnp.logical_not(self.even)
            total = total + jnp.where(is_near, self.near[:, i].astype(f32), self.far[:, i].astype(f32))
            if side is not None:
                total = total + jnp.where(
                    is_near, self.corner[side, 0].astype(f32), self.corner[side, 1].astype(f32)
                )
        return total


def corner_edges(sz):
    return [(i, j) for i in (0, sz.ex) for j in (0, sz.ey)]


def main_products(sz, prepare, u_ref, mat_refs, rhs_ref, out_ref):
    width = sz.width
    flat = sz.gx * sz.gy * sz.gz
    u_flat = u_ref.reshape(sz.blocks * flat, width)
    matrices = [ref.at[c] for ref in mat_refs for c in range(ref.shape[0])]
    last = sz.nodes // 8 * 8
    ready = set()
    for cell, (x0, y0, z0) in enumerate(sz.origins):
        slot = cell % 2
        if cell < 2:
            rhs_ref[slot, : sz.base] = jnp.zeros((sz.base, sz.full), f32)
            rhs_ref[slot, last:] = jnp.zeros((sz.depth - last, sz.full), f32)
        for place, i, j, count in sz.runs(cell):
            for at in range(j, j + count):
                if (x0 + i, y0 + at) not in ready:
                    prepare(x0 + i, y0 + at)
                    ready.add((x0 + i, y0 + at))
        z1 = z0 + sz.p
        wrap = z1 % sz.gz
        for b in range(sz.blocks):
            lanes = slice(b * width, (b + 1) * width)
            for place, i, j, count in sz.runs(cell):
                row = sz.base + place * sz.p
                rhs_ref[slot, row : row + count * sz.p, lanes] = u_ref[
                    b, x0 + i, y0 + j : y0 + j + count, z0:z1
                ].reshape(count * sz.p, width)
        for b in range(sz.blocks):
            lanes = slice(b * width, (b + 1) * width)
            for place, i, j, count in sz.runs(cell):
                start = b * flat + ((x0 + i) * sz.gy + y0 + j) * sz.gz + wrap
                rhs_ref[slot, sz.tail + place : sz.tail + place + count, lanes] = u_flat[
                    pl.ds(start, count, stride=sz.gz)
                ]
        out_ref[cell] = jnp.dot(
            matrices[cell][...], rhs_ref[slot].astype(bf16), preferred_element_type=f32
        )


def corner_products(sz, u_corner, prod_ref, mat_refs, small_ref, tail_ref, acc_ref):
    width = sz.width
    flat = sz.gx * sz.gy * sz.gz
    acc_flat = acc_ref.reshape(sz.blocks * flat, width)
    matrices = [ref.at[c] for ref in mat_refs for c in range(ref.shape[0])]
    small_ref[...] = jnp.zeros_like(small_ref)
    touched = set()
    for cell, (x0, y0, z0) in enumerate(sz.origins):
        z1 = z0 + sz.p
        wrap = z1 % sz.gz
        corners = sz.cell_corners(cell)
        for rank, (i, j) in enumerate(corners):
            value = u_corner[sz.corner(x0 + i, y0 + j)]
            last = len(corners) * sz.p + rank
            for b in range(sz.blocks):
                lanes = slice(b * width, (b + 1) * width)
                small_ref[rank * sz.p : (rank + 1) * sz.p, lanes] = value[b, z0:z1]
                small_ref[last : last + 1, lanes] = value[b, wrap : wrap + 1]
        total = prod_ref[cell] + jnp.dot(
            matrices[cell][:, : small_ref.shape[0]], small_ref[...].astype(bf16),
            preferred_element_type=f32,
        )
        tail_ref[cell, : sz.base] = total[: sz.base]
        tail_ref[cell, sz.base :] = total[sz.tail :]
        spans = [(rank * sz.p, i, j, 1) for rank, (i, j) in enumerate(corners)]
        spans += [(sz.base + place * sz.p, i, j, count) for place, i, j, count in sz.runs(cell)]
        for row, i, j, count in spans:
            for at in range(count):
                part = total[row + at * sz.p : row + (at + 1) * sz.p]
                key = (x0 + i, y0 + j + at, z0)
                for b in range(sz.blocks):
                    value = part[:, b * width : (b + 1) * width]
                    if key in touched:
                        value = acc_ref[b, key[0], key[1], z0:z1] + value
                    acc_ref[b, key[0], key[1], z0:z1] = value
                touched.add(key)
    for cell, (x0, y0, z0) in enumerate(sz.origins):
        wrap = (z0 + sz.p) % sz.gz
        corners = sz.cell_corners(cell)
        spans = [(len(corners) * sz.p + rank, i, j, 1) for rank, (i, j) in enumerate(corners)]
        spans += [(sz.base + place, i, j, count) for place, i, j, count in sz.runs(cell)]
        for row, i, j, count in spans:
            for b in range(sz.blocks):
                start = b * flat + ((x0 + i) * sz.gy + y0 + j) * sz.gz + wrap
                rows = pl.ds(start, count, stride=sz.gz) if count > 1 else pl.ds(start, 1)
                lanes = slice(b * width, (b + 1) * width)
                acc_flat[rows] = acc_flat[rows] + tail_ref[cell, row : row + count, lanes]


def write_messages(sz, even, acc_ref, face, near, far):
    at_near = jnp.where(even, sz.ey, 0)
    for b in range(sz.blocks):
        face[0, b] = acc_ref[b, 0].astype(bf16)
        face[1, b] = acc_ref[b, sz.ex].astype(bf16)
        near[b] = acc_ref[b, :, at_near].astype(bf16)
        far[b] = acc_ref[b, :, sz.ey - at_near].astype(bf16)


def corner_pack_kernel(sz, near, far, out_ref):
    for side, i in enumerate((0, sz.ex)):
        for slot, ref in enumerate((near, far)):
            out_ref[side, slot] = ref[:, i]


def first_main(sz, n_mat, vec, from_x, from_y, own_inv, own_pot, *refs):
    mats = refs[:n_mat]
    prod_ref, ghost_x, ghost_y, u_ref, rhs_ref = refs[n_mat:]
    for j in range(sz.ey):
        ghost_x[0, j], ghost_x[1, j] = fields_of(from_x[j, :, sz.res + sz.full :])
    for i in range(sz.ex):
        ghost_y[0, i], ghost_y[1, i] = fields_of(from_y[i, :, sz.res + sz.full :])
    nodes = Nodes(sz, vec, from_x, from_y, own_inv, own_pot, ghost_x, ghost_y)

    def prepare(i, j):
        u_ref[:, i, j] = nodes.x(i, j) * nodes.inv(i, j)

    main_products(sz, prepare, u_ref, mats, rhs_ref, prod_ref)


def first_corner(sz, n_mat, even_ref, vec, from_x, from_y, corner, own_inv, own_pot, ghost_x, ghost_y,
                 prod_ref, *refs):
    mats = refs[:n_mat]
    acc_ref, face, near, far, last_x, last_field, small_ref, tail_ref = refs[n_mat:]
    last_field[0], last_field[1] = fields_of(corner[0, :, sz.res + sz.full :])
    last_x[...] = vectors_of(sz, corner[0])
    nodes = Nodes(sz, vec, from_x, from_y, own_inv, own_pot, ghost_x, ghost_y, last_field)
    u_corner = []
    for i, j in corner_edges(sz):
        x = last_x[...] if (i, j) == (sz.ex, sz.ey) else nodes.x(i, j)
        u_corner.append(x * nodes.inv(i, j))
    corner_products(sz, u_corner, prod_ref, mats, small_ref, tail_ref, acc_ref)
    write_messages(sz, even_ref[0] == 0, acc_ref, face, near, far)


def second_main(sz, n_mat, even_ref, vec, from_x, from_y, own_inv, own_pot, ghost_x, ghost_y,
                acc_in, face_in, near_in, far_in, *refs):
    mats = refs[:n_mat]
    prod_ref, y_ref, u_ref, rhs_ref = refs[n_mat:]
    nodes = Nodes(sz, vec, from_x, from_y, own_inv, own_pot, ghost_x, ghost_y)
    sums = Sums(sz, even_ref[0] == 0, acc_in, face_in, near_in, far_in)

    def prepare(i, j):
        old, inv = nodes.x(i, j), nodes.inv(i, j)
        image = inv * sums.at(i, j) + nodes.pot(i, j) * old
        new = (image - center_shift * old) / half_width
        y_ref[:, i, j] = new
        u_ref[:, i, j] = inv * new

    main_products(sz, prepare, u_ref, mats, rhs_ref, prod_ref)


def second_corner(sz, n_mat, even_ref, vec, from_x, from_y, own_inv, own_pot, ghost_x, ghost_y, last_x,
                  last_field, acc_in, face_in, near_in, far_in, corner_in, prod_ref, *refs):
    mats = refs[:n_mat]
    acc_ref, face, near, far, y_corner, small_ref, tail_ref = refs[n_mat:]
    even = even_ref[0] == 0
    nodes = Nodes(sz, vec, from_x, from_y, own_inv, own_pot, ghost_x, ghost_y, last_field)
    sums = Sums(sz, even, acc_in, face_in, near_in, far_in, corner_in)
    u_corner = []
    for at, (i, j) in enumerate(corner_edges(sz)):
        old = last_x[...] if (i, j) == (sz.ex, sz.ey) else nodes.x(i, j)
        inv = nodes.inv(i, j)
        image = inv * sums.at(i, j) + nodes.pot(i, j) * old
        new = (image - center_shift * old) / half_width
        y_corner[at] = new
        u_corner.append(inv * new)
    corner_products(sz, u_corner, prod_ref, mats, small_ref, tail_ref, acc_ref)
    write_messages(sz, even, acc_ref, face, near, far)


def third_main(sz, n_mat, even_ref, vec, from_x, from_y, own_inv, own_pot, ghost_x, ghost_y,
               acc_in, face_in, near_in, far_in, y_ref, *refs):
    mats = refs[:n_mat]
    prod_ref, new_ref, u_ref, rhs_ref = refs[n_mat:]
    nodes = Nodes(sz, vec, from_x, from_y, own_inv, own_pot, ghost_x, ghost_y)
    sums = Sums(sz, even_ref[0] == 0, acc_in, face_in, near_in, far_in)

    def prepare(i, j):
        old, inv = y_ref[:, i, j], nodes.inv(i, j)
        image = inv * sums.at(i, j) + nodes.pot(i, j) * old
        new = 2.0 * (image - center_shift * old) / half_width - nodes.x(i, j)
        new_ref[:, i, j] = new
        u_ref[:, i, j] = inv * new

    main_products(sz, prepare, u_ref, mats, rhs_ref, prod_ref)


def third_corner(sz, n_mat, norm_scale, even_ref, vec, from_x, from_y, own_inv, own_pot, ghost_x, ghost_y,
                 last_x, last_field, acc_in, face_in, near_in, far_in, corner_in, prod_ref, y_ref,
                 y_corner, new_ref, turned, *refs):
    mats = refs[:n_mat]
    out_hbm, edge_x, edge_y, face, side, give, keep = refs[n_mat : n_mat + 7]
    part_ref, sem, acc_ref, rows_ref, small_ref, tail_ref = refs[n_mat + 7 :]
    nodes = Nodes(sz, vec, from_x, from_y, own_inv, own_pot, ghost_x, ghost_y, last_field)
    sums = Sums(sz, even_ref[0] == 0, acc_in, face_in, near_in, far_in, corner_in)
    u_corner, new_corner = [], []
    for at, (i, j) in enumerate(corner_edges(sz)):
        x = last_x[...] if (i, j) == (sz.ex, sz.ey) else nodes.x(i, j)
        old, inv = y_corner[at], nodes.inv(i, j)
        image = inv * sums.at(i, j) + nodes.pot(i, j) * old
        new_corner.append(2.0 * (image - center_shift * old) / half_width - x)
        u_corner.append(inv * new_corner[-1])
    corner_products(sz, u_corner, prod_ref, mats, small_ref, tail_ref, acc_ref)

    def put_row(at, value):
        for b in range(sz.blocks):
            rows_ref[at, :, b * sz.width : (b + 1) * sz.width] = value[b]

    copies = []
    for i in range(sz.gx):
        for j in range(sz.gy):
            acc, inv = acc_ref[:, i, j], nodes.inv(i, j)
            if i == sz.ex or j == sz.ey:
                value = gain * (inv * acc)
                rounded = value.astype(bf16)
                if i == sz.ex:
                    face[:, j] = rounded
                else:
                    side[:, i] = value
                put_row(sz.own_edges + (j if j < sz.ey else sz.ey + i), rounded)
                continue
            at = sz.corner(i, j)
            old = y_ref[:, i, j] if at is None else y_corner[at]
            new = new_ref[:, i, j] if at is None else new_corner[at]
            image = inv * acc + nodes.pot(i, j) * new
            value = 2.0 * (image - center_shift * new) / half_width - old
            part_ref[:, i, j] = value
            if i == 0:
                edge_x[:, j] = value
            elif j == 0:
                edge_y[:, i - 1] = value
            put_row(i * sz.ey + j, value.astype(bf16))
        if i < sz.ex:
            copies.append(pltpu.make_async_copy(part_ref.at[:, i], out_hbm.at[:, i], sem.at[i]))
            copies[-1].start()
    for at in range(sz.own_edges + sz.ey + sz.gx, sz.edges):
        rows_ref[at] = jnp.zeros((sz.ez, sz.full), bf16)
    rows = rows_ref[...].reshape(sz.edges * sz.ez, sz.full)
    mine = even_ref[0]
    for half, out in ((1 - mine, give), (mine, keep)):
        local = jnp.dot(turned[half], rows, preferred_element_type=f32)
        out[...] = (local * norm_scale).astype(out.dtype)
    for copy in copies:
        copy.wait()


def pieces_kernel(keep, taken, pieces):
    rows = pieces.shape[2]
    for at in range(pieces.shape[1]):
        span = slice(at * rows, (at + 1) * rows)
        value = (keep[span] + taken[span].astype(f32)).astype(pieces.dtype)
        for copy in range(pieces.shape[0]):
            pieces[copy, at] = value


def last_side_kernel(sz, side_ref, face, out_ref):
    for i in range(sz.ex):
        value = side_ref[:, i]
        if i == 0:
            value = value + face[:, sz.ey].astype(f32)
        out_ref[:, i] = value.astype(out_ref.dtype)


def last_kernel(sz, old_hbm, edge_x, edge_y, face, side, out_hbm, at_x, at_y, sems):
    del old_hbm
    for j in range(sz.ey):
        value = edge_x[:, j] + face[:, j].astype(f32)
        if j == 0:
            value = value + side[:, 0].astype(f32)
        at_x[:, j] = value
    for i in range(1, sz.ex):
        at_y[:, i - 1] = edge_y[:, i - 1] + side[:, i].astype(f32)
    copies = [
        pltpu.make_async_copy(at_x, out_hbm.at[:, 0], sems.at[0]),
        pltpu.make_async_copy(at_y, out_hbm.at[:, pl.ds(1, sz.ex - 1), 0], sems.at[1]),
    ]
    for copy in copies:
        copy.start()
    for copy in copies:
        copy.wait()


def like(shape, dtype):
    return jax.ShapeDtypeStruct(shape, dtype)


def call(kernel, name, flops, out_shape, scratch, operands, hbm=0, scalar_first=False, aliases=None,
         out_hbm=0):
    out_shape = [like(s.shape, s.dtype) for s in out_shape]
    size = sum(math.prod(s.shape) * jnp.dtype(s.dtype).itemsize for s in (*operands, *out_shape))
    whole = pl.BlockSpec(memory_space=pltpu.VMEM)
    specs = [pl.BlockSpec(memory_space=pltpu.HBM)] * hbm + [whole] * (len(operands) - hbm)
    if scalar_first:
        specs[0] = pl.BlockSpec(memory_space=pltpu.SMEM)
    out_specs = [pl.BlockSpec(memory_space=pltpu.HBM)] * out_hbm + [whole] * (len(out_shape) - out_hbm)
    out_shape = [pltpu.HBM(s.shape, s.dtype) for s in out_shape[:out_hbm]] + out_shape[out_hbm:]
    operands = [pltpu.with_memory_space_constraint(a, pltpu.HBM) for a in operands[:hbm]] + list(
        operands[hbm:]
    )
    return pl.pallas_call(
        kernel,
        in_specs=specs,
        out_specs=out_specs,
        out_shape=out_shape,
        scratch_shapes=scratch,
        input_output_aliases=aliases or {},
        compiler_params=pltpu.CompilerParams(vmem_limit_bytes=VMEM_LIMIT),
        cost_estimate=pl.CostEstimate(flops=flops, bytes_accessed=size, transcendentals=0),
        name=name,
    )(*operands)


def body(vectors, resident, inv_mass, potential, cell_matrix, connectivity):
    sz = Sizes(vectors, resident, inv_mass, connectivity)
    nx, ny = lax.axis_size("dx"), lax.axis_size("dy")
    norm_scale = 1.0 / math.sqrt(sz.ex * sz.ey * sz.ez * nx * ny)
    blocks, ez, width, full = sz.blocks, sz.ez, sz.width, sz.full
    res_count = resident.shape[-1]
    tile = (ez, width)

    conn = connectivity.reshape(sz.cells, sz.nodes)
    to_x, to_y, loaded, conn = call(
        functools.partial(pack_kernel, sz), "pack", 0,
        [like((sz.ey, ez, sz.wide), bf16), like((sz.ex, ez, sz.wide), bf16), cell_matrix, conn],
        [
            pltpu.VMEM((2, sz.ey, ez), f32), pltpu.VMEM((2, sz.ex, ez), f32),
            pltpu.SemaphoreType.DMA((8 + 2 * blocks,)),
        ],
        [vectors, resident, inv_mass, potential, cell_matrix, conn], hbm=6,
    )
    from_x = send(to_x, -1, 0)
    from_y = send(to_y, 0, -1)

    halves = 2 if sz.cells % 2 == 0 else 1
    step = sz.cells // halves
    mats = []
    for at in range(0, sz.cells, step):
        mats += call(
            functools.partial(order_kernel, sz, at), "order_cells", 4 * step * sz.depth**3,
            [like((step, sz.rows, sz.depth), bf16)], [], [conn, loaded if at == 0 else cell_matrix],
        )
    own_inv = jnp.broadcast_to(inv_mass[..., None], inv_mass.shape + (width,))
    own_pot = jnp.broadcast_to(potential[..., None], inv_mass.shape + (width,))
    parity = jnp.reshape(lax.axis_index("dy") % 2, (1,)).astype(jnp.int32)
    ghost_corner = send(from_y[:1], -1, 0)

    grid = (blocks, sz.gx, sz.gy) + tile
    own = (blocks, sz.ex, sz.ey) + tile
    products = like((sz.cells, sz.rows, full), f32)
    state_grid = like(grid, f32)
    messages = [
        like((2, blocks, sz.gy) + tile, bf16),
        like((blocks, sz.gx) + tile, bf16),
        like((blocks, sz.gx) + tile, bf16),
    ]
    main_scratch = [pltpu.VMEM(grid, f32), pltpu.VMEM((2, sz.depth, full), f32)]
    corner_scratch = [
        pltpu.VMEM((LANES, full), f32),
        pltpu.VMEM((sz.cells, sz.base + sz.rows - sz.tail, full), f32),
    ]
    n_mat = len(mats)
    flops = 2 * sz.cells * sz.rows * sz.depth * full
    small_flops = 2 * sz.cells * sz.rows * LANES * full

    def exchange(face, near, far):
        face = swap_x(face)
        near, far = swap_y(near, far)
        (corner,) = call(
            functools.partial(corner_pack_kernel, sz), "corner_pack", 0,
            [like((2, 2) + sz.edge, bf16)], [], [near, far],
        )
        return [face, near, far], swap_x(corner)

    prod, ghost_x, ghost_y = call(
        functools.partial(first_main, sz, n_mat), "first_main", flops,
        [products, like((2, sz.ey) + tile, f32), like((2, sz.ex) + tile, f32)], main_scratch,
        [vectors, from_x, from_y, own_inv, own_pot, *mats],
    )
    acc, face, near, far, last_x, last_field = call(
        functools.partial(first_corner, sz, n_mat), "first_corner", small_flops,
        [state_grid, *messages, like(sz.edge, f32), like((2,) + tile, f32)], corner_scratch,
        [
            parity, vectors, from_x, from_y, ghost_corner, own_inv, own_pot, ghost_x, ghost_y, prod, *mats,
        ],
        scalar_first=True,
    )
    (turned,) = call(
        functools.partial(turn_kernel, sz, ny // 2), "turn_residents", flops // 2,
        [like((2, res_count // 2, sz.edges * ez), bf16)], [],
        [resident.reshape(-1, res_count), from_x, from_y, ghost_corner],
    )
    got, corner = exchange(face, near, far)
    state = [vectors, from_x, from_y, own_inv, own_pot, ghost_x, ghost_y]
    ends = [last_x, last_field]
    prod, y1 = call(
        functools.partial(second_main, sz, n_mat), "second_main", flops,
        [products, state_grid], main_scratch,
        [parity, *state, acc, *got, *mats], scalar_first=True,
    )
    acc, face, near, far, y1_corner = call(
        functools.partial(second_corner, sz, n_mat), "second_corner", small_flops,
        [state_grid, *messages, like((4,) + sz.edge, f32)], corner_scratch,
        [parity, *state, *ends, acc, *got, corner, prod, *mats], scalar_first=True,
    )
    got, corner = exchange(face, near, far)
    prod, y2 = call(
        functools.partial(third_main, sz, n_mat), "third_main", flops,
        [products, state_grid], main_scratch,
        [parity, *state, acc, *got, y1, *mats], scalar_first=True,
    )
    filtered, edge_x, edge_y, face, side, give, keep = call(
        functools.partial(third_corner, sz, n_mat, norm_scale), "third_corner",
        small_flops + 2 * res_count * sz.edges * ez * full,
        [
            like(own, f32), like((blocks, sz.ey) + tile, f32), like((blocks, sz.ex - 1) + tile, f32),
            like((blocks, sz.gy) + tile, bf16), like((blocks, sz.ex) + tile, f32),
            like((res_count // 2, full), bf16), like((res_count // 2, full), f32),
        ],
        [pltpu.VMEM(own, f32), pltpu.SemaphoreType.DMA((sz.ex,)), pltpu.VMEM(grid, f32), pltpu.VMEM((sz.edges, ez, full), bf16)] + corner_scratch,
        [parity, *state, *ends, acc, *got, corner, prod, y1, y1_corner, y2, turned, *mats],
        scalar_first=True, out_hbm=1,
    )

    (pieces,) = call(
        pieces_kernel, "pieces", 0, [like((nx, ny // 2, res_count // ny, full), bf16)], [],
        [keep, send_near(give)],
    )
    pieces = pieces.reshape(nx * ny // 2, -1, full)
    groups = [[a * ny + b for a in range(nx) for b in range(c, ny, 2)] for c in range(2)]
    pieces = lax.all_to_all(pieces, ("dx", "dy"), 0, 0, axis_index_groups=groups)
    margin = jnp.sum(pieces.astype(f32), axis=0)

    face = send(face, 1, 0)
    (side,) = call(
        functools.partial(last_side_kernel, sz), "last_side", 0,
        [like((blocks, sz.ex) + tile, bf16)], [], [side, face],
    )
    side = send(side, 0, 1)
    (filtered,) = call(
        functools.partial(last_kernel, sz), "last", 0, [like(own, f32)],
        [
            pltpu.VMEM((blocks, sz.ey) + tile, f32), pltpu.VMEM((blocks, sz.ex - 1) + tile, f32),
            pltpu.SemaphoreType.DMA((2,)),
        ],
        [filtered, edge_x, edge_y, face, side], hbm=1, out_hbm=1, aliases={0: 0},
    )
    return (filtered, margin)


def solution(mesh):
    return jax.shard_map(
        body,
        mesh=mesh,
        in_specs=(
            P(None, "dx", "dy", None, None),
            P("dx", "dy", None, None),
            P("dx", "dy", None),
            P("dx", "dy", None),
            P(),
            P("dx", "dy", None, None),
        ),
        out_specs=(P(None, "dx", "dy", None, None), P("dy", None)),
        check_vma=False,
    )
```

```python
import functools
import math

import jax
import jax.numpy as jnp
from jax import lax
from jax.experimental import pallas as pl
from jax.experimental.pallas import tpu as pltpu
from jax.sharding import PartitionSpec as P

LANES = 128
TILE = 256
SUB = 16
VMEM_LIMIT = 16 * 1024 * 1024

center_shift = 1.2
half_width = 2.0
gain = 2.0 / half_width

f32, bf16 = jnp.float32, jnp.bfloat16


def round_up(value, step):
    return -(-value // step) * step


class Sizes:
    def __init__(self, vectors, resident, inv_mass, connectivity):
        self.blocks = vectors.shape[0]
        self.width = vectors.shape[-1]
        self.full = self.blocks * self.width
        self.res = resident.shape[-1]
        self.wide = self.res + self.full + self.width
        self.ex, self.ey, self.ez = inv_mass.shape
        self.cells, self.nodes = connectivity.shape[2:]
        self.n1 = round(self.nodes ** (1.0 / 3.0))
        self.p = self.n1 - 1
        self.cx, self.cy, self.cz = self.ex // self.p, self.ey // self.p, self.ez // self.p
        self.gx, self.gy, self.gz = self.ex + 1, self.ey + 1, self.ez
        self.edge = (self.blocks, self.ez, self.width)
        self.origins = [
            (a * self.p, b * self.p, c * self.p)
            for a in range(self.cx)
            for b in range(self.cy)
            for c in range(self.cz)
        ]
        self.most = max(len(self.cell_corners(cell)) for cell in range(self.cells))
        self.base = round_up(self.most * self.n1, 8)
        plain = self.n1 * self.n1 - min(len(self.cell_corners(cell)) for cell in range(self.cells))
        self.tail = self.base + plain * self.p
        self.rows = round_up(self.tail + plain, SUB)
        self.depth = round_up(self.rows, LANES)
        self.own_edges = self.ex * self.ey
        self.edges = round_up(self.own_edges + self.ey + self.gx, LANES // self.ez)

    def corner(self, i, j):
        if i in (0, self.ex) and j in (0, self.ey):
            return 2 * (i // self.ex) + j // self.ey
        return None

    def cell_corners(self, cell):
        x0, y0, _ = self.origins[cell]
        return [
            (i, j)
            for i in range(self.n1)
            for j in range(self.n1)
            if self.corner(x0 + i, y0 + j) is not None
        ]

    def runs(self, cell):
        corners = self.cell_corners(cell)
        place = 0
        for i in range(self.n1):
            js = [j for j in range(self.n1) if (i, j) not in corners]
            while js:
                count = 1
                while count < len(js) and js[count] == js[0] + count:
                    count += 1
                yield place, i, js[0], count
                place += count
                js = js[count:]


def send(value, steps_x, steps_y):
    nx, ny = lax.axis_size("dx"), lax.axis_size("dy")
    pairs = [
        (a * ny + b, ((a + steps_x) % nx) * ny + (b + steps_y) % ny)
        for a in range(nx)
        for b in range(ny)
    ]
    return lax.ppermute(value, ("dx", "dy"), pairs)


def swap_x(value):
    if lax.axis_size("dx") == 2:
        return send(value, 1, 0)
    return jnp.stack([send(value[0], -1, 0), send(value[1], 1, 0)])


def send_near(value):
    pairs = [(b, b + 1 if b % 2 == 0 else b - 1) for b in range(lax.axis_size("dy"))]
    return lax.ppermute(value, "dy", pairs)


def swap_y(near, far):
    ny = lax.axis_size("dy")
    far_pairs = [(b, (b - 1 if b % 2 == 0 else b + 1) % ny) for b in range(ny)]
    far = lax.ppermute(far, "dy", far_pairs)
    return send_near(near), far


def order_kernel(sz, first, matrix_ref, conn_ref, out_ref, *load):
    copy = None
    if load:
        copy = pltpu.make_async_copy(matrix_ref, *load)
        copy.start()
        matrix_ref = load[0]
    for slot in range(out_ref.shape[0]):
        cell = first + slot
        x0, y0, z0 = sz.origins[cell]
        conn = conn_ref[cell : cell + 1, :].astype(f32)
        li = jnp.floor((conn + 0.5) * (1.0 / (sz.gy * sz.gz)))
        rest = conn - li * (sz.gy * sz.gz)
        lj = jnp.floor((rest + 0.5) * (1.0 / sz.gz))
        lk = rest - lj * sz.gz - z0
        lk = jnp.where(lk < 0, lk + sz.gz, lk)
        column = (li - x0) * sz.n1 + (lj - y0)
        corners = [i * sz.n1 + j for i, j in sz.cell_corners(cell)]
        place = column
        for at in corners:
            place = place - jnp.where(column > at, 1.0, 0.0)
        index = jnp.where(lk < sz.p, sz.base + place * sz.p + lk, sz.tail + place)
        for rank, at in enumerate(corners):
            special = jnp.where(lk < sz.p, rank * sz.p + lk, len(corners) * sz.p + rank)
            index = jnp.where(column == at, special, index)
        index = index.astype(jnp.int32)
        row = lax.broadcasted_iota(jnp.int32, (sz.depth, sz.nodes), 0)
        pick = (row == index).astype(f32).astype(bf16)
        if copy is not None and slot == 0:
            copy.wait()
        half = jnp.dot(pick[: sz.rows], matrix_ref[...], preferred_element_type=f32)
        half = half.astype(bf16)
        cuts = list(range(0, sz.depth, TILE)) + [sz.depth]
        for r0, r1 in zip(cuts[:-1], cuts[1:]):
            r1 = min(r1, sz.rows)
            block = lax.dot_general(
                half[r0:r1], pick[r0:], (((1,), (1,)), ((), ())), preferred_element_type=f32
            ).astype(bf16)
            out_ref[slot, r0:r1, r0:] = block
            for c0, c1 in zip(cuts[:-1], cuts[1:]):
                if c0 > r0:
                    mirror = block[:, c0 - r0 : c1 - r0].T
                    c1 = min(c1, sz.rows)
                    out_ref[slot, c0:c1, r0:r1] = mirror[: c1 - c0]


def field_row(inv, pot):
    lane = lax.broadcasted_iota(jnp.int32, inv.shape, inv.ndim - 1)
    row = jnp.zeros_like(inv)
    for at, rest in enumerate((inv, pot)):
        for k in range(3):
            part = rest.astype(bf16).astype(f32)
            rest = rest - part
            row = jnp.where(lane == 3 * at + k, part, row)
    return row.astype(bf16)


def field_rows(sz, inv, pot, count):
    inv, pot = inv.T, pot.T
    shape = (sz.ez, sz.width)
    for at in range(count):
        yield at, field_row(
            jnp.broadcast_to(inv[:, at : at + 1], shape), jnp.broadcast_to(pot[:, at : at + 1], shape)
        )


def fields_of(row):
    row = row.astype(f32)
    return [
        jnp.broadcast_to(sum(row[:, 3 * at + k : 3 * at + k + 1] for k in range(3)), row.shape)
        for at in range(2)
    ]


def pack_kernel(
    sz, vec_hbm, res_hbm, inv_hbm, pot_hbm, conn_hbm, to_x, to_y, conn_ref, at_x, at_y, sems
):
    pairs = [
        (inv_hbm.at[0], at_x.at[0]), (pot_hbm.at[0], at_x.at[1]),
        (inv_hbm.at[:, 0], at_y.at[0]), (pot_hbm.at[:, 0], at_y.at[1]),
        (res_hbm.at[0], to_x.at[:, :, pl.ds(0, sz.res)]),
        (res_hbm.at[:, 0], to_y.at[:, :, pl.ds(0, sz.res)]),
    ]
    for b in range(sz.blocks):
        lanes = pl.ds(sz.res + b * sz.width, sz.width)
        pairs.append((vec_hbm.at[b, 0], to_x.at[:, :, lanes]))
        pairs.append((vec_hbm.at[b, :, 0], to_y.at[:, :, lanes]))
    pairs.append((conn_hbm, conn_ref))
    copies = [pltpu.make_async_copy(a, b, sems.at[k]) for k, (a, b) in enumerate(pairs)]
    for copy in copies:
        copy.start()
    for copy in copies[:4]:
        copy.wait()
    for j, row in field_rows(sz, at_x[0], at_x[1], sz.ey):
        to_x[j, :, sz.res + sz.full :] = row
    for i, row in field_rows(sz, at_y[0], at_y[1], sz.ex):
        to_y[i, :, sz.res + sz.full :] = row
    for copy in copies[4:]:
        copy.wait()


def turn_kernel(sz, pieces, res_ref, from_x, from_y, corner, out_ref):
    own = sz.own_edges * sz.ez
    share = sz.res // out_ref.shape[0] // pieces

    def put(g, columns, value):
        for at in range(0, LANES, share):
            owner = (g + at) // share
            row = owner // 2 * share
            out_ref[owner % 2, row : row + share, columns] = value[at : at + share]

    for g in range(0, sz.res, LANES):
        lanes = slice(g, g + LANES)
        put(g, slice(0, own), res_ref[:, lanes].T)
        rest = sz.edges - sz.own_edges - sz.ey - sz.gx
        parts = [from_x[:, :, lanes], from_y[:, :, lanes], corner[:, :, lanes]]
        if rest:
            parts.append(jnp.zeros((rest, sz.ez, LANES), bf16))
        ghosts = jnp.concatenate(parts, axis=0)
        put(g, slice(own, sz.edges * sz.ez), ghosts.reshape(-1, LANES).T)


def vectors_of(sz, edge):
    lanes = [slice(sz.res + b * sz.width, sz.res + (b + 1) * sz.width) for b in range(sz.blocks)]
    return jnp.stack([edge[:, at] for at in lanes]).astype(f32)


class Nodes:
    def __init__(self, sz, vec, from_x, from_y, own_inv, own_pot, ghost_x, ghost_y, corners=None):
        self.sz, self.vec, self.from_x, self.from_y = sz, vec, from_x, from_y
        self.own, self.ghost_x, self.ghost_y, self.corners = (own_inv, own_pot), ghost_x, ghost_y, corners

    def x(self, i, j):
        sz = self.sz
        if i < sz.ex and j < sz.ey:
            return self.vec[:, i, j].astype(f32)
        return vectors_of(sz, self.from_x[j] if i == sz.ex else self.from_y[i])

    def field(self, at, i, j):
        sz = self.sz
        if i < sz.ex and j < sz.ey:
            return self.own[at][i, j]
        if i < sz.ex:
            return self.ghost_y[at, i]
        if j < sz.ey:
            return self.ghost_x[at, j]
        return self.corners[at]

    def inv(self, i, j):
        return self.field(0, i, j)

    def pot(self, i, j):
        return self.field(1, i, j)


class Sums:
    def __init__(self, sz, even, acc, face, near, far, corner=None):
        self.sz, self.even, self.acc, self.face = sz, even, acc, face
        self.near, self.far, self.corner = near, far, corner

    def at(self, i, j):
        sz = self.sz
        total = self.acc[:, i, j]
        side = 1 if i == 0 else 0 if i == sz.ex else None
        if side is not None:
            total = total + self.face[side, :, j].astype(f32)
        if j in (0, sz.ey):
            is_near = self.even if j == sz.ey else jnp.logical_not(self.even)
            total = total + jnp.where(is_near, self.near[:, i].astype(f32), self.far[:, i].astype(f32))
            if side is not None:
                total = total + jnp.where(
                    is_near, self.corner[side, 0].astype(f32), self.corner[side, 1].astype(f32)
                )
        return total


def corner_edges(sz):
    return [(i, j) for i in (0, sz.ex) for j in (0, sz.ey)]


def main_products(sz, prepare, u_ref, mat_refs, rhs_ref, out_ref):
    width = sz.width
    flat = sz.gx * sz.gy * sz.gz
    u_flat = u_ref.reshape(sz.blocks * flat, width)
    matrices = [ref.at[c] for ref in mat_refs for c in range(ref.shape[0])]
    last = sz.nodes // 8 * 8
    ready = set()
    for cell, (x0, y0, z0) in enumerate(sz.origins):
        slot = cell % 2
        if cell < 2:
            rhs_ref[slot, : sz.base] = jnp.zeros((sz.base, sz.full), f32)
            rhs_ref[slot, last:] = jnp.zeros((sz.depth - last, sz.full), f32)
        for place, i, j, count in sz.runs(cell):
            for at in range(j, j + count):
                if (x0 + i, y0 + at) not in ready:
                    prepare(x0 + i, y0 + at)
                    ready.add((x0 + i, y0 + at))
        z1 = z0 + sz.p
        wrap = z1 % sz.gz
        for b in range(sz.blocks):
            lanes = slice(b * width, (b + 1) * width)
            for place, i, j, count in sz.runs(cell):
                row = sz.base + place * sz.p
                rhs_ref[slot, row : row + count * sz.p, lanes] = u_ref[
                    b, x0 + i, y0 + j : y0 + j + count, z0:z1
                ].reshape(count * sz.p, width)
        for b in range(sz.blocks):
            lanes = slice(b * width, (b + 1) * width)
            for place, i, j, count in sz.runs(cell):
                start = b * flat + ((x0 + i) * sz.gy + y0 + j) * sz.gz + wrap
                rhs_ref[slot, sz.tail + place : sz.tail + place + count, lanes] = u_flat[
                    pl.ds(start, count, stride=sz.gz)
                ]
        out_ref[cell] = jnp.dot(
            matrices[cell][...], rhs_ref[slot].astype(bf16), preferred_element_type=f32
        )


def corner_products(sz, u_corner, prod_ref, mat_refs, small_ref, tail_ref, acc_ref):
    width = sz.width
    flat = sz.gx * sz.gy * sz.gz
    acc_flat = acc_ref.reshape(sz.blocks * flat, width)
    matrices = [ref.at[c] for ref in mat_refs for c in range(ref.shape[0])]
    small_ref[...] = jnp.zeros_like(small_ref)
    touched = set()
    for cell, (x0, y0, z0) in enumerate(sz.origins):
        z1 = z0 + sz.p
        wrap = z1 % sz.gz
        corners = sz.cell_corners(cell)
        for rank, (i, j) in enumerate(corners):
            value = u_corner[sz.corner(x0 + i, y0 + j)]
            last = len(corners) * sz.p + rank
            for b in range(sz.blocks):
                lanes = slice(b * width, (b + 1) * width)
                small_ref[rank * sz.p : (rank + 1) * sz.p, lanes] = value[b, z0:z1]
                small_ref[last : last + 1, lanes] = value[b, wrap : wrap + 1]
        total = prod_ref[cell] + jnp.dot(
            matrices[cell][:, : small_ref.shape[0]], small_ref[...].astype(bf16),
            preferred_element_type=f32,
        )
        tail_ref[cell, : sz.base] = total[: sz.base]
        tail_ref[cell, sz.base :] = total[sz.tail :]
        spans = [(rank * sz.p, i, j, 1) for rank, (i, j) in enumerate(corners)]
        spans += [(sz.base + place * sz.p, i, j, count) for place, i, j, count in sz.runs(cell)]
        for row, i, j, count in spans:
            for at in range(count):
                part = total[row + at * sz.p : row + (at + 1) * sz.p]
                key = (x0 + i, y0 + j + at, z0)
                for b in range(sz.blocks):
                    value = part[:, b * width : (b + 1) * width]
                    if key in touched:
                        value = acc_ref[b, key[0], key[1], z0:z1] + value
                    acc_ref[b, key[0], key[1], z0:z1] = value
                touched.add(key)
    for cell, (x0, y0, z0) in enumerate(sz.origins):
        wrap = (z0 + sz.p) % sz.gz
        corners = sz.cell_corners(cell)
        spans = [(len(corners) * sz.p + rank, i, j, 1) for rank, (i, j) in enumerate(corners)]
        spans += [(sz.base + place, i, j, count) for place, i, j, count in sz.runs(cell)]
        for row, i, j, count in spans:
            for b in range(sz.blocks):
                start = b * flat + ((x0 + i) * sz.gy + y0 + j) * sz.gz + wrap
                rows = pl.ds(start, count, stride=sz.gz) if count > 1 else pl.ds(start, 1)
                lanes = slice(b * width, (b + 1) * width)
                acc_flat[rows] = acc_flat[rows] + tail_ref[cell, row : row + count, lanes]


def write_messages(sz, even, acc_ref, face, near, far):
    at_near = jnp.where(even, sz.ey, 0)
    for b in range(sz.blocks):
        face[0, b] = acc_ref[b, 0].astype(bf16)
        face[1, b] = acc_ref[b, sz.ex].astype(bf16)
        near[b] = acc_ref[b, :, at_near].astype(bf16)
        far[b] = acc_ref[b, :, sz.ey - at_near].astype(bf16)


def corner_pack_kernel(sz, near, far, out_ref):
    for side, i in enumerate((0, sz.ex)):
        for slot, ref in enumerate((near, far)):
            out_ref[side, slot] = ref[:, i]


def first_main(sz, n_mat, vec, from_x, from_y, own_inv, own_pot, *refs):
    mats = refs[:n_mat]
    prod_ref, ghost_x, ghost_y, u_ref, rhs_ref = refs[n_mat:]
    for j in range(sz.ey):
        ghost_x[0, j], ghost_x[1, j] = fields_of(from_x[j, :, sz.res + sz.full :])
    for i in range(sz.ex):
        ghost_y[0, i], ghost_y[1, i] = fields_of(from_y[i, :, sz.res + sz.full :])
    nodes = Nodes(sz, vec, from_x, from_y, own_inv, own_pot, ghost_x, ghost_y)

    def prepare(i, j):
        u_ref[:, i, j] = nodes.x(i, j) * nodes.inv(i, j)

    main_products(sz, prepare, u_ref, mats, rhs_ref, prod_ref)


def first_corner(sz, n_mat, even_ref, vec, from_x, from_y, corner, own_inv, own_pot, ghost_x, ghost_y,
                 prod_ref, *refs):
    mats = refs[:n_mat]
    acc_ref, face, near, far, last_x, last_field, small_ref, tail_ref = refs[n_mat:]
    last_field[0], last_field[1] = fields_of(corner[0, :, sz.res + sz.full :])
    last_x[...] = vectors_of(sz, corner[0])
    nodes = Nodes(sz, vec, from_x, from_y, own_inv, own_pot, ghost_x, ghost_y, last_field)
    u_corner = []
    for i, j in corner_edges(sz):
        x = last_x[...] if (i, j) == (sz.ex, sz.ey) else nodes.x(i, j)
        u_corner.append(x * nodes.inv(i, j))
    corner_products(sz, u_corner, prod_ref, mats, small_ref, tail_ref, acc_ref)
    write_messages(sz, even_ref[0] == 0, acc_ref, face, near, far)


def second_main(sz, n_mat, even_ref, vec, from_x, from_y, own_inv, own_pot, ghost_x, ghost_y,
                acc_in, face_in, near_in, far_in, *refs):
    mats = refs[:n_mat]
    prod_ref, y_ref, u_ref, rhs_ref = refs[n_mat:]
    nodes = Nodes(sz, vec, from_x, from_y, own_inv, own_pot, ghost_x, ghost_y)
    sums = Sums(sz, even_ref[0] == 0, acc_in, face_in, near_in, far_in)

    def prepare(i, j):
        old, inv = nodes.x(i, j), nodes.inv(i, j)
        image = inv * sums.at(i, j) + nodes.pot(i, j) * old
        new = (image - center_shift * old) / half_width
        y_ref[:, i, j] = new
        u_ref[:, i, j] = inv * new

    main_products(sz, prepare, u_ref, mats, rhs_ref, prod_ref)


def second_corner(sz, n_mat, even_ref, vec, from_x, from_y, own_inv, own_pot, ghost_x, ghost_y, last_x,
                  last_field, acc_in, face_in, near_in, far_in, corner_in, prod_ref, *refs):
    mats = refs[:n_mat]
    acc_ref, face, near, far, y_corner, small_ref, tail_ref = refs[n_mat:]
    even = even_ref[0] == 0
    nodes = Nodes(sz, vec, from_x, from_y, own_inv, own_pot, ghost_x, ghost_y, last_field)
    sums = Sums(sz, even, acc_in, face_in, near_in, far_in, corner_in)
    u_corner = []
    for at, (i, j) in enumerate(corner_edges(sz)):
        old = last_x[...] if (i, j) == (sz.ex, sz.ey) else nodes.x(i, j)
        inv = nodes.inv(i, j)
        image = inv * sums.at(i, j) + nodes.pot(i, j) * old
        new = (image - center_shift * old) / half_width
        y_corner[at] = new
        u_corner.append(inv * new)
    corner_products(sz, u_corner, prod_ref, mats, small_ref, tail_ref, acc_ref)
    write_messages(sz, even, acc_ref, face, near, far)


def third_main(sz, n_mat, even_ref, vec, from_x, from_y, own_inv, own_pot, ghost_x, ghost_y,
               acc_in, face_in, near_in, far_in, y_ref, *refs):
    mats = refs[:n_mat]
    prod_ref, new_ref, u_ref, rhs_ref = refs[n_mat:]
    nodes = Nodes(sz, vec, from_x, from_y, own_inv, own_pot, ghost_x, ghost_y)
    sums = Sums(sz, even_ref[0] == 0, acc_in, face_in, near_in, far_in)

    def prepare(i, j):
        old, inv = y_ref[:, i, j], nodes.inv(i, j)
        image = inv * sums.at(i, j) + nodes.pot(i, j) * old
        new = 2.0 * (image - center_shift * old) / half_width - nodes.x(i, j)
        new_ref[:, i, j] = new
        u_ref[:, i, j] = inv * new

    main_products(sz, prepare, u_ref, mats, rhs_ref, prod_ref)


def third_corner(sz, n_mat, norm_scale, even_ref, vec, from_x, from_y, own_inv, own_pot, ghost_x, ghost_y,
                 last_x, last_field, acc_in, face_in, near_in, far_in, corner_in, prod_ref, y_ref,
                 y_corner, new_ref, turned, *refs):
    mats = refs[:n_mat]
    out_hbm, edge_x, edge_y, face, side, corner, give, keep = refs[n_mat : n_mat + 8]
    part_ref, sem, acc_ref, rows_ref, small_ref, tail_ref = refs[n_mat + 8 :]
    nodes = Nodes(sz, vec, from_x, from_y, own_inv, own_pot, ghost_x, ghost_y, last_field)
    sums = Sums(sz, even_ref[0] == 0, acc_in, face_in, near_in, far_in, corner_in)
    u_corner, new_corner = [], []
    for at, (i, j) in enumerate(corner_edges(sz)):
        x = last_x[...] if (i, j) == (sz.ex, sz.ey) else nodes.x(i, j)
        old, inv = y_corner[at], nodes.inv(i, j)
        image = inv * sums.at(i, j) + nodes.pot(i, j) * old
        new_corner.append(2.0 * (image - center_shift * old) / half_width - x)
        u_corner.append(inv * new_corner[-1])
    corner_products(sz, u_corner, prod_ref, mats, small_ref, tail_ref, acc_ref)

    def put_row(at, value):
        for b in range(sz.blocks):
            rows_ref[at, :, b * sz.width : (b + 1) * sz.width] = value[b]

    copies = []
    for i in range(sz.gx):
        for j in range(sz.gy):
            acc, inv = acc_ref[:, i, j], nodes.inv(i, j)
            if i == sz.ex or j == sz.ey:
                value = gain * (inv * acc)
                rounded = value.astype(bf16)
                if j < sz.ey:
                    face[:, j] = rounded
                elif i < sz.ex:
                    side[:, i] = value
                else:
                    corner[...] = rounded
                put_row(sz.own_edges + (j if j < sz.ey else sz.ey + i), rounded)
                continue
            at = sz.corner(i, j)
            old = y_ref[:, i, j] if at is None else y_corner[at]
            new = new_ref[:, i, j] if at is None else new_corner[at]
            image = inv * acc + nodes.pot(i, j) * new
            value = 2.0 * (image - center_shift * new) / half_width - old
            part_ref[:, i, j] = value
            if i == 0:
                edge_x[:, j] = value
            elif j == 0:
                edge_y[:, i - 1] = value
            put_row(i * sz.ey + j, value.astype(bf16))
        if i < sz.ex:
            copies.append(pltpu.make_async_copy(part_ref.at[:, i], out_hbm.at[:, i], sem.at[i]))
            copies[-1].start()
    for at in range(sz.own_edges + sz.ey + sz.gx, sz.edges):
        rows_ref[at] = jnp.zeros((sz.ez, sz.full), bf16)
    rows = rows_ref[...].reshape(sz.edges * sz.ez, sz.full)
    mine = even_ref[0]
    for half, out in ((1 - mine, give), (mine, keep)):
        local = jnp.dot(turned[half], rows, preferred_element_type=f32)
        out[...] = (local * norm_scale).astype(out.dtype)
    for copy in copies:
        copy.wait()


def pieces_kernel(keep, taken, pieces):
    rows = pieces.shape[2]
    for at in range(pieces.shape[1]):
        span = slice(at * rows, (at + 1) * rows)
        value = (keep[span] + taken[span].astype(f32)).astype(pieces.dtype)
        for copy in range(pieces.shape[0]):
            pieces[copy, at] = value


def last_side_kernel(sz, side_ref, corner_ref, face_in, out_ref, face_out):
    del face_in, face_out
    for i in range(sz.ex):
        value = side_ref[:, i]
        if i == 0:
            value = value + corner_ref[...].astype(f32)
        out_ref[:, i] = value.astype(out_ref.dtype)


def last_kernel(sz, old_hbm, edge_x, edge_y, face, side, out_hbm, at_x, at_y, sems):
    del old_hbm
    for j in range(sz.ey):
        value = edge_x[:, j] + face[:, j].astype(f32)
        if j == 0:
            value = value + side[:, 0].astype(f32)
        at_x[:, j] = value
    for i in range(1, sz.ex):
        at_y[:, i - 1] = edge_y[:, i - 1] + side[:, i].astype(f32)
    copies = [
        pltpu.make_async_copy(at_x, out_hbm.at[:, 0], sems.at[0]),
        pltpu.make_async_copy(at_y, out_hbm.at[:, pl.ds(1, sz.ex - 1), 0], sems.at[1]),
    ]
    for copy in copies:
        copy.start()
    for copy in copies:
        copy.wait()


def like(shape, dtype):
    return jax.ShapeDtypeStruct(shape, dtype)


def call(kernel, name, flops, out_shape, scratch, operands, hbm=0, scalar_first=False, aliases=None,
         out_hbm=0):
    out_shape = [like(s.shape, s.dtype) for s in out_shape]
    size = sum(math.prod(s.shape) * jnp.dtype(s.dtype).itemsize for s in (*operands, *out_shape))
    whole = pl.BlockSpec(memory_space=pltpu.VMEM)
    specs = [pl.BlockSpec(memory_space=pltpu.HBM)] * hbm + [whole] * (len(operands) - hbm)
    if scalar_first:
        specs[0] = pl.BlockSpec(memory_space=pltpu.SMEM)
    out_specs = [pl.BlockSpec(memory_space=pltpu.HBM)] * out_hbm + [whole] * (len(out_shape) - out_hbm)
    out_shape = [pltpu.HBM(s.shape, s.dtype) for s in out_shape[:out_hbm]] + out_shape[out_hbm:]
    operands = [pltpu.with_memory_space_constraint(a, pltpu.HBM) for a in operands[:hbm]] + list(
        operands[hbm:]
    )
    return pl.pallas_call(
        kernel,
        in_specs=specs,
        out_specs=out_specs,
        out_shape=out_shape,
        scratch_shapes=scratch,
        input_output_aliases=aliases or {},
        compiler_params=pltpu.CompilerParams(vmem_limit_bytes=VMEM_LIMIT),
        cost_estimate=pl.CostEstimate(flops=flops, bytes_accessed=size, transcendentals=0),
        name=name,
    )(*operands)


def body(vectors, resident, inv_mass, potential, cell_matrix, connectivity):
    sz = Sizes(vectors, resident, inv_mass, connectivity)
    nx, ny = lax.axis_size("dx"), lax.axis_size("dy")
    norm_scale = 1.0 / math.sqrt(sz.ex * sz.ey * sz.ez * nx * ny)
    blocks, ez, width, full = sz.blocks, sz.ez, sz.width, sz.full
    res_count = resident.shape[-1]
    tile = (ez, width)

    conn = connectivity.reshape(sz.cells, sz.nodes)
    to_x, to_y, conn = call(
        functools.partial(pack_kernel, sz), "pack", 0,
        [like((sz.ey, ez, sz.wide), bf16), like((sz.ex, ez, sz.wide), bf16), conn],
        [
            pltpu.VMEM((2, sz.ey, ez), f32), pltpu.VMEM((2, sz.ex, ez), f32),
            pltpu.SemaphoreType.DMA((7 + 2 * blocks,)),
        ],
        [vectors, resident, inv_mass, potential, conn], hbm=5,
    )
    from_x = send(to_x, -1, 0)
    from_y = send(to_y, 0, -1)

    halves = 2 if sz.cells % 2 == 0 else 1
    step = sz.cells // halves
    mats = []
    for at in range(0, sz.cells, step):
        mats += call(
            functools.partial(order_kernel, sz, at), "order_cells", 4 * step * sz.depth**3,
            [like((step, sz.rows, sz.depth), bf16)],
            [pltpu.VMEM(cell_matrix.shape, bf16), pltpu.SemaphoreType.DMA] if at == 0 else [],
            [cell_matrix, conn], hbm=1 if at == 0 else 0,
        )
    own_inv = jnp.broadcast_to(inv_mass[..., None], inv_mass.shape + (width,))
    own_pot = jnp.broadcast_to(potential[..., None], inv_mass.shape + (width,))
    parity = jnp.reshape(lax.axis_index("dy") % 2, (1,)).astype(jnp.int32)
    ghost_corner = send(from_y[:1], -1, 0)

    grid = (blocks, sz.gx, sz.gy) + tile
    own = (blocks, sz.ex, sz.ey) + tile
    products = like((sz.cells, sz.rows, full), f32)
    state_grid = like(grid, f32)
    messages = [
        like((2, blocks, sz.gy) + tile, bf16),
        like((blocks, sz.gx) + tile, bf16),
        like((blocks, sz.gx) + tile, bf16),
    ]
    main_scratch = [pltpu.VMEM(grid, f32), pltpu.VMEM((2, sz.depth, full), f32)]
    corner_scratch = [
        pltpu.VMEM((LANES, full), f32),
        pltpu.VMEM((sz.cells, sz.base + sz.rows - sz.tail, full), f32),
    ]
    n_mat = len(mats)
    flops = 2 * sz.cells * sz.rows * sz.depth * full
    small_flops = 2 * sz.cells * sz.rows * LANES * full

    def exchange(face, near, far):
        face = swap_x(face)
        near, far = swap_y(near, far)
        (corner,) = call(
            functools.partial(corner_pack_kernel, sz), "corner_pack", 0,
            [like((2, 2) + sz.edge, bf16)], [], [near, far],
        )
        return [face, near, far], swap_x(corner)

    prod, ghost_x, ghost_y = call(
        functools.partial(first_main, sz, n_mat), "first_main", flops,
        [products, like((2, sz.ey) + tile, f32), like((2, sz.ex) + tile, f32)], main_scratch,
        [vectors, from_x, from_y, own_inv, own_pot, *mats],
    )
    acc, face, near, far, last_x, last_field = call(
        functools.partial(first_corner, sz, n_mat), "first_corner", small_flops,
        [state_grid, *messages, like(sz.edge, f32), like((2,) + tile, f32)], corner_scratch,
        [
            parity, vectors, from_x, from_y, ghost_corner, own_inv, own_pot, ghost_x, ghost_y, prod, *mats,
        ],
        scalar_first=True,
    )
    (turned,) = call(
        functools.partial(turn_kernel, sz, ny // 2), "turn_residents", flops // 2,
        [like((2, res_count // 2, sz.edges * ez), bf16)], [],
        [resident.reshape(-1, res_count), from_x, from_y, ghost_corner],
    )
    got, corner = exchange(face, near, far)
    state = [vectors, from_x, from_y, own_inv, own_pot, ghost_x, ghost_y]
    ends = [last_x, last_field]
    prod, y1 = call(
        functools.partial(second_main, sz, n_mat), "second_main", flops,
        [products, state_grid], main_scratch,
        [parity, *state, acc, *got, *mats], scalar_first=True,
    )
    acc, face, near, far, y1_corner = call(
        functools.partial(second_corner, sz, n_mat), "second_corner", small_flops,
        [state_grid, *messages, like((4,) + sz.edge, f32)], corner_scratch,
        [parity, *state, *ends, acc, *got, corner, prod, *mats], scalar_first=True,
    )
    got, corner = exchange(face, near, far)
    prod, y2 = call(
        functools.partial(third_main, sz, n_mat), "third_main", flops,
        [products, state_grid], main_scratch,
        [parity, *state, acc, *got, y1, *mats], scalar_first=True,
    )
    filtered, edge_x, edge_y, face, side, corner, give, keep = call(
        functools.partial(third_corner, sz, n_mat, norm_scale), "third_corner",
        small_flops + 2 * res_count * sz.edges * ez * full,
        [
            like(own, f32), like((blocks, sz.ey) + tile, f32), like((blocks, sz.ex - 1) + tile, f32),
            like((blocks, sz.ey) + tile, bf16), like((blocks, sz.ex) + tile, f32), like(sz.edge, bf16),
            like((res_count // 2, full), bf16), like((res_count // 2, full), f32),
        ],
        [pltpu.VMEM(own, f32), pltpu.SemaphoreType.DMA((sz.ex,)), pltpu.VMEM(grid, f32), pltpu.VMEM((sz.edges, ez, full), bf16)] + corner_scratch,
        [parity, *state, *ends, acc, *got, corner, prod, y1, y1_corner, y2, turned, *mats],
        scalar_first=True, out_hbm=1,
    )

    (pieces,) = call(
        pieces_kernel, "pieces", 0, [like((nx, ny // 2, res_count // ny, full), bf16)], [],
        [keep, send_near(give)],
    )
    pieces = pieces.reshape(nx * ny // 2, -1, full)
    groups = [[a * ny + b for a in range(nx) for b in range(c, ny, 2)] for c in range(2)]
    pieces = lax.all_to_all(pieces, ("dx", "dy"), 0, 0, axis_index_groups=groups)
    margin = jnp.sum(pieces.astype(f32), axis=0)

    corner = send(corner, 1, 0)
    side, face = call(
        functools.partial(last_side_kernel, sz), "last_side", 0,
        [like((blocks, sz.ex) + tile, bf16), face], [], [side, corner, face], aliases={2: 1},
    )
    face = send(face, 1, 0)
    side = send(side, 0, 1)
    (filtered,) = call(
        functools.partial(last_kernel, sz), "last", 0, [like(own, f32)],
        [
            pltpu.VMEM((blocks, sz.ey) + tile, f32), pltpu.VMEM((blocks, sz.ex - 1) + tile, f32),
            pltpu.SemaphoreType.DMA((2,)),
        ],
        [filtered, edge_x, edge_y, face, side], hbm=1, out_hbm=1, aliases={0: 0},
    )
    return (filtered, margin)


def solution(mesh):
    return jax.shard_map(
        body,
        mesh=mesh,
        in_specs=(
            P(None, "dx", "dy", None, None),
            P("dx", "dy", None, None),
            P("dx", "dy", None),
            P("dx", "dy", None),
            P(),
            P("dx", "dy", None, None),
        ),
        out_specs=(P(None, "dx", "dy", None, None), P("dy", None)),
        check_vma=False,
    )
```

```python
import functools
import math

import jax
import jax.numpy as jnp
from jax import lax
from jax.experimental import pallas as pl
from jax.experimental.pallas import tpu as pltpu
from jax.sharding import PartitionSpec as P

LANES = 128
TILE = 256
SUB = 16
VMEM_LIMIT = 16 * 1024 * 1024

center_shift = 1.2
half_width = 2.0
gain = 2.0 / half_width

f32, bf16 = jnp.float32, jnp.bfloat16


def round_up(value, step):
    return -(-value // step) * step


class Sizes:
    def __init__(self, vectors, resident, inv_mass, connectivity):
        self.blocks = vectors.shape[0]
        self.width = vectors.shape[-1]
        self.full = self.blocks * self.width
        self.res = resident.shape[-1]
        self.wide = self.full + self.width
        self.ex, self.ey, self.ez = inv_mass.shape
        self.cells, self.nodes = connectivity.shape[2:]
        self.n1 = round(self.nodes ** (1.0 / 3.0))
        self.p = self.n1 - 1
        self.cx, self.cy, self.cz = self.ex // self.p, self.ey // self.p, self.ez // self.p
        self.gx, self.gy, self.gz = self.ex + 1, self.ey + 1, self.ez
        self.edge = (self.blocks, self.ez, self.width)
        self.origins = [
            (a * self.p, b * self.p, c * self.p)
            for a in range(self.cx)
            for b in range(self.cy)
            for c in range(self.cz)
        ]
        self.most = max(len(self.cell_corners(cell)) for cell in range(self.cells))
        self.base = round_up(self.most * self.n1, 8)
        plain = self.n1 * self.n1 - min(len(self.cell_corners(cell)) for cell in range(self.cells))
        self.tail = self.base + plain * self.p
        self.rows = round_up(self.tail + plain, SUB)
        self.depth = round_up(self.rows, LANES)
        self.own_edges = self.ex * self.ey
        self.edges = round_up(self.own_edges + self.ey + self.gx, LANES // self.ez)

    def corner(self, i, j):
        if i in (0, self.ex) and j in (0, self.ey):
            return 2 * (i // self.ex) + j // self.ey
        return None

    def cell_corners(self, cell):
        x0, y0, _ = self.origins[cell]
        return [
            (i, j)
            for i in range(self.n1)
            for j in range(self.n1)
            if self.corner(x0 + i, y0 + j) is not None
        ]

    def runs(self, cell):
        corners = self.cell_corners(cell)
        place = 0
        for i in range(self.n1):
            js = [j for j in range(self.n1) if (i, j) not in corners]
            while js:
                count = 1
                while count < len(js) and js[count] == js[0] + count:
                    count += 1
                yield place, i, js[0], count
                place += count
                js = js[count:]


def send(value, steps_x, steps_y):
    nx, ny = lax.axis_size("dx"), lax.axis_size("dy")
    pairs = [
        (a * ny + b, ((a + steps_x) % nx) * ny + (b + steps_y) % ny)
        for a in range(nx)
        for b in range(ny)
    ]
    return lax.ppermute(value, ("dx", "dy"), pairs)


def swap_x(value):
    if lax.axis_size("dx") == 2:
        return send(value, 1, 0)
    return jnp.stack([send(value[0], -1, 0), send(value[1], 1, 0)])


def send_near(value):
    pairs = [(b, b + 1 if b % 2 == 0 else b - 1) for b in range(lax.axis_size("dy"))]
    return lax.ppermute(value, "dy", pairs)


def swap_y(near, far):
    ny = lax.axis_size("dy")
    far_pairs = [(b, (b - 1 if b % 2 == 0 else b + 1) % ny) for b in range(ny)]
    far = lax.ppermute(far, "dy", far_pairs)
    return send_near(near), far


def order_kernel(sz, first, matrix_ref, conn_ref, out_ref):
    for slot in range(out_ref.shape[0]):
        cell = first + slot
        x0, y0, z0 = sz.origins[cell]
        conn = conn_ref[cell : cell + 1, :].astype(f32)
        li = jnp.floor((conn + 0.5) * (1.0 / (sz.gy * sz.gz)))
        rest = conn - li * (sz.gy * sz.gz)
        lj = jnp.floor((rest + 0.5) * (1.0 / sz.gz))
        lk = rest - lj * sz.gz - z0
        lk = jnp.where(lk < 0, lk + sz.gz, lk)
        column = (li - x0) * sz.n1 + (lj - y0)
        corners = [i * sz.n1 + j for i, j in sz.cell_corners(cell)]
        place = column
        for at in corners:
            place = place - jnp.where(column > at, 1.0, 0.0)
        index = jnp.where(lk < sz.p, sz.base + place * sz.p + lk, sz.tail + place)
        for rank, at in enumerate(corners):
            special = jnp.where(lk < sz.p, rank * sz.p + lk, len(corners) * sz.p + rank)
            index = jnp.where(column == at, special, index)
        index = index.astype(jnp.int32)
        row = lax.broadcasted_iota(jnp.int32, (sz.depth, sz.nodes), 0)
        pick = (row == index).astype(f32).astype(bf16)
        half = jnp.dot(pick[: sz.rows], matrix_ref[...], preferred_element_type=f32)
        half = half.astype(bf16)
        cuts = list(range(0, sz.depth, TILE)) + [sz.depth]
        for r0, r1 in zip(cuts[:-1], cuts[1:]):
            r1 = min(r1, sz.rows)
            block = lax.dot_general(
                half[r0:r1], pick[r0:], (((1,), (1,)), ((), ())), preferred_element_type=f32
            ).astype(bf16)
            out_ref[slot, r0:r1, r0:] = block
            for c0, c1 in zip(cuts[:-1], cuts[1:]):
                if c0 > r0:
                    mirror = block[:, c0 - r0 : c1 - r0].T
                    c1 = min(c1, sz.rows)
                    out_ref[slot, c0:c1, r0:r1] = mirror[: c1 - c0]


def field_row(inv, pot):
    lane = lax.broadcasted_iota(jnp.int32, inv.shape, inv.ndim - 1)
    row = jnp.zeros_like(inv)
    for at, rest in enumerate((inv, pot)):
        for k in range(3):
            part = rest.astype(bf16).astype(f32)
            rest = rest - part
            row = jnp.where(lane == 3 * at + k, part, row)
    return row.astype(bf16)


def field_rows(sz, inv, pot, count):
    inv, pot = inv.T, pot.T
    shape = (sz.ez, sz.width)
    for at in range(count):
        yield at, field_row(
            jnp.broadcast_to(inv[:, at : at + 1], shape), jnp.broadcast_to(pot[:, at : at + 1], shape)
        )


def fields_of(row):
    row = row.astype(f32)
    return [
        jnp.broadcast_to(sum(row[:, 3 * at + k : 3 * at + k + 1] for k in range(3)), row.shape)
        for at in range(2)
    ]


def pack_kernel(
    sz, vec_hbm, res_hbm, inv_hbm, pot_hbm, conn_hbm, to_x, to_y, res_x, conn_ref, at_x, at_y, sems
):
    pairs = [
        (inv_hbm.at[0], at_x.at[0]), (pot_hbm.at[0], at_x.at[1]),
        (inv_hbm.at[:, 0], at_y.at[0]), (pot_hbm.at[:, 0], at_y.at[1]),
        (res_hbm.at[0], res_x),
        (res_hbm.at[:, 0], to_y.at[:, :, pl.ds(sz.wide, sz.res)]),
    ]
    for b in range(sz.blocks):
        lanes = pl.ds(b * sz.width, sz.width)
        pairs.append((vec_hbm.at[b, 0], to_x.at[:, :, lanes]))
        pairs.append((vec_hbm.at[b, :, 0], to_y.at[:, :, lanes]))
    pairs.append((conn_hbm, conn_ref))
    copies = [pltpu.make_async_copy(a, b, sems.at[k]) for k, (a, b) in enumerate(pairs)]
    for copy in copies:
        copy.start()
    for copy in copies[:4]:
        copy.wait()
    for j, row in field_rows(sz, at_x[0], at_x[1], sz.ey):
        to_x[j, :, sz.full : sz.wide] = row
    for i, row in field_rows(sz, at_y[0], at_y[1], sz.ex):
        to_y[i, :, sz.full : sz.wide] = row
    for copy in copies[4:]:
        copy.wait()


def turn_kernel(sz, pieces, res_ref, res_x, from_y, corner, out_ref):
    own = sz.own_edges * sz.ez
    share = sz.res // out_ref.shape[0] // pieces

    def put(g, columns, value):
        for at in range(0, LANES, share):
            owner = (g + at) // share
            row = owner // 2 * share
            out_ref[owner % 2, row : row + share, columns] = value[at : at + share]

    for g in range(0, sz.res, LANES):
        lanes = slice(g, g + LANES)
        put(g, slice(0, own), res_ref[:, lanes].T)
        rest = sz.edges - sz.own_edges - sz.ey - sz.gx
        tail = slice(sz.wide + g, sz.wide + g + LANES)
        parts = [res_x[:, :, lanes], from_y[:, :, tail], corner[:, :, tail]]
        if rest:
            parts.append(jnp.zeros((rest, sz.ez, LANES), bf16))
        ghosts = jnp.concatenate(parts, axis=0)
        put(g, slice(own, sz.edges * sz.ez), ghosts.reshape(-1, LANES).T)


def vectors_of(sz, edge):
    lanes = [slice(b * sz.width, (b + 1) * sz.width) for b in range(sz.blocks)]
    return jnp.stack([edge[:, at] for at in lanes]).astype(f32)


class Nodes:
    def __init__(self, sz, vec, from_x, from_y, own_inv, own_pot, ghost_x, ghost_y, corners=None):
        self.sz, self.vec, self.from_x, self.from_y = sz, vec, from_x, from_y
        self.own, self.ghost_x, self.ghost_y, self.corners = (own_inv, own_pot), ghost_x, ghost_y, corners

    def x(self, i, j):
        sz = self.sz
        if i < sz.ex and j < sz.ey:
            return self.vec[:, i, j].astype(f32)
        return vectors_of(sz, self.from_x[j] if i == sz.ex else self.from_y[i])

    def field(self, at, i, j):
        sz = self.sz
        if i < sz.ex and j < sz.ey:
            return self.own[at][i, j]
        if i < sz.ex:
            return self.ghost_y[at, i]
        if j < sz.ey:
            return self.ghost_x[at, j]
        return self.corners[at]

    def inv(self, i, j):
        return self.field(0, i, j)

    def pot(self, i, j):
        return self.field(1, i, j)


class Sums:
    def __init__(self, sz, even, acc, face, near, far, corner=None):
        self.sz, self.even, self.acc, self.face = sz, even, acc, face
        self.near, self.far, self.corner = near, far, corner

    def at(self, i, j):
        sz = self.sz
        total = self.acc[:, i, j]
        side = 1 if i == 0 else 0 if i == sz.ex else None
        if side is not None:
            total = total + self.face[side, :, j].astype(f32)
        if j in (0, sz.ey):
            is_near = self.even if j == sz.ey else jnp.logical_not(self.even)
            total = total + jnp.where(is_near, self.near[:, i].astype(f32), self.far[:, i].astype(f32))
            if side is not None:
                total = total + jnp.where(
                    is_near, self.corner[side, 0].astype(f32), self.corner[side, 1].astype(f32)
                )
        return total


def corner_edges(sz):
    return [(i, j) for i in (0, sz.ex) for j in (0, sz.ey)]


def main_products(sz, prepare, u_ref, mat_refs, rhs_ref, out_ref):
    width = sz.width
    flat = sz.gx * sz.gy * sz.gz
    u_flat = u_ref.reshape(sz.blocks * flat, width)
    matrices = [ref.at[c] for ref in mat_refs for c in range(ref.shape[0])]
    last = sz.nodes // 8 * 8
    ready = set()
    for cell, (x0, y0, z0) in enumerate(sz.origins):
        slot = cell % 2
        if cell < 2:
            rhs_ref[slot, : sz.base] = jnp.zeros((sz.base, sz.full), f32)
            rhs_ref[slot, last:] = jnp.zeros((sz.depth - last, sz.full), f32)
        for place, i, j, count in sz.runs(cell):
            for at in range(j, j + count):
                if (x0 + i, y0 + at) not in ready:
                    prepare(x0 + i, y0 + at)
                    ready.add((x0 + i, y0 + at))
        z1 = z0 + sz.p
        wrap = z1 % sz.gz
        for b in range(sz.blocks):
            lanes = slice(b * width, (b + 1) * width)
            for place, i, j, count in sz.runs(cell):
                row = sz.base + place * sz.p
                rhs_ref[slot, row : row + count * sz.p, lanes] = u_ref[
                    b, x0 + i, y0 + j : y0 + j + count, z0:z1
                ].reshape(count * sz.p, width)
        for b in range(sz.blocks):
            lanes = slice(b * width, (b + 1) * width)
            for place, i, j, count in sz.runs(cell):
                start = b * flat + ((x0 + i) * sz.gy + y0 + j) * sz.gz + wrap
                rhs_ref[slot, sz.tail + place : sz.tail + place + count, lanes] = u_flat[
                    pl.ds(start, count, stride=sz.gz)
                ]
        out_ref[cell] = jnp.dot(
            matrices[cell][...], rhs_ref[slot].astype(bf16), preferred_element_type=f32
        )


def corner_products(sz, u_corner, prod_ref, mat_refs, small_ref, tail_ref, acc_ref):
    width = sz.width
    flat = sz.gx * sz.gy * sz.gz
    acc_flat = acc_ref.reshape(sz.blocks * flat, width)
    matrices = [ref.at[c] for ref in mat_refs for c in range(ref.shape[0])]
    small_ref[...] = jnp.zeros_like(small_ref)
    touched = set()
    for cell, (x0, y0, z0) in enumerate(sz.origins):
        z1 = z0 + sz.p
        wrap = z1 % sz.gz
        corners = sz.cell_corners(cell)
        for rank, (i, j) in enumerate(corners):
            value = u_corner[sz.corner(x0 + i, y0 + j)]
            last = len(corners) * sz.p + rank
            for b in range(sz.blocks):
                lanes = slice(b * width, (b + 1) * width)
                small_ref[rank * sz.p : (rank + 1) * sz.p, lanes] = value[b, z0:z1]
                small_ref[last : last + 1, lanes] = value[b, wrap : wrap + 1]
        total = prod_ref[cell] + jnp.dot(
            matrices[cell][:, : small_ref.shape[0]], small_ref[...].astype(bf16),
            preferred_element_type=f32,
        )
        tail_ref[cell, : sz.base] = total[: sz.base]
        tail_ref[cell, sz.base :] = total[sz.tail :]
        spans = [(rank * sz.p, i, j, 1) for rank, (i, j) in enumerate(corners)]
        spans += [(sz.base + place * sz.p, i, j, count) for place, i, j, count in sz.runs(cell)]
        for row, i, j, count in spans:
            for at in range(count):
                part = total[row + at * sz.p : row + (at + 1) * sz.p]
                key = (x0 + i, y0 + j + at, z0)
                for b in range(sz.blocks):
                    value = part[:, b * width : (b + 1) * width]
                    if key in touched:
                        value = acc_ref[b, key[0], key[1], z0:z1] + value
                    acc_ref[b, key[0], key[1], z0:z1] = value
                touched.add(key)
    for cell, (x0, y0, z0) in enumerate(sz.origins):
        wrap = (z0 + sz.p) % sz.gz
        corners = sz.cell_corners(cell)
        spans = [(len(corners) * sz.p + rank, i, j, 1) for rank, (i, j) in enumerate(corners)]
        spans += [(sz.base + place, i, j, count) for place, i, j, count in sz.runs(cell)]
        for row, i, j, count in spans:
            for b in range(sz.blocks):
                start = b * flat + ((x0 + i) * sz.gy + y0 + j) * sz.gz + wrap
                rows = pl.ds(start, count, stride=sz.gz) if count > 1 else pl.ds(start, 1)
                lanes = slice(b * width, (b + 1) * width)
                acc_flat[rows] = acc_flat[rows] + tail_ref[cell, row : row + count, lanes]


def write_messages(sz, even, acc_ref, face, near, far):
    at_near = jnp.where(even, sz.ey, 0)
    for b in range(sz.blocks):
        face[0, b] = acc_ref[b, 0].astype(bf16)
        face[1, b] = acc_ref[b, sz.ex].astype(bf16)
        near[b] = acc_ref[b, :, at_near].astype(bf16)
        far[b] = acc_ref[b, :, sz.ey - at_near].astype(bf16)


def corner_pack_kernel(sz, near, far, out_ref):
    for side, i in enumerate((0, sz.ex)):
        for slot, ref in enumerate((near, far)):
            out_ref[side, slot] = ref[:, i]


def first_main(sz, n_mat, vec, from_x, from_y, own_inv, own_pot, *refs):
    mats = refs[:n_mat]
    prod_ref, ghost_x, ghost_y, u_ref, rhs_ref = refs[n_mat:]
    for j in range(sz.ey):
        ghost_x[0, j], ghost_x[1, j] = fields_of(from_x[j, :, sz.full : sz.wide])
    for i in range(sz.ex):
        ghost_y[0, i], ghost_y[1, i] = fields_of(from_y[i, :, sz.full : sz.wide])
    nodes = Nodes(sz, vec, from_x, from_y, own_inv, own_pot, ghost_x, ghost_y)

    def prepare(i, j):
        u_ref[:, i, j] = nodes.x(i, j) * nodes.inv(i, j)

    main_products(sz, prepare, u_ref, mats, rhs_ref, prod_ref)


def first_corner(sz, n_mat, even_ref, res_in, vec, from_x, from_y, corner, own_inv, own_pot, ghost_x,
                 ghost_y, prod_ref, *refs):
    mats = refs[:n_mat]
    res_out, acc_ref, face, near, far, last_x, last_field, small_ref, tail_ref = refs[n_mat:]
    del res_in, res_out
    last_field[0], last_field[1] = fields_of(corner[0, :, sz.full : sz.wide])
    last_x[...] = vectors_of(sz, corner[0])
    nodes = Nodes(sz, vec, from_x, from_y, own_inv, own_pot, ghost_x, ghost_y, last_field)
    u_corner = []
    for i, j in corner_edges(sz):
        x = last_x[...] if (i, j) == (sz.ex, sz.ey) else nodes.x(i, j)
        u_corner.append(x * nodes.inv(i, j))
    corner_products(sz, u_corner, prod_ref, mats, small_ref, tail_ref, acc_ref)
    write_messages(sz, even_ref[0] == 0, acc_ref, face, near, far)


def second_main(sz, n_mat, even_ref, vec, from_x, from_y, own_inv, own_pot, ghost_x, ghost_y,
                acc_in, face_in, near_in, far_in, *refs):
    mats = refs[:n_mat]
    prod_ref, y_ref, u_ref, rhs_ref = refs[n_mat:]
    nodes = Nodes(sz, vec, from_x, from_y, own_inv, own_pot, ghost_x, ghost_y)
    sums = Sums(sz, even_ref[0] == 0, acc_in, face_in, near_in, far_in)

    def prepare(i, j):
        old, inv = nodes.x(i, j), nodes.inv(i, j)
        image = inv * sums.at(i, j) + nodes.pot(i, j) * old
        new = (image - center_shift * old) / half_width
        y_ref[:, i, j] = new
        u_ref[:, i, j] = inv * new

    main_products(sz, prepare, u_ref, mats, rhs_ref, prod_ref)


def second_corner(sz, n_mat, even_ref, vec, from_x, from_y, own_inv, own_pot, ghost_x, ghost_y, last_x,
                  last_field, acc_in, face_in, near_in, far_in, corner_in, prod_ref, *refs):
    mats = refs[:n_mat]
    acc_ref, face, near, far, y_corner, small_ref, tail_ref = refs[n_mat:]
    even = even_ref[0] == 0
    nodes = Nodes(sz, vec, from_x, from_y, own_inv, own_pot, ghost_x, ghost_y, last_field)
    sums = Sums(sz, even, acc_in, face_in, near_in, far_in, corner_in)
    u_corner = []
    for at, (i, j) in enumerate(corner_edges(sz)):
        old = last_x[...] if (i, j) == (sz.ex, sz.ey) else nodes.x(i, j)
        inv = nodes.inv(i, j)
        image = inv * sums.at(i, j) + nodes.pot(i, j) * old
        new = (image - center_shift * old) / half_width
        y_corner[at] = new
        u_corner.append(inv * new)
    corner_products(sz, u_corner, prod_ref, mats, small_ref, tail_ref, acc_ref)
    write_messages(sz, even, acc_ref, face, near, far)


def third_main(sz, n_mat, even_ref, vec, from_x, from_y, own_inv, own_pot, ghost_x, ghost_y,
               acc_in, face_in, near_in, far_in, y_ref, *refs):
    mats = refs[:n_mat]
    prod_ref, new_ref, u_ref, rhs_ref = refs[n_mat:]
    nodes = Nodes(sz, vec, from_x, from_y, own_inv, own_pot, ghost_x, ghost_y)
    sums = Sums(sz, even_ref[0] == 0, acc_in, face_in, near_in, far_in)

    def prepare(i, j):
        old, inv = y_ref[:, i, j], nodes.inv(i, j)
        image = inv * sums.at(i, j) + nodes.pot(i, j) * old
        new = 2.0 * (image - center_shift * old) / half_width - nodes.x(i, j)
        new_ref[:, i, j] = new
        u_ref[:, i, j] = inv * new

    main_products(sz, prepare, u_ref, mats, rhs_ref, prod_ref)


def third_corner(sz, n_mat, even_ref, vec, from_x, from_y, own_inv, own_pot, ghost_x, ghost_y,
                 last_x, last_field, acc_in, face_in, near_in, far_in, corner_in, prod_ref, y_ref,
                 y_corner, new_ref, *refs):
    mats = refs[:n_mat]
    out_hbm, edge_x, edge_y, face, side, corner, rows_ref = refs[n_mat : n_mat + 7]
    part_ref, sem, acc_ref, small_ref, tail_ref = refs[n_mat + 7 :]
    nodes = Nodes(sz, vec, from_x, from_y, own_inv, own_pot, ghost_x, ghost_y, last_field)
    sums = Sums(sz, even_ref[0] == 0, acc_in, face_in, near_in, far_in, corner_in)
    u_corner, new_corner = [], []
    for at, (i, j) in enumerate(corner_edges(sz)):
        x = last_x[...] if (i, j) == (sz.ex, sz.ey) else nodes.x(i, j)
        old, inv = y_corner[at], nodes.inv(i, j)
        image = inv * sums.at(i, j) + nodes.pot(i, j) * old
        new_corner.append(2.0 * (image - center_shift * old) / half_width - x)
        u_corner.append(inv * new_corner[-1])
    corner_products(sz, u_corner, prod_ref, mats, small_ref, tail_ref, acc_ref)

    def put_row(at, value):
        for b in range(sz.blocks):
            rows_ref[at, :, b * sz.width : (b + 1) * sz.width] = value[b]

    copies = []
    for i in range(sz.gx):
        for j in range(sz.gy):
            acc, inv = acc_ref[:, i, j], nodes.inv(i, j)
            if i == sz.ex or j == sz.ey:
                value = gain * (inv * acc)
                rounded = value.astype(bf16)
                if j < sz.ey:
                    face[:, j] = rounded
                elif i < sz.ex:
                    side[:, i] = value
                else:
                    corner[...] = rounded
                put_row(sz.own_edges + (j if j < sz.ey else sz.ey + i), rounded)
                continue
            at = sz.corner(i, j)
            old = y_ref[:, i, j] if at is None else y_corner[at]
            new = new_ref[:, i, j] if at is None else new_corner[at]
            image = inv * acc + nodes.pot(i, j) * new
            value = 2.0 * (image - center_shift * new) / half_width - old
            part_ref[:, i, j] = value
            if i == 0:
                edge_x[:, j] = value
            elif j == 0:
                edge_y[:, i - 1] = value
            put_row(i * sz.ey + j, value.astype(bf16))
        if i < sz.ex:
            copies.append(pltpu.make_async_copy(part_ref.at[:, i], out_hbm.at[:, i], sem.at[i]))
            copies[-1].start()
    for at in range(sz.own_edges + sz.ey + sz.gx, sz.edges):
        rows_ref[at] = jnp.zeros((sz.ez, sz.full), bf16)
    for copy in copies:
        copy.wait()


def margin_kernel(sz, norm_scale, even_ref, turned, rows_ref, give, keep):
    rows = rows_ref[...].reshape(sz.edges * sz.ez, sz.full)
    mine = even_ref[0]
    for half, out in ((1 - mine, give), (mine, keep)):
        local = jnp.dot(turned[half], rows, preferred_element_type=f32)
        out[...] = (local * norm_scale).astype(out.dtype)


def ready_kernel(sz, keep, taken, side_ref, corner_ref, face_in, pieces, out_ref, face_out):
    del face_in, face_out
    rows = pieces.shape[2]
    for at in range(pieces.shape[1]):
        span = slice(at * rows, (at + 1) * rows)
        value = (keep[span] + taken[span].astype(f32)).astype(pieces.dtype)
        for copy in range(pieces.shape[0]):
            pieces[copy, at] = value
    for i in range(sz.ex):
        value = side_ref[:, i]
        if i == 0:
            value = value + corner_ref[...].astype(f32)
        out_ref[:, i] = value.astype(out_ref.dtype)


def last_kernel(sz, old_hbm, edge_x, edge_y, face, side, pieces, out_hbm, margin, at_x, at_y, sems):
    del old_hbm
    for j in range(sz.ey):
        value = edge_x[:, j] + face[:, j].astype(f32)
        if j == 0:
            value = value + side[:, 0].astype(f32)
        at_x[:, j] = value
    for i in range(1, sz.ex):
        at_y[:, i - 1] = edge_y[:, i - 1] + side[:, i].astype(f32)
    copies = [
        pltpu.make_async_copy(at_x, out_hbm.at[:, 0], sems.at[0]),
        pltpu.make_async_copy(at_y, out_hbm.at[:, pl.ds(1, sz.ex - 1), 0], sems.at[1]),
    ]
    for copy in copies:
        copy.start()
    margin[...] = sum(pieces[at].astype(f32) for at in range(pieces.shape[0]))
    for copy in copies:
        copy.wait()


def like(shape, dtype):
    return jax.ShapeDtypeStruct(shape, dtype)


def call(kernel, name, flops, out_shape, scratch, operands, hbm=0, scalar_first=False, aliases=None,
         out_hbm=0):
    out_shape = [like(s.shape, s.dtype) for s in out_shape]
    size = sum(math.prod(s.shape) * jnp.dtype(s.dtype).itemsize for s in (*operands, *out_shape))
    whole = pl.BlockSpec(memory_space=pltpu.VMEM)
    specs = [pl.BlockSpec(memory_space=pltpu.HBM)] * hbm + [whole] * (len(operands) - hbm)
    if scalar_first:
        specs[0] = pl.BlockSpec(memory_space=pltpu.SMEM)
    out_specs = [pl.BlockSpec(memory_space=pltpu.HBM)] * out_hbm + [whole] * (len(out_shape) - out_hbm)
    for source, target in (aliases or {}).items():
        if source >= hbm:
            specs[source] = out_specs[target] = pl.BlockSpec(memory_space=pl.ANY)
    out_shape = [pltpu.HBM(s.shape, s.dtype) for s in out_shape[:out_hbm]] + out_shape[out_hbm:]
    operands = [pltpu.with_memory_space_constraint(a, pltpu.HBM) for a in operands[:hbm]] + list(
        operands[hbm:]
    )
    return pl.pallas_call(
        kernel,
        in_specs=specs,
        out_specs=out_specs,
        out_shape=out_shape,
        scratch_shapes=scratch,
        input_output_aliases=aliases or {},
        compiler_params=pltpu.CompilerParams(vmem_limit_bytes=VMEM_LIMIT),
        cost_estimate=pl.CostEstimate(flops=flops, bytes_accessed=size, transcendentals=0),
        name=name,
    )(*operands)


def body(vectors, resident, inv_mass, potential, cell_matrix, connectivity):
    sz = Sizes(vectors, resident, inv_mass, connectivity)
    nx, ny = lax.axis_size("dx"), lax.axis_size("dy")
    norm_scale = 1.0 / math.sqrt(sz.ex * sz.ey * sz.ez * nx * ny)
    blocks, ez, width, full = sz.blocks, sz.ez, sz.width, sz.full
    res_count = resident.shape[-1]
    tile = (ez, width)

    conn = connectivity.reshape(sz.cells, sz.nodes)
    to_x, to_y, res_x, conn = call(
        functools.partial(pack_kernel, sz), "pack", 0,
        [
            like((sz.ey, ez, sz.wide), bf16), like((sz.ex, ez, sz.wide + sz.res), bf16),
            like((sz.ey, ez, sz.res), bf16), conn,
        ],
        [
            pltpu.VMEM((2, sz.ey, ez), f32), pltpu.VMEM((2, sz.ex, ez), f32),
            pltpu.SemaphoreType.DMA((7 + 2 * blocks,)),
        ],
        [vectors, resident, inv_mass, potential, conn], hbm=5,
    )
    from_x = send(to_x, -1, 0)
    from_y = send(to_y, 0, -1)
    res_x = send(res_x, -1, 0)

    halves = 2 if sz.cells % 2 == 0 else 1
    step = sz.cells // halves
    mats = []
    for at in range(0, sz.cells, step):
        mats += call(
            functools.partial(order_kernel, sz, at), "order_cells", 4 * step * sz.depth**3,
            [like((step, sz.rows, sz.depth), bf16)],
            [], [cell_matrix, conn],
        )
    own_inv = jnp.broadcast_to(inv_mass[..., None], inv_mass.shape + (width,))
    own_pot = jnp.broadcast_to(potential[..., None], inv_mass.shape + (width,))
    parity = jnp.reshape(lax.axis_index("dy") % 2, (1,)).astype(jnp.int32)
    ghost_corner = send(from_y[:1], -1, 0)

    grid = (blocks, sz.gx, sz.gy) + tile
    own = (blocks, sz.ex, sz.ey) + tile
    products = like((sz.cells, sz.rows, full), f32)
    state_grid = like(grid, f32)
    messages = [
        like((2, blocks, sz.gy) + tile, bf16),
        like((blocks, sz.gx) + tile, bf16),
        like((blocks, sz.gx) + tile, bf16),
    ]
    main_scratch = [pltpu.VMEM(grid, f32), pltpu.VMEM((2, sz.depth, full), f32)]
    corner_scratch = [
        pltpu.VMEM((LANES, full), f32),
        pltpu.VMEM((sz.cells, sz.base + sz.rows - sz.tail, full), f32),
    ]
    n_mat = len(mats)
    flops = 2 * sz.cells * sz.rows * sz.depth * full
    small_flops = 2 * sz.cells * sz.rows * LANES * full

    def exchange(face, near, far):
        face = swap_x(face)
        near, far = swap_y(near, far)
        (corner,) = call(
            functools.partial(corner_pack_kernel, sz), "corner_pack", 0,
            [like((2, 2) + sz.edge, bf16)], [], [near, far],
        )
        return [face, near, far], swap_x(corner)

    prod, ghost_x, ghost_y = call(
        functools.partial(first_main, sz, n_mat), "first_main", flops,
        [products, like((2, sz.ey) + tile, f32), like((2, sz.ex) + tile, f32)], main_scratch,
        [vectors, from_x, from_y, own_inv, own_pot, *mats],
    )
    res_x, acc, face, near, far, last_x, last_field = call(
        functools.partial(first_corner, sz, n_mat), "first_corner", small_flops,
        [res_x, state_grid, *messages, like(sz.edge, f32), like((2,) + tile, f32)], corner_scratch,
        [
            parity, res_x, vectors, from_x, from_y, ghost_corner, own_inv, own_pot, ghost_x, ghost_y, prod,
            *mats,
        ],
        scalar_first=True, aliases={1: 0},
    )
    (turned,) = call(
        functools.partial(turn_kernel, sz, ny // 2), "turn_residents", flops // 2,
        [like((2, res_count // 2, sz.edges * ez), bf16)], [],
        [resident.reshape(-1, res_count), res_x, from_y, ghost_corner],
    )
    got, corner = exchange(face, near, far)
    state = [vectors, from_x, from_y, own_inv, own_pot, ghost_x, ghost_y]
    ends = [last_x, last_field]
    prod, y1 = call(
        functools.partial(second_main, sz, n_mat), "second_main", flops,
        [products, state_grid], main_scratch,
        [parity, *state, acc, *got, *mats], scalar_first=True,
    )
    acc, face, near, far, y1_corner = call(
        functools.partial(second_corner, sz, n_mat), "second_corner", small_flops,
        [state_grid, *messages, like((4,) + sz.edge, f32)], corner_scratch,
        [parity, *state, *ends, acc, *got, corner, prod, *mats], scalar_first=True,
    )
    got, corner = exchange(face, near, far)
    prod, y2 = call(
        functools.partial(third_main, sz, n_mat), "third_main", flops,
        [products, state_grid], main_scratch,
        [parity, *state, acc, *got, y1, *mats], scalar_first=True,
    )
    filtered, edge_x, edge_y, face, side, corner, rows = call(
        functools.partial(third_corner, sz, n_mat), "third_corner", small_flops,
        [
            like(own, f32), like((blocks, sz.ey) + tile, f32), like((blocks, sz.ex - 1) + tile, f32),
            like((blocks, sz.ey) + tile, bf16), like((blocks, sz.ex) + tile, f32), like(sz.edge, bf16),
            like((sz.edges, ez, full), bf16),
        ],
        [pltpu.VMEM(own, f32), pltpu.SemaphoreType.DMA((sz.ex,)), pltpu.VMEM(grid, f32)] + corner_scratch,
        [parity, *state, *ends, acc, *got, corner, prod, y1, y1_corner, y2, *mats],
        scalar_first=True, out_hbm=1,
    )
    corner = send(corner, 1, 0)
    give, keep = call(
        functools.partial(margin_kernel, sz, norm_scale), "margin", 2 * res_count * sz.edges * ez * full,
        [like((res_count // 2, full), bf16), like((res_count // 2, full), f32)], [],
        [parity, turned, rows], scalar_first=True,
    )

    pieces, side, face = call(
        functools.partial(ready_kernel, sz), "ready", 0,
        [like((nx, ny // 2, res_count // ny, full), bf16), like((blocks, sz.ex) + tile, bf16), face],
        [], [keep, send_near(give), side, corner, face], aliases={4: 2},
    )
    pieces = pieces.reshape(nx * ny // 2, -1, full)
    groups = [[a * ny + b for a in range(nx) for b in range(c, ny, 2)] for c in range(2)]
    pieces = lax.all_to_all(pieces, ("dx", "dy"), 0, 0, axis_index_groups=groups)

    face = send(face, 1, 0)
    side = send(side, 0, 1)
    filtered, margin = call(
        functools.partial(last_kernel, sz), "last", 0, [like(own, f32), like(pieces.shape[1:], f32)],
        [
            pltpu.VMEM((blocks, sz.ey) + tile, f32), pltpu.VMEM((blocks, sz.ex - 1) + tile, f32),
            pltpu.SemaphoreType.DMA((2,)),
        ],
        [filtered, edge_x, edge_y, face, side, pieces], hbm=1, out_hbm=1, aliases={0: 0},
    )
    return (filtered, margin)


def solution(mesh):
    return jax.shard_map(
        body,
        mesh=mesh,
        in_specs=(
            P(None, "dx", "dy", None, None),
            P("dx", "dy", None, None),
            P("dx", "dy", None),
            P("dx", "dy", None),
            P(),
            P("dx", "dy", None, None),
        ),
        out_specs=(P(None, "dx", "dy", None, None), P("dy", None)),
        check_vma=False,
    )
```

```python
import functools
import math

import jax
import jax.numpy as jnp
from jax import lax
from jax.experimental import pallas as pl
from jax.experimental.pallas import tpu as pltpu
from jax.sharding import PartitionSpec as P

LANES = 128
TILE = 256
SUB = 16
VMEM_LIMIT = 16 * 1024 * 1024

center_shift = 1.2
half_width = 2.0
gain = 2.0 / half_width

f32, bf16 = jnp.float32, jnp.bfloat16


def round_up(value, step):
    return -(-value // step) * step


class Sizes:
    def __init__(self, vectors, resident, inv_mass, connectivity):
        self.blocks = vectors.shape[0]
        self.width = vectors.shape[-1]
        self.full = self.blocks * self.width
        self.res = resident.shape[-1]
        self.wide = self.full + self.width
        self.ex, self.ey, self.ez = inv_mass.shape
        self.cells, self.nodes = connectivity.shape[2:]
        self.n1 = round(self.nodes ** (1.0 / 3.0))
        self.p = self.n1 - 1
        self.cx, self.cy, self.cz = self.ex // self.p, self.ey // self.p, self.ez // self.p
        self.gx, self.gy, self.gz = self.ex + 1, self.ey + 1, self.ez
        self.edge = (self.blocks, self.ez, self.width)
        self.origins = [
            (a * self.p, b * self.p, c * self.p)
            for a in range(self.cx)
            for b in range(self.cy)
            for c in range(self.cz)
        ]
        self.most = max(len(self.cell_corners(cell)) for cell in range(self.cells))
        self.base = round_up(self.most * self.n1, 8)
        plain = self.n1 * self.n1 - min(len(self.cell_corners(cell)) for cell in range(self.cells))
        self.tail = self.base + plain * self.p
        self.rows = round_up(self.tail + plain, SUB)
        self.depth = round_up(self.rows, LANES)
        self.own_edges = self.ex * self.ey
        self.edges = round_up(self.own_edges + self.ey + self.gx, LANES // self.ez)

    def corner(self, i, j):
        if i in (0, self.ex) and j in (0, self.ey):
            return 2 * (i // self.ex) + j // self.ey
        return None

    def cell_corners(self, cell):
        x0, y0, _ = self.origins[cell]
        return [
            (i, j)
            for i in range(self.n1)
            for j in range(self.n1)
            if self.corner(x0 + i, y0 + j) is not None
        ]

    def runs(self, cell):
        corners = self.cell_corners(cell)
        place = 0
        for i in range(self.n1):
            js = [j for j in range(self.n1) if (i, j) not in corners]
            while js:
                count = 1
                while count < len(js) and js[count] == js[0] + count:
                    count += 1
                yield place, i, js[0], count
                place += count
                js = js[count:]


def send(value, steps_x, steps_y):
    nx, ny = lax.axis_size("dx"), lax.axis_size("dy")
    pairs = [
        (a * ny + b, ((a + steps_x) % nx) * ny + (b + steps_y) % ny)
        for a in range(nx)
        for b in range(ny)
    ]
    return lax.ppermute(value, ("dx", "dy"), pairs)


def swap_x(value):
    if lax.axis_size("dx") == 2:
        return send(value, 1, 0)
    return jnp.stack([send(value[0], -1, 0), send(value[1], 1, 0)])


def send_near(value):
    pairs = [(b, b + 1 if b % 2 == 0 else b - 1) for b in range(lax.axis_size("dy"))]
    return lax.ppermute(value, "dy", pairs)


def swap_y(near, far):
    ny = lax.axis_size("dy")
    far_pairs = [(b, (b - 1 if b % 2 == 0 else b + 1) % ny) for b in range(ny)]
    far = lax.ppermute(far, "dy", far_pairs)
    return send_near(near), far


def order_kernel(sz, first, matrix_ref, conn_ref, out_ref):
    for slot in range(out_ref.shape[0]):
        cell = first + slot
        x0, y0, z0 = sz.origins[cell]
        conn = conn_ref[cell : cell + 1, :].astype(f32)
        li = jnp.floor((conn + 0.5) * (1.0 / (sz.gy * sz.gz)))
        rest = conn - li * (sz.gy * sz.gz)
        lj = jnp.floor((rest + 0.5) * (1.0 / sz.gz))
        lk = rest - lj * sz.gz - z0
        lk = jnp.where(lk < 0, lk + sz.gz, lk)
        column = (li - x0) * sz.n1 + (lj - y0)
        corners = [i * sz.n1 + j for i, j in sz.cell_corners(cell)]
        place = column
        for at in corners:
            place = place - jnp.where(column > at, 1.0, 0.0)
        index = jnp.where(lk < sz.p, sz.base + place * sz.p + lk, sz.tail + place)
        for rank, at in enumerate(corners):
            special = jnp.where(lk < sz.p, rank * sz.p + lk, len(corners) * sz.p + rank)
            index = jnp.where(column == at, special, index)
        index = index.astype(jnp.int32)
        row = lax.broadcasted_iota(jnp.int32, (sz.depth, sz.nodes), 0)
        pick = (row == index).astype(f32).astype(bf16)
        half = jnp.dot(pick[: sz.rows], matrix_ref[...], preferred_element_type=f32)
        half = half.astype(bf16)
        cuts = list(range(0, sz.depth, TILE)) + [sz.depth]
        for r0, r1 in zip(cuts[:-1], cuts[1:]):
            r1 = min(r1, sz.rows)
            block = lax.dot_general(
                half[r0:r1], pick[r0:], (((1,), (1,)), ((), ())), preferred_element_type=f32
            ).astype(bf16)
            out_ref[slot, r0:r1, r0:] = block
            for c0, c1 in zip(cuts[:-1], cuts[1:]):
                if c0 > r0:
                    mirror = block[:, c0 - r0 : c1 - r0].T
                    c1 = min(c1, sz.rows)
                    out_ref[slot, c0:c1, r0:r1] = mirror[: c1 - c0]


def field_row(inv, pot):
    lane = lax.broadcasted_iota(jnp.int32, inv.shape, inv.ndim - 1)
    row = jnp.zeros_like(inv)
    for at, rest in enumerate((inv, pot)):
        for k in range(3):
            part = rest.astype(bf16).astype(f32)
            rest = rest - part
            row = jnp.where(lane == 3 * at + k, part, row)
    return row.astype(bf16)


def field_rows(sz, inv, pot, count):
    inv, pot = inv.T, pot.T
    shape = (sz.ez, sz.width)
    for at in range(count):
        yield at, field_row(
            jnp.broadcast_to(inv[:, at : at + 1], shape), jnp.broadcast_to(pot[:, at : at + 1], shape)
        )


def fields_of(row):
    row = row.astype(f32)
    return [
        jnp.broadcast_to(sum(row[:, 3 * at + k : 3 * at + k + 1] for k in range(3)), row.shape)
        for at in range(2)
    ]


def pack_kernel(
    sz, vec_hbm, res_hbm, inv_hbm, pot_hbm, conn_hbm, to_x, to_y, res_x, conn_ref, at_x, at_y, sems
):
    pairs = [
        (inv_hbm.at[0], at_x.at[0]), (pot_hbm.at[0], at_x.at[1]),
        (inv_hbm.at[:, 0], at_y.at[0]), (pot_hbm.at[:, 0], at_y.at[1]),
        (res_hbm.at[0], res_x),
        (res_hbm.at[:, 0], to_y.at[:, :, pl.ds(sz.wide, sz.res)]),
    ]
    for b in range(sz.blocks):
        lanes = pl.ds(b * sz.width, sz.width)
        pairs.append((vec_hbm.at[b, 0], to_x.at[:, :, lanes]))
        pairs.append((vec_hbm.at[b, :, 0], to_y.at[:, :, lanes]))
    pairs.append((conn_hbm, conn_ref))
    copies = [pltpu.make_async_copy(a, b, sems.at[k]) for k, (a, b) in enumerate(pairs)]
    for copy in copies:
        copy.start()
    for copy in copies[:4]:
        copy.wait()
    for j, row in field_rows(sz, at_x[0], at_x[1], sz.ey):
        to_x[j, :, sz.full : sz.wide] = row
    for i, row in field_rows(sz, at_y[0], at_y[1], sz.ex):
        to_y[i, :, sz.full : sz.wide] = row
    for copy in copies[4:]:
        copy.wait()


def turn_kernel(sz, pieces, res_ref, res_x, from_y, corner, out_ref):
    own = sz.own_edges * sz.ez
    share = sz.res // out_ref.shape[0] // pieces

    def put(g, columns, value):
        for at in range(0, LANES, share):
            owner = (g + at) // share
            row = owner // 2 * share
            out_ref[owner % 2, row : row + share, columns] = value[at : at + share]

    for g in range(0, sz.res, LANES):
        lanes = slice(g, g + LANES)
        put(g, slice(0, own), res_ref[:, lanes].T)
        rest = sz.edges - sz.own_edges - sz.ey - sz.gx
        tail = slice(sz.wide + g, sz.wide + g + LANES)
        parts = [res_x[:, :, lanes], from_y[:, :, tail], corner[:, :, tail]]
        if rest:
            parts.append(jnp.zeros((rest, sz.ez, LANES), bf16))
        ghosts = jnp.concatenate(parts, axis=0)
        put(g, slice(own, sz.edges * sz.ez), ghosts.reshape(-1, LANES).T)


def vectors_of(sz, edge):
    lanes = [slice(b * sz.width, (b + 1) * sz.width) for b in range(sz.blocks)]
    return jnp.stack([edge[:, at] for at in lanes]).astype(f32)


class Nodes:
    def __init__(self, sz, vec, from_x, from_y, own_inv, own_pot, ghost_x, ghost_y, corners=None):
        self.sz, self.vec, self.from_x, self.from_y = sz, vec, from_x, from_y
        self.own, self.ghost_x, self.ghost_y, self.corners = (own_inv, own_pot), ghost_x, ghost_y, corners

    def x(self, i, j):
        sz = self.sz
        if i < sz.ex and j < sz.ey:
            return self.vec[:, i, j].astype(f32)
        return vectors_of(sz, self.from_x[j] if i == sz.ex else self.from_y[i])

    def field(self, at, i, j):
        sz = self.sz
        if i < sz.ex and j < sz.ey:
            return self.own[at][i, j]
        if i < sz.ex:
            return self.ghost_y[at, i]
        if j < sz.ey:
            return self.ghost_x[at, j]
        return self.corners[at]

    def inv(self, i, j):
        return self.field(0, i, j)

    def pot(self, i, j):
        return self.field(1, i, j)


class Sums:
    def __init__(self, sz, even, acc, face, near, far, corner=None):
        self.sz, self.even, self.acc, self.face = sz, even, acc, face
        self.near, self.far, self.corner = near, far, corner

    def at(self, i, j):
        sz = self.sz
        total = self.acc[:, i, j]
        side = 1 if i == 0 else 0 if i == sz.ex else None
        if side is not None:
            total = total + self.face[side, :, j].astype(f32)
        if j in (0, sz.ey):
            is_near = self.even if j == sz.ey else jnp.logical_not(self.even)
            total = total + jnp.where(is_near, self.near[:, i].astype(f32), self.far[:, i].astype(f32))
            if side is not None:
                total = total + jnp.where(
                    is_near, self.corner[side, 0].astype(f32), self.corner[side, 1].astype(f32)
                )
        return total


def corner_edges(sz):
    return [(i, j) for i in (0, sz.ex) for j in (0, sz.ey)]


def main_products(sz, prepare, u_ref, mat_refs, rhs_ref, out_ref):
    width = sz.width
    flat = sz.gx * sz.gy * sz.gz
    u_flat = u_ref.reshape(sz.blocks * flat, width)
    matrices = [ref.at[c] for ref in mat_refs for c in range(ref.shape[0])]
    last = sz.nodes // 8 * 8
    ready = set()
    for cell, (x0, y0, z0) in enumerate(sz.origins):
        slot = cell % 2
        if cell < 2:
            rhs_ref[slot, : sz.base] = jnp.zeros((sz.base, sz.full), f32)
            rhs_ref[slot, last:] = jnp.zeros((sz.depth - last, sz.full), f32)
        for place, i, j, count in sz.runs(cell):
            for at in range(j, j + count):
                if (x0 + i, y0 + at) not in ready:
                    prepare(x0 + i, y0 + at)
                    ready.add((x0 + i, y0 + at))
        z1 = z0 + sz.p
        wrap = z1 % sz.gz
        for b in range(sz.blocks):
            lanes = slice(b * width, (b + 1) * width)
            for place, i, j, count in sz.runs(cell):
                row = sz.base + place * sz.p
                rhs_ref[slot, row : row + count * sz.p, lanes] = u_ref[
                    b, x0 + i, y0 + j : y0 + j + count, z0:z1
                ].reshape(count * sz.p, width)
        for b in range(sz.blocks):
            lanes = slice(b * width, (b + 1) * width)
            for place, i, j, count in sz.runs(cell):
                start = b * flat + ((x0 + i) * sz.gy + y0 + j) * sz.gz + wrap
                rhs_ref[slot, sz.tail + place : sz.tail + place + count, lanes] = u_flat[
                    pl.ds(start, count, stride=sz.gz)
                ]
        out_ref[cell] = jnp.dot(
            matrices[cell][...], rhs_ref[slot].astype(bf16), preferred_element_type=f32
        )


def corner_products(sz, u_corner, prod_ref, mat_refs, small_ref, tail_ref, acc_ref):
    width = sz.width
    flat = sz.gx * sz.gy * sz.gz
    acc_flat = acc_ref.reshape(sz.blocks * flat, width)
    matrices = [ref.at[c] for ref in mat_refs for c in range(ref.shape[0])]
    small_ref[...] = jnp.zeros_like(small_ref)
    touched = set()
    for cell, (x0, y0, z0) in enumerate(sz.origins):
        z1 = z0 + sz.p
        wrap = z1 % sz.gz
        corners = sz.cell_corners(cell)
        for rank, (i, j) in enumerate(corners):
            value = u_corner[sz.corner(x0 + i, y0 + j)]
            last = len(corners) * sz.p + rank
            for b in range(sz.blocks):
                lanes = slice(b * width, (b + 1) * width)
                small_ref[rank * sz.p : (rank + 1) * sz.p, lanes] = value[b, z0:z1]
                small_ref[last : last + 1, lanes] = value[b, wrap : wrap + 1]
        total = prod_ref[cell] + jnp.dot(
            matrices[cell][:, : small_ref.shape[0]], small_ref[...].astype(bf16),
            preferred_element_type=f32,
        )
        tail_ref[cell, : sz.base] = total[: sz.base]
        tail_ref[cell, sz.base :] = total[sz.tail :]
        spans = [(rank * sz.p, i, j, 1) for rank, (i, j) in enumerate(corners)]
        spans += [(sz.base + place * sz.p, i, j, count) for place, i, j, count in sz.runs(cell)]
        for row, i, j, count in spans:
            for at in range(count):
                part = total[row + at * sz.p : row + (at + 1) * sz.p]
                key = (x0 + i, y0 + j + at, z0)
                for b in range(sz.blocks):
                    value = part[:, b * width : (b + 1) * width]
                    if key in touched:
                        value = acc_ref[b, key[0], key[1], z0:z1] + value
                    acc_ref[b, key[0], key[1], z0:z1] = value
                touched.add(key)
    for cell, (x0, y0, z0) in enumerate(sz.origins):
        wrap = (z0 + sz.p) % sz.gz
        corners = sz.cell_corners(cell)
        spans = [(len(corners) * sz.p + rank, i, j, 1) for rank, (i, j) in enumerate(corners)]
        spans += [(sz.base + place, i, j, count) for place, i, j, count in sz.runs(cell)]
        for row, i, j, count in spans:
            for b in range(sz.blocks):
                start = b * flat + ((x0 + i) * sz.gy + y0 + j) * sz.gz + wrap
                rows = pl.ds(start, count, stride=sz.gz) if count > 1 else pl.ds(start, 1)
                lanes = slice(b * width, (b + 1) * width)
                acc_flat[rows] = acc_flat[rows] + tail_ref[cell, row : row + count, lanes]


def write_messages(sz, even, acc_ref, face, near, far):
    at_near = jnp.where(even, sz.ey, 0)
    for b in range(sz.blocks):
        face[0, b] = acc_ref[b, 0].astype(bf16)
        face[1, b] = acc_ref[b, sz.ex].astype(bf16)
        near[b] = acc_ref[b, :, at_near].astype(bf16)
        far[b] = acc_ref[b, :, sz.ey - at_near].astype(bf16)


def corner_pack_kernel(sz, near, far, out_ref):
    for side, i in enumerate((0, sz.ex)):
        for slot, ref in enumerate((near, far)):
            out_ref[side, slot] = ref[:, i]


def first_main(sz, n_mat, vec, from_x, from_y, own_inv, own_pot, *refs):
    mats = refs[:n_mat]
    prod_ref, ghost_x, ghost_y, u_ref, rhs_ref = refs[n_mat:]
    for j in range(sz.ey):
        ghost_x[0, j], ghost_x[1, j] = fields_of(from_x[j, :, sz.full : sz.wide])
    for i in range(sz.ex):
        ghost_y[0, i], ghost_y[1, i] = fields_of(from_y[i, :, sz.full : sz.wide])
    nodes = Nodes(sz, vec, from_x, from_y, own_inv, own_pot, ghost_x, ghost_y)

    def prepare(i, j):
        u_ref[:, i, j] = nodes.x(i, j) * nodes.inv(i, j)

    main_products(sz, prepare, u_ref, mats, rhs_ref, prod_ref)


def first_corner(sz, n_mat, even_ref, res_in, vec, from_x, from_y, corner, own_inv, own_pot, ghost_x,
                 ghost_y, prod_ref, *refs):
    mats = refs[:n_mat]
    res_out, acc_ref, face, near, far, last_x, last_field, small_ref, tail_ref = refs[n_mat:]
    del res_in, res_out
    last_field[0], last_field[1] = fields_of(corner[0, :, sz.full : sz.wide])
    last_x[...] = vectors_of(sz, corner[0])
    nodes = Nodes(sz, vec, from_x, from_y, own_inv, own_pot, ghost_x, ghost_y, last_field)
    u_corner = []
    for i, j in corner_edges(sz):
        x = last_x[...] if (i, j) == (sz.ex, sz.ey) else nodes.x(i, j)
        u_corner.append(x * nodes.inv(i, j))
    corner_products(sz, u_corner, prod_ref, mats, small_ref, tail_ref, acc_ref)
    write_messages(sz, even_ref[0] == 0, acc_ref, face, near, far)


def second_main(sz, n_mat, even_ref, vec, from_x, from_y, own_inv, own_pot, ghost_x, ghost_y,
                acc_in, face_in, near_in, far_in, *refs):
    mats = refs[:n_mat]
    prod_ref, y_ref, u_ref, rhs_ref = refs[n_mat:]
    nodes = Nodes(sz, vec, from_x, from_y, own_inv, own_pot, ghost_x, ghost_y)
    sums = Sums(sz, even_ref[0] == 0, acc_in, face_in, near_in, far_in)

    def prepare(i, j):
        old, inv = nodes.x(i, j), nodes.inv(i, j)
        image = inv * sums.at(i, j) + nodes.pot(i, j) * old
        new = (image - center_shift * old) / half_width
        y_ref[:, i, j] = new
        u_ref[:, i, j] = inv * new

    main_products(sz, prepare, u_ref, mats, rhs_ref, prod_ref)


def second_corner(sz, n_mat, even_ref, vec, from_x, from_y, own_inv, own_pot, ghost_x, ghost_y, last_x,
                  last_field, acc_in, face_in, near_in, far_in, corner_in, prod_ref, *refs):
    mats = refs[:n_mat]
    acc_ref, face, near, far, y_corner, small_ref, tail_ref = refs[n_mat:]
    even = even_ref[0] == 0
    nodes = Nodes(sz, vec, from_x, from_y, own_inv, own_pot, ghost_x, ghost_y, last_field)
    sums = Sums(sz, even, acc_in, face_in, near_in, far_in, corner_in)
    u_corner = []
    for at, (i, j) in enumerate(corner_edges(sz)):
        old = last_x[...] if (i, j) == (sz.ex, sz.ey) else nodes.x(i, j)
        inv = nodes.inv(i, j)
        image = inv * sums.at(i, j) + nodes.pot(i, j) * old
        new = (image - center_shift * old) / half_width
        y_corner[at] = new
        u_corner.append(inv * new)
    corner_products(sz, u_corner, prod_ref, mats, small_ref, tail_ref, acc_ref)
    write_messages(sz, even, acc_ref, face, near, far)


def third_main(sz, n_mat, even_ref, vec, from_x, from_y, own_inv, own_pot, ghost_x, ghost_y,
               acc_in, face_in, near_in, far_in, y_ref, *refs):
    mats = refs[:n_mat]
    prod_ref, new_ref, u_ref, rhs_ref = refs[n_mat:]
    nodes = Nodes(sz, vec, from_x, from_y, own_inv, own_pot, ghost_x, ghost_y)
    sums = Sums(sz, even_ref[0] == 0, acc_in, face_in, near_in, far_in)

    def prepare(i, j):
        old, inv = y_ref[:, i, j], nodes.inv(i, j)
        image = inv * sums.at(i, j) + nodes.pot(i, j) * old
        new = 2.0 * (image - center_shift * old) / half_width - nodes.x(i, j)
        new_ref[:, i, j] = new
        u_ref[:, i, j] = inv * new

    main_products(sz, prepare, u_ref, mats, rhs_ref, prod_ref)


def third_corner(sz, n_mat, even_ref, vec, from_x, from_y, own_inv, own_pot, ghost_x, ghost_y,
                 last_x, last_field, acc_in, face_in, near_in, far_in, corner_in, prod_ref, y_ref,
                 y_corner, new_ref, *refs):
    mats = refs[:n_mat]
    out_hbm, face_hbm, side_hbm, rows_ref = refs[n_mat : n_mat + 4]
    part_ref, face, side, sem, acc_ref, small_ref, tail_ref = refs[n_mat + 4 :]
    nodes = Nodes(sz, vec, from_x, from_y, own_inv, own_pot, ghost_x, ghost_y, last_field)
    sums = Sums(sz, even_ref[0] == 0, acc_in, face_in, near_in, far_in, corner_in)
    u_corner, new_corner = [], []
    for at, (i, j) in enumerate(corner_edges(sz)):
        x = last_x[...] if (i, j) == (sz.ex, sz.ey) else nodes.x(i, j)
        old, inv = y_corner[at], nodes.inv(i, j)
        image = inv * sums.at(i, j) + nodes.pot(i, j) * old
        new_corner.append(2.0 * (image - center_shift * old) / half_width - x)
        u_corner.append(inv * new_corner[-1])
    corner_products(sz, u_corner, prod_ref, mats, small_ref, tail_ref, acc_ref)

    def put_row(at, value):
        for b in range(sz.blocks):
            rows_ref[at, :, b * sz.width : (b + 1) * sz.width] = value[b]

    copies = []
    for i in range(sz.gx):
        for j in range(sz.gy):
            acc, inv = acc_ref[:, i, j], nodes.inv(i, j)
            if i == sz.ex or j == sz.ey:
                value = gain * (inv * acc)
                rounded = value.astype(bf16)
                if j < sz.ey:
                    face[:, j] = rounded
                else:
                    side[:, i] = rounded
                put_row(sz.own_edges + (j if j < sz.ey else sz.ey + i), rounded)
                continue
            at = sz.corner(i, j)
            old = y_ref[:, i, j] if at is None else y_corner[at]
            new = new_ref[:, i, j] if at is None else new_corner[at]
            image = inv * acc + nodes.pot(i, j) * new
            value = 2.0 * (image - center_shift * new) / half_width - old
            part_ref[:, i, j] = value
            put_row(i * sz.ey + j, value.astype(bf16))
        if i < sz.ex:
            copies.append(pltpu.make_async_copy(part_ref.at[:, i], out_hbm.at[:, i], sem.at[i]))
            copies[-1].start()
    for at in range(sz.own_edges + sz.ey + sz.gx, sz.edges):
        rows_ref[at] = jnp.zeros((sz.ez, sz.full), bf16)
    copies.append(pltpu.make_async_copy(face, face_hbm, sem.at[sz.ex]))
    copies.append(pltpu.make_async_copy(side, side_hbm, sem.at[sz.ex + 1]))
    for copy in copies[-2:]:
        copy.start()
    for copy in copies:
        copy.wait()


def margin_kernel(sz, norm_scale, even_ref, turned, rows_ref, give, keep):
    rows = rows_ref[...].reshape(sz.edges * sz.ez, sz.full)
    mine = even_ref[0]
    for half, out in ((1 - mine, give), (mine, keep)):
        local = jnp.dot(turned[half], rows, preferred_element_type=f32)
        out[...] = (local * norm_scale).astype(out.dtype)


def pieces_kernel(keep, taken, pieces):
    rows = pieces.shape[2]
    for at in range(pieces.shape[1]):
        span = slice(at * rows, (at + 1) * rows)
        value = (keep[span] + taken[span].astype(f32)).astype(pieces.dtype)
        for copy in range(pieces.shape[0]):
            pieces[copy, at] = value


def last_kernel(sz, old_hbm, face, side, corner, pieces, out_hbm, margin, at_x, at_y, sems):
    del old_hbm
    pairs = [(at_x, out_hbm.at[:, 0]), (at_y, out_hbm.at[:, pl.ds(1, sz.ex - 1), 0])]
    loads = [pltpu.make_async_copy(b, a, sems.at[k]) for k, (a, b) in enumerate(pairs)]
    stores = [pltpu.make_async_copy(a, b, sems.at[k]) for k, (a, b) in enumerate(pairs)]
    for copy in loads:
        copy.start()
    margin[...] = sum(pieces[at].astype(f32) for at in range(pieces.shape[0]))
    for copy in loads:
        copy.wait()
    at_x[:, 0] += side[:, 0].astype(f32) + corner[:, 0].astype(f32)
    for j in range(sz.ey):
        at_x[:, j] += face[:, j].astype(f32)
    for i in range(1, sz.ex):
        at_y[:, i - 1] += side[:, i].astype(f32)
    for copy in stores:
        copy.start()
    for copy in stores:
        copy.wait()


def like(shape, dtype):
    return jax.ShapeDtypeStruct(shape, dtype)


def call(kernel, name, flops, out_shape, scratch, operands, hbm=0, scalar_first=False, aliases=None,
         out_hbm=0):
    out_shape = [like(s.shape, s.dtype) for s in out_shape]
    size = sum(math.prod(s.shape) * jnp.dtype(s.dtype).itemsize for s in (*operands, *out_shape))
    whole = pl.BlockSpec(memory_space=pltpu.VMEM)
    specs = [pl.BlockSpec(memory_space=pltpu.HBM)] * hbm + [whole] * (len(operands) - hbm)
    if scalar_first:
        specs[0] = pl.BlockSpec(memory_space=pltpu.SMEM)
    out_specs = [pl.BlockSpec(memory_space=pltpu.HBM)] * out_hbm + [whole] * (len(out_shape) - out_hbm)
    for source, target in (aliases or {}).items():
        if source >= hbm:
            specs[source] = out_specs[target] = pl.BlockSpec(memory_space=pl.ANY)
    out_shape = [pltpu.HBM(s.shape, s.dtype) for s in out_shape[:out_hbm]] + out_shape[out_hbm:]
    operands = [pltpu.with_memory_space_constraint(a, pltpu.HBM) for a in operands[:hbm]] + list(
        operands[hbm:]
    )
    return pl.pallas_call(
        kernel,
        in_specs=specs,
        out_specs=out_specs,
        out_shape=out_shape,
        scratch_shapes=scratch,
        input_output_aliases=aliases or {},
        compiler_params=pltpu.CompilerParams(vmem_limit_bytes=VMEM_LIMIT),
        cost_estimate=pl.CostEstimate(flops=flops, bytes_accessed=size, transcendentals=0),
        name=name,
    )(*operands)


def body(vectors, resident, inv_mass, potential, cell_matrix, connectivity):
    sz = Sizes(vectors, resident, inv_mass, connectivity)
    nx, ny = lax.axis_size("dx"), lax.axis_size("dy")
    norm_scale = 1.0 / math.sqrt(sz.ex * sz.ey * sz.ez * nx * ny)
    blocks, ez, width, full = sz.blocks, sz.ez, sz.width, sz.full
    res_count = resident.shape[-1]
    tile = (ez, width)

    conn = connectivity.reshape(sz.cells, sz.nodes)
    to_x, to_y, res_x, conn = call(
        functools.partial(pack_kernel, sz), "pack", 0,
        [
            like((sz.ey, ez, sz.wide), bf16), like((sz.ex, ez, sz.wide + sz.res), bf16),
            like((sz.ey, ez, sz.res), bf16), conn,
        ],
        [
            pltpu.VMEM((2, sz.ey, ez), f32), pltpu.VMEM((2, sz.ex, ez), f32),
            pltpu.SemaphoreType.DMA((7 + 2 * blocks,)),
        ],
        [vectors, resident, inv_mass, potential, conn], hbm=5,
    )
    from_x = send(to_x, -1, 0)
    from_y = send(to_y, 0, -1)
    res_x = send(res_x, -1, 0)

    halves = 2 if sz.cells % 2 == 0 else 1
    step = sz.cells // halves
    mats = []
    for at in range(0, sz.cells, step):
        mats += call(
            functools.partial(order_kernel, sz, at), "order_cells", 4 * step * sz.depth**3,
            [like((step, sz.rows, sz.depth), bf16)],
            [], [cell_matrix, conn],
        )
    own_inv = jnp.broadcast_to(inv_mass[..., None], inv_mass.shape + (width,))
    own_pot = jnp.broadcast_to(potential[..., None], inv_mass.shape + (width,))
    parity = jnp.reshape(lax.axis_index("dy") % 2, (1,)).astype(jnp.int32)
    ghost_corner = send(from_y[:1], -1, 0)

    grid = (blocks, sz.gx, sz.gy) + tile
    own = (blocks, sz.ex, sz.ey) + tile
    products = like((sz.cells, sz.rows, full), f32)
    state_grid = like(grid, f32)
    messages = [
        like((2, blocks, sz.gy) + tile, bf16),
        like((blocks, sz.gx) + tile, bf16),
        like((blocks, sz.gx) + tile, bf16),
    ]
    main_scratch = [pltpu.VMEM(grid, f32), pltpu.VMEM((2, sz.depth, full), f32)]
    corner_scratch = [
        pltpu.VMEM((LANES, full), f32),
        pltpu.VMEM((sz.cells, sz.base + sz.rows - sz.tail, full), f32),
    ]
    n_mat = len(mats)
    flops = 2 * sz.cells * sz.rows * sz.depth * full
    small_flops = 2 * sz.cells * sz.rows * LANES * full

    def exchange(face, near, far):
        face = swap_x(face)
        near, far = swap_y(near, far)
        (corner,) = call(
            functools.partial(corner_pack_kernel, sz), "corner_pack", 0,
            [like((2, 2) + sz.edge, bf16)], [], [near, far],
        )
        return [face, near, far], swap_x(corner)

    prod, ghost_x, ghost_y = call(
        functools.partial(first_main, sz, n_mat), "first_main", flops,
        [products, like((2, sz.ey) + tile, f32), like((2, sz.ex) + tile, f32)], main_scratch,
        [vectors, from_x, from_y, own_inv, own_pot, *mats],
    )
    res_x, acc, face, near, far, last_x, last_field = call(
        functools.partial(first_corner, sz, n_mat), "first_corner", small_flops,
        [res_x, state_grid, *messages, like(sz.edge, f32), like((2,) + tile, f32)], corner_scratch,
        [
            parity, res_x, vectors, from_x, from_y, ghost_corner, own_inv, own_pot, ghost_x, ghost_y, prod,
            *mats,
        ],
        scalar_first=True, aliases={1: 0},
    )
    (turned,) = call(
        functools.partial(turn_kernel, sz, ny // 2), "turn_residents", flops // 2,
        [like((2, res_count // 2, sz.edges * ez), bf16)], [],
        [resident.reshape(-1, res_count), res_x, from_y, ghost_corner],
    )
    got, corner = exchange(face, near, far)
    state = [vectors, from_x, from_y, own_inv, own_pot, ghost_x, ghost_y]
    ends = [last_x, last_field]
    prod, y1 = call(
        functools.partial(second_main, sz, n_mat), "second_main", flops,
        [products, state_grid], main_scratch,
        [parity, *state, acc, *got, *mats], scalar_first=True,
    )
    acc, face, near, far, y1_corner = call(
        functools.partial(second_corner, sz, n_mat), "second_corner", small_flops,
        [state_grid, *messages, like((4,) + sz.edge, f32)], corner_scratch,
        [parity, *state, *ends, acc, *got, corner, prod, *mats], scalar_first=True,
    )
    got, corner = exchange(face, near, far)
    prod, y2 = call(
        functools.partial(third_main, sz, n_mat), "third_main", flops,
        [products, state_grid], main_scratch,
        [parity, *state, acc, *got, y1, *mats], scalar_first=True,
    )
    filtered, face, side, rows = call(
        functools.partial(third_corner, sz, n_mat), "third_corner", small_flops,
        [
            like(own, f32), like((blocks, sz.ey) + tile, bf16), like((blocks, sz.gx) + tile, bf16),
            like((sz.edges, ez, full), bf16),
        ],
        [
            pltpu.VMEM(own, f32), pltpu.VMEM((blocks, sz.ey) + tile, bf16),
            pltpu.VMEM((blocks, sz.gx) + tile, bf16), pltpu.SemaphoreType.DMA((sz.ex + 2,)),
            pltpu.VMEM(grid, f32),
        ] + corner_scratch,
        [parity, *state, *ends, acc, *got, corner, prod, y1, y1_corner, y2, *mats],
        scalar_first=True, out_hbm=3,
    )
    give, keep = call(
        functools.partial(margin_kernel, sz, norm_scale), "margin", 2 * res_count * sz.edges * ez * full,
        [like((res_count // 2, full), bf16), like((res_count // 2, full), f32)], [],
        [parity, turned, rows], scalar_first=True,
    )

    (pieces,) = call(
        pieces_kernel, "pieces", 0, [like((nx, ny // 2, res_count // ny, full), bf16)], [],
        [keep, send_near(give)],
    )
    pieces = pieces.reshape(nx * ny // 2, -1, full)
    groups = [[a * ny + b for a in range(nx) for b in range(c, ny, 2)] for c in range(2)]
    pieces = lax.all_to_all(pieces, ("dx", "dy"), 0, 0, axis_index_groups=groups)

    side = send(side, 0, 1)
    corner = send(side[:, sz.ex :], 1, 0)
    face = send(face, 1, 0)
    filtered, margin = call(
        functools.partial(last_kernel, sz), "last", 0, [like(own, f32), like(pieces.shape[1:], f32)],
        [
            pltpu.VMEM((blocks, sz.ey) + tile, f32), pltpu.VMEM((blocks, sz.ex - 1) + tile, f32),
            pltpu.SemaphoreType.DMA((2,)),
        ],
        [filtered, face, side, corner, pieces], hbm=1, out_hbm=1, aliases={0: 0},
    )
    return (filtered, margin)


def solution(mesh):
    return jax.shard_map(
        body,
        mesh=mesh,
        in_specs=(
            P(None, "dx", "dy", None, None),
            P("dx", "dy", None, None),
            P("dx", "dy", None),
            P("dx", "dy", None),
            P(),
            P("dx", "dy", None, None),
        ),
        out_specs=(P(None, "dx", "dy", None, None), P("dy", None)),
        check_vma=False,
    )
```

```python
import functools
import math

import jax
import jax.numpy as jnp
from jax import lax
from jax.experimental import pallas as pl
from jax.experimental.pallas import tpu as pltpu
from jax.sharding import PartitionSpec as P

LANES = 128
TILE = 256
SUB = 16
VMEM_LIMIT = 16 * 1024 * 1024

center_shift = 1.2
half_width = 2.0
gain = 2.0 / half_width

f32, bf16 = jnp.float32, jnp.bfloat16


def round_up(value, step):
    return -(-value // step) * step


class Sizes:
    def __init__(self, vectors, resident, inv_mass, connectivity):
        self.blocks = vectors.shape[0]
        self.width = vectors.shape[-1]
        self.full = self.blocks * self.width
        self.res = resident.shape[-1]
        self.wide = self.full + self.width
        self.ex, self.ey, self.ez = inv_mass.shape
        self.cells, self.nodes = connectivity.shape[2:]
        self.n1 = round(self.nodes ** (1.0 / 3.0))
        self.p = self.n1 - 1
        self.cx, self.cy, self.cz = self.ex // self.p, self.ey // self.p, self.ez // self.p
        self.gx, self.gy, self.gz = self.ex + 1, self.ey + 1, self.ez
        self.edge = (self.blocks, self.ez, self.width)
        self.origins = [
            (a * self.p, b * self.p, c * self.p)
            for a in range(self.cx)
            for b in range(self.cy)
            for c in range(self.cz)
        ]
        self.most = max(len(self.cell_corners(cell)) for cell in range(self.cells))
        self.base = round_up(self.most * self.n1, 8)
        plain = self.n1 * self.n1 - min(len(self.cell_corners(cell)) for cell in range(self.cells))
        self.tail = self.base + plain * self.p
        self.rows = round_up(self.tail + plain, SUB)
        self.depth = round_up(self.rows, LANES)
        self.own_edges = self.ex * self.ey
        self.edges = round_up(self.own_edges + self.ey + self.gx, LANES // self.ez)

    def corner(self, i, j):
        if i in (0, self.ex) and j in (0, self.ey):
            return 2 * (i // self.ex) + j // self.ey
        return None

    def cell_corners(self, cell):
        x0, y0, _ = self.origins[cell]
        return [
            (i, j)
            for i in range(self.n1)
            for j in range(self.n1)
            if self.corner(x0 + i, y0 + j) is not None
        ]

    def runs(self, cell):
        corners = self.cell_corners(cell)
        place = 0
        for i in range(self.n1):
            js = [j for j in range(self.n1) if (i, j) not in corners]
            while js:
                count = 1
                while count < len(js) and js[count] == js[0] + count:
                    count += 1
                yield place, i, js[0], count
                place += count
                js = js[count:]


def send(value, steps_x, steps_y):
    nx, ny = lax.axis_size("dx"), lax.axis_size("dy")
    pairs = [
        (a * ny + b, ((a + steps_x) % nx) * ny + (b + steps_y) % ny)
        for a in range(nx)
        for b in range(ny)
    ]
    return lax.ppermute(value, ("dx", "dy"), pairs)


def swap_x(value):
    if lax.axis_size("dx") == 2:
        return send(value, 1, 0)
    return jnp.stack([send(value[0], -1, 0), send(value[1], 1, 0)])


def send_near(value):
    pairs = [(b, b + 1 if b % 2 == 0 else b - 1) for b in range(lax.axis_size("dy"))]
    return lax.ppermute(value, "dy", pairs)


def swap_y(near, far):
    ny = lax.axis_size("dy")
    far_pairs = [(b, (b - 1 if b % 2 == 0 else b + 1) % ny) for b in range(ny)]
    far = lax.ppermute(far, "dy", far_pairs)
    return send_near(near), far


def order_kernel(sz, first, matrix_ref, conn_ref, out_ref):
    for slot in range(out_ref.shape[0]):
        cell = first + slot
        x0, y0, z0 = sz.origins[cell]
        conn = conn_ref[cell : cell + 1, :].astype(f32)
        li = jnp.floor((conn + 0.5) * (1.0 / (sz.gy * sz.gz)))
        rest = conn - li * (sz.gy * sz.gz)
        lj = jnp.floor((rest + 0.5) * (1.0 / sz.gz))
        lk = rest - lj * sz.gz - z0
        lk = jnp.where(lk < 0, lk + sz.gz, lk)
        column = (li - x0) * sz.n1 + (lj - y0)
        corners = [i * sz.n1 + j for i, j in sz.cell_corners(cell)]
        place = column
        for at in corners:
            place = place - jnp.where(column > at, 1.0, 0.0)
        index = jnp.where(lk < sz.p, sz.base + place * sz.p + lk, sz.tail + place)
        for rank, at in enumerate(corners):
            special = jnp.where(lk < sz.p, rank * sz.p + lk, len(corners) * sz.p + rank)
            index = jnp.where(column == at, special, index)
        index = index.astype(jnp.int32)
        row = lax.broadcasted_iota(jnp.int32, (sz.depth, sz.nodes), 0)
        pick = (row == index).astype(f32).astype(bf16)
        half = jnp.dot(pick[: sz.rows], matrix_ref[...], preferred_element_type=f32)
        half = half.astype(bf16)
        cuts = list(range(0, sz.depth, TILE)) + [sz.depth]
        for r0, r1 in zip(cuts[:-1], cuts[1:]):
            r1 = min(r1, sz.rows)
            block = lax.dot_general(
                half[r0:r1], pick[r0:], (((1,), (1,)), ((), ())), preferred_element_type=f32
            ).astype(bf16)
            out_ref[slot, r0:r1, r0:] = block
            for c0, c1 in zip(cuts[:-1], cuts[1:]):
                if c0 > r0:
                    mirror = block[:, c0 - r0 : c1 - r0].T
                    c1 = min(c1, sz.rows)
                    out_ref[slot, c0:c1, r0:r1] = mirror[: c1 - c0]


def field_row(inv, pot):
    lane = lax.broadcasted_iota(jnp.int32, inv.shape, inv.ndim - 1)
    row = jnp.zeros_like(inv)
    for at, rest in enumerate((inv, pot)):
        for k in range(3):
            part = rest.astype(bf16).astype(f32)
            rest = rest - part
            row = jnp.where(lane == 3 * at + k, part, row)
    return row.astype(bf16)


def field_rows(sz, inv, pot, count):
    inv, pot = inv.T, pot.T
    shape = (sz.ez, sz.width)
    for at in range(count):
        yield at, field_row(
            jnp.broadcast_to(inv[:, at : at + 1], shape), jnp.broadcast_to(pot[:, at : at + 1], shape)
        )


def fields_of(row):
    row = row.astype(f32)
    return [
        jnp.broadcast_to(sum(row[:, 3 * at + k : 3 * at + k + 1] for k in range(3)), row.shape)
        for at in range(2)
    ]


def pack_kernel(
    sz, vec_hbm, res_hbm, inv_hbm, pot_hbm, conn_hbm, to_x, to_y, res_x, conn_ref, at_x, at_y, sems
):
    pairs = [
        (inv_hbm.at[0], at_x.at[0]), (pot_hbm.at[0], at_x.at[1]),
        (inv_hbm.at[:, 0], at_y.at[0]), (pot_hbm.at[:, 0], at_y.at[1]),
        (res_hbm.at[0], res_x),
        (res_hbm.at[:, 0], to_y.at[:, :, pl.ds(sz.wide, sz.res)]),
    ]
    for b in range(sz.blocks):
        lanes = pl.ds(b * sz.width, sz.width)
        pairs.append((vec_hbm.at[b, 0], to_x.at[:, :, lanes]))
        pairs.append((vec_hbm.at[b, :, 0], to_y.at[:, :, lanes]))
    pairs.append((conn_hbm, conn_ref))
    copies = [pltpu.make_async_copy(a, b, sems.at[k]) for k, (a, b) in enumerate(pairs)]
    for copy in copies:
        copy.start()
    for copy in copies[:4]:
        copy.wait()
    for j, row in field_rows(sz, at_x[0], at_x[1], sz.ey):
        to_x[j, :, sz.full : sz.wide] = row
    for i, row in field_rows(sz, at_y[0], at_y[1], sz.ex):
        to_y[i, :, sz.full : sz.wide] = row
    for copy in copies[4:]:
        copy.wait()


def turn_kernel(sz, pieces, res_ref, res_x, from_y, corner, out_ref):
    own = sz.own_edges * sz.ez
    share = sz.res // out_ref.shape[0] // pieces

    def put(g, columns, value):
        for at in range(0, LANES, share):
            owner = (g + at) // share
            row = owner // 2 * share
            out_ref[owner % 2, row : row + share, columns] = value[at : at + share]

    for g in range(0, sz.res, LANES):
        lanes = slice(g, g + LANES)
        put(g, slice(0, own), res_ref[:, lanes].T)
        rest = sz.edges - sz.own_edges - sz.ey - sz.gx
        tail = slice(sz.wide + g, sz.wide + g + LANES)
        parts = [res_x[:, :, lanes], from_y[:, :, tail], corner[:, :, tail]]
        if rest:
            parts.append(jnp.zeros((rest, sz.ez, LANES), bf16))
        ghosts = jnp.concatenate(parts, axis=0)
        put(g, slice(own, sz.edges * sz.ez), ghosts.reshape(-1, LANES).T)


def vectors_of(sz, edge):
    lanes = [slice(b * sz.width, (b + 1) * sz.width) for b in range(sz.blocks)]
    return jnp.stack([edge[:, at] for at in lanes]).astype(f32)


class Nodes:
    def __init__(self, sz, vec, from_x, from_y, own_inv, own_pot, ghost_x, ghost_y, corners=None):
        self.sz, self.vec, self.from_x, self.from_y = sz, vec, from_x, from_y
        self.own, self.ghost_x, self.ghost_y, self.corners = (own_inv, own_pot), ghost_x, ghost_y, corners

    def x(self, i, j):
        sz = self.sz
        if i < sz.ex and j < sz.ey:
            return self.vec[:, i, j].astype(f32)
        return vectors_of(sz, self.from_x[j] if i == sz.ex else self.from_y[i])

    def field(self, at, i, j):
        sz = self.sz
        if i < sz.ex and j < sz.ey:
            return self.own[at][i, j]
        if i < sz.ex:
            return self.ghost_y[at, i]
        if j < sz.ey:
            return self.ghost_x[at, j]
        return self.corners[at]

    def inv(self, i, j):
        return self.field(0, i, j)

    def pot(self, i, j):
        return self.field(1, i, j)


class Sums:
    def __init__(self, sz, even, acc, face, near, far, corner=None):
        self.sz, self.even, self.acc, self.face = sz, even, acc, face
        self.near, self.far, self.corner = near, far, corner

    def at(self, i, j):
        sz = self.sz
        total = self.acc[:, i, j]
        side = 1 if i == 0 else 0 if i == sz.ex else None
        if side is not None:
            total = total + self.face[side, :, j].astype(f32)
        if j in (0, sz.ey):
            is_near = self.even if j == sz.ey else jnp.logical_not(self.even)
            total = total + jnp.where(is_near, self.near[:, i].astype(f32), self.far[:, i].astype(f32))
            if side is not None:
                total = total + jnp.where(
                    is_near, self.corner[side, 0].astype(f32), self.corner[side, 1].astype(f32)
                )
        return total


def corner_edges(sz):
    return [(i, j) for i in (0, sz.ex) for j in (0, sz.ey)]


def main_products(sz, prepare, u_ref, mat_refs, rhs_ref, out_ref):
    width = sz.width
    flat = sz.gx * sz.gy * sz.gz
    u_flat = u_ref.reshape(sz.blocks * flat, width)
    matrices = [ref.at[c] for ref in mat_refs for c in range(ref.shape[0])]
    last = sz.nodes // 8 * 8
    ready = set()
    for cell, (x0, y0, z0) in enumerate(sz.origins):
        slot = cell % 2
        if cell < 2:
            rhs_ref[slot, : sz.base] = jnp.zeros((sz.base, sz.full), f32)
            rhs_ref[slot, last:] = jnp.zeros((sz.depth - last, sz.full), f32)
        for place, i, j, count in sz.runs(cell):
            for at in range(j, j + count):
                if (x0 + i, y0 + at) not in ready:
                    prepare(x0 + i, y0 + at)
                    ready.add((x0 + i, y0 + at))
        z1 = z0 + sz.p
        wrap = z1 % sz.gz
        for b in range(sz.blocks):
            lanes = slice(b * width, (b + 1) * width)
            for place, i, j, count in sz.runs(cell):
                row = sz.base + place * sz.p
                rhs_ref[slot, row : row + count * sz.p, lanes] = u_ref[
                    b, x0 + i, y0 + j : y0 + j + count, z0:z1
                ].reshape(count * sz.p, width)
        for b in range(sz.blocks):
            lanes = slice(b * width, (b + 1) * width)
            for place, i, j, count in sz.runs(cell):
                start = b * flat + ((x0 + i) * sz.gy + y0 + j) * sz.gz + wrap
                rhs_ref[slot, sz.tail + place : sz.tail + place + count, lanes] = u_flat[
                    pl.ds(start, count, stride=sz.gz)
                ]
        out_ref[cell] = jnp.dot(
            matrices[cell][...], rhs_ref[slot].astype(bf16), preferred_element_type=f32
        )


def corner_products(sz, u_corner, prod_ref, mat_refs, small_ref, tail_ref, acc_ref):
    width = sz.width
    flat = sz.gx * sz.gy * sz.gz
    acc_flat = acc_ref.reshape(sz.blocks * flat, width)
    matrices = [ref.at[c] for ref in mat_refs for c in range(ref.shape[0])]
    small_ref[...] = jnp.zeros_like(small_ref)
    touched = set()
    for cell, (x0, y0, z0) in enumerate(sz.origins):
        z1 = z0 + sz.p
        wrap = z1 % sz.gz
        corners = sz.cell_corners(cell)
        for rank, (i, j) in enumerate(corners):
            value = u_corner[sz.corner(x0 + i, y0 + j)]
            last = len(corners) * sz.p + rank
            for b in range(sz.blocks):
                lanes = slice(b * width, (b + 1) * width)
                small_ref[rank * sz.p : (rank + 1) * sz.p, lanes] = value[b, z0:z1]
                small_ref[last : last + 1, lanes] = value[b, wrap : wrap + 1]
        total = prod_ref[cell] + jnp.dot(
            matrices[cell][:, : small_ref.shape[0]], small_ref[...].astype(bf16),
            preferred_element_type=f32,
        )
        tail_ref[cell, : sz.base] = total[: sz.base]
        tail_ref[cell, sz.base :] = total[sz.tail :]
        spans = [(rank * sz.p, i, j, 1) for rank, (i, j) in enumerate(corners)]
        spans += [(sz.base + place * sz.p, i, j, count) for place, i, j, count in sz.runs(cell)]
        for row, i, j, count in spans:
            for at in range(count):
                part = total[row + at * sz.p : row + (at + 1) * sz.p]
                key = (x0 + i, y0 + j + at, z0)
                for b in range(sz.blocks):
                    value = part[:, b * width : (b + 1) * width]
                    if key in touched:
                        value = acc_ref[b, key[0], key[1], z0:z1] + value
                    acc_ref[b, key[0], key[1], z0:z1] = value
                touched.add(key)
    for cell, (x0, y0, z0) in enumerate(sz.origins):
        wrap = (z0 + sz.p) % sz.gz
        corners = sz.cell_corners(cell)
        spans = [(len(corners) * sz.p + rank, i, j, 1) for rank, (i, j) in enumerate(corners)]
        spans += [(sz.base + place, i, j, count) for place, i, j, count in sz.runs(cell)]
        for row, i, j, count in spans:
            for b in range(sz.blocks):
                start = b * flat + ((x0 + i) * sz.gy + y0 + j) * sz.gz + wrap
                rows = pl.ds(start, count, stride=sz.gz) if count > 1 else pl.ds(start, 1)
                lanes = slice(b * width, (b + 1) * width)
                acc_flat[rows] = acc_flat[rows] + tail_ref[cell, row : row + count, lanes]


def write_messages(sz, even, acc_ref, face, near, far):
    at_near = jnp.where(even, sz.ey, 0)
    for b in range(sz.blocks):
        face[0, b] = acc_ref[b, 0].astype(bf16)
        face[1, b] = acc_ref[b, sz.ex].astype(bf16)
        near[b] = acc_ref[b, :, at_near].astype(bf16)
        far[b] = acc_ref[b, :, sz.ey - at_near].astype(bf16)


def corner_pack_kernel(sz, near, far, out_ref):
    for side, i in enumerate((0, sz.ex)):
        for slot, ref in enumerate((near, far)):
            out_ref[side, slot] = ref[:, i]


def first_main(sz, n_mat, vec, from_x, from_y, own_inv, own_pot, *refs):
    mats = refs[:n_mat]
    prod_ref, ghost_x, ghost_y, u_ref, rhs_ref = refs[n_mat:]
    for j in range(sz.ey):
        ghost_x[0, j], ghost_x[1, j] = fields_of(from_x[j, :, sz.full : sz.wide])
    for i in range(sz.ex):
        ghost_y[0, i], ghost_y[1, i] = fields_of(from_y[i, :, sz.full : sz.wide])
    nodes = Nodes(sz, vec, from_x, from_y, own_inv, own_pot, ghost_x, ghost_y)

    def prepare(i, j):
        u_ref[:, i, j] = nodes.x(i, j) * nodes.inv(i, j)

    main_products(sz, prepare, u_ref, mats, rhs_ref, prod_ref)


def first_corner(sz, n_mat, even_ref, res_in, vec, from_x, from_y, corner, own_inv, own_pot, ghost_x,
                 ghost_y, prod_ref, *refs):
    mats = refs[:n_mat]
    res_out, acc_ref, face, near, far, last_x, last_field, small_ref, tail_ref = refs[n_mat:]
    del res_in, res_out
    last_field[0], last_field[1] = fields_of(corner[0, :, sz.full : sz.wide])
    last_x[...] = vectors_of(sz, corner[0])
    nodes = Nodes(sz, vec, from_x, from_y, own_inv, own_pot, ghost_x, ghost_y, last_field)
    u_corner = []
    for i, j in corner_edges(sz):
        x = last_x[...] if (i, j) == (sz.ex, sz.ey) else nodes.x(i, j)
        u_corner.append(x * nodes.inv(i, j))
    corner_products(sz, u_corner, prod_ref, mats, small_ref, tail_ref, acc_ref)
    write_messages(sz, even_ref[0] == 0, acc_ref, face, near, far)


def second_main(sz, n_mat, even_ref, vec, from_x, from_y, own_inv, own_pot, ghost_x, ghost_y,
                acc_in, face_in, near_in, far_in, *refs):
    mats = refs[:n_mat]
    prod_ref, y_ref, u_ref, rhs_ref = refs[n_mat:]
    nodes = Nodes(sz, vec, from_x, from_y, own_inv, own_pot, ghost_x, ghost_y)
    sums = Sums(sz, even_ref[0] == 0, acc_in, face_in, near_in, far_in)

    def prepare(i, j):
        old, inv = nodes.x(i, j), nodes.inv(i, j)
        image = inv * sums.at(i, j) + nodes.pot(i, j) * old
        new = (image - center_shift * old) / half_width
        y_ref[:, i, j] = new
        u_ref[:, i, j] = inv * new

    main_products(sz, prepare, u_ref, mats, rhs_ref, prod_ref)


def second_corner(sz, n_mat, even_ref, vec, from_x, from_y, own_inv, own_pot, ghost_x, ghost_y, last_x,
                  last_field, acc_in, face_in, near_in, far_in, corner_in, prod_ref, *refs):
    mats = refs[:n_mat]
    acc_ref, face, near, far, y_corner, small_ref, tail_ref = refs[n_mat:]
    even = even_ref[0] == 0
    nodes = Nodes(sz, vec, from_x, from_y, own_inv, own_pot, ghost_x, ghost_y, last_field)
    sums = Sums(sz, even, acc_in, face_in, near_in, far_in, corner_in)
    u_corner = []
    for at, (i, j) in enumerate(corner_edges(sz)):
        old = last_x[...] if (i, j) == (sz.ex, sz.ey) else nodes.x(i, j)
        inv = nodes.inv(i, j)
        image = inv * sums.at(i, j) + nodes.pot(i, j) * old
        new = (image - center_shift * old) / half_width
        y_corner[at] = new
        u_corner.append(inv * new)
    corner_products(sz, u_corner, prod_ref, mats, small_ref, tail_ref, acc_ref)
    write_messages(sz, even, acc_ref, face, near, far)


def third_main(sz, n_mat, even_ref, vec, from_x, from_y, own_inv, own_pot, ghost_x, ghost_y,
               acc_in, face_in, near_in, far_in, y_ref, *refs):
    mats = refs[:n_mat]
    prod_ref, new_ref, u_ref, rhs_ref = refs[n_mat:]
    nodes = Nodes(sz, vec, from_x, from_y, own_inv, own_pot, ghost_x, ghost_y)
    sums = Sums(sz, even_ref[0] == 0, acc_in, face_in, near_in, far_in)

    def prepare(i, j):
        old, inv = y_ref[:, i, j], nodes.inv(i, j)
        image = inv * sums.at(i, j) + nodes.pot(i, j) * old
        new = 2.0 * (image - center_shift * old) / half_width - nodes.x(i, j)
        new_ref[:, i, j] = new
        u_ref[:, i, j] = inv * new

    main_products(sz, prepare, u_ref, mats, rhs_ref, prod_ref)


def third_corner(sz, n_mat, norm_scale, even_ref, vec, from_x, from_y, own_inv, own_pot, ghost_x, ghost_y,
                 last_x, last_field, acc_in, face_in, near_in, far_in, corner_in, prod_ref, y_ref,
                 y_corner, new_ref, turned, *refs):
    mats = refs[:n_mat]
    out_hbm, face, side, corner, give, keep = refs[n_mat : n_mat + 6]
    part_ref, sem, acc_ref, rows_ref, small_ref, tail_ref = refs[n_mat + 6 :]
    nodes = Nodes(sz, vec, from_x, from_y, own_inv, own_pot, ghost_x, ghost_y, last_field)
    sums = Sums(sz, even_ref[0] == 0, acc_in, face_in, near_in, far_in, corner_in)
    u_corner, new_corner = [], []
    for at, (i, j) in enumerate(corner_edges(sz)):
        x = last_x[...] if (i, j) == (sz.ex, sz.ey) else nodes.x(i, j)
        old, inv = y_corner[at], nodes.inv(i, j)
        image = inv * sums.at(i, j) + nodes.pot(i, j) * old
        new_corner.append(2.0 * (image - center_shift * old) / half_width - x)
        u_corner.append(inv * new_corner[-1])
    corner_products(sz, u_corner, prod_ref, mats, small_ref, tail_ref, acc_ref)

    def put_row(at, value):
        for b in range(sz.blocks):
            rows_ref[at, :, b * sz.width : (b + 1) * sz.width] = value[b]

    copies = []
    for i in range(sz.gx):
        for j in range(sz.gy):
            acc, inv = acc_ref[:, i, j], nodes.inv(i, j)
            if i == sz.ex or j == sz.ey:
                value = gain * (inv * acc)
                rounded = value.astype(bf16)
                if j < sz.ey:
                    face[:, j] = rounded
                elif i < sz.ex:
                    side[:, i] = value
                else:
                    corner[...] = rounded
                put_row(sz.own_edges + (j if j < sz.ey else sz.ey + i), rounded)
                continue
            at = sz.corner(i, j)
            old = y_ref[:, i, j] if at is None else y_corner[at]
            new = new_ref[:, i, j] if at is None else new_corner[at]
            image = inv * acc + nodes.pot(i, j) * new
            value = 2.0 * (image - center_shift * new) / half_width - old
            part_ref[:, i, j] = value
            put_row(i * sz.ey + j, value.astype(bf16))
        if i < sz.ex:
            copies.append(pltpu.make_async_copy(part_ref.at[:, i], out_hbm.at[:, i], sem.at[i]))
            copies[-1].start()
    for at in range(sz.own_edges + sz.ey + sz.gx, sz.edges):
        rows_ref[at] = jnp.zeros((sz.ez, sz.full), bf16)
    rows = rows_ref[...].reshape(sz.edges * sz.ez, sz.full)
    mine = even_ref[0]
    for half, out in ((1 - mine, give), (mine, keep)):
        local = jnp.dot(turned[half], rows, preferred_element_type=f32)
        out[...] = (local * norm_scale).astype(out.dtype)
    for copy in copies:
        copy.wait()


def pieces_kernel(keep, taken, pieces):
    rows = pieces.shape[2]
    for at in range(pieces.shape[1]):
        span = slice(at * rows, (at + 1) * rows)
        value = (keep[span] + taken[span].astype(f32)).astype(pieces.dtype)
        for copy in range(pieces.shape[0]):
            pieces[copy, at] = value


def last_side_kernel(sz, side_ref, corner_ref, face_in, out_ref, face_out):
    del face_in, face_out
    for i in range(sz.ex):
        value = side_ref[:, i]
        if i == 0:
            value = value + corner_ref[...].astype(f32)
        out_ref[:, i] = value.astype(out_ref.dtype)


def last_kernel(sz, old_hbm, face, side, pieces, out_hbm, margin, at_x, at_y, sems):
    del old_hbm
    pairs = [(at_x, out_hbm.at[:, 0]), (at_y, out_hbm.at[:, pl.ds(1, sz.ex - 1), 0])]
    loads = [pltpu.make_async_copy(b, a, sems.at[k]) for k, (a, b) in enumerate(pairs)]
    stores = [pltpu.make_async_copy(a, b, sems.at[k]) for k, (a, b) in enumerate(pairs)]
    for copy in loads:
        copy.start()
    margin[...] = sum(pieces[at].astype(f32) for at in range(pieces.shape[0]))
    for copy in loads:
        copy.wait()
    at_x[:, 0] += side[:, 0].astype(f32)
    for j in range(sz.ey):
        at_x[:, j] += face[:, j].astype(f32)
    for i in range(1, sz.ex):
        at_y[:, i - 1] += side[:, i].astype(f32)
    for copy in stores:
        copy.start()
    for copy in stores:
        copy.wait()


def like(shape, dtype):
    return jax.ShapeDtypeStruct(shape, dtype)


def call(kernel, name, flops, out_shape, scratch, operands, hbm=0, scalar_first=False, aliases=None,
         out_hbm=0):
    out_shape = [like(s.shape, s.dtype) for s in out_shape]
    size = sum(math.prod(s.shape) * jnp.dtype(s.dtype).itemsize for s in (*operands, *out_shape))
    whole = pl.BlockSpec(memory_space=pltpu.VMEM)
    specs = [pl.BlockSpec(memory_space=pltpu.HBM)] * hbm + [whole] * (len(operands) - hbm)
    if scalar_first:
        specs[0] = pl.BlockSpec(memory_space=pltpu.SMEM)
    out_specs = [pl.BlockSpec(memory_space=pltpu.HBM)] * out_hbm + [whole] * (len(out_shape) - out_hbm)
    for source, target in (aliases or {}).items():
        if source >= hbm:
            specs[source] = out_specs[target] = pl.BlockSpec(memory_space=pl.ANY)
    out_shape = [pltpu.HBM(s.shape, s.dtype) for s in out_shape[:out_hbm]] + out_shape[out_hbm:]
    operands = [pltpu.with_memory_space_constraint(a, pltpu.HBM) for a in operands[:hbm]] + list(
        operands[hbm:]
    )
    return pl.pallas_call(
        kernel,
        in_specs=specs,
        out_specs=out_specs,
        out_shape=out_shape,
        scratch_shapes=scratch,
        input_output_aliases=aliases or {},
        compiler_params=pltpu.CompilerParams(vmem_limit_bytes=VMEM_LIMIT),
        cost_estimate=pl.CostEstimate(flops=flops, bytes_accessed=size, transcendentals=0),
        name=name,
    )(*operands)


def body(vectors, resident, inv_mass, potential, cell_matrix, connectivity):
    sz = Sizes(vectors, resident, inv_mass, connectivity)
    nx, ny = lax.axis_size("dx"), lax.axis_size("dy")
    norm_scale = 1.0 / math.sqrt(sz.ex * sz.ey * sz.ez * nx * ny)
    blocks, ez, width, full = sz.blocks, sz.ez, sz.width, sz.full
    res_count = resident.shape[-1]
    tile = (ez, width)

    conn = connectivity.reshape(sz.cells, sz.nodes)
    to_x, to_y, res_x, conn = call(
        functools.partial(pack_kernel, sz), "pack", 0,
        [
            like((sz.ey, ez, sz.wide), bf16), like((sz.ex, ez, sz.wide + sz.res), bf16),
            like((sz.ey, ez, sz.res), bf16), conn,
        ],
        [
            pltpu.VMEM((2, sz.ey, ez), f32), pltpu.VMEM((2, sz.ex, ez), f32),
            pltpu.SemaphoreType.DMA((7 + 2 * blocks,)),
        ],
        [vectors, resident, inv_mass, potential, conn], hbm=5,
    )
    from_x = send(to_x, -1, 0)
    from_y = send(to_y, 0, -1)
    res_x = send(res_x, -1, 0)

    halves = 2 if sz.cells % 2 == 0 else 1
    step = sz.cells // halves
    mats = []
    for at in range(0, sz.cells, step):
        mats += call(
            functools.partial(order_kernel, sz, at), "order_cells", 4 * step * sz.depth**3,
            [like((step, sz.rows, sz.depth), bf16)],
            [], [cell_matrix, conn],
        )
    own_inv = jnp.broadcast_to(inv_mass[..., None], inv_mass.shape + (width,))
    own_pot = jnp.broadcast_to(potential[..., None], inv_mass.shape + (width,))
    parity = jnp.reshape(lax.axis_index("dy") % 2, (1,)).astype(jnp.int32)
    ghost_corner = send(from_y[:1], -1, 0)

    grid = (blocks, sz.gx, sz.gy) + tile
    own = (blocks, sz.ex, sz.ey) + tile
    products = like((sz.cells, sz.rows, full), f32)
    state_grid = like(grid, f32)
    messages = [
        like((2, blocks, sz.gy) + tile, bf16),
        like((blocks, sz.gx) + tile, bf16),
        like((blocks, sz.gx) + tile, bf16),
    ]
    main_scratch = [pltpu.VMEM(grid, f32), pltpu.VMEM((2, sz.depth, full), f32)]
    corner_scratch = [
        pltpu.VMEM((LANES, full), f32),
        pltpu.VMEM((sz.cells, sz.base + sz.rows - sz.tail, full), f32),
    ]
    n_mat = len(mats)
    flops = 2 * sz.cells * sz.rows * sz.depth * full
    small_flops = 2 * sz.cells * sz.rows * LANES * full

    def exchange(face, near, far):
        face = swap_x(face)
        near, far = swap_y(near, far)
        (corner,) = call(
            functools.partial(corner_pack_kernel, sz), "corner_pack", 0,
            [like((2, 2) + sz.edge, bf16)], [], [near, far],
        )
        return [face, near, far], swap_x(corner)

    prod, ghost_x, ghost_y = call(
        functools.partial(first_main, sz, n_mat), "first_main", flops,
        [products, like((2, sz.ey) + tile, f32), like((2, sz.ex) + tile, f32)], main_scratch,
        [vectors, from_x, from_y, own_inv, own_pot, *mats],
    )
    res_x, acc, face, near, far, last_x, last_field = call(
        functools.partial(first_corner, sz, n_mat), "first_corner", small_flops,
        [res_x, state_grid, *messages, like(sz.edge, f32), like((2,) + tile, f32)], corner_scratch,
        [
            parity, res_x, vectors, from_x, from_y, ghost_corner, own_inv, own_pot, ghost_x, ghost_y, prod,
            *mats,
        ],
        scalar_first=True, aliases={1: 0},
    )
    (turned,) = call(
        functools.partial(turn_kernel, sz, ny // 2), "turn_residents", flops // 2,
        [like((2, res_count // 2, sz.edges * ez), bf16)], [],
        [resident.reshape(-1, res_count), res_x, from_y, ghost_corner],
    )
    got, corner = exchange(face, near, far)
    state = [vectors, from_x, from_y, own_inv, own_pot, ghost_x, ghost_y]
    ends = [last_x, last_field]
    prod, y1 = call(
        functools.partial(second_main, sz, n_mat), "second_main", flops,
        [products, state_grid], main_scratch,
        [parity, *state, acc, *got, *mats], scalar_first=True,
    )
    acc, face, near, far, y1_corner = call(
        functools.partial(second_corner, sz, n_mat), "second_corner", small_flops,
        [state_grid, *messages, like((4,) + sz.edge, f32)], corner_scratch,
        [parity, *state, *ends, acc, *got, corner, prod, *mats], scalar_first=True,
    )
    got, corner = exchange(face, near, far)
    prod, y2 = call(
        functools.partial(third_main, sz, n_mat), "third_main", flops,
        [products, state_grid], main_scratch,
        [parity, *state, acc, *got, y1, *mats], scalar_first=True,
    )
    filtered, face, side, corner, give, keep = call(
        functools.partial(third_corner, sz, n_mat, norm_scale), "third_corner",
        small_flops + 2 * res_count * sz.edges * ez * full,
        [
            like(own, f32), like((blocks, sz.ey) + tile, bf16), like((blocks, sz.ex) + tile, f32),
            like(sz.edge, bf16), like((res_count // 2, full), bf16), like((res_count // 2, full), f32),
        ],
        [
            pltpu.VMEM(own, f32), pltpu.SemaphoreType.DMA((sz.ex,)), pltpu.VMEM(grid, f32),
            pltpu.VMEM((sz.edges, ez, full), bf16),
        ] + corner_scratch,
        [parity, *state, *ends, acc, *got, corner, prod, y1, y1_corner, y2, turned, *mats],
        scalar_first=True, out_hbm=1,
    )

    (pieces,) = call(
        pieces_kernel, "pieces", 0, [like((nx, ny // 2, res_count // ny, full), bf16)], [],
        [keep, send_near(give)],
    )
    pieces = pieces.reshape(nx * ny // 2, -1, full)
    groups = [[a * ny + b for a in range(nx) for b in range(c, ny, 2)] for c in range(2)]
    pieces = lax.all_to_all(pieces, ("dx", "dy"), 0, 0, axis_index_groups=groups)

    corner = send(corner, 1, 0)
    side, face = call(
        functools.partial(last_side_kernel, sz), "last_side", 0,
        [like((blocks, sz.ex) + tile, bf16), face], [], [side, corner, face], aliases={2: 1},
    )
    face = send(face, 1, 0)
    side = send(side, 0, 1)
    filtered, margin = call(
        functools.partial(last_kernel, sz), "last", 0, [like(own, f32), like(pieces.shape[1:], f32)],
        [
            pltpu.VMEM((blocks, sz.ey) + tile, f32), pltpu.VMEM((blocks, sz.ex - 1) + tile, f32),
            pltpu.SemaphoreType.DMA((2,)),
        ],
        [filtered, face, side, pieces], hbm=1, out_hbm=1, aliases={0: 0},
    )
    return (filtered, margin)


def solution(mesh):
    return jax.shard_map(
        body,
        mesh=mesh,
        in_specs=(
            P(None, "dx", "dy", None, None),
            P("dx", "dy", None, None),
            P("dx", "dy", None),
            P("dx", "dy", None),
            P(),
            P("dx", "dy", None, None),
        ),
        out_specs=(P(None, "dx", "dy", None, None), P("dy", None)),
        check_vma=False,
    )
```

```python
import functools
import math

import jax
import jax.numpy as jnp
from jax import lax
from jax.experimental import pallas as pl
from jax.experimental.pallas import tpu as pltpu
from jax.sharding import PartitionSpec as P

LANES = 128
TILE = 256
SUB = 16
VMEM_LIMIT = 16 * 1024 * 1024

center_shift = 1.2
half_width = 2.0
gain = 2.0 / half_width

f32, bf16 = jnp.float32, jnp.bfloat16


def round_up(value, step):
    return -(-value // step) * step


class Sizes:
    def __init__(self, vectors, resident, inv_mass, connectivity):
        self.blocks = vectors.shape[0]
        self.width = vectors.shape[-1]
        self.full = self.blocks * self.width
        self.res = resident.shape[-1]
        self.wide = self.full + self.width
        self.ex, self.ey, self.ez = inv_mass.shape
        self.cells, self.nodes = connectivity.shape[2:]
        self.n1 = round(self.nodes ** (1.0 / 3.0))
        self.p = self.n1 - 1
        self.cx, self.cy, self.cz = self.ex // self.p, self.ey // self.p, self.ez // self.p
        self.gx, self.gy, self.gz = self.ex + 1, self.ey + 1, self.ez
        self.edge = (self.blocks, self.ez, self.width)
        self.origins = [
            (a * self.p, b * self.p, c * self.p)
            for a in range(self.cx)
            for b in range(self.cy)
            for c in range(self.cz)
        ]
        self.most = max(len(self.cell_corners(cell)) for cell in range(self.cells))
        self.base = round_up(self.most * self.n1, 8)
        plain = self.n1 * self.n1 - min(len(self.cell_corners(cell)) for cell in range(self.cells))
        self.tail = self.base + plain * self.p
        self.rows = round_up(self.tail + plain, SUB)
        self.depth = round_up(self.rows, LANES)
        self.own_edges = self.ex * self.ey
        self.edges = round_up(self.own_edges + self.ey + self.gx, LANES // self.ez)

    def corner(self, i, j):
        if i in (0, self.ex) and j in (0, self.ey):
            return 2 * (i // self.ex) + j // self.ey
        return None

    def cell_corners(self, cell):
        x0, y0, _ = self.origins[cell]
        return [
            (i, j)
            for i in range(self.n1)
            for j in range(self.n1)
            if self.corner(x0 + i, y0 + j) is not None
        ]

    def runs(self, cell):
        corners = self.cell_corners(cell)
        place = 0
        for i in range(self.n1):
            js = [j for j in range(self.n1) if (i, j) not in corners]
            while js:
                count = 1
                while count < len(js) and js[count] == js[0] + count:
                    count += 1
                yield place, i, js[0], count
                place += count
                js = js[count:]


def send(value, steps_x, steps_y):
    nx, ny = lax.axis_size("dx"), lax.axis_size("dy")
    pairs = [
        (a * ny + b, ((a + steps_x) % nx) * ny + (b + steps_y) % ny)
        for a in range(nx)
        for b in range(ny)
    ]
    return lax.ppermute(value, ("dx", "dy"), pairs)


def swap_x(value):
    if lax.axis_size("dx") == 2:
        return send(value, 1, 0)
    return jnp.stack([send(value[0], -1, 0), send(value[1], 1, 0)])


def swap_bit(value, bit):
    pairs = [(b, b ^ (1 << bit)) for b in range(lax.axis_size("dy"))]
    return lax.ppermute(value, "dy", pairs)


def swap_y(near, far):
    ny = lax.axis_size("dy")
    far_pairs = [(b, (b - 1 if b % 2 == 0 else b + 1) % ny) for b in range(ny)]
    far = lax.ppermute(far, "dy", far_pairs)
    return swap_bit(near, 0), far


def order_kernel(sz, first, matrix_ref, conn_ref, out_ref):
    for slot in range(out_ref.shape[0]):
        cell = first + slot
        x0, y0, z0 = sz.origins[cell]
        conn = conn_ref[cell : cell + 1, :].astype(f32)
        li = jnp.floor((conn + 0.5) * (1.0 / (sz.gy * sz.gz)))
        rest = conn - li * (sz.gy * sz.gz)
        lj = jnp.floor((rest + 0.5) * (1.0 / sz.gz))
        lk = rest - lj * sz.gz - z0
        lk = jnp.where(lk < 0, lk + sz.gz, lk)
        column = (li - x0) * sz.n1 + (lj - y0)
        corners = [i * sz.n1 + j for i, j in sz.cell_corners(cell)]
        place = column
        for at in corners:
            place = place - jnp.where(column > at, 1.0, 0.0)
        index = jnp.where(lk < sz.p, sz.base + place * sz.p + lk, sz.tail + place)
        for rank, at in enumerate(corners):
            special = jnp.where(lk < sz.p, rank * sz.p + lk, len(corners) * sz.p + rank)
            index = jnp.where(column == at, special, index)
        index = index.astype(jnp.int32)
        row = lax.broadcasted_iota(jnp.int32, (sz.depth, sz.nodes), 0)
        pick = (row == index).astype(f32).astype(bf16)
        half = jnp.dot(pick[: sz.rows], matrix_ref[...], preferred_element_type=f32)
        half = half.astype(bf16)
        cuts = list(range(0, sz.depth, TILE)) + [sz.depth]
        for r0, r1 in zip(cuts[:-1], cuts[1:]):
            r1 = min(r1, sz.rows)
            block = lax.dot_general(
                half[r0:r1], pick[r0:], (((1,), (1,)), ((), ())), preferred_element_type=f32
            ).astype(bf16)
            out_ref[slot, r0:r1, r0:] = block
            for c0, c1 in zip(cuts[:-1], cuts[1:]):
                if c0 > r0:
                    mirror = block[:, c0 - r0 : c1 - r0].T
                    c1 = min(c1, sz.rows)
                    out_ref[slot, c0:c1, r0:r1] = mirror[: c1 - c0]


def field_row(inv, pot):
    lane = lax.broadcasted_iota(jnp.int32, inv.shape, inv.ndim - 1)
    row = jnp.zeros_like(inv)
    for at, rest in enumerate((inv, pot)):
        for k in range(3):
            part = rest.astype(bf16).astype(f32)
            rest = rest - part
            row = jnp.where(lane == 3 * at + k, part, row)
    return row.astype(bf16)


def field_rows(sz, inv, pot, count):
    inv, pot = inv.T, pot.T
    shape = (sz.ez, sz.width)
    for at in range(count):
        yield at, field_row(
            jnp.broadcast_to(inv[:, at : at + 1], shape), jnp.broadcast_to(pot[:, at : at + 1], shape)
        )


def fields_of(row):
    row = row.astype(f32)
    return [
        jnp.broadcast_to(sum(row[:, 3 * at + k : 3 * at + k + 1] for k in range(3)), row.shape)
        for at in range(2)
    ]


def pack_kernel(
    sz, vec_hbm, res_hbm, inv_hbm, pot_hbm, conn_hbm, to_x, to_y, res_x, conn_ref, at_x, at_y, sems
):
    pairs = [
        (inv_hbm.at[0], at_x.at[0]), (pot_hbm.at[0], at_x.at[1]),
        (inv_hbm.at[:, 0], at_y.at[0]), (pot_hbm.at[:, 0], at_y.at[1]),
        (res_hbm.at[0], res_x),
        (res_hbm.at[:, 0], to_y.at[:, :, pl.ds(sz.wide, sz.res)]),
    ]
    for b in range(sz.blocks):
        lanes = pl.ds(b * sz.width, sz.width)
        pairs.append((vec_hbm.at[b, 0], to_x.at[:, :, lanes]))
        pairs.append((vec_hbm.at[b, :, 0], to_y.at[:, :, lanes]))
    pairs.append((conn_hbm, conn_ref))
    copies = [pltpu.make_async_copy(a, b, sems.at[k]) for k, (a, b) in enumerate(pairs)]
    for copy in copies:
        copy.start()
    for copy in copies[:4]:
        copy.wait()
    for j, row in field_rows(sz, at_x[0], at_x[1], sz.ey):
        to_x[j, :, sz.full : sz.wide] = row
    for i, row in field_rows(sz, at_y[0], at_y[1], sz.ex):
        to_y[i, :, sz.full : sz.wide] = row
    for copy in copies[4:]:
        copy.wait()


def reversed_bits(value, count):
    out = 0
    while count > 1:
        out, value, count = 2 * out + value % 2, value // 2, count // 2
    return out


def turn_kernel(sz, owners, res_ref, res_x, from_y, corner, out_ref):
    own = sz.own_edges * sz.ez
    half = owners // 2
    share = sz.res // owners

    def put(g, columns, value):
        for at in range(0, LANES, share):
            place = reversed_bits((g + at) // share, owners)
            row = place % half * share
            out_ref[place // half, row : row + share, columns] = value[at : at + share]

    for g in range(0, sz.res, LANES):
        lanes = slice(g, g + LANES)
        put(g, slice(0, own), res_ref[:, lanes].T)
        rest = sz.edges - sz.own_edges - sz.ey - sz.gx
        tail = slice(sz.wide + g, sz.wide + g + LANES)
        parts = [res_x[:, :, lanes], from_y[:, :, tail], corner[:, :, tail]]
        if rest:
            parts.append(jnp.zeros((rest, sz.ez, LANES), bf16))
        ghosts = jnp.concatenate(parts, axis=0)
        put(g, slice(own, sz.edges * sz.ez), ghosts.reshape(-1, LANES).T)


def vectors_of(sz, edge):
    lanes = [slice(b * sz.width, (b + 1) * sz.width) for b in range(sz.blocks)]
    return jnp.stack([edge[:, at] for at in lanes]).astype(f32)


class Nodes:
    def __init__(self, sz, vec, from_x, from_y, own_inv, own_pot, ghost_x, ghost_y, corners=None):
        self.sz, self.vec, self.from_x, self.from_y = sz, vec, from_x, from_y
        self.own, self.ghost_x, self.ghost_y, self.corners = (own_inv, own_pot), ghost_x, ghost_y, corners

    def x(self, i, j):
        sz = self.sz
        if i < sz.ex and j < sz.ey:
            return self.vec[:, i, j].astype(f32)
        return vectors_of(sz, self.from_x[j] if i == sz.ex else self.from_y[i])

    def field(self, at, i, j):
        sz = self.sz
        if i < sz.ex and j < sz.ey:
            return self.own[at][i, j]
        if i < sz.ex:
            return self.ghost_y[at, i]
        if j < sz.ey:
            return self.ghost_x[at, j]
        return self.corners[at]

    def inv(self, i, j):
        return self.field(0, i, j)

    def pot(self, i, j):
        return self.field(1, i, j)


class Sums:
    def __init__(self, sz, even, acc, face, near, far, corner=None):
        self.sz, self.even, self.acc, self.face = sz, even, acc, face
        self.near, self.far, self.corner = near, far, corner

    def at(self, i, j):
        sz = self.sz
        total = self.acc[:, i, j]
        side = 1 if i == 0 else 0 if i == sz.ex else None
        if side is not None:
            total = total + self.face[side, :, j].astype(f32)
        if j in (0, sz.ey):
            is_near = self.even if j == sz.ey else jnp.logical_not(self.even)
            total = total + jnp.where(is_near, self.near[:, i].astype(f32), self.far[:, i].astype(f32))
            if side is not None:
                total = total + jnp.where(
                    is_near, self.corner[side, 0].astype(f32), self.corner[side, 1].astype(f32)
                )
        return total


def corner_edges(sz):
    return [(i, j) for i in (0, sz.ex) for j in (0, sz.ey)]


def main_products(sz, prepare, u_ref, mat_refs, rhs_ref, out_ref):
    width = sz.width
    flat = sz.gx * sz.gy * sz.gz
    u_flat = u_ref.reshape(sz.blocks * flat, width)
    matrices = [ref.at[c] for ref in mat_refs for c in range(ref.shape[0])]
    last = sz.nodes // 8 * 8
    ready = set()
    for cell, (x0, y0, z0) in enumerate(sz.origins):
        slot = cell % 2
        if cell < 2:
            rhs_ref[slot, : sz.base] = jnp.zeros((sz.base, sz.full), f32)
            rhs_ref[slot, last:] = jnp.zeros((sz.depth - last, sz.full), f32)
        for place, i, j, count in sz.runs(cell):
            for at in range(j, j + count):
                if (x0 + i, y0 + at) not in ready:
                    prepare(x0 + i, y0 + at)
                    ready.add((x0 + i, y0 + at))
        z1 = z0 + sz.p
        wrap = z1 % sz.gz
        for b in range(sz.blocks):
            lanes = slice(b * width, (b + 1) * width)
            for place, i, j, count in sz.runs(cell):
                row = sz.base + place * sz.p
                rhs_ref[slot, row : row + count * sz.p, lanes] = u_ref[
                    b, x0 + i, y0 + j : y0 + j + count, z0:z1
                ].reshape(count * sz.p, width)
        for b in range(sz.blocks):
            lanes = slice(b * width, (b + 1) * width)
            for place, i, j, count in sz.runs(cell):
                start = b * flat + ((x0 + i) * sz.gy + y0 + j) * sz.gz + wrap
                rhs_ref[slot, sz.tail + place : sz.tail + place + count, lanes] = u_flat[
                    pl.ds(start, count, stride=sz.gz)
                ]
        out_ref[cell] = jnp.dot(
            matrices[cell][...], rhs_ref[slot].astype(bf16), preferred_element_type=f32
        )


def corner_products(sz, u_corner, prod_ref, mat_refs, small_ref, tail_ref, acc_ref):
    width = sz.width
    flat = sz.gx * sz.gy * sz.gz
    acc_flat = acc_ref.reshape(sz.blocks * flat, width)
    matrices = [ref.at[c] for ref in mat_refs for c in range(ref.shape[0])]
    small_ref[...] = jnp.zeros_like(small_ref)
    touched = set()
    for cell, (x0, y0, z0) in enumerate(sz.origins):
        z1 = z0 + sz.p
        wrap = z1 % sz.gz
        corners = sz.cell_corners(cell)
        for rank, (i, j) in enumerate(corners):
            value = u_corner[sz.corner(x0 + i, y0 + j)]
            last = len(corners) * sz.p + rank
            for b in range(sz.blocks):
                lanes = slice(b * width, (b + 1) * width)
                small_ref[rank * sz.p : (rank + 1) * sz.p, lanes] = value[b, z0:z1]
                small_ref[last : last + 1, lanes] = value[b, wrap : wrap + 1]
        total = prod_ref[cell] + jnp.dot(
            matrices[cell][:, : small_ref.shape[0]], small_ref[...].astype(bf16),
            preferred_element_type=f32,
        )
        tail_ref[cell, : sz.base] = total[: sz.base]
        tail_ref[cell, sz.base :] = total[sz.tail :]
        spans = [(rank * sz.p, i, j, 1) for rank, (i, j) in enumerate(corners)]
        spans += [(sz.base + place * sz.p, i, j, count) for place, i, j, count in sz.runs(cell)]
        for row, i, j, count in spans:
            for at in range(count):
                part = total[row + at * sz.p : row + (at + 1) * sz.p]
                key = (x0 + i, y0 + j + at, z0)
                for b in range(sz.blocks):
                    value = part[:, b * width : (b + 1) * width]
                    if key in touched:
                        value = acc_ref[b, key[0], key[1], z0:z1] + value
                    acc_ref[b, key[0], key[1], z0:z1] = value
                touched.add(key)
    for cell, (x0, y0, z0) in enumerate(sz.origins):
        wrap = (z0 + sz.p) % sz.gz
        corners = sz.cell_corners(cell)
        spans = [(len(corners) * sz.p + rank, i, j, 1) for rank, (i, j) in enumerate(corners)]
        spans += [(sz.base + place, i, j, count) for place, i, j, count in sz.runs(cell)]
        for row, i, j, count in spans:
            for b in range(sz.blocks):
                start = b * flat + ((x0 + i) * sz.gy + y0 + j) * sz.gz + wrap
                rows = pl.ds(start, count, stride=sz.gz) if count > 1 else pl.ds(start, 1)
                lanes = slice(b * width, (b + 1) * width)
                acc_flat[rows] = acc_flat[rows] + tail_ref[cell, row : row + count, lanes]


def write_messages(sz, even, acc_ref, face, near, far):
    at_near = jnp.where(even, sz.ey, 0)
    for b in range(sz.blocks):
        face[0, b] = acc_ref[b, 0].astype(bf16)
        face[1, b] = acc_ref[b, sz.ex].astype(bf16)
        near[b] = acc_ref[b, :, at_near].astype(bf16)
        far[b] = acc_ref[b, :, sz.ey - at_near].astype(bf16)


def corner_pack_kernel(sz, near, far, out_ref):
    for side, i in enumerate((0, sz.ex)):
        for slot, ref in enumerate((near, far)):
            out_ref[side, slot] = ref[:, i]


def first_main(sz, n_mat, vec, from_x, from_y, own_inv, own_pot, *refs):
    mats = refs[:n_mat]
    prod_ref, ghost_x, ghost_y, u_ref, rhs_ref = refs[n_mat:]
    for j in range(sz.ey):
        ghost_x[0, j], ghost_x[1, j] = fields_of(from_x[j, :, sz.full : sz.wide])
    for i in range(sz.ex):
        ghost_y[0, i], ghost_y[1, i] = fields_of(from_y[i, :, sz.full : sz.wide])
    nodes = Nodes(sz, vec, from_x, from_y, own_inv, own_pot, ghost_x, ghost_y)

    def prepare(i, j):
        u_ref[:, i, j] = nodes.x(i, j) * nodes.inv(i, j)

    main_products(sz, prepare, u_ref, mats, rhs_ref, prod_ref)


def first_corner(sz, n_mat, even_ref, res_in, vec, from_x, from_y, corner, own_inv, own_pot, ghost_x,
                 ghost_y, prod_ref, *refs):
    mats = refs[:n_mat]
    res_out, acc_ref, face, near, far, last_x, last_field, small_ref, tail_ref = refs[n_mat:]
    del res_in, res_out
    last_field[0], last_field[1] = fields_of(corner[0, :, sz.full : sz.wide])
    last_x[...] = vectors_of(sz, corner[0])
    nodes = Nodes(sz, vec, from_x, from_y, own_inv, own_pot, ghost_x, ghost_y, last_field)
    u_corner = []
    for i, j in corner_edges(sz):
        x = last_x[...] if (i, j) == (sz.ex, sz.ey) else nodes.x(i, j)
        u_corner.append(x * nodes.inv(i, j))
    corner_products(sz, u_corner, prod_ref, mats, small_ref, tail_ref, acc_ref)
    write_messages(sz, even_ref[0] == 0, acc_ref, face, near, far)


def second_main(sz, n_mat, even_ref, vec, from_x, from_y, own_inv, own_pot, ghost_x, ghost_y,
                acc_in, face_in, near_in, far_in, *refs):
    mats = refs[:n_mat]
    prod_ref, y_ref, u_ref, rhs_ref = refs[n_mat:]
    nodes = Nodes(sz, vec, from_x, from_y, own_inv, own_pot, ghost_x, ghost_y)
    sums = Sums(sz, even_ref[0] == 0, acc_in, face_in, near_in, far_in)

    def prepare(i, j):
        old, inv = nodes.x(i, j), nodes.inv(i, j)
        image = inv * sums.at(i, j) + nodes.pot(i, j) * old
        new = (image - center_shift * old) / half_width
        y_ref[:, i, j] = new
        u_ref[:, i, j] = inv * new

    main_products(sz, prepare, u_ref, mats, rhs_ref, prod_ref)


def second_corner(sz, n_mat, even_ref, vec, from_x, from_y, own_inv, own_pot, ghost_x, ghost_y, last_x,
                  last_field, acc_in, face_in, near_in, far_in, corner_in, prod_ref, *refs):
    mats = refs[:n_mat]
    acc_ref, face, near, far, y_corner, small_ref, tail_ref = refs[n_mat:]
    even = even_ref[0] == 0
    nodes = Nodes(sz, vec, from_x, from_y, own_inv, own_pot, ghost_x, ghost_y, last_field)
    sums = Sums(sz, even, acc_in, face_in, near_in, far_in, corner_in)
    u_corner = []
    for at, (i, j) in enumerate(corner_edges(sz)):
        old = last_x[...] if (i, j) == (sz.ex, sz.ey) else nodes.x(i, j)
        inv = nodes.inv(i, j)
        image = inv * sums.at(i, j) + nodes.pot(i, j) * old
        new = (image - center_shift * old) / half_width
        y_corner[at] = new
        u_corner.append(inv * new)
    corner_products(sz, u_corner, prod_ref, mats, small_ref, tail_ref, acc_ref)
    write_messages(sz, even, acc_ref, face, near, far)


def third_main(sz, n_mat, even_ref, vec, from_x, from_y, own_inv, own_pot, ghost_x, ghost_y,
               acc_in, face_in, near_in, far_in, y_ref, *refs):
    mats = refs[:n_mat]
    prod_ref, new_ref, u_ref, rhs_ref = refs[n_mat:]
    nodes = Nodes(sz, vec, from_x, from_y, own_inv, own_pot, ghost_x, ghost_y)
    sums = Sums(sz, even_ref[0] == 0, acc_in, face_in, near_in, far_in)

    def prepare(i, j):
        old, inv = y_ref[:, i, j], nodes.inv(i, j)
        image = inv * sums.at(i, j) + nodes.pot(i, j) * old
        new = 2.0 * (image - center_shift * old) / half_width - nodes.x(i, j)
        new_ref[:, i, j] = new
        u_ref[:, i, j] = inv * new

    main_products(sz, prepare, u_ref, mats, rhs_ref, prod_ref)


def third_corner(sz, n_mat, norm_scale, even_ref, vec, from_x, from_y, own_inv, own_pot, ghost_x, ghost_y,
                 last_x, last_field, acc_in, face_in, near_in, far_in, corner_in, prod_ref, y_ref,
                 y_corner, new_ref, turned, *refs):
    mats = refs[:n_mat]
    out_hbm, face, side, corner, give, keep = refs[n_mat : n_mat + 6]
    part_ref, sem, acc_ref, rows_ref, small_ref, tail_ref = refs[n_mat + 6 :]
    nodes = Nodes(sz, vec, from_x, from_y, own_inv, own_pot, ghost_x, ghost_y, last_field)
    sums = Sums(sz, even_ref[0] == 0, acc_in, face_in, near_in, far_in, corner_in)
    u_corner, new_corner = [], []
    for at, (i, j) in enumerate(corner_edges(sz)):
        x = last_x[...] if (i, j) == (sz.ex, sz.ey) else nodes.x(i, j)
        old, inv = y_corner[at], nodes.inv(i, j)
        image = inv * sums.at(i, j) + nodes.pot(i, j) * old
        new_corner.append(2.0 * (image - center_shift * old) / half_width - x)
        u_corner.append(inv * new_corner[-1])
    corner_products(sz, u_corner, prod_ref, mats, small_ref, tail_ref, acc_ref)

    def put_row(at, value):
        for b in range(sz.blocks):
            rows_ref[at, :, b * sz.width : (b + 1) * sz.width] = value[b]

    copies = []
    for i in range(sz.gx):
        for j in range(sz.gy):
            acc, inv = acc_ref[:, i, j], nodes.inv(i, j)
            if i == sz.ex or j == sz.ey:
                value = gain * (inv * acc)
                rounded = value.astype(bf16)
                if j < sz.ey:
                    face[:, j] = rounded
                elif i < sz.ex:
                    side[:, i] = value
                else:
                    corner[...] = rounded
                put_row(sz.own_edges + (j if j < sz.ey else sz.ey + i), rounded)
                continue
            at = sz.corner(i, j)
            old = y_ref[:, i, j] if at is None else y_corner[at]
            new = new_ref[:, i, j] if at is None else new_corner[at]
            image = inv * acc + nodes.pot(i, j) * new
            value = 2.0 * (image - center_shift * new) / half_width - old
            part_ref[:, i, j] = value
            put_row(i * sz.ey + j, value.astype(bf16))
        if i < sz.ex:
            copies.append(pltpu.make_async_copy(part_ref.at[:, i], out_hbm.at[:, i], sem.at[i]))
            copies[-1].start()
    for at in range(sz.own_edges + sz.ey + sz.gx, sz.edges):
        rows_ref[at] = jnp.zeros((sz.ez, sz.full), bf16)
    rows = rows_ref[...].reshape(sz.edges * sz.ez, sz.full)
    mine = even_ref[0]
    for half, out in ((1 - mine, give), (mine, keep)):
        local = jnp.dot(turned[half], rows, preferred_element_type=f32)
        out[...] = (local * norm_scale).astype(out.dtype)
    for copy in copies:
        copy.wait()


def halve_kernel(bit_ref, keep, taken, give, left):
    mine = bit_ref[0]
    give[...] = (keep[1 - mine] + taken[1 - mine].astype(f32)).astype(give.dtype)
    left[...] = keep[mine] + taken[mine].astype(f32)


def last_side_kernel(sz, side_ref, corner_ref, face_in, out_ref, face_out):
    del face_in, face_out
    for i in range(sz.ex):
        value = side_ref[:, i]
        if i == 0:
            value = value + corner_ref[...].astype(f32)
        out_ref[:, i] = value.astype(out_ref.dtype)


def last_kernel(sz, old_hbm, face, side, *refs):
    del old_hbm
    sums, (out_hbm, margin, at_x, at_y, sems) = refs[:-5], refs[-5:]
    pairs = [(at_x, out_hbm.at[:, 0]), (at_y, out_hbm.at[:, pl.ds(1, sz.ex - 1), 0])]
    loads = [pltpu.make_async_copy(b, a, sems.at[k]) for k, (a, b) in enumerate(pairs)]
    stores = [pltpu.make_async_copy(a, b, sems.at[k]) for k, (a, b) in enumerate(pairs)]
    for copy in loads:
        copy.start()
    margin[...] = sum(ref[...] for ref in sums)
    for copy in loads:
        copy.wait()
    at_x[:, 0] += side[:, 0].astype(f32)
    for j in range(sz.ey):
        at_x[:, j] += face[:, j].astype(f32)
    for i in range(1, sz.ex):
        at_y[:, i - 1] += side[:, i].astype(f32)
    for copy in stores:
        copy.start()
    for copy in stores:
        copy.wait()


def like(shape, dtype):
    return jax.ShapeDtypeStruct(shape, dtype)


def call(kernel, name, flops, out_shape, scratch, operands, hbm=0, scalar_first=False, aliases=None,
         out_hbm=0):
    out_shape = [like(s.shape, s.dtype) for s in out_shape]
    size = sum(math.prod(s.shape) * jnp.dtype(s.dtype).itemsize for s in (*operands, *out_shape))
    whole = pl.BlockSpec(memory_space=pltpu.VMEM)
    specs = [pl.BlockSpec(memory_space=pltpu.HBM)] * hbm + [whole] * (len(operands) - hbm)
    if scalar_first:
        specs[0] = pl.BlockSpec(memory_space=pltpu.SMEM)
    out_specs = [pl.BlockSpec(memory_space=pltpu.HBM)] * out_hbm + [whole] * (len(out_shape) - out_hbm)
    for source, target in (aliases or {}).items():
        if source >= hbm:
            specs[source] = out_specs[target] = pl.BlockSpec(memory_space=pl.ANY)
    out_shape = [pltpu.HBM(s.shape, s.dtype) for s in out_shape[:out_hbm]] + out_shape[out_hbm:]
    operands = [pltpu.with_memory_space_constraint(a, pltpu.HBM) for a in operands[:hbm]] + list(
        operands[hbm:]
    )
    return pl.pallas_call(
        kernel,
        in_specs=specs,
        out_specs=out_specs,
        out_shape=out_shape,
        scratch_shapes=scratch,
        input_output_aliases=aliases or {},
        compiler_params=pltpu.CompilerParams(vmem_limit_bytes=VMEM_LIMIT),
        cost_estimate=pl.CostEstimate(flops=flops, bytes_accessed=size, transcendentals=0),
        name=name,
    )(*operands)


def body(vectors, resident, inv_mass, potential, cell_matrix, connectivity):
    sz = Sizes(vectors, resident, inv_mass, connectivity)
    nx, ny = lax.axis_size("dx"), lax.axis_size("dy")
    norm_scale = 1.0 / math.sqrt(sz.ex * sz.ey * sz.ez * nx * ny)
    blocks, ez, width, full = sz.blocks, sz.ez, sz.width, sz.full
    res_count = resident.shape[-1]
    tile = (ez, width)

    conn = connectivity.reshape(sz.cells, sz.nodes)
    to_x, to_y, res_x, conn = call(
        functools.partial(pack_kernel, sz), "pack", 0,
        [
            like((sz.ey, ez, sz.wide), bf16), like((sz.ex, ez, sz.wide + sz.res), bf16),
            like((sz.ey, ez, sz.res), bf16), conn,
        ],
        [
            pltpu.VMEM((2, sz.ey, ez), f32), pltpu.VMEM((2, sz.ex, ez), f32),
            pltpu.SemaphoreType.DMA((7 + 2 * blocks,)),
        ],
        [vectors, resident, inv_mass, potential, conn], hbm=5,
    )
    from_x = send(to_x, -1, 0)
    from_y = send(to_y, 0, -1)
    res_x = send(res_x, -1, 0)

    halves = 2 if sz.cells % 2 == 0 else 1
    step = sz.cells // halves
    mats = []
    for at in range(0, sz.cells, step):
        mats += call(
            functools.partial(order_kernel, sz, at), "order_cells", 4 * step * sz.depth**3,
            [like((step, sz.rows, sz.depth), bf16)],
            [], [cell_matrix, conn],
        )
    own_inv = jnp.broadcast_to(inv_mass[..., None], inv_mass.shape + (width,))
    own_pot = jnp.broadcast_to(potential[..., None], inv_mass.shape + (width,))
    parity = jnp.reshape(lax.axis_index("dy") % 2, (1,)).astype(jnp.int32)
    ghost_corner = send(from_y[:1], -1, 0)

    grid = (blocks, sz.gx, sz.gy) + tile
    own = (blocks, sz.ex, sz.ey) + tile
    products = like((sz.cells, sz.rows, full), f32)
    state_grid = like(grid, f32)
    messages = [
        like((2, blocks, sz.gy) + tile, bf16),
        like((blocks, sz.gx) + tile, bf16),
        like((blocks, sz.gx) + tile, bf16),
    ]
    main_scratch = [pltpu.VMEM(grid, f32), pltpu.VMEM((2, sz.depth, full), f32)]
    corner_scratch = [
        pltpu.VMEM((LANES, full), f32),
        pltpu.VMEM((sz.cells, sz.base + sz.rows - sz.tail, full), f32),
    ]
    n_mat = len(mats)
    flops = 2 * sz.cells * sz.rows * sz.depth * full
    small_flops = 2 * sz.cells * sz.rows * LANES * full

    def exchange(face, near, far):
        face = swap_x(face)
        near, far = swap_y(near, far)
        (corner,) = call(
            functools.partial(corner_pack_kernel, sz), "corner_pack", 0,
            [like((2, 2) + sz.edge, bf16)], [], [near, far],
        )
        return [face, near, far], swap_x(corner)

    prod, ghost_x, ghost_y = call(
        functools.partial(first_main, sz, n_mat), "first_main", flops,
        [products, like((2, sz.ey) + tile, f32), like((2, sz.ex) + tile, f32)], main_scratch,
        [vectors, from_x, from_y, own_inv, own_pot, *mats],
    )
    res_x, acc, face, near, far, last_x, last_field = call(
        functools.partial(first_corner, sz, n_mat), "first_corner", small_flops,
        [res_x, state_grid, *messages, like(sz.edge, f32), like((2,) + tile, f32)], corner_scratch,
        [
            parity, res_x, vectors, from_x, from_y, ghost_corner, own_inv, own_pot, ghost_x, ghost_y, prod,
            *mats,
        ],
        scalar_first=True, aliases={1: 0},
    )
    (turned,) = call(
        functools.partial(turn_kernel, sz, ny), "turn_residents", flops // 2,
        [like((2, res_count // 2, sz.edges * ez), bf16)], [],
        [resident.reshape(-1, res_count), res_x, from_y, ghost_corner],
    )
    got, corner = exchange(face, near, far)
    state = [vectors, from_x, from_y, own_inv, own_pot, ghost_x, ghost_y]
    ends = [last_x, last_field]
    prod, y1 = call(
        functools.partial(second_main, sz, n_mat), "second_main", flops,
        [products, state_grid], main_scratch,
        [parity, *state, acc, *got, *mats], scalar_first=True,
    )
    acc, face, near, far, y1_corner = call(
        functools.partial(second_corner, sz, n_mat), "second_corner", small_flops,
        [state_grid, *messages, like((4,) + sz.edge, f32)], corner_scratch,
        [parity, *state, *ends, acc, *got, corner, prod, *mats], scalar_first=True,
    )
    got, corner = exchange(face, near, far)
    prod, y2 = call(
        functools.partial(third_main, sz, n_mat), "third_main", flops,
        [products, state_grid], main_scratch,
        [parity, *state, acc, *got, y1, *mats], scalar_first=True,
    )
    filtered, face, side, corner, give, keep = call(
        functools.partial(third_corner, sz, n_mat, norm_scale), "third_corner",
        small_flops + 2 * res_count * sz.edges * ez * full,
        [
            like(own, f32), like((blocks, sz.ey) + tile, bf16), like((blocks, sz.ex) + tile, f32),
            like(sz.edge, bf16), like((res_count // 2, full), bf16), like((res_count // 2, full), f32),
        ],
        [
            pltpu.VMEM(own, f32), pltpu.SemaphoreType.DMA((sz.ex,)), pltpu.VMEM(grid, f32),
            pltpu.VMEM((sz.edges, ez, full), bf16),
        ] + corner_scratch,
        [parity, *state, *ends, acc, *got, corner, prod, y1, y1_corner, y2, turned, *mats],
        scalar_first=True, out_hbm=1,
    )

    taken = swap_bit(give, 0)
    for bit in range(1, (ny - 1).bit_length()):
        rows = keep.shape[0] // 2
        mine = jnp.reshape((lax.axis_index("dy") >> bit) & 1, (1,)).astype(jnp.int32)
        give, keep = call(
            halve_kernel, "halve", 0, [like((rows, full), bf16), like((rows, full), f32)], [],
            [mine, keep.reshape(2, rows, full), taken.reshape(2, rows, full)], scalar_first=True,
        )
        taken = swap_bit(give, bit)
    keep = keep + taken.astype(f32)
    sums = [keep] + [send(keep, steps, 0) for steps in range(1, nx)]

    corner = send(corner, 1, 0)
    side, face = call(
        functools.partial(last_side_kernel, sz), "last_side", 0,
        [like((blocks, sz.ex) + tile, bf16), face], [], [side, corner, face], aliases={2: 1},
    )
    face = send(face, 1, 0)
    side = send(side, 0, 1)
    filtered, margin = call(
        functools.partial(last_kernel, sz), "last", 0, [like(own, f32), like(keep.shape, f32)],
        [
            pltpu.VMEM((blocks, sz.ey) + tile, f32), pltpu.VMEM((blocks, sz.ex - 1) + tile, f32),
            pltpu.SemaphoreType.DMA((2,)),
        ],
        [filtered, face, side, *sums], hbm=1, out_hbm=1, aliases={0: 0},
    )
    return (filtered, margin)


def solution(mesh):
    return jax.shard_map(
        body,
        mesh=mesh,
        in_specs=(
            P(None, "dx", "dy", None, None),
            P("dx", "dy", None, None),
            P("dx", "dy", None),
            P("dx", "dy", None),
            P(),
            P("dx", "dy", None, None),
        ),
        out_specs=(P(None, "dx", "dy", None, None), P("dy", None)),
        check_vma=False,
    )
```

```python
import functools
import math

import jax
import jax.numpy as jnp
from jax import lax
from jax.experimental import pallas as pl
from jax.experimental.pallas import tpu as pltpu
from jax.sharding import PartitionSpec as P

LANES = 128
TILE = 256
SUB = 16
VMEM_LIMIT = 16 * 1024 * 1024

center_shift = 1.2
half_width = 2.0
gain = 2.0 / half_width

f32, bf16 = jnp.float32, jnp.bfloat16


def round_up(value, step):
    return -(-value // step) * step


class Sizes:
    def __init__(self, vectors, resident, inv_mass, connectivity):
        self.blocks = vectors.shape[0]
        self.width = vectors.shape[-1]
        self.full = self.blocks * self.width
        self.res = resident.shape[-1]
        self.wide = self.full + self.width
        self.ex, self.ey, self.ez = inv_mass.shape
        self.cells, self.nodes = connectivity.shape[2:]
        self.n1 = round(self.nodes ** (1.0 / 3.0))
        self.p = self.n1 - 1
        self.cx, self.cy, self.cz = self.ex // self.p, self.ey // self.p, self.ez // self.p
        self.gx, self.gy, self.gz = self.ex + 1, self.ey + 1, self.ez
        self.edge = (self.blocks, self.ez, self.width)
        self.origins = [
            (a * self.p, b * self.p, c * self.p)
            for a in range(self.cx)
            for b in range(self.cy)
            for c in range(self.cz)
        ]
        self.most = max(len(self.cell_corners(cell)) for cell in range(self.cells))
        self.base = round_up(self.most * self.n1, 8)
        plain = self.n1 * self.n1 - min(len(self.cell_corners(cell)) for cell in range(self.cells))
        self.tail = self.base + plain * self.p
        self.rows = round_up(self.tail + plain, SUB)
        self.depth = round_up(self.rows, LANES)
        self.own_edges = self.ex * self.ey
        self.edges = round_up(self.own_edges + self.ey + self.gx, LANES // self.ez)

    def corner(self, i, j):
        if i in (0, self.ex) and j in (0, self.ey):
            return 2 * (i // self.ex) + j // self.ey
        return None

    def cell_corners(self, cell):
        x0, y0, _ = self.origins[cell]
        return [
            (i, j)
            for i in range(self.n1)
            for j in range(self.n1)
            if self.corner(x0 + i, y0 + j) is not None
        ]

    def runs(self, cell):
        corners = self.cell_corners(cell)
        place = 0
        for i in range(self.n1):
            js = [j for j in range(self.n1) if (i, j) not in corners]
            while js:
                count = 1
                while count < len(js) and js[count] == js[0] + count:
                    count += 1
                yield place, i, js[0], count
                place += count
                js = js[count:]


def send(value, steps_x, steps_y):
    nx, ny = lax.axis_size("dx"), lax.axis_size("dy")
    pairs = [
        (a * ny + b, ((a + steps_x) % nx) * ny + (b + steps_y) % ny)
        for a in range(nx)
        for b in range(ny)
    ]
    return lax.ppermute(value, ("dx", "dy"), pairs)


def swap_x(value):
    if lax.axis_size("dx") == 2:
        return send(value, 1, 0)
    return jnp.stack([send(value[0], -1, 0), send(value[1], 1, 0)])


def send_near(value):
    pairs = [(b, b + 1 if b % 2 == 0 else b - 1) for b in range(lax.axis_size("dy"))]
    return lax.ppermute(value, "dy", pairs)


def swap_y(near, far):
    ny = lax.axis_size("dy")
    far_pairs = [(b, (b - 1 if b % 2 == 0 else b + 1) % ny) for b in range(ny)]
    far = lax.ppermute(far, "dy", far_pairs)
    return send_near(near), far


def order_kernel(sz, first, matrix_ref, conn_ref, out_ref):
    for slot in range(out_ref.shape[0]):
        cell = first + slot
        x0, y0, z0 = sz.origins[cell]
        conn = conn_ref[cell : cell + 1, :].astype(f32)
        li = jnp.floor((conn + 0.5) * (1.0 / (sz.gy * sz.gz)))
        rest = conn - li * (sz.gy * sz.gz)
        lj = jnp.floor((rest + 0.5) * (1.0 / sz.gz))
        lk = rest - lj * sz.gz - z0
        lk = jnp.where(lk < 0, lk + sz.gz, lk)
        column = (li - x0) * sz.n1 + (lj - y0)
        corners = [i * sz.n1 + j for i, j in sz.cell_corners(cell)]
        place = column
        for at in corners:
            place = place - jnp.where(column > at, 1.0, 0.0)
        index = jnp.where(lk < sz.p, sz.base + place * sz.p + lk, sz.tail + place)
        for rank, at in enumerate(corners):
            special = jnp.where(lk < sz.p, rank * sz.p + lk, len(corners) * sz.p + rank)
            index = jnp.where(column == at, special, index)
        index = index.astype(jnp.int32)
        row = lax.broadcasted_iota(jnp.int32, (sz.depth, sz.nodes), 0)
        pick = (row == index).astype(f32).astype(bf16)
        half = jnp.dot(pick[: sz.rows], matrix_ref[...], preferred_element_type=f32)
        half = half.astype(bf16)
        cuts = list(range(0, sz.depth, TILE)) + [sz.depth]
        for r0, r1 in zip(cuts[:-1], cuts[1:]):
            r1 = min(r1, sz.rows)
            block = lax.dot_general(
                half[r0:r1], pick[r0:], (((1,), (1,)), ((), ())), preferred_element_type=f32
            ).astype(bf16)
            out_ref[slot, r0:r1, r0:] = block
            for c0, c1 in zip(cuts[:-1], cuts[1:]):
                if c0 > r0:
                    mirror = block[:, c0 - r0 : c1 - r0].T
                    c1 = min(c1, sz.rows)
                    out_ref[slot, c0:c1, r0:r1] = mirror[: c1 - c0]


def field_row(inv, pot):
    lane = lax.broadcasted_iota(jnp.int32, inv.shape, inv.ndim - 1)
    row = jnp.zeros_like(inv)
    for at, rest in enumerate((inv, pot)):
        for k in range(3):
            part = rest.astype(bf16).astype(f32)
            rest = rest - part
            row = jnp.where(lane == 3 * at + k, part, row)
    return row.astype(bf16)


def field_rows(sz, inv, pot, count):
    inv, pot = inv.T, pot.T
    shape = (sz.ez, sz.width)
    for at in range(count):
        yield at, field_row(
            jnp.broadcast_to(inv[:, at : at + 1], shape), jnp.broadcast_to(pot[:, at : at + 1], shape)
        )


def fields_of(row):
    row = row.astype(f32)
    return [
        jnp.broadcast_to(sum(row[:, 3 * at + k : 3 * at + k + 1] for k in range(3)), row.shape)
        for at in range(2)
    ]


def pack_kernel(
    sz, vec_hbm, res_hbm, inv_hbm, pot_hbm, conn_hbm, to_x, to_y, res_x, conn_ref, at_x, at_y, sems
):
    pairs = [
        (inv_hbm.at[0], at_x.at[0]), (pot_hbm.at[0], at_x.at[1]),
        (inv_hbm.at[:, 0], at_y.at[0]), (pot_hbm.at[:, 0], at_y.at[1]),
        (res_hbm.at[0], res_x),
        (res_hbm.at[:, 0], to_y.at[:, :, pl.ds(sz.wide, sz.res)]),
    ]
    for b in range(sz.blocks):
        lanes = pl.ds(b * sz.width, sz.width)
        pairs.append((vec_hbm.at[b, 0], to_x.at[:, :, lanes]))
        pairs.append((vec_hbm.at[b, :, 0], to_y.at[:, :, lanes]))
    pairs.append((conn_hbm, conn_ref))
    copies = [pltpu.make_async_copy(a, b, sems.at[k]) for k, (a, b) in enumerate(pairs)]
    for copy in copies:
        copy.start()
    for copy in copies[:4]:
        copy.wait()
    for j, row in field_rows(sz, at_x[0], at_x[1], sz.ey):
        to_x[j, :, sz.full : sz.wide] = row
    for i, row in field_rows(sz, at_y[0], at_y[1], sz.ex):
        to_y[i, :, sz.full : sz.wide] = row
    for copy in copies[4:]:
        copy.wait()


def turn_kernel(sz, pieces, res_ref, res_x, from_y, corner, out_ref):
    own = sz.own_edges * sz.ez
    share = sz.res // out_ref.shape[0] // pieces

    def put(g, columns, value):
        for at in range(0, LANES, share):
            owner = (g + at) // share
            row = owner // 2 * share
            out_ref[owner % 2, row : row + share, columns] = value[at : at + share]

    for g in range(0, sz.res, LANES):
        lanes = slice(g, g + LANES)
        put(g, slice(0, own), res_ref[:, lanes].T)
        rest = sz.edges - sz.own_edges - sz.ey - sz.gx
        tail = slice(sz.wide + g, sz.wide + g + LANES)
        parts = [res_x[:, :, lanes], from_y[:, :, tail], corner[:, :, tail]]
        if rest:
            parts.append(jnp.zeros((rest, sz.ez, LANES), bf16))
        ghosts = jnp.concatenate(parts, axis=0)
        put(g, slice(own, sz.edges * sz.ez), ghosts.reshape(-1, LANES).T)


def vectors_of(sz, edge):
    lanes = [slice(b * sz.width, (b + 1) * sz.width) for b in range(sz.blocks)]
    return jnp.stack([edge[:, at] for at in lanes]).astype(f32)


class Nodes:
    def __init__(self, sz, vec, from_x, from_y, own_inv, own_pot, ghost_x, ghost_y, corners=None):
        self.sz, self.vec, self.from_x, self.from_y = sz, vec, from_x, from_y
        self.own, self.ghost_x, self.ghost_y, self.corners = (own_inv, own_pot), ghost_x, ghost_y, corners

    def x(self, i, j):
        sz = self.sz
        if i < sz.ex and j < sz.ey:
            return self.vec[:, i, j].astype(f32)
        return vectors_of(sz, self.from_x[j] if i == sz.ex else self.from_y[i])

    def field(self, at, i, j):
        sz = self.sz
        if i < sz.ex and j < sz.ey:
            return self.own[at][i, j]
        if i < sz.ex:
            return self.ghost_y[at, i]
        if j < sz.ey:
            return self.ghost_x[at, j]
        return self.corners[at]

    def inv(self, i, j):
        return self.field(0, i, j)

    def pot(self, i, j):
        return self.field(1, i, j)


class Sums:
    def __init__(self, sz, even, acc, face, near, far, corner=None):
        self.sz, self.even, self.acc, self.face = sz, even, acc, face
        self.near, self.far, self.corner = near, far, corner

    def at(self, i, j):
        sz = self.sz
        total = self.acc[:, i, j]
        side = 1 if i == 0 else 0 if i == sz.ex else None
        if side is not None:
            total = total + self.face[side, :, j].astype(f32)
        if j in (0, sz.ey):
            is_near = self.even if j == sz.ey else jnp.logical_not(self.even)
            total = total + jnp.where(is_near, self.near[:, i].astype(f32), self.far[:, i].astype(f32))
            if side is not None:
                total = total + jnp.where(
                    is_near, self.corner[side, 0].astype(f32), self.corner[side, 1].astype(f32)
                )
        return total


def corner_edges(sz):
    return [(i, j) for i in (0, sz.ex) for j in (0, sz.ey)]


def main_products(sz, prepare, u_ref, mat_refs, rhs_ref, out_ref):
    width = sz.width
    flat = sz.gx * sz.gy * sz.gz
    u_flat = u_ref.reshape(sz.blocks * flat, width)
    matrices = [ref.at[c] for ref in mat_refs for c in range(ref.shape[0])]
    last = sz.nodes // 8 * 8
    ready = set()
    for cell, (x0, y0, z0) in enumerate(sz.origins):
        slot = cell % 2
        if cell < 2:
            rhs_ref[slot, : sz.base] = jnp.zeros((sz.base, sz.full), f32)
            rhs_ref[slot, last:] = jnp.zeros((sz.depth - last, sz.full), f32)
        for place, i, j, count in sz.runs(cell):
            for at in range(j, j + count):
                if (x0 + i, y0 + at) not in ready:
                    prepare(x0 + i, y0 + at)
                    ready.add((x0 + i, y0 + at))
        z1 = z0 + sz.p
        wrap = z1 % sz.gz
        for b in range(sz.blocks):
            lanes = slice(b * width, (b + 1) * width)
            for place, i, j, count in sz.runs(cell):
                row = sz.base + place * sz.p
                rhs_ref[slot, row : row + count * sz.p, lanes] = u_ref[
                    b, x0 + i, y0 + j : y0 + j + count, z0:z1
                ].reshape(count * sz.p, width)
        for b in range(sz.blocks):
            lanes = slice(b * width, (b + 1) * width)
            for place, i, j, count in sz.runs(cell):
                start = b * flat + ((x0 + i) * sz.gy + y0 + j) * sz.gz + wrap
                rhs_ref[slot, sz.tail + place : sz.tail + place + count, lanes] = u_flat[
                    pl.ds(start, count, stride=sz.gz)
                ]
        out_ref[cell] = jnp.dot(
            matrices[cell][...], rhs_ref[slot].astype(bf16), preferred_element_type=f32
        )


def corner_products(sz, u_corner, prod_ref, mat_refs, small_ref, tail_ref, acc_ref):
    width = sz.width
    flat = sz.gx * sz.gy * sz.gz
    acc_flat = acc_ref.reshape(sz.blocks * flat, width)
    matrices = [ref.at[c] for ref in mat_refs for c in range(ref.shape[0])]
    small_ref[...] = jnp.zeros_like(small_ref)
    touched = set()
    for cell, (x0, y0, z0) in enumerate(sz.origins):
        z1 = z0 + sz.p
        wrap = z1 % sz.gz
        corners = sz.cell_corners(cell)
        for rank, (i, j) in enumerate(corners):
            value = u_corner[sz.corner(x0 + i, y0 + j)]
            last = len(corners) * sz.p + rank
            for b in range(sz.blocks):
                lanes = slice(b * width, (b + 1) * width)
                small_ref[rank * sz.p : (rank + 1) * sz.p, lanes] = value[b, z0:z1]
                small_ref[last : last + 1, lanes] = value[b, wrap : wrap + 1]
        total = prod_ref[cell] + jnp.dot(
            matrices[cell][:, : small_ref.shape[0]], small_ref[...].astype(bf16),
            preferred_element_type=f32,
        )
        tail_ref[cell, : sz.base] = total[: sz.base]
        tail_ref[cell, sz.base :] = total[sz.tail :]
        spans = [(rank * sz.p, i, j, 1) for rank, (i, j) in enumerate(corners)]
        spans += [(sz.base + place * sz.p, i, j, count) for place, i, j, count in sz.runs(cell)]
        for row, i, j, count in spans:
            for at in range(count):
                part = total[row + at * sz.p : row + (at + 1) * sz.p]
                key = (x0 + i, y0 + j + at, z0)
                for b in range(sz.blocks):
                    value = part[:, b * width : (b + 1) * width]
                    if key in touched:
                        value = acc_ref[b, key[0], key[1], z0:z1] + value
                    acc_ref[b, key[0], key[1], z0:z1] = value
                touched.add(key)
    for cell, (x0, y0, z0) in enumerate(sz.origins):
        wrap = (z0 + sz.p) % sz.gz
        corners = sz.cell_corners(cell)
        spans = [(len(corners) * sz.p + rank, i, j, 1) for rank, (i, j) in enumerate(corners)]
        spans += [(sz.base + place, i, j, count) for place, i, j, count in sz.runs(cell)]
        for row, i, j, count in spans:
            for b in range(sz.blocks):
                start = b * flat + ((x0 + i) * sz.gy + y0 + j) * sz.gz + wrap
                rows = pl.ds(start, count, stride=sz.gz) if count > 1 else pl.ds(start, 1)
                lanes = slice(b * width, (b + 1) * width)
                acc_flat[rows] = acc_flat[rows] + tail_ref[cell, row : row + count, lanes]


def write_messages(sz, even, acc_ref, face, near, far):
    at_near = jnp.where(even, sz.ey, 0)
    for b in range(sz.blocks):
        face[0, b] = acc_ref[b, 0].astype(bf16)
        face[1, b] = acc_ref[b, sz.ex].astype(bf16)
        near[b] = acc_ref[b, :, at_near].astype(bf16)
        far[b] = acc_ref[b, :, sz.ey - at_near].astype(bf16)


def corner_pack_kernel(sz, near, far, out_ref):
    for side, i in enumerate((0, sz.ex)):
        for slot, ref in enumerate((near, far)):
            out_ref[side, slot] = ref[:, i]


def first_main(sz, n_mat, vec, from_x, from_y, own_inv, own_pot, *refs):
    mats = refs[:n_mat]
    prod_ref, ghost_x, ghost_y, u_ref, rhs_ref = refs[n_mat:]
    for j in range(sz.ey):
        ghost_x[0, j], ghost_x[1, j] = fields_of(from_x[j, :, sz.full : sz.wide])
    for i in range(sz.ex):
        ghost_y[0, i], ghost_y[1, i] = fields_of(from_y[i, :, sz.full : sz.wide])
    nodes = Nodes(sz, vec, from_x, from_y, own_inv, own_pot, ghost_x, ghost_y)

    def prepare(i, j):
        u_ref[:, i, j] = nodes.x(i, j) * nodes.inv(i, j)

    main_products(sz, prepare, u_ref, mats, rhs_ref, prod_ref)


def first_corner(sz, n_mat, even_ref, res_in, vec, from_x, from_y, corner, own_inv, own_pot, ghost_x,
                 ghost_y, prod_ref, *refs):
    mats = refs[:n_mat]
    res_out, acc_ref, face, near, far, last_x, last_field, small_ref, tail_ref = refs[n_mat:]
    del res_in, res_out
    last_field[0], last_field[1] = fields_of(corner[0, :, sz.full : sz.wide])
    last_x[...] = vectors_of(sz, corner[0])
    nodes = Nodes(sz, vec, from_x, from_y, own_inv, own_pot, ghost_x, ghost_y, last_field)
    u_corner = []
    for i, j in corner_edges(sz):
        x = last_x[...] if (i, j) == (sz.ex, sz.ey) else nodes.x(i, j)
        u_corner.append(x * nodes.inv(i, j))
    corner_products(sz, u_corner, prod_ref, mats, small_ref, tail_ref, acc_ref)
    write_messages(sz, even_ref[0] == 0, acc_ref, face, near, far)


def second_main(sz, n_mat, even_ref, vec, from_x, from_y, own_inv, own_pot, ghost_x, ghost_y,
                acc_in, face_in, near_in, far_in, *refs):
    mats = refs[:n_mat]
    prod_ref, y_ref, u_ref, rhs_ref = refs[n_mat:]
    nodes = Nodes(sz, vec, from_x, from_y, own_inv, own_pot, ghost_x, ghost_y)
    sums = Sums(sz, even_ref[0] == 0, acc_in, face_in, near_in, far_in)

    def prepare(i, j):
        old, inv = nodes.x(i, j), nodes.inv(i, j)
        image = inv * sums.at(i, j) + nodes.pot(i, j) * old
        new = (image - center_shift * old) / half_width
        y_ref[:, i, j] = new
        u_ref[:, i, j] = inv * new

    main_products(sz, prepare, u_ref, mats, rhs_ref, prod_ref)


def second_corner(sz, n_mat, even_ref, vec, from_x, from_y, own_inv, own_pot, ghost_x, ghost_y, last_x,
                  last_field, acc_in, face_in, near_in, far_in, corner_in, prod_ref, *refs):
    mats = refs[:n_mat]
    acc_ref, face, near, far, y_corner, small_ref, tail_ref = refs[n_mat:]
    even = even_ref[0] == 0
    nodes = Nodes(sz, vec, from_x, from_y, own_inv, own_pot, ghost_x, ghost_y, last_field)
    sums = Sums(sz, even, acc_in, face_in, near_in, far_in, corner_in)
    u_corner = []
    for at, (i, j) in enumerate(corner_edges(sz)):
        old = last_x[...] if (i, j) == (sz.ex, sz.ey) else nodes.x(i, j)
        inv = nodes.inv(i, j)
        image = inv * sums.at(i, j) + nodes.pot(i, j) * old
        new = (image - center_shift * old) / half_width
        y_corner[at] = new
        u_corner.append(inv * new)
    corner_products(sz, u_corner, prod_ref, mats, small_ref, tail_ref, acc_ref)
    write_messages(sz, even, acc_ref, face, near, far)


def third_main(sz, n_mat, even_ref, vec, from_x, from_y, own_inv, own_pot, ghost_x, ghost_y,
               acc_in, face_in, near_in, far_in, y_ref, *refs):
    mats = refs[:n_mat]
    prod_ref, new_ref, u_ref, rhs_ref = refs[n_mat:]
    nodes = Nodes(sz, vec, from_x, from_y, own_inv, own_pot, ghost_x, ghost_y)
    sums = Sums(sz, even_ref[0] == 0, acc_in, face_in, near_in, far_in)

    def prepare(i, j):
        old, inv = y_ref[:, i, j], nodes.inv(i, j)
        image = inv * sums.at(i, j) + nodes.pot(i, j) * old
        new = 2.0 * (image - center_shift * old) / half_width - nodes.x(i, j)
        new_ref[:, i, j] = new
        u_ref[:, i, j] = inv * new

    main_products(sz, prepare, u_ref, mats, rhs_ref, prod_ref)


def third_corner(sz, n_mat, norm_scale, even_ref, vec, from_x, from_y, own_inv, own_pot, ghost_x, ghost_y,
                 last_x, last_field, acc_in, face_in, near_in, far_in, corner_in, prod_ref, y_ref,
                 y_corner, new_ref, turned, *refs):
    mats = refs[:n_mat]
    out_hbm, face, side, corner, give, keep = refs[n_mat : n_mat + 6]
    part_ref, sem, acc_ref, rows_ref, small_ref, tail_ref = refs[n_mat + 6 :]
    nodes = Nodes(sz, vec, from_x, from_y, own_inv, own_pot, ghost_x, ghost_y, last_field)
    sums = Sums(sz, even_ref[0] == 0, acc_in, face_in, near_in, far_in, corner_in)
    u_corner, new_corner = [], []
    for at, (i, j) in enumerate(corner_edges(sz)):
        x = last_x[...] if (i, j) == (sz.ex, sz.ey) else nodes.x(i, j)
        old, inv = y_corner[at], nodes.inv(i, j)
        image = inv * sums.at(i, j) + nodes.pot(i, j) * old
        new_corner.append(2.0 * (image - center_shift * old) / half_width - x)
        u_corner.append(inv * new_corner[-1])
    corner_products(sz, u_corner, prod_ref, mats, small_ref, tail_ref, acc_ref)

    def put_row(at, value):
        for b in range(sz.blocks):
            rows_ref[at, :, b * sz.width : (b + 1) * sz.width] = value[b]

    copies = []
    for i in range(sz.gx):
        for j in range(sz.gy):
            acc, inv = acc_ref[:, i, j], nodes.inv(i, j)
            if i == sz.ex or j == sz.ey:
                value = gain * (inv * acc)
                rounded = value.astype(bf16)
                if j < sz.ey:
                    face[:, j] = rounded
                elif i < sz.ex:
                    side[:, i] = value
                else:
                    corner[...] = rounded
                put_row(sz.own_edges + (j if j < sz.ey else sz.ey + i), rounded)
                continue
            at = sz.corner(i, j)
            old = y_ref[:, i, j] if at is None else y_corner[at]
            new = new_ref[:, i, j] if at is None else new_corner[at]
            image = inv * acc + nodes.pot(i, j) * new
            value = 2.0 * (image - center_shift * new) / half_width - old
            part_ref[:, i, j] = value
            put_row(i * sz.ey + j, value.astype(bf16))
        if i < sz.ex:
            copies.append(pltpu.make_async_copy(part_ref.at[:, i], out_hbm.at[:, i], sem.at[i]))
            copies[-1].start()
    for at in range(sz.own_edges + sz.ey + sz.gx, sz.edges):
        rows_ref[at] = jnp.zeros((sz.ez, sz.full), bf16)
    rows = rows_ref[...].reshape(sz.edges * sz.ez, sz.full)
    mine = even_ref[0]
    for half, out in ((1 - mine, give), (mine, keep)):
        local = jnp.dot(turned[half], rows, preferred_element_type=f32)
        out[...] = (local * norm_scale).astype(out.dtype)
    for copy in copies:
        copy.wait()


def pieces_kernel(keep, taken, pieces):
    rows = pieces.shape[2]
    for at in range(pieces.shape[1]):
        span = slice(at * rows, (at + 1) * rows)
        value = (keep[span] + taken[span].astype(f32)).astype(pieces.dtype)
        for copy in range(pieces.shape[0]):
            pieces[copy, at] = value


def last_side_kernel(sz, side_ref, corner_ref, face_in, out_ref, face_out):
    del face_in, face_out
    for i in range(sz.ex):
        value = side_ref[:, i]
        if i == 0:
            value = value + corner_ref[...].astype(f32)
        out_ref[:, i] = value.astype(out_ref.dtype)


def last_kernel(sz, old_hbm, face, side, pieces, out_hbm, margin, at_x, at_y, sems):
    del old_hbm
    pairs = [(at_x, out_hbm.at[:, 0]), (at_y, out_hbm.at[:, pl.ds(1, sz.ex - 1), 0])]
    loads = [pltpu.make_async_copy(b, a, sems.at[k]) for k, (a, b) in enumerate(pairs)]
    stores = [pltpu.make_async_copy(a, b, sems.at[k]) for k, (a, b) in enumerate(pairs)]
    for copy in loads:
        copy.start()
    margin[...] = sum(pieces[at].astype(f32) for at in range(pieces.shape[0]))
    for copy in loads:
        copy.wait()
    at_x[:, 0] += side[:, 0].astype(f32)
    for j in range(sz.ey):
        at_x[:, j] += face[:, j].astype(f32)
    for i in range(1, sz.ex):
        at_y[:, i - 1] += side[:, i].astype(f32)
    for copy in stores:
        copy.start()
    for copy in stores:
        copy.wait()


def like(shape, dtype):
    return jax.ShapeDtypeStruct(shape, dtype)


def call(kernel, name, flops, out_shape, scratch, operands, hbm=0, scalar_first=False, aliases=None,
         out_hbm=0):
    out_shape = [like(s.shape, s.dtype) for s in out_shape]
    size = sum(math.prod(s.shape) * jnp.dtype(s.dtype).itemsize for s in (*operands, *out_shape))
    whole = pl.BlockSpec(memory_space=pltpu.VMEM)
    specs = [pl.BlockSpec(memory_space=pltpu.HBM)] * hbm + [whole] * (len(operands) - hbm)
    if scalar_first:
        specs[0] = pl.BlockSpec(memory_space=pltpu.SMEM)
    out_specs = [pl.BlockSpec(memory_space=pltpu.HBM)] * out_hbm + [whole] * (len(out_shape) - out_hbm)
    for source, target in (aliases or {}).items():
        if source >= hbm:
            specs[source] = out_specs[target] = pl.BlockSpec(memory_space=pl.ANY)
    out_shape = [pltpu.HBM(s.shape, s.dtype) for s in out_shape[:out_hbm]] + out_shape[out_hbm:]
    operands = [pltpu.with_memory_space_constraint(a, pltpu.HBM) for a in operands[:hbm]] + list(
        operands[hbm:]
    )
    return pl.pallas_call(
        kernel,
        in_specs=specs,
        out_specs=out_specs,
        out_shape=out_shape,
        scratch_shapes=scratch,
        input_output_aliases=aliases or {},
        compiler_params=pltpu.CompilerParams(vmem_limit_bytes=VMEM_LIMIT),
        cost_estimate=pl.CostEstimate(flops=flops, bytes_accessed=size, transcendentals=0),
        name=name,
    )(*operands)


def in_vmem(value):
    return pltpu.with_memory_space_constraint(value, pltpu.VMEM)


def body(vectors, resident, inv_mass, potential, cell_matrix, connectivity):
    sz = Sizes(vectors, resident, inv_mass, connectivity)
    nx, ny = lax.axis_size("dx"), lax.axis_size("dy")
    norm_scale = 1.0 / math.sqrt(sz.ex * sz.ey * sz.ez * nx * ny)
    blocks, ez, width, full = sz.blocks, sz.ez, sz.width, sz.full
    res_count = resident.shape[-1]
    tile = (ez, width)

    conn = connectivity.reshape(sz.cells, sz.nodes)
    to_x, to_y, res_x, conn = call(
        functools.partial(pack_kernel, sz), "pack", 0,
        [
            like((sz.ey, ez, sz.wide), bf16), like((sz.ex, ez, sz.wide + sz.res), bf16),
            like((sz.ey, ez, sz.res), bf16), conn,
        ],
        [
            pltpu.VMEM((2, sz.ey, ez), f32), pltpu.VMEM((2, sz.ex, ez), f32),
            pltpu.SemaphoreType.DMA((7 + 2 * blocks,)),
        ],
        [vectors, resident, inv_mass, potential, conn], hbm=5,
    )
    from_x = send(to_x, -1, 0)
    from_y = send(to_y, 0, -1)
    res_x = send(res_x, -1, 0)

    halves = 2 if sz.cells % 2 == 0 else 1
    step = sz.cells // halves
    mats = []
    for at in range(0, sz.cells, step):
        mats += call(
            functools.partial(order_kernel, sz, at), "order_cells", 4 * step * sz.depth**3,
            [like((step, sz.rows, sz.depth), bf16)],
            [], [cell_matrix, conn],
        )
    own_inv = jnp.broadcast_to(inv_mass[..., None], inv_mass.shape + (width,))
    own_pot = jnp.broadcast_to(potential[..., None], inv_mass.shape + (width,))
    parity = jnp.reshape(lax.axis_index("dy") % 2, (1,)).astype(jnp.int32)
    ghost_corner = send(from_y[:1], -1, 0)

    grid = (blocks, sz.gx, sz.gy) + tile
    own = (blocks, sz.ex, sz.ey) + tile
    products = like((sz.cells, sz.rows, full), f32)
    state_grid = like(grid, f32)
    messages = [
        like((2, blocks, sz.gy) + tile, bf16),
        like((blocks, sz.gx) + tile, bf16),
        like((blocks, sz.gx) + tile, bf16),
    ]
    main_scratch = [pltpu.VMEM(grid, f32), pltpu.VMEM((2, sz.depth, full), f32)]
    corner_scratch = [
        pltpu.VMEM((LANES, full), f32),
        pltpu.VMEM((sz.cells, sz.base + sz.rows - sz.tail, full), f32),
    ]
    n_mat = len(mats)
    flops = 2 * sz.cells * sz.rows * sz.depth * full
    small_flops = 2 * sz.cells * sz.rows * LANES * full

    def exchange(face, near, far):
        face = swap_x(face)
        near, far = swap_y(near, far)
        (corner,) = call(
            functools.partial(corner_pack_kernel, sz), "corner_pack", 0,
            [like((2, 2) + sz.edge, bf16)], [], [near, far],
        )
        return [face, near, far], swap_x(corner)

    state = [vectors, *map(in_vmem, (from_x, from_y, own_inv, own_pot))]
    prod, ghost_x, ghost_y = call(
        functools.partial(first_main, sz, n_mat), "first_main", flops,
        [products, like((2, sz.ey) + tile, f32), like((2, sz.ex) + tile, f32)], main_scratch,
        [*state, *mats],
    )
    res_x, acc, face, near, far, last_x, last_field = call(
        functools.partial(first_corner, sz, n_mat), "first_corner", small_flops,
        [res_x, state_grid, *messages, like(sz.edge, f32), like((2,) + tile, f32)], corner_scratch,
        [
            parity, res_x, *state[:3], ghost_corner, *state[3:], ghost_x, ghost_y, prod, *mats,
        ],
        scalar_first=True, aliases={1: 0},
    )
    (turned,) = call(
        functools.partial(turn_kernel, sz, ny // 2), "turn_residents", flops // 2,
        [like((2, res_count // 2, sz.edges * ez), bf16)], [],
        [resident.reshape(-1, res_count), res_x, from_y, ghost_corner],
    )
    got, corner = exchange(face, near, far)
    state += [ghost_x, ghost_y]
    ends = [last_x, last_field]
    prod, y1 = call(
        functools.partial(second_main, sz, n_mat), "second_main", flops,
        [products, state_grid], main_scratch,
        [parity, *state, acc, *got, *mats], scalar_first=True,
    )
    acc, face, near, far, y1_corner = call(
        functools.partial(second_corner, sz, n_mat), "second_corner", small_flops,
        [state_grid, *messages, like((4,) + sz.edge, f32)], corner_scratch,
        [parity, *state, *ends, acc, *got, corner, prod, *mats], scalar_first=True,
    )
    got, corner = exchange(face, near, far)
    prod, y2 = call(
        functools.partial(third_main, sz, n_mat), "third_main", flops,
        [products, state_grid], main_scratch,
        [parity, *state, acc, *got, y1, *mats], scalar_first=True,
    )
    filtered, face, side, corner, give, keep = call(
        functools.partial(third_corner, sz, n_mat, norm_scale), "third_corner",
        small_flops + 2 * res_count * sz.edges * ez * full,
        [
            like(own, f32), like((blocks, sz.ey) + tile, bf16), like((blocks, sz.ex) + tile, f32),
            like(sz.edge, bf16), like((res_count // 2, full), bf16), like((res_count // 2, full), f32),
        ],
        [
            pltpu.VMEM(own, f32), pltpu.SemaphoreType.DMA((sz.ex,)), pltpu.VMEM(grid, f32),
            pltpu.VMEM((sz.edges, ez, full), bf16),
        ] + corner_scratch,
        [parity, *state, *ends, acc, *got, corner, prod, y1, y1_corner, y2, turned, *mats],
        scalar_first=True, out_hbm=1,
    )

    (pieces,) = call(
        pieces_kernel, "pieces", 0, [like((nx, ny // 2, res_count // ny, full), bf16)], [],
        [keep, send_near(give)],
    )
    pieces = pieces.reshape(nx * ny // 2, -1, full)
    groups = [[a * ny + b for a in range(nx) for b in range(c, ny, 2)] for c in range(2)]
    pieces = lax.all_to_all(pieces, ("dx", "dy"), 0, 0, axis_index_groups=groups)

    corner = send(corner, 1, 0)
    side, face = call(
        functools.partial(last_side_kernel, sz), "last_side", 0,
        [like((blocks, sz.ex) + tile, bf16), face], [], [side, corner, face], aliases={2: 1},
    )
    face = send(face, 1, 0)
    side = send(side, 0, 1)
    filtered, margin = call(
        functools.partial(last_kernel, sz), "last", 0, [like(own, f32), like(pieces.shape[1:], f32)],
        [
            pltpu.VMEM((blocks, sz.ey) + tile, f32), pltpu.VMEM((blocks, sz.ex - 1) + tile, f32),
            pltpu.SemaphoreType.DMA((2,)),
        ],
        [filtered, face, side, pieces], hbm=1, out_hbm=1, aliases={0: 0},
    )
    return (filtered, margin)


def solution(mesh):
    return jax.shard_map(
        body,
        mesh=mesh,
        in_specs=(
            P(None, "dx", "dy", None, None),
            P("dx", "dy", None, None),
            P("dx", "dy", None),
            P("dx", "dy", None),
            P(),
            P("dx", "dy", None, None),
        ),
        out_specs=(P(None, "dx", "dy", None, None), P("dy", None)),
        check_vma=False,
    )
```

```python
import functools
import math

import jax
import jax.numpy as jnp
from jax import lax
from jax.experimental import pallas as pl
from jax.experimental.pallas import tpu as pltpu
from jax.sharding import PartitionSpec as P

LANES = 128
TILE = 256
SUB = 16
VMEM_LIMIT = 16 * 1024 * 1024

center_shift = 1.2
half_width = 2.0
gain = 2.0 / half_width

f32, bf16 = jnp.float32, jnp.bfloat16


def round_up(value, step):
    return -(-value // step) * step


class Sizes:
    def __init__(self, vectors, resident, inv_mass, connectivity):
        self.blocks = vectors.shape[0]
        self.width = vectors.shape[-1]
        self.full = self.blocks * self.width
        self.res = resident.shape[-1]
        self.wide = self.res + self.full + self.width
        self.ex, self.ey, self.ez = inv_mass.shape
        self.cells, self.nodes = connectivity.shape[2:]
        self.n1 = round(self.nodes ** (1.0 / 3.0))
        self.p = self.n1 - 1
        self.cx, self.cy, self.cz = self.ex // self.p, self.ey // self.p, self.ez // self.p
        self.gx, self.gy, self.gz = self.ex + 1, self.ey + 1, self.ez
        self.edge = (self.blocks, self.ez, self.width)
        self.origins = [
            (a * self.p, b * self.p, c * self.p)
            for a in range(self.cx)
            for b in range(self.cy)
            for c in range(self.cz)
        ]
        self.most = max(len(self.cell_corners(cell)) for cell in range(self.cells))
        self.base = round_up(self.most * self.n1, 8)
        plain = self.n1 * self.n1 - min(len(self.cell_corners(cell)) for cell in range(self.cells))
        self.tail = self.base + plain * self.p
        self.rows = round_up(self.tail + plain, SUB)
        self.depth = round_up(self.rows, LANES)
        self.own_edges = self.ex * self.ey
        self.edges = round_up(self.own_edges + self.ey + self.gx, LANES // self.ez)

    def corner(self, i, j):
        if i in (0, self.ex) and j in (0, self.ey):
            return 2 * (i // self.ex) + j // self.ey
        return None

    def cell_corners(self, cell):
        x0, y0, _ = self.origins[cell]
        return [
            (i, j)
            for i in range(self.n1)
            for j in range(self.n1)
            if self.corner(x0 + i, y0 + j) is not None
        ]

    def runs(self, cell):
        corners = self.cell_corners(cell)
        place = 0
        for i in range(self.n1):
            js = [j for j in range(self.n1) if (i, j) not in corners]
            while js:
                count = 1
                while count < len(js) and js[count] == js[0] + count:
                    count += 1
                yield place, i, js[0], count
                place += count
                js = js[count:]


def send(value, steps_x, steps_y):
    nx, ny = lax.axis_size("dx"), lax.axis_size("dy")
    pairs = [
        (a * ny + b, ((a + steps_x) % nx) * ny + (b + steps_y) % ny)
        for a in range(nx)
        for b in range(ny)
    ]
    return lax.ppermute(value, ("dx", "dy"), pairs)


def swap_x(value):
    if lax.axis_size("dx") == 2:
        return send(value, 1, 0)
    return jnp.stack([send(value[0], -1, 0), send(value[1], 1, 0)])


def send_near(value):
    pairs = [(b, b + 1 if b % 2 == 0 else b - 1) for b in range(lax.axis_size("dy"))]
    return lax.ppermute(value, "dy", pairs)


def swap_y(near, far):
    ny = lax.axis_size("dy")
    far_pairs = [(b, (b - 1 if b % 2 == 0 else b + 1) % ny) for b in range(ny)]
    far = lax.ppermute(far, "dy", far_pairs)
    return send_near(near), far


def order_kernel(sz, first, matrix_ref, conn_ref, out_ref):
    for slot in range(out_ref.shape[0]):
        cell = first + slot
        x0, y0, z0 = sz.origins[cell]
        conn = conn_ref[cell : cell + 1, :].astype(f32)
        li = jnp.floor((conn + 0.5) * (1.0 / (sz.gy * sz.gz)))
        rest = conn - li * (sz.gy * sz.gz)
        lj = jnp.floor((rest + 0.5) * (1.0 / sz.gz))
        lk = rest - lj * sz.gz - z0
        lk = jnp.where(lk < 0, lk + sz.gz, lk)
        column = (li - x0) * sz.n1 + (lj - y0)
        corners = [i * sz.n1 + j for i, j in sz.cell_corners(cell)]
        place = column
        for at in corners:
            place = place - jnp.where(column > at, 1.0, 0.0)
        index = jnp.where(lk < sz.p, sz.base + place * sz.p + lk, sz.tail + place)
        for rank, at in enumerate(corners):
            special = jnp.where(lk < sz.p, rank * sz.p + lk, len(corners) * sz.p + rank)
            index = jnp.where(column == at, special, index)
        index = index.astype(jnp.int32)
        row = lax.broadcasted_iota(jnp.int32, (sz.depth, sz.nodes), 0)
        pick = (row == index).astype(f32).astype(bf16)
        half = jnp.dot(pick[: sz.rows], matrix_ref[...], preferred_element_type=f32)
        half = half.astype(bf16)
        cuts = list(range(0, sz.depth, TILE)) + [sz.depth]
        for r0, r1 in zip(cuts[:-1], cuts[1:]):
            r1 = min(r1, sz.rows)
            block = lax.dot_general(
                half[r0:r1], pick[r0:], (((1,), (1,)), ((), ())), preferred_element_type=f32
            ).astype(bf16)
            out_ref[slot, r0:r1, r0:] = block
            for c0, c1 in zip(cuts[:-1], cuts[1:]):
                if c0 > r0:
                    mirror = block[:, c0 - r0 : c1 - r0].T
                    c1 = min(c1, sz.rows)
                    out_ref[slot, c0:c1, r0:r1] = mirror[: c1 - c0]


def field_row(inv, pot):
    lane = lax.broadcasted_iota(jnp.int32, inv.shape, inv.ndim - 1)
    row = jnp.zeros_like(inv)
    for at, rest in enumerate((inv, pot)):
        for k in range(3):
            part = rest.astype(bf16).astype(f32)
            rest = rest - part
            row = jnp.where(lane == 3 * at + k, part, row)
    return row.astype(bf16)


def field_rows(sz, inv, pot, count):
    inv, pot = inv.T, pot.T
    shape = (sz.ez, sz.width)
    for at in range(count):
        yield at, field_row(
            jnp.broadcast_to(inv[:, at : at + 1], shape), jnp.broadcast_to(pot[:, at : at + 1], shape)
        )


def fields_of(row):
    row = row.astype(f32)
    return [
        jnp.broadcast_to(sum(row[:, 3 * at + k : 3 * at + k + 1] for k in range(3)), row.shape)
        for at in range(2)
    ]


def pack_kernel(
    sz, vec_hbm, res_hbm, inv_hbm, pot_hbm, conn_hbm, to_x, to_y, conn_ref, at_x, at_y, sems
):
    pairs = [
        (inv_hbm.at[0], at_x.at[0]), (pot_hbm.at[0], at_x.at[1]),
        (inv_hbm.at[:, 0], at_y.at[0]), (pot_hbm.at[:, 0], at_y.at[1]),
        (res_hbm.at[0], to_x.at[:, :, pl.ds(0, sz.res)]),
        (res_hbm.at[:, 0], to_y.at[:, :, pl.ds(0, sz.res)]),
    ]
    for b in range(sz.blocks):
        lanes = pl.ds(sz.res + b * sz.width, sz.width)
        pairs.append((vec_hbm.at[b, 0], to_x.at[:, :, lanes]))
        pairs.append((vec_hbm.at[b, :, 0], to_y.at[:, :, lanes]))
    pairs.append((conn_hbm, conn_ref))
    copies = [pltpu.make_async_copy(a, b, sems.at[k]) for k, (a, b) in enumerate(pairs)]
    for copy in copies:
        copy.start()
    for copy in copies[:4]:
        copy.wait()
    for j, row in field_rows(sz, at_x[0], at_x[1], sz.ey):
        to_x[j, :, sz.res + sz.full :] = row
    for i, row in field_rows(sz, at_y[0], at_y[1], sz.ex):
        to_y[i, :, sz.res + sz.full :] = row
    for copy in copies[4:]:
        copy.wait()


def turn_kernel(sz, res_ref, from_x, from_y, corner, out_ref):
    own = sz.own_edges * sz.ez
    for g in range(0, sz.res, LANES):
        lanes = slice(g, g + LANES)
        out_ref[lanes, :own] = res_ref[:, lanes].T
        rest = sz.edges - sz.own_edges - sz.ey - sz.gx
        parts = [from_x[:, :, lanes], from_y[:, :, lanes], corner[:, :, lanes]]
        if rest:
            parts.append(jnp.zeros((rest, sz.ez, LANES), bf16))
        ghosts = jnp.concatenate(parts, axis=0)
        out_ref[lanes, own:] = ghosts.reshape(-1, LANES).T


def vectors_of(sz, edge):
    lanes = [slice(sz.res + b * sz.width, sz.res + (b + 1) * sz.width) for b in range(sz.blocks)]
    return jnp.stack([edge[:, at] for at in lanes]).astype(f32)


class Nodes:
    def __init__(self, sz, vec, from_x, from_y, own_inv, own_pot, ghost_x, ghost_y, corners=None):
        self.sz, self.vec, self.from_x, self.from_y = sz, vec, from_x, from_y
        self.own, self.ghost_x, self.ghost_y, self.corners = (own_inv, own_pot), ghost_x, ghost_y, corners

    def x(self, i, j):
        sz = self.sz
        if i < sz.ex and j < sz.ey:
            return self.vec[:, i, j].astype(f32)
        return vectors_of(sz, self.from_x[j] if i == sz.ex else self.from_y[i])

    def field(self, at, i, j):
        sz = self.sz
        if i < sz.ex and j < sz.ey:
            return self.own[at][i, j]
        if i < sz.ex:
            return self.ghost_y[at, i]
        if j < sz.ey:
            return self.ghost_x[at, j]
        return self.corners[at]

    def inv(self, i, j):
        return self.field(0, i, j)

    def pot(self, i, j):
        return self.field(1, i, j)


class Sums:
    def __init__(self, sz, even, acc, face, near, far, corner=None):
        self.sz, self.even, self.acc, self.face = sz, even, acc, face
        self.near, self.far, self.corner = near, far, corner

    def at(self, i, j):
        sz = self.sz
        total = self.acc[:, i, j]
        side = 1 if i == 0 else 0 if i == sz.ex else None
        if side is not None:
            total = total + self.face[side, :, j].astype(f32)
        if j in (0, sz.ey):
            is_near = self.even if j == sz.ey else jnp.logical_not(self.even)
            total = total + jnp.where(is_near, self.near[:, i].astype(f32), self.far[:, i].astype(f32))
            if side is not None:
                total = total + jnp.where(
                    is_near, self.corner[side, 0].astype(f32), self.corner[side, 1].astype(f32)
                )
        return total


def corner_edges(sz):
    return [(i, j) for i in (0, sz.ex) for j in (0, sz.ey)]


def main_products(sz, prepare, u_ref, mat_refs, rhs_ref, out_ref):
    width = sz.width
    flat = sz.gx * sz.gy * sz.gz
    u_flat = u_ref.reshape(sz.blocks * flat, width)
    matrices = [ref.at[c] for ref in mat_refs for c in range(ref.shape[0])]
    last = sz.nodes // 8 * 8
    ready = set()
    for cell, (x0, y0, z0) in enumerate(sz.origins):
        slot = cell % 2
        if cell < 2:
            rhs_ref[slot, : sz.base] = jnp.zeros((sz.base, sz.full), f32)
            rhs_ref[slot, last:] = jnp.zeros((sz.depth - last, sz.full), f32)
        for place, i, j, count in sz.runs(cell):
            for at in range(j, j + count):
                if (x0 + i, y0 + at) not in ready:
                    prepare(x0 + i, y0 + at)
                    ready.add((x0 + i, y0 + at))
        z1 = z0 + sz.p
        wrap = z1 % sz.gz
        for b in range(sz.blocks):
            lanes = slice(b * width, (b + 1) * width)
            for place, i, j, count in sz.runs(cell):
                row = sz.base + place * sz.p
                rhs_ref[slot, row : row + count * sz.p, lanes] = u_ref[
                    b, x0 + i, y0 + j : y0 + j + count, z0:z1
                ].reshape(count * sz.p, width)
        for b in range(sz.blocks):
            lanes = slice(b * width, (b + 1) * width)
            for place, i, j, count in sz.runs(cell):
                start = b * flat + ((x0 + i) * sz.gy + y0 + j) * sz.gz + wrap
                rhs_ref[slot, sz.tail + place : sz.tail + place + count, lanes] = u_flat[
                    pl.ds(start, count, stride=sz.gz)
                ]
        out_ref[cell] = jnp.dot(
            matrices[cell][...], rhs_ref[slot].astype(bf16), preferred_element_type=f32
        )


def corner_products(sz, u_corner, prod_ref, mat_refs, small_ref, tail_ref, acc_ref):
    width = sz.width
    flat = sz.gx * sz.gy * sz.gz
    acc_flat = acc_ref.reshape(sz.blocks * flat, width)
    matrices = [ref.at[c] for ref in mat_refs for c in range(ref.shape[0])]
    small_ref[...] = jnp.zeros_like(small_ref)
    touched = set()
    for cell, (x0, y0, z0) in enumerate(sz.origins):
        z1 = z0 + sz.p
        wrap = z1 % sz.gz
        corners = sz.cell_corners(cell)
        for rank, (i, j) in enumerate(corners):
            value = u_corner[sz.corner(x0 + i, y0 + j)]
            last = len(corners) * sz.p + rank
            for b in range(sz.blocks):
                lanes = slice(b * width, (b + 1) * width)
                small_ref[rank * sz.p : (rank + 1) * sz.p, lanes] = value[b, z0:z1]
                small_ref[last : last + 1, lanes] = value[b, wrap : wrap + 1]
        total = prod_ref[cell] + jnp.dot(
            matrices[cell][:, : small_ref.shape[0]], small_ref[...].astype(bf16),
            preferred_element_type=f32,
        )
        tail_ref[cell, : sz.base] = total[: sz.base]
        tail_ref[cell, sz.base :] = total[sz.tail :]
        spans = [(rank * sz.p, i, j, 1) for rank, (i, j) in enumerate(corners)]
        spans += [(sz.base + place * sz.p, i, j, count) for place, i, j, count in sz.runs(cell)]
        for row, i, j, count in spans:
            for at in range(count):
                part = total[row + at * sz.p : row + (at + 1) * sz.p]
                key = (x0 + i, y0 + j + at, z0)
                for b in range(sz.blocks):
                    value = part[:, b * width : (b + 1) * width]
                    if key in touched:
                        value = acc_ref[b, key[0], key[1], z0:z1] + value
                    acc_ref[b, key[0], key[1], z0:z1] = value
                touched.add(key)
    for cell, (x0, y0, z0) in enumerate(sz.origins):
        wrap = (z0 + sz.p) % sz.gz
        corners = sz.cell_corners(cell)
        spans = [(len(corners) * sz.p + rank, i, j, 1) for rank, (i, j) in enumerate(corners)]
        spans += [(sz.base + place, i, j, count) for place, i, j, count in sz.runs(cell)]
        for row, i, j, count in spans:
            for b in range(sz.blocks):
                start = b * flat + ((x0 + i) * sz.gy + y0 + j) * sz.gz + wrap
                rows = pl.ds(start, count, stride=sz.gz) if count > 1 else pl.ds(start, 1)
                lanes = slice(b * width, (b + 1) * width)
                acc_flat[rows] = acc_flat[rows] + tail_ref[cell, row : row + count, lanes]


def write_messages(sz, even, acc_ref, face, near, far):
    at_near = jnp.where(even, sz.ey, 0)
    for b in range(sz.blocks):
        face[0, b] = acc_ref[b, 0].astype(bf16)
        face[1, b] = acc_ref[b, sz.ex].astype(bf16)
        near[b] = acc_ref[b, :, at_near].astype(bf16)
        far[b] = acc_ref[b, :, sz.ey - at_near].astype(bf16)


def corner_pack_kernel(sz, near, far, out_ref):
    for side, i in enumerate((0, sz.ex)):
        for slot, ref in enumerate((near, far)):
            out_ref[side, slot] = ref[:, i]


def first_main(sz, n_mat, vec, from_x, from_y, own_inv, own_pot, *refs):
    mats = refs[:n_mat]
    prod_ref, ghost_x, ghost_y, u_ref, rhs_ref = refs[n_mat:]
    for j in range(sz.ey):
        ghost_x[0, j], ghost_x[1, j] = fields_of(from_x[j, :, sz.res + sz.full :])
    for i in range(sz.ex):
        ghost_y[0, i], ghost_y[1, i] = fields_of(from_y[i, :, sz.res + sz.full :])
    nodes = Nodes(sz, vec, from_x, from_y, own_inv, own_pot, ghost_x, ghost_y)

    def prepare(i, j):
        u_ref[:, i, j] = nodes.x(i, j) * nodes.inv(i, j)

    main_products(sz, prepare, u_ref, mats, rhs_ref, prod_ref)


def first_corner(sz, n_mat, even_ref, vec, from_x, from_y, corner, own_inv, own_pot, ghost_x, ghost_y,
                 prod_ref, *refs):
    mats = refs[:n_mat]
    acc_ref, face, near, far, last_x, last_field, small_ref, tail_ref = refs[n_mat:]
    last_field[0], last_field[1] = fields_of(corner[0, :, sz.res + sz.full :])
    last_x[...] = vectors_of(sz, corner[0])
    nodes = Nodes(sz, vec, from_x, from_y, own_inv, own_pot, ghost_x, ghost_y, last_field)
    u_corner = []
    for i, j in corner_edges(sz):
        x = last_x[...] if (i, j) == (sz.ex, sz.ey) else nodes.x(i, j)
        u_corner.append(x * nodes.inv(i, j))
    corner_products(sz, u_corner, prod_ref, mats, small_ref, tail_ref, acc_ref)
    write_messages(sz, even_ref[0] == 0, acc_ref, face, near, far)


def second_main(sz, n_mat, even_ref, vec, from_x, from_y, own_inv, own_pot, ghost_x, ghost_y,
                acc_in, face_in, near_in, far_in, *refs):
    mats = refs[:n_mat]
    prod_ref, y_ref, u_ref, rhs_ref = refs[n_mat:]
    nodes = Nodes(sz, vec, from_x, from_y, own_inv, own_pot, ghost_x, ghost_y)
    sums = Sums(sz, even_ref[0] == 0, acc_in, face_in, near_in, far_in)

    def prepare(i, j):
        old, inv = nodes.x(i, j), nodes.inv(i, j)
        image = inv * sums.at(i, j) + nodes.pot(i, j) * old
        new = (image - center_shift * old) / half_width
        y_ref[:, i, j] = new
        u_ref[:, i, j] = inv * new

    main_products(sz, prepare, u_ref, mats, rhs_ref, prod_ref)


def second_corner(sz, n_mat, even_ref, vec, from_x, from_y, own_inv, own_pot, ghost_x, ghost_y, last_x,
                  last_field, acc_in, face_in, near_in, far_in, corner_in, prod_ref, *refs):
    mats = refs[:n_mat]
    acc_ref, face, near, far, y_corner, small_ref, tail_ref = refs[n_mat:]
    even = even_ref[0] == 0
    nodes = Nodes(sz, vec, from_x, from_y, own_inv, own_pot, ghost_x, ghost_y, last_field)
    sums = Sums(sz, even, acc_in, face_in, near_in, far_in, corner_in)
    u_corner = []
    for at, (i, j) in enumerate(corner_edges(sz)):
        old = last_x[...] if (i, j) == (sz.ex, sz.ey) else nodes.x(i, j)
        inv = nodes.inv(i, j)
        image = inv * sums.at(i, j) + nodes.pot(i, j) * old
        new = (image - center_shift * old) / half_width
        y_corner[at] = new
        u_corner.append(inv * new)
    corner_products(sz, u_corner, prod_ref, mats, small_ref, tail_ref, acc_ref)
    write_messages(sz, even, acc_ref, face, near, far)


def third_main(sz, n_mat, even_ref, vec, from_x, from_y, own_inv, own_pot, ghost_x, ghost_y,
               acc_in, face_in, near_in, far_in, y_ref, *refs):
    mats = refs[:n_mat]
    prod_ref, new_ref, u_ref, rhs_ref = refs[n_mat:]
    nodes = Nodes(sz, vec, from_x, from_y, own_inv, own_pot, ghost_x, ghost_y)
    sums = Sums(sz, even_ref[0] == 0, acc_in, face_in, near_in, far_in)

    def prepare(i, j):
        old, inv = y_ref[:, i, j], nodes.inv(i, j)
        image = inv * sums.at(i, j) + nodes.pot(i, j) * old
        new = 2.0 * (image - center_shift * old) / half_width - nodes.x(i, j)
        new_ref[:, i, j] = new
        u_ref[:, i, j] = inv * new

    main_products(sz, prepare, u_ref, mats, rhs_ref, prod_ref)


def third_corner(sz, n_mat, norm_scale, even_ref, vec, from_x, from_y, own_inv, own_pot, ghost_x, ghost_y,
                 last_x, last_field, acc_in, face_in, near_in, far_in, corner_in, prod_ref, y_ref,
                 y_corner, new_ref, turned, *refs):
    mats = refs[:n_mat]
    out_hbm, edge_x, edge_y, face, side, corner, margin = refs[n_mat : n_mat + 7]
    part_ref, sem, acc_ref, rows_ref, small_ref, tail_ref = refs[n_mat + 7 :]
    nodes = Nodes(sz, vec, from_x, from_y, own_inv, own_pot, ghost_x, ghost_y, last_field)
    sums = Sums(sz, even_ref[0] == 0, acc_in, face_in, near_in, far_in, corner_in)
    u_corner, new_corner = [], []
    for at, (i, j) in enumerate(corner_edges(sz)):
        x = last_x[...] if (i, j) == (sz.ex, sz.ey) else nodes.x(i, j)
        old, inv = y_corner[at], nodes.inv(i, j)
        image = inv * sums.at(i, j) + nodes.pot(i, j) * old
        new_corner.append(2.0 * (image - center_shift * old) / half_width - x)
        u_corner.append(inv * new_corner[-1])
    corner_products(sz, u_corner, prod_ref, mats, small_ref, tail_ref, acc_ref)

    def put_row(at, value):
        for b in range(sz.blocks):
            rows_ref[at, :, b * sz.width : (b + 1) * sz.width] = value[b]

    copies = []
    for i in range(sz.gx):
        for j in range(sz.gy):
            acc, inv = acc_ref[:, i, j], nodes.inv(i, j)
            if i == sz.ex or j == sz.ey:
                value = gain * (inv * acc)
                rounded = value.astype(bf16)
                if j < sz.ey:
                    face[:, j] = rounded
                elif i < sz.ex:
                    side[:, i] = value
                else:
                    corner[...] = rounded
                put_row(sz.own_edges + (j if j < sz.ey else sz.ey + i), rounded)
                continue
            at = sz.corner(i, j)
            old = y_ref[:, i, j] if at is None else y_corner[at]
            new = new_ref[:, i, j] if at is None else new_corner[at]
            image = inv * acc + nodes.pot(i, j) * new
            value = 2.0 * (image - center_shift * new) / half_width - old
            part_ref[:, i, j] = value
            if i == 0:
                edge_x[:, j] = value
            elif j == 0:
                edge_y[:, i - 1] = value
            put_row(i * sz.ey + j, value.astype(bf16))
        if i < sz.ex:
            copies.append(pltpu.make_async_copy(part_ref.at[:, i], out_hbm.at[:, i], sem.at[i]))
            copies[-1].start()
    for at in range(sz.own_edges + sz.ey + sz.gx, sz.edges):
        rows_ref[at] = jnp.zeros((sz.ez, sz.full), bf16)
    local = jnp.dot(
        turned[...], rows_ref[...].reshape(sz.edges * sz.ez, sz.full), preferred_element_type=f32
    )
    margin[...] = (local * norm_scale).astype(bf16)
    for copy in copies:
        copy.wait()


def last_side_kernel(sz, side_ref, corner_ref, face_in, out_ref, face_out):
    del face_in, face_out
    for i in range(sz.ex):
        value = side_ref[:, i]
        if i == 0:
            value = value + corner_ref[...].astype(f32)
        out_ref[:, i] = value.astype(out_ref.dtype)


def last_kernel(sz, old_hbm, edge_x, edge_y, face, side, out_hbm, at_x, at_y, sems):
    del old_hbm
    for j in range(sz.ey):
        value = edge_x[:, j] + face[:, j].astype(f32)
        if j == 0:
            value = value + side[:, 0].astype(f32)
        at_x[:, j] = value
    for i in range(1, sz.ex):
        at_y[:, i - 1] = edge_y[:, i - 1] + side[:, i].astype(f32)
    copies = [
        pltpu.make_async_copy(at_x, out_hbm.at[:, 0], sems.at[0]),
        pltpu.make_async_copy(at_y, out_hbm.at[:, pl.ds(1, sz.ex - 1), 0], sems.at[1]),
    ]
    for copy in copies:
        copy.start()
    for copy in copies:
        copy.wait()


def like(shape, dtype):
    return jax.ShapeDtypeStruct(shape, dtype)


def call(kernel, name, flops, out_shape, scratch, operands, hbm=0, scalar_first=False, aliases=None,
         out_hbm=0):
    out_shape = [like(s.shape, s.dtype) for s in out_shape]
    size = sum(math.prod(s.shape) * jnp.dtype(s.dtype).itemsize for s in (*operands, *out_shape))
    whole = pl.BlockSpec(memory_space=pltpu.VMEM)
    specs = [pl.BlockSpec(memory_space=pltpu.HBM)] * hbm + [whole] * (len(operands) - hbm)
    if scalar_first:
        specs[0] = pl.BlockSpec(memory_space=pltpu.SMEM)
    out_specs = [pl.BlockSpec(memory_space=pltpu.HBM)] * out_hbm + [whole] * (len(out_shape) - out_hbm)
    for source, target in (aliases or {}).items():
        if source >= hbm:
            specs[source] = out_specs[target] = pl.BlockSpec(memory_space=pl.ANY)
    out_shape = [pltpu.HBM(s.shape, s.dtype) for s in out_shape[:out_hbm]] + out_shape[out_hbm:]
    operands = [pltpu.with_memory_space_constraint(a, pltpu.HBM) for a in operands[:hbm]] + list(
        operands[hbm:]
    )
    return pl.pallas_call(
        kernel,
        in_specs=specs,
        out_specs=out_specs,
        out_shape=out_shape,
        scratch_shapes=scratch,
        input_output_aliases=aliases or {},
        compiler_params=pltpu.CompilerParams(vmem_limit_bytes=VMEM_LIMIT),
        cost_estimate=pl.CostEstimate(flops=flops, bytes_accessed=size, transcendentals=0),
        name=name,
    )(*operands)


def body(vectors, resident, inv_mass, potential, cell_matrix, connectivity):
    sz = Sizes(vectors, resident, inv_mass, connectivity)
    nx, ny = lax.axis_size("dx"), lax.axis_size("dy")
    norm_scale = 1.0 / math.sqrt(sz.ex * sz.ey * sz.ez * nx * ny)
    blocks, ez, width, full = sz.blocks, sz.ez, sz.width, sz.full
    res_count = resident.shape[-1]
    tile = (ez, width)

    conn = connectivity.reshape(sz.cells, sz.nodes)
    to_x, to_y, conn = call(
        functools.partial(pack_kernel, sz), "pack", 0,
        [like((sz.ey, ez, sz.wide), bf16), like((sz.ex, ez, sz.wide), bf16), conn],
        [
            pltpu.VMEM((2, sz.ey, ez), f32), pltpu.VMEM((2, sz.ex, ez), f32),
            pltpu.SemaphoreType.DMA((7 + 2 * blocks,)),
        ],
        [vectors, resident, inv_mass, potential, conn], hbm=5,
    )
    from_x = send(to_x, -1, 0)
    from_y = send(to_y, 0, -1)

    halves = 2 if sz.cells % 2 == 0 else 1
    step = sz.cells // halves
    mats = []
    for at in range(0, sz.cells, step):
        mats += call(
            functools.partial(order_kernel, sz, at), "order_cells", 4 * step * sz.depth**3,
            [like((step, sz.rows, sz.depth), bf16)],
            [], [cell_matrix, conn],
        )
    own_inv = jnp.broadcast_to(inv_mass[..., None], inv_mass.shape + (width,))
    own_pot = jnp.broadcast_to(potential[..., None], inv_mass.shape + (width,))
    parity = jnp.reshape(lax.axis_index("dy") % 2, (1,)).astype(jnp.int32)
    ghost_corner = send(from_y[:1], -1, 0)

    grid = (blocks, sz.gx, sz.gy) + tile
    own = (blocks, sz.ex, sz.ey) + tile
    products = like((sz.cells, sz.rows, full), f32)
    state_grid = like(grid, f32)
    messages = [
        like((2, blocks, sz.gy) + tile, bf16),
        like((blocks, sz.gx) + tile, bf16),
        like((blocks, sz.gx) + tile, bf16),
    ]
    main_scratch = [pltpu.VMEM(grid, f32), pltpu.VMEM((2, sz.depth, full), f32)]
    corner_scratch = [
        pltpu.VMEM((LANES, full), f32),
        pltpu.VMEM((sz.cells, sz.base + sz.rows - sz.tail, full), f32),
    ]
    n_mat = len(mats)
    flops = 2 * sz.cells * sz.rows * sz.depth * full
    small_flops = 2 * sz.cells * sz.rows * LANES * full

    def exchange(face, near, far):
        face = swap_x(face)
        near, far = swap_y(near, far)
        (corner,) = call(
            functools.partial(corner_pack_kernel, sz), "corner_pack", 0,
            [like((2, 2) + sz.edge, bf16)], [], [near, far],
        )
        return [face, near, far], swap_x(corner)

    prod, ghost_x, ghost_y = call(
        functools.partial(first_main, sz, n_mat), "first_main", flops,
        [products, like((2, sz.ey) + tile, f32), like((2, sz.ex) + tile, f32)], main_scratch,
        [vectors, from_x, from_y, own_inv, own_pot, *mats],
    )
    acc, face, near, far, last_x, last_field = call(
        functools.partial(first_corner, sz, n_mat), "first_corner", small_flops,
        [state_grid, *messages, like(sz.edge, f32), like((2,) + tile, f32)], corner_scratch,
        [
            parity, vectors, from_x, from_y, ghost_corner, own_inv, own_pot, ghost_x, ghost_y, prod, *mats,
        ],
        scalar_first=True,
    )
    (turned,) = call(
        functools.partial(turn_kernel, sz), "turn_residents", flops // 2,
        [like((res_count, sz.edges * ez), bf16)], [],
        [resident.reshape(-1, res_count), from_x, from_y, ghost_corner],
    )
    got, corner = exchange(face, near, far)
    state = [vectors, from_x, from_y, own_inv, own_pot, ghost_x, ghost_y]
    ends = [last_x, last_field]
    prod, y1 = call(
        functools.partial(second_main, sz, n_mat), "second_main", flops,
        [products, state_grid], main_scratch,
        [parity, *state, acc, *got, *mats], scalar_first=True,
    )
    acc, face, near, far, y1_corner = call(
        functools.partial(second_corner, sz, n_mat), "second_corner", small_flops,
        [state_grid, *messages, like((4,) + sz.edge, f32)], corner_scratch,
        [parity, *state, *ends, acc, *got, corner, prod, *mats], scalar_first=True,
    )
    got, corner = exchange(face, near, far)
    prod, y2 = call(
        functools.partial(third_main, sz, n_mat), "third_main", flops,
        [products, state_grid], main_scratch,
        [parity, *state, acc, *got, y1, *mats], scalar_first=True,
    )
    filtered, edge_x, edge_y, face, side, corner, local = call(
        functools.partial(third_corner, sz, n_mat, norm_scale), "third_corner",
        small_flops + 2 * res_count * sz.edges * ez * full,
        [
            like(own, f32), like((blocks, sz.ey) + tile, f32), like((blocks, sz.ex - 1) + tile, f32),
            like((blocks, sz.ey) + tile, bf16), like((blocks, sz.ex) + tile, f32), like(sz.edge, bf16),
            like((res_count, full), bf16),
        ],
        [pltpu.VMEM(own, f32), pltpu.SemaphoreType.DMA((sz.ex,)), pltpu.VMEM(grid, f32), pltpu.VMEM((sz.edges, ez, full), bf16)] + corner_scratch,
        [parity, *state, *ends, acc, *got, corner, prod, y1, y1_corner, y2, turned, *mats],
        scalar_first=True, out_hbm=1,
    )

    pieces = lax.all_to_all(local.reshape(ny, -1, full), "dy", 0, 0)
    mine = jnp.sum(pieces.astype(f32), axis=0)
    margin = mine
    for steps in range(1, nx):
        margin = margin + send(mine, steps, 0)

    corner = send(corner, 1, 0)
    side, face = call(
        functools.partial(last_side_kernel, sz), "last_side", 0,
        [like((blocks, sz.ex) + tile, bf16), face], [], [side, corner, face], aliases={2: 1},
    )
    face = send(face, 1, 0)
    side = send(side, 0, 1)
    (filtered,) = call(
        functools.partial(last_kernel, sz), "last", 0, [like(own, f32)],
        [
            pltpu.VMEM((blocks, sz.ey) + tile, f32), pltpu.VMEM((blocks, sz.ex - 1) + tile, f32),
            pltpu.SemaphoreType.DMA((2,)),
        ],
        [filtered, edge_x, edge_y, face, side], hbm=1, out_hbm=1, aliases={0: 0},
    )
    return (filtered, margin)


def solution(mesh):
    return jax.shard_map(
        body,
        mesh=mesh,
        in_specs=(
            P(None, "dx", "dy", None, None),
            P("dx", "dy", None, None),
            P("dx", "dy", None),
            P("dx", "dy", None),
            P(),
            P("dx", "dy", None, None),
        ),
        out_specs=(P(None, "dx", "dy", None, None), P("dy", None)),
        check_vma=False,
    )
```

```python
import functools
import math

import jax
import jax.numpy as jnp
from jax import lax
from jax.experimental import pallas as pl
from jax.experimental.pallas import tpu as pltpu
from jax.sharding import PartitionSpec as P

LANES = 128
TILE = 256
SUB = 16
VMEM_LIMIT = 16 * 1024 * 1024

center_shift = 1.2
half_width = 2.0
gain = 2.0 / half_width

f32, bf16 = jnp.float32, jnp.bfloat16


def round_up(value, step):
    return -(-value // step) * step


class Sizes:
    def __init__(self, vectors, resident, inv_mass, connectivity):
        self.blocks = vectors.shape[0]
        self.width = vectors.shape[-1]
        self.full = self.blocks * self.width
        self.res = resident.shape[-1]
        self.wide = self.res + self.full + self.width
        self.ex, self.ey, self.ez = inv_mass.shape
        self.cells, self.nodes = connectivity.shape[2:]
        self.n1 = round(self.nodes ** (1.0 / 3.0))
        self.p = self.n1 - 1
        self.cx, self.cy, self.cz = self.ex // self.p, self.ey // self.p, self.ez // self.p
        self.gx, self.gy, self.gz = self.ex + 1, self.ey + 1, self.ez
        self.edge = (self.blocks, self.ez, self.width)
        self.origins = [
            (a * self.p, b * self.p, c * self.p)
            for a in range(self.cx)
            for b in range(self.cy)
            for c in range(self.cz)
        ]
        self.most = max(len(self.cell_corners(cell)) for cell in range(self.cells))
        self.base = round_up(self.most * self.n1, 8)
        plain = self.n1 * self.n1 - min(len(self.cell_corners(cell)) for cell in range(self.cells))
        self.tail = self.base + plain * self.p
        self.rows = round_up(self.tail + plain, SUB)
        self.depth = round_up(self.rows, LANES)
        self.own_edges = self.ex * self.ey
        self.edges = round_up(self.own_edges + self.ey + self.gx, LANES // self.ez)

    def corner(self, i, j):
        if i in (0, self.ex) and j in (0, self.ey):
            return 2 * (i // self.ex) + j // self.ey
        return None

    def cell_corners(self, cell):
        x0, y0, _ = self.origins[cell]
        return [
            (i, j)
            for i in range(self.n1)
            for j in range(self.n1)
            if self.corner(x0 + i, y0 + j) is not None
        ]

    def runs(self, cell):
        corners = self.cell_corners(cell)
        place = 0
        for i in range(self.n1):
            js = [j for j in range(self.n1) if (i, j) not in corners]
            while js:
                count = 1
                while count < len(js) and js[count] == js[0] + count:
                    count += 1
                yield place, i, js[0], count
                place += count
                js = js[count:]


def send(value, steps_x, steps_y):
    nx, ny = lax.axis_size("dx"), lax.axis_size("dy")
    pairs = [
        (a * ny + b, ((a + steps_x) % nx) * ny + (b + steps_y) % ny)
        for a in range(nx)
        for b in range(ny)
    ]
    return lax.ppermute(value, ("dx", "dy"), pairs)


def swap_x(value):
    if lax.axis_size("dx") == 2:
        return send(value, 1, 0)
    return jnp.stack([send(value[0], -1, 0), send(value[1], 1, 0)])


def send_near(value):
    pairs = [(b, b + 1 if b % 2 == 0 else b - 1) for b in range(lax.axis_size("dy"))]
    return lax.ppermute(value, "dy", pairs)


def swap_y(near, far):
    ny = lax.axis_size("dy")
    far_pairs = [(b, (b - 1 if b % 2 == 0 else b + 1) % ny) for b in range(ny)]
    far = lax.ppermute(far, "dy", far_pairs)
    return send_near(near), far


def order_kernel(sz, first, matrix_ref, conn_ref, out_ref):
    for slot in range(out_ref.shape[0]):
        cell = first + slot
        x0, y0, z0 = sz.origins[cell]
        conn = conn_ref[cell : cell + 1, :].astype(f32)
        li = jnp.floor((conn + 0.5) * (1.0 / (sz.gy * sz.gz)))
        rest = conn - li * (sz.gy * sz.gz)
        lj = jnp.floor((rest + 0.5) * (1.0 / sz.gz))
        lk = rest - lj * sz.gz - z0
        lk = jnp.where(lk < 0, lk + sz.gz, lk)
        column = (li - x0) * sz.n1 + (lj - y0)
        corners = [i * sz.n1 + j for i, j in sz.cell_corners(cell)]
        place = column
        for at in corners:
            place = place - jnp.where(column > at, 1.0, 0.0)
        index = jnp.where(lk < sz.p, sz.base + place * sz.p + lk, sz.tail + place)
        for rank, at in enumerate(corners):
            special = jnp.where(lk < sz.p, rank * sz.p + lk, len(corners) * sz.p + rank)
            index = jnp.where(column == at, special, index)
        index = index.astype(jnp.int32)
        row = lax.broadcasted_iota(jnp.int32, (sz.depth, sz.nodes), 0)
        pick = (row == index).astype(f32).astype(bf16)
        half = jnp.dot(pick[: sz.rows], matrix_ref[...], preferred_element_type=f32)
        half = half.astype(bf16)
        cuts = list(range(0, sz.depth, TILE)) + [sz.depth]
        for r0, r1 in zip(cuts[:-1], cuts[1:]):
            r1 = min(r1, sz.rows)
            block = lax.dot_general(
                half[r0:r1], pick[r0:], (((1,), (1,)), ((), ())), preferred_element_type=f32
            ).astype(bf16)
            out_ref[slot, r0:r1, r0:] = block
            for c0, c1 in zip(cuts[:-1], cuts[1:]):
                if c0 > r0:
                    mirror = block[:, c0 - r0 : c1 - r0].T
                    c1 = min(c1, sz.rows)
                    out_ref[slot, c0:c1, r0:r1] = mirror[: c1 - c0]


def field_row(inv, pot):
    lane = lax.broadcasted_iota(jnp.int32, inv.shape, inv.ndim - 1)
    row = jnp.zeros_like(inv)
    for at, rest in enumerate((inv, pot)):
        for k in range(3):
            part = rest.astype(bf16).astype(f32)
            rest = rest - part
            row = jnp.where(lane == 3 * at + k, part, row)
    return row.astype(bf16)


def field_rows(sz, inv, pot, count):
    inv, pot = inv.T, pot.T
    shape = (sz.ez, sz.width)
    for at in range(count):
        yield at, field_row(
            jnp.broadcast_to(inv[:, at : at + 1], shape), jnp.broadcast_to(pot[:, at : at + 1], shape)
        )


def fields_of(row):
    row = row.astype(f32)
    return [
        jnp.broadcast_to(sum(row[:, 3 * at + k : 3 * at + k + 1] for k in range(3)), row.shape)
        for at in range(2)
    ]


def pack_kernel(
    sz, vec_hbm, res_hbm, inv_hbm, pot_hbm, conn_hbm, to_x, to_y, conn_ref, at_x, at_y, sems
):
    pairs = [
        (inv_hbm.at[0], at_x.at[0]), (pot_hbm.at[0], at_x.at[1]),
        (inv_hbm.at[:, 0], at_y.at[0]), (pot_hbm.at[:, 0], at_y.at[1]),
        (res_hbm.at[0], to_x.at[:, :, pl.ds(0, sz.res)]),
        (res_hbm.at[:, 0], to_y.at[:, :, pl.ds(0, sz.res)]),
    ]
    for b in range(sz.blocks):
        lanes = pl.ds(sz.res + b * sz.width, sz.width)
        pairs.append((vec_hbm.at[b, 0], to_x.at[:, :, lanes]))
        pairs.append((vec_hbm.at[b, :, 0], to_y.at[:, :, lanes]))
    pairs.append((conn_hbm, conn_ref))
    copies = [pltpu.make_async_copy(a, b, sems.at[k]) for k, (a, b) in enumerate(pairs)]
    for copy in copies:
        copy.start()
    for copy in copies[:4]:
        copy.wait()
    for j, row in field_rows(sz, at_x[0], at_x[1], sz.ey):
        to_x[j, :, sz.res + sz.full :] = row
    for i, row in field_rows(sz, at_y[0], at_y[1], sz.ex):
        to_y[i, :, sz.res + sz.full :] = row
    for copy in copies[4:]:
        copy.wait()


def turn_kernel(sz, res_ref, from_x, from_y, corner, out_ref):
    own = sz.own_edges * sz.ez
    for g in range(0, sz.res, LANES):
        lanes = slice(g, g + LANES)
        out_ref[lanes, :own] = res_ref[:, lanes].T
        rest = sz.edges - sz.own_edges - sz.ey - sz.gx
        parts = [from_x[:, :, lanes], from_y[:, :, lanes], corner[:, :, lanes]]
        if rest:
            parts.append(jnp.zeros((rest, sz.ez, LANES), bf16))
        ghosts = jnp.concatenate(parts, axis=0)
        out_ref[lanes, own:] = ghosts.reshape(-1, LANES).T


def vectors_of(sz, edge):
    lanes = [slice(sz.res + b * sz.width, sz.res + (b + 1) * sz.width) for b in range(sz.blocks)]
    return jnp.stack([edge[:, at] for at in lanes]).astype(f32)


class Nodes:
    def __init__(self, sz, vec, from_x, from_y, own_inv, own_pot, ghost_x, ghost_y, corners=None):
        self.sz, self.vec, self.from_x, self.from_y = sz, vec, from_x, from_y
        self.own, self.ghost_x, self.ghost_y, self.corners = (own_inv, own_pot), ghost_x, ghost_y, corners

    def x(self, i, j):
        sz = self.sz
        if i < sz.ex and j < sz.ey:
            return self.vec[:, i, j].astype(f32)
        return vectors_of(sz, self.from_x[j] if i == sz.ex else self.from_y[i])

    def field(self, at, i, j):
        sz = self.sz
        if i < sz.ex and j < sz.ey:
            return self.own[at][i, j]
        if i < sz.ex:
            return self.ghost_y[at, i]
        if j < sz.ey:
            return self.ghost_x[at, j]
        return self.corners[at]

    def inv(self, i, j):
        return self.field(0, i, j)

    def pot(self, i, j):
        return self.field(1, i, j)


class Sums:
    def __init__(self, sz, even, acc, face, near, far, corner=None):
        self.sz, self.even, self.acc, self.face = sz, even, acc, face
        self.near, self.far, self.corner = near, far, corner

    def at(self, i, j):
        sz = self.sz
        total = self.acc[:, i, j]
        side = 1 if i == 0 else 0 if i == sz.ex else None
        if side is not None:
            total = total + self.face[side, :, j].astype(f32)
        if j in (0, sz.ey):
            is_near = self.even if j == sz.ey else jnp.logical_not(self.even)
            total = total + jnp.where(is_near, self.near[:, i].astype(f32), self.far[:, i].astype(f32))
            if side is not None:
                total = total + jnp.where(
                    is_near, self.corner[side, 0].astype(f32), self.corner[side, 1].astype(f32)
                )
        return total


def corner_edges(sz):
    return [(i, j) for i in (0, sz.ex) for j in (0, sz.ey)]


def main_products(sz, prepare, u_ref, mat_refs, rhs_ref, out_ref):
    width = sz.width
    flat = sz.gx * sz.gy * sz.gz
    u_flat = u_ref.reshape(sz.blocks * flat, width)
    matrices = [ref.at[c] for ref in mat_refs for c in range(ref.shape[0])]
    last = sz.nodes // 8 * 8
    ready = set()
    for cell, (x0, y0, z0) in enumerate(sz.origins):
        slot = cell % 2
        if cell < 2:
            rhs_ref[slot, : sz.base] = jnp.zeros((sz.base, sz.full), f32)
            rhs_ref[slot, last:] = jnp.zeros((sz.depth - last, sz.full), f32)
        for place, i, j, count in sz.runs(cell):
            for at in range(j, j + count):
                if (x0 + i, y0 + at) not in ready:
                    prepare(x0 + i, y0 + at)
                    ready.add((x0 + i, y0 + at))
        z1 = z0 + sz.p
        wrap = z1 % sz.gz
        for b in range(sz.blocks):
            lanes = slice(b * width, (b + 1) * width)
            for place, i, j, count in sz.runs(cell):
                row = sz.base + place * sz.p
                rhs_ref[slot, row : row + count * sz.p, lanes] = u_ref[
                    b, x0 + i, y0 + j : y0 + j + count, z0:z1
                ].reshape(count * sz.p, width)
        for b in range(sz.blocks):
            lanes = slice(b * width, (b + 1) * width)
            for place, i, j, count in sz.runs(cell):
                start = b * flat + ((x0 + i) * sz.gy + y0 + j) * sz.gz + wrap
                rhs_ref[slot, sz.tail + place : sz.tail + place + count, lanes] = u_flat[
                    pl.ds(start, count, stride=sz.gz)
                ]
        out_ref[cell] = jnp.dot(
            matrices[cell][...], rhs_ref[slot].astype(bf16), preferred_element_type=f32
        )


def corner_products(sz, u_corner, prod_ref, mat_refs, small_ref, tail_ref, acc_ref):
    width = sz.width
    flat = sz.gx * sz.gy * sz.gz
    acc_flat = acc_ref.reshape(sz.blocks * flat, width)
    matrices = [ref.at[c] for ref in mat_refs for c in range(ref.shape[0])]
    small_ref[...] = jnp.zeros_like(small_ref)
    touched = set()
    for cell, (x0, y0, z0) in enumerate(sz.origins):
        z1 = z0 + sz.p
        wrap = z1 % sz.gz
        corners = sz.cell_corners(cell)
        for rank, (i, j) in enumerate(corners):
            value = u_corner[sz.corner(x0 + i, y0 + j)]
            last = len(corners) * sz.p + rank
            for b in range(sz.blocks):
                lanes = slice(b * width, (b + 1) * width)
                small_ref[rank * sz.p : (rank + 1) * sz.p, lanes] = value[b, z0:z1]
                small_ref[last : last + 1, lanes] = value[b, wrap : wrap + 1]
        total = prod_ref[cell] + jnp.dot(
            matrices[cell][:, : small_ref.shape[0]], small_ref[...].astype(bf16),
            preferred_element_type=f32,
        )
        tail_ref[cell, : sz.base] = total[: sz.base]
        tail_ref[cell, sz.base :] = total[sz.tail :]
        spans = [(rank * sz.p, i, j, 1) for rank, (i, j) in enumerate(corners)]
        spans += [(sz.base + place * sz.p, i, j, count) for place, i, j, count in sz.runs(cell)]
        for row, i, j, count in spans:
            for at in range(count):
                part = total[row + at * sz.p : row + (at + 1) * sz.p]
                key = (x0 + i, y0 + j + at, z0)
                for b in range(sz.blocks):
                    value = part[:, b * width : (b + 1) * width]
                    if key in touched:
                        value = acc_ref[b, key[0], key[1], z0:z1] + value
                    acc_ref[b, key[0], key[1], z0:z1] = value
                touched.add(key)
    for cell, (x0, y0, z0) in enumerate(sz.origins):
        wrap = (z0 + sz.p) % sz.gz
        corners = sz.cell_corners(cell)
        spans = [(len(corners) * sz.p + rank, i, j, 1) for rank, (i, j) in enumerate(corners)]
        spans += [(sz.base + place, i, j, count) for place, i, j, count in sz.runs(cell)]
        for row, i, j, count in spans:
            for b in range(sz.blocks):
                start = b * flat + ((x0 + i) * sz.gy + y0 + j) * sz.gz + wrap
                rows = pl.ds(start, count, stride=sz.gz) if count > 1 else pl.ds(start, 1)
                lanes = slice(b * width, (b + 1) * width)
                acc_flat[rows] = acc_flat[rows] + tail_ref[cell, row : row + count, lanes]


def write_messages(sz, even, acc_ref, face, near, far):
    at_near = jnp.where(even, sz.ey, 0)
    for b in range(sz.blocks):
        face[0, b] = acc_ref[b, 0].astype(bf16)
        face[1, b] = acc_ref[b, sz.ex].astype(bf16)
        near[b] = acc_ref[b, :, at_near].astype(bf16)
        far[b] = acc_ref[b, :, sz.ey - at_near].astype(bf16)


def corner_pack_kernel(sz, near, far, out_ref):
    for side, i in enumerate((0, sz.ex)):
        for slot, ref in enumerate((near, far)):
            out_ref[side, slot] = ref[:, i]


def first_main(sz, n_mat, vec, from_x, from_y, own_inv, own_pot, *refs):
    mats = refs[:n_mat]
    prod_ref, ghost_x, ghost_y, u_ref, rhs_ref = refs[n_mat:]
    for j in range(sz.ey):
        ghost_x[0, j], ghost_x[1, j] = fields_of(from_x[j, :, sz.res + sz.full :])
    for i in range(sz.ex):
        ghost_y[0, i], ghost_y[1, i] = fields_of(from_y[i, :, sz.res + sz.full :])
    nodes = Nodes(sz, vec, from_x, from_y, own_inv, own_pot, ghost_x, ghost_y)

    def prepare(i, j):
        u_ref[:, i, j] = nodes.x(i, j) * nodes.inv(i, j)

    main_products(sz, prepare, u_ref, mats, rhs_ref, prod_ref)


def first_corner(sz, n_mat, even_ref, vec, from_x, from_y, corner, own_inv, own_pot, ghost_x, ghost_y,
                 prod_ref, *refs):
    mats = refs[:n_mat]
    acc_ref, face, near, far, last_x, last_field, small_ref, tail_ref = refs[n_mat:]
    last_field[0], last_field[1] = fields_of(corner[0, :, sz.res + sz.full :])
    last_x[...] = vectors_of(sz, corner[0])
    nodes = Nodes(sz, vec, from_x, from_y, own_inv, own_pot, ghost_x, ghost_y, last_field)
    u_corner = []
    for i, j in corner_edges(sz):
        x = last_x[...] if (i, j) == (sz.ex, sz.ey) else nodes.x(i, j)
        u_corner.append(x * nodes.inv(i, j))
    corner_products(sz, u_corner, prod_ref, mats, small_ref, tail_ref, acc_ref)
    write_messages(sz, even_ref[0] == 0, acc_ref, face, near, far)


def second_main(sz, n_mat, even_ref, vec, from_x, from_y, own_inv, own_pot, ghost_x, ghost_y,
                acc_in, face_in, near_in, far_in, *refs):
    mats = refs[:n_mat]
    prod_ref, y_ref, u_ref, rhs_ref = refs[n_mat:]
    nodes = Nodes(sz, vec, from_x, from_y, own_inv, own_pot, ghost_x, ghost_y)
    sums = Sums(sz, even_ref[0] == 0, acc_in, face_in, near_in, far_in)

    def prepare(i, j):
        old, inv = nodes.x(i, j), nodes.inv(i, j)
        image = inv * sums.at(i, j) + nodes.pot(i, j) * old
        new = (image - center_shift * old) / half_width
        y_ref[:, i, j] = new
        u_ref[:, i, j] = inv * new

    main_products(sz, prepare, u_ref, mats, rhs_ref, prod_ref)


def second_corner(sz, n_mat, even_ref, vec, from_x, from_y, own_inv, own_pot, ghost_x, ghost_y, last_x,
                  last_field, acc_in, face_in, near_in, far_in, corner_in, prod_ref, *refs):
    mats = refs[:n_mat]
    acc_ref, face, near, far, y_corner, small_ref, tail_ref = refs[n_mat:]
    even = even_ref[0] == 0
    nodes = Nodes(sz, vec, from_x, from_y, own_inv, own_pot, ghost_x, ghost_y, last_field)
    sums = Sums(sz, even, acc_in, face_in, near_in, far_in, corner_in)
    u_corner = []
    for at, (i, j) in enumerate(corner_edges(sz)):
        old = last_x[...] if (i, j) == (sz.ex, sz.ey) else nodes.x(i, j)
        inv = nodes.inv(i, j)
        image = inv * sums.at(i, j) + nodes.pot(i, j) * old
        new = (image - center_shift * old) / half_width
        y_corner[at] = new
        u_corner.append(inv * new)
    corner_products(sz, u_corner, prod_ref, mats, small_ref, tail_ref, acc_ref)
    write_messages(sz, even, acc_ref, face, near, far)


def third_main(sz, n_mat, even_ref, vec, from_x, from_y, own_inv, own_pot, ghost_x, ghost_y,
               acc_in, face_in, near_in, far_in, y_ref, *refs):
    mats = refs[:n_mat]
    prod_ref, new_ref, u_ref, rhs_ref = refs[n_mat:]
    nodes = Nodes(sz, vec, from_x, from_y, own_inv, own_pot, ghost_x, ghost_y)
    sums = Sums(sz, even_ref[0] == 0, acc_in, face_in, near_in, far_in)

    def prepare(i, j):
        old, inv = y_ref[:, i, j], nodes.inv(i, j)
        image = inv * sums.at(i, j) + nodes.pot(i, j) * old
        new = 2.0 * (image - center_shift * old) / half_width - nodes.x(i, j)
        new_ref[:, i, j] = new
        u_ref[:, i, j] = inv * new

    main_products(sz, prepare, u_ref, mats, rhs_ref, prod_ref)


def third_corner(sz, n_mat, norm_scale, even_ref, vec, from_x, from_y, own_inv, own_pot, ghost_x, ghost_y,
                 last_x, last_field, acc_in, face_in, near_in, far_in, corner_in, prod_ref, y_ref,
                 y_corner, new_ref, turned, *refs):
    mats = refs[:n_mat]
    out_hbm, face, side, corner, margin = refs[n_mat : n_mat + 5]
    part_ref, sem, acc_ref, rows_ref, small_ref, tail_ref = refs[n_mat + 5 :]
    nodes = Nodes(sz, vec, from_x, from_y, own_inv, own_pot, ghost_x, ghost_y, last_field)
    sums = Sums(sz, even_ref[0] == 0, acc_in, face_in, near_in, far_in, corner_in)
    u_corner, new_corner = [], []
    for at, (i, j) in enumerate(corner_edges(sz)):
        x = last_x[...] if (i, j) == (sz.ex, sz.ey) else nodes.x(i, j)
        old, inv = y_corner[at], nodes.inv(i, j)
        image = inv * sums.at(i, j) + nodes.pot(i, j) * old
        new_corner.append(2.0 * (image - center_shift * old) / half_width - x)
        u_corner.append(inv * new_corner[-1])
    corner_products(sz, u_corner, prod_ref, mats, small_ref, tail_ref, acc_ref)

    def put_row(at, value):
        for b in range(sz.blocks):
            rows_ref[at, :, b * sz.width : (b + 1) * sz.width] = value[b]

    copies = []
    for i in range(sz.gx):
        for j in range(sz.gy):
            acc, inv = acc_ref[:, i, j], nodes.inv(i, j)
            if i == sz.ex or j == sz.ey:
                value = gain * (inv * acc)
                rounded = value.astype(bf16)
                if j < sz.ey:
                    face[:, j] = rounded
                elif i < sz.ex:
                    side[:, i] = value
                else:
                    corner[...] = rounded
                put_row(sz.own_edges + (j if j < sz.ey else sz.ey + i), rounded)
                continue
            at = sz.corner(i, j)
            old = y_ref[:, i, j] if at is None else y_corner[at]
            new = new_ref[:, i, j] if at is None else new_corner[at]
            image = inv * acc + nodes.pot(i, j) * new
            value = 2.0 * (image - center_shift * new) / half_width - old
            part_ref[:, i, j] = value
            put_row(i * sz.ey + j, value.astype(bf16))
        if i < sz.ex:
            copies.append(pltpu.make_async_copy(part_ref.at[:, i], out_hbm.at[:, i], sem.at[i]))
            copies[-1].start()
    for at in range(sz.own_edges + sz.ey + sz.gx, sz.edges):
        rows_ref[at] = jnp.zeros((sz.ez, sz.full), bf16)
    local = jnp.dot(
        turned[...], rows_ref[...].reshape(sz.edges * sz.ez, sz.full), preferred_element_type=f32
    )
    margin[...] = (local * norm_scale).astype(bf16)
    for copy in copies:
        copy.wait()


def last_side_kernel(sz, side_ref, corner_ref, face_in, out_ref, face_out):
    del face_in, face_out
    for i in range(sz.ex):
        value = side_ref[:, i]
        if i == 0:
            value = value + corner_ref[...].astype(f32)
        out_ref[:, i] = value.astype(out_ref.dtype)


def last_kernel(sz, old_hbm, face, side, out_hbm, at_x, at_y, sems):
    del old_hbm
    pairs = [(at_x, out_hbm.at[:, 0]), (at_y, out_hbm.at[:, pl.ds(1, sz.ex - 1), 0])]
    loads = [pltpu.make_async_copy(b, a, sems.at[k]) for k, (a, b) in enumerate(pairs)]
    stores = [pltpu.make_async_copy(a, b, sems.at[k]) for k, (a, b) in enumerate(pairs)]
    for copy in loads:
        copy.start()
    for copy in loads:
        copy.wait()
    at_x[:, 0] += side[:, 0].astype(f32)
    for j in range(sz.ey):
        at_x[:, j] += face[:, j].astype(f32)
    for i in range(1, sz.ex):
        at_y[:, i - 1] += side[:, i].astype(f32)
    for copy in stores:
        copy.start()
    for copy in stores:
        copy.wait()


def like(shape, dtype):
    return jax.ShapeDtypeStruct(shape, dtype)


def call(kernel, name, flops, out_shape, scratch, operands, hbm=0, scalar_first=False, aliases=None,
         out_hbm=0):
    out_shape = [like(s.shape, s.dtype) for s in out_shape]
    size = sum(math.prod(s.shape) * jnp.dtype(s.dtype).itemsize for s in (*operands, *out_shape))
    whole = pl.BlockSpec(memory_space=pltpu.VMEM)
    specs = [pl.BlockSpec(memory_space=pltpu.HBM)] * hbm + [whole] * (len(operands) - hbm)
    if scalar_first:
        specs[0] = pl.BlockSpec(memory_space=pltpu.SMEM)
    out_specs = [pl.BlockSpec(memory_space=pltpu.HBM)] * out_hbm + [whole] * (len(out_shape) - out_hbm)
    for source, target in (aliases or {}).items():
        if source >= hbm:
            specs[source] = out_specs[target] = pl.BlockSpec(memory_space=pl.ANY)
    out_shape = [pltpu.HBM(s.shape, s.dtype) for s in out_shape[:out_hbm]] + out_shape[out_hbm:]
    operands = [pltpu.with_memory_space_constraint(a, pltpu.HBM) for a in operands[:hbm]] + list(
        operands[hbm:]
    )
    return pl.pallas_call(
        kernel,
        in_specs=specs,
        out_specs=out_specs,
        out_shape=out_shape,
        scratch_shapes=scratch,
        input_output_aliases=aliases or {},
        compiler_params=pltpu.CompilerParams(vmem_limit_bytes=VMEM_LIMIT),
        cost_estimate=pl.CostEstimate(flops=flops, bytes_accessed=size, transcendentals=0),
        name=name,
    )(*operands)


def body(vectors, resident, inv_mass, potential, cell_matrix, connectivity):
    sz = Sizes(vectors, resident, inv_mass, connectivity)
    nx, ny = lax.axis_size("dx"), lax.axis_size("dy")
    norm_scale = 1.0 / math.sqrt(sz.ex * sz.ey * sz.ez * nx * ny)
    blocks, ez, width, full = sz.blocks, sz.ez, sz.width, sz.full
    res_count = resident.shape[-1]
    tile = (ez, width)

    conn = connectivity.reshape(sz.cells, sz.nodes)
    to_x, to_y, conn = call(
        functools.partial(pack_kernel, sz), "pack", 0,
        [like((sz.ey, ez, sz.wide), bf16), like((sz.ex, ez, sz.wide), bf16), conn],
        [
            pltpu.VMEM((2, sz.ey, ez), f32), pltpu.VMEM((2, sz.ex, ez), f32),
            pltpu.SemaphoreType.DMA((7 + 2 * blocks,)),
        ],
        [vectors, resident, inv_mass, potential, conn], hbm=5,
    )
    from_x = send(to_x, -1, 0)
    from_y = send(to_y, 0, -1)

    halves = 2 if sz.cells % 2 == 0 else 1
    step = sz.cells // halves
    mats = []
    for at in range(0, sz.cells, step):
        mats += call(
            functools.partial(order_kernel, sz, at), "order_cells", 4 * step * sz.depth**3,
            [like((step, sz.rows, sz.depth), bf16)],
            [], [cell_matrix, conn],
        )
    own_inv = jnp.broadcast_to(inv_mass[..., None], inv_mass.shape + (width,))
    own_pot = jnp.broadcast_to(potential[..., None], inv_mass.shape + (width,))
    parity = jnp.reshape(lax.axis_index("dy") % 2, (1,)).astype(jnp.int32)
    ghost_corner = send(from_y[:1], -1, 0)

    grid = (blocks, sz.gx, sz.gy) + tile
    own = (blocks, sz.ex, sz.ey) + tile
    products = like((sz.cells, sz.rows, full), f32)
    state_grid = like(grid, f32)
    messages = [
        like((2, blocks, sz.gy) + tile, bf16),
        like((blocks, sz.gx) + tile, bf16),
        like((blocks, sz.gx) + tile, bf16),
    ]
    main_scratch = [pltpu.VMEM(grid, f32), pltpu.VMEM((2, sz.depth, full), f32)]
    corner_scratch = [
        pltpu.VMEM((LANES, full), f32),
        pltpu.VMEM((sz.cells, sz.base + sz.rows - sz.tail, full), f32),
    ]
    n_mat = len(mats)
    flops = 2 * sz.cells * sz.rows * sz.depth * full
    small_flops = 2 * sz.cells * sz.rows * LANES * full

    def exchange(face, near, far):
        face = swap_x(face)
        near, far = swap_y(near, far)
        (corner,) = call(
            functools.partial(corner_pack_kernel, sz), "corner_pack", 0,
            [like((2, 2) + sz.edge, bf16)], [], [near, far],
        )
        return [face, near, far], swap_x(corner)

    prod, ghost_x, ghost_y = call(
        functools.partial(first_main, sz, n_mat), "first_main", flops,
        [products, like((2, sz.ey) + tile, f32), like((2, sz.ex) + tile, f32)], main_scratch,
        [vectors, from_x, from_y, own_inv, own_pot, *mats],
    )
    acc, face, near, far, last_x, last_field = call(
        functools.partial(first_corner, sz, n_mat), "first_corner", small_flops,
        [state_grid, *messages, like(sz.edge, f32), like((2,) + tile, f32)], corner_scratch,
        [
            parity, vectors, from_x, from_y, ghost_corner, own_inv, own_pot, ghost_x, ghost_y, prod, *mats,
        ],
        scalar_first=True,
    )
    (turned,) = call(
        functools.partial(turn_kernel, sz), "turn_residents", flops // 2,
        [like((res_count, sz.edges * ez), bf16)], [],
        [resident.reshape(-1, res_count), from_x, from_y, ghost_corner],
    )
    got, corner = exchange(face, near, far)
    state = [vectors, from_x, from_y, own_inv, own_pot, ghost_x, ghost_y]
    ends = [last_x, last_field]
    prod, y1 = call(
        functools.partial(second_main, sz, n_mat), "second_main", flops,
        [products, state_grid], main_scratch,
        [parity, *state, acc, *got, *mats], scalar_first=True,
    )
    acc, face, near, far, y1_corner = call(
        functools.partial(second_corner, sz, n_mat), "second_corner", small_flops,
        [state_grid, *messages, like((4,) + sz.edge, f32)], corner_scratch,
        [parity, *state, *ends, acc, *got, corner, prod, *mats], scalar_first=True,
    )
    got, corner = exchange(face, near, far)
    prod, y2 = call(
        functools.partial(third_main, sz, n_mat), "third_main", flops,
        [products, state_grid], main_scratch,
        [parity, *state, acc, *got, y1, *mats], scalar_first=True,
    )
    filtered, face, side, corner, local = call(
        functools.partial(third_corner, sz, n_mat, norm_scale), "third_corner",
        small_flops + 2 * res_count * sz.edges * ez * full,
        [
            like(own, f32),
            like((blocks, sz.ey) + tile, bf16), like((blocks, sz.ex) + tile, f32), like(sz.edge, bf16),
            like((res_count, full), bf16),
        ],
        [pltpu.VMEM(own, f32), pltpu.SemaphoreType.DMA((sz.ex,)), pltpu.VMEM(grid, f32), pltpu.VMEM((sz.edges, ez, full), bf16)] + corner_scratch,
        [parity, *state, *ends, acc, *got, corner, prod, y1, y1_corner, y2, turned, *mats],
        scalar_first=True, out_hbm=1,
    )

    pieces = lax.all_to_all(local.reshape(ny, -1, full), "dy", 0, 0)
    mine = jnp.sum(pieces.astype(f32), axis=0)
    margin = mine
    for steps in range(1, nx):
        margin = margin + send(mine, steps, 0)

    corner = send(corner, 1, 0)
    side, face = call(
        functools.partial(last_side_kernel, sz), "last_side", 0,
        [like((blocks, sz.ex) + tile, bf16), face], [], [side, corner, face], aliases={2: 1},
    )
    face = send(face, 1, 0)
    side = send(side, 0, 1)
    (filtered,) = call(
        functools.partial(last_kernel, sz), "last", 0, [like(own, f32)],
        [
            pltpu.VMEM((blocks, sz.ey) + tile, f32), pltpu.VMEM((blocks, sz.ex - 1) + tile, f32),
            pltpu.SemaphoreType.DMA((2,)),
        ],
        [filtered, face, side], hbm=1, out_hbm=1, aliases={0: 0},
    )
    return (filtered, margin)


def solution(mesh):
    return jax.shard_map(
        body,
        mesh=mesh,
        in_specs=(
            P(None, "dx", "dy", None, None),
            P("dx", "dy", None, None),
            P("dx", "dy", None),
            P("dx", "dy", None),
            P(),
            P("dx", "dy", None, None),
        ),
        out_specs=(P(None, "dx", "dy", None, None), P("dy", None)),
        check_vma=False,
    )
```

```python
import functools
import math

import jax
import jax.numpy as jnp
from jax import lax
from jax.experimental import pallas as pl
from jax.experimental.pallas import tpu as pltpu
from jax.sharding import PartitionSpec as P

LANES = 128
TILE = 256
SUB = 16
VMEM_LIMIT = 16 * 1024 * 1024

center_shift = 1.2
half_width = 2.0
gain = 2.0 / half_width

f32, bf16 = jnp.float32, jnp.bfloat16


def round_up(value, step):
    return -(-value // step) * step


class Sizes:
    def __init__(self, vectors, resident, inv_mass, connectivity):
        self.blocks = vectors.shape[0]
        self.width = vectors.shape[-1]
        self.full = self.blocks * self.width
        self.res = resident.shape[-1]
        self.wide = self.res + self.full + self.width
        self.ex, self.ey, self.ez = inv_mass.shape
        self.cells, self.nodes = connectivity.shape[2:]
        self.n1 = round(self.nodes ** (1.0 / 3.0))
        self.p = self.n1 - 1
        self.cx, self.cy, self.cz = self.ex // self.p, self.ey // self.p, self.ez // self.p
        self.gx, self.gy, self.gz = self.ex + 1, self.ey + 1, self.ez
        self.edge = (self.blocks, self.ez, self.width)
        self.origins = [
            (a * self.p, b * self.p, c * self.p)
            for a in range(self.cx)
            for b in range(self.cy)
            for c in range(self.cz)
        ]
        self.most = max(len(self.cell_corners(cell)) for cell in range(self.cells))
        self.base = round_up(self.most * self.n1, 8)
        plain = self.n1 * self.n1 - min(len(self.cell_corners(cell)) for cell in range(self.cells))
        self.tail = self.base + plain * self.p
        self.rows = round_up(self.tail + plain, SUB)
        self.depth = round_up(self.rows, LANES)
        self.own_edges = self.ex * self.ey
        self.edges = round_up(self.own_edges + self.ey + self.gx, LANES // self.ez)

    def corner(self, i, j):
        if i in (0, self.ex) and j in (0, self.ey):
            return 2 * (i // self.ex) + j // self.ey
        return None

    def cell_corners(self, cell):
        x0, y0, _ = self.origins[cell]
        return [
            (i, j)
            for i in range(self.n1)
            for j in range(self.n1)
            if self.corner(x0 + i, y0 + j) is not None
        ]

    def runs(self, cell):
        corners = self.cell_corners(cell)
        place = 0
        for i in range(self.n1):
            js = [j for j in range(self.n1) if (i, j) not in corners]
            while js:
                count = 1
                while count < len(js) and js[count] == js[0] + count:
                    count += 1
                yield place, i, js[0], count
                place += count
                js = js[count:]


def send(value, steps_x, steps_y):
    nx, ny = lax.axis_size("dx"), lax.axis_size("dy")
    pairs = [
        (a * ny + b, ((a + steps_x) % nx) * ny + (b + steps_y) % ny)
        for a in range(nx)
        for b in range(ny)
    ]
    return lax.ppermute(value, ("dx", "dy"), pairs)


def swap_x(value):
    if lax.axis_size("dx") == 2:
        return send(value, 1, 0)
    return jnp.stack([send(value[0], -1, 0), send(value[1], 1, 0)])


def send_near(value):
    pairs = [(b, b + 1 if b % 2 == 0 else b - 1) for b in range(lax.axis_size("dy"))]
    return lax.ppermute(value, "dy", pairs)


def swap_y(near, far):
    ny = lax.axis_size("dy")
    far_pairs = [(b, (b - 1 if b % 2 == 0 else b + 1) % ny) for b in range(ny)]
    far = lax.ppermute(far, "dy", far_pairs)
    return send_near(near), far


def order_kernel(sz, first, matrix_ref, conn_ref, out_ref):
    for slot in range(out_ref.shape[0]):
        cell = first + slot
        x0, y0, z0 = sz.origins[cell]
        conn = conn_ref[cell : cell + 1, :].astype(f32)
        li = jnp.floor((conn + 0.5) * (1.0 / (sz.gy * sz.gz)))
        rest = conn - li * (sz.gy * sz.gz)
        lj = jnp.floor((rest + 0.5) * (1.0 / sz.gz))
        lk = rest - lj * sz.gz - z0
        lk = jnp.where(lk < 0, lk + sz.gz, lk)
        column = (li - x0) * sz.n1 + (lj - y0)
        corners = [i * sz.n1 + j for i, j in sz.cell_corners(cell)]
        place = column
        for at in corners:
            place = place - jnp.where(column > at, 1.0, 0.0)
        index = jnp.where(lk < sz.p, sz.base + place * sz.p + lk, sz.tail + place)
        for rank, at in enumerate(corners):
            special = jnp.where(lk < sz.p, rank * sz.p + lk, len(corners) * sz.p + rank)
            index = jnp.where(column == at, special, index)
        index = index.astype(jnp.int32)
        row = lax.broadcasted_iota(jnp.int32, (sz.depth, sz.nodes), 0)
        pick = (row == index).astype(f32).astype(bf16)
        half = jnp.dot(pick[: sz.rows], matrix_ref[...], preferred_element_type=f32)
        half = half.astype(bf16)
        cuts = list(range(0, sz.depth, TILE)) + [sz.depth]
        for r0, r1 in zip(cuts[:-1], cuts[1:]):
            r1 = min(r1, sz.rows)
            block = lax.dot_general(
                half[r0:r1], pick[r0:], (((1,), (1,)), ((), ())), preferred_element_type=f32
            ).astype(bf16)
            out_ref[slot, r0:r1, r0:] = block
            for c0, c1 in zip(cuts[:-1], cuts[1:]):
                if c0 > r0:
                    mirror = block[:, c0 - r0 : c1 - r0].T
                    c1 = min(c1, sz.rows)
                    out_ref[slot, c0:c1, r0:r1] = mirror[: c1 - c0]


def field_row(inv, pot):
    lane = lax.broadcasted_iota(jnp.int32, inv.shape, inv.ndim - 1)
    row = jnp.zeros_like(inv)
    for at, rest in enumerate((inv, pot)):
        for k in range(3):
            part = rest.astype(bf16).astype(f32)
            rest = rest - part
            row = jnp.where(lane == 3 * at + k, part, row)
    return row.astype(bf16)


def field_rows(sz, inv, pot, count):
    inv, pot = inv.T, pot.T
    shape = (sz.ez, sz.width)
    for at in range(count):
        yield at, field_row(
            jnp.broadcast_to(inv[:, at : at + 1], shape), jnp.broadcast_to(pot[:, at : at + 1], shape)
        )


def fields_of(row):
    row = row.astype(f32)
    return [
        jnp.broadcast_to(sum(row[:, 3 * at + k : 3 * at + k + 1] for k in range(3)), row.shape)
        for at in range(2)
    ]


def pack_kernel(
    sz, vec_hbm, res_hbm, inv_hbm, pot_hbm, conn_hbm, to_x, to_y, conn_ref, at_x, at_y, sems
):
    pairs = [
        (inv_hbm.at[0], at_x.at[0]), (pot_hbm.at[0], at_x.at[1]),
        (inv_hbm.at[:, 0], at_y.at[0]), (pot_hbm.at[:, 0], at_y.at[1]),
        (res_hbm.at[0], to_x.at[:, :, pl.ds(0, sz.res)]),
        (res_hbm.at[:, 0], to_y.at[:, :, pl.ds(0, sz.res)]),
    ]
    for b in range(sz.blocks):
        lanes = pl.ds(sz.res + b * sz.width, sz.width)
        pairs.append((vec_hbm.at[b, 0], to_x.at[:, :, lanes]))
        pairs.append((vec_hbm.at[b, :, 0], to_y.at[:, :, lanes]))
    pairs.append((conn_hbm, conn_ref))
    copies = [pltpu.make_async_copy(a, b, sems.at[k]) for k, (a, b) in enumerate(pairs)]
    for copy in copies:
        copy.start()
    for copy in copies[:4]:
        copy.wait()
    for j, row in field_rows(sz, at_x[0], at_x[1], sz.ey):
        to_x[j, :, sz.res + sz.full :] = row
    for i, row in field_rows(sz, at_y[0], at_y[1], sz.ex):
        to_y[i, :, sz.res + sz.full :] = row
    for copy in copies[4:]:
        copy.wait()


def turn_kernel(sz, res_ref, from_x, from_y, corner, out_ref):
    own = sz.own_edges * sz.ez
    for g in range(0, sz.res, LANES):
        lanes = slice(g, g + LANES)
        out_ref[lanes, :own] = res_ref[:, lanes].T
        rest = sz.edges - sz.own_edges - sz.ey - sz.gx
        parts = [from_x[:, :, lanes], from_y[:, :, lanes], corner[:, :, lanes]]
        if rest:
            parts.append(jnp.zeros((rest, sz.ez, LANES), bf16))
        ghosts = jnp.concatenate(parts, axis=0)
        out_ref[lanes, own:] = ghosts.reshape(-1, LANES).T


def vectors_of(sz, edge):
    lanes = [slice(sz.res + b * sz.width, sz.res + (b + 1) * sz.width) for b in range(sz.blocks)]
    return jnp.stack([edge[:, at] for at in lanes]).astype(f32)


class Nodes:
    def __init__(self, sz, vec, from_x, from_y, own_inv, own_pot, ghost_x, ghost_y, corners=None):
        self.sz, self.vec, self.from_x, self.from_y = sz, vec, from_x, from_y
        self.own, self.ghost_x, self.ghost_y, self.corners = (own_inv, own_pot), ghost_x, ghost_y, corners

    def x(self, i, j):
        sz = self.sz
        if i < sz.ex and j < sz.ey:
            return self.vec[:, i, j].astype(f32)
        return vectors_of(sz, self.from_x[j] if i == sz.ex else self.from_y[i])

    def field(self, at, i, j):
        sz = self.sz
        if i < sz.ex and j < sz.ey:
            return self.own[at][i, j]
        if i < sz.ex:
            return self.ghost_y[at, i]
        if j < sz.ey:
            return self.ghost_x[at, j]
        return self.corners[at]

    def inv(self, i, j):
        return self.field(0, i, j)

    def pot(self, i, j):
        return self.field(1, i, j)


class Sums:
    def __init__(self, sz, even, acc, face, near, far, corner=None):
        self.sz, self.even, self.acc, self.face = sz, even, acc, face
        self.near, self.far, self.corner = near, far, corner

    def at(self, i, j):
        sz = self.sz
        total = self.acc[:, i, j]
        side = 1 if i == 0 else 0 if i == sz.ex else None
        if side is not None:
            total = total + self.face[side, :, j].astype(f32)
        if j in (0, sz.ey):
            is_near = self.even if j == sz.ey else jnp.logical_not(self.even)
            total = total + jnp.where(is_near, self.near[:, i].astype(f32), self.far[:, i].astype(f32))
            if side is not None:
                total = total + jnp.where(
                    is_near, self.corner[side, 0].astype(f32), self.corner[side, 1].astype(f32)
                )
        return total


def corner_edges(sz):
    return [(i, j) for i in (0, sz.ex) for j in (0, sz.ey)]


def main_products(sz, prepare, u_ref, mat_refs, rhs_ref, out_ref):
    width = sz.width
    flat = sz.gx * sz.gy * sz.gz
    u_flat = u_ref.reshape(sz.blocks * flat, width)
    matrices = [ref.at[c] for ref in mat_refs for c in range(ref.shape[0])]
    last = sz.nodes // 8 * 8
    ready = set()
    for cell, (x0, y0, z0) in enumerate(sz.origins):
        slot = cell % 2
        if cell < 2:
            rhs_ref[slot, : sz.base] = jnp.zeros((sz.base, sz.full), f32)
            rhs_ref[slot, last:] = jnp.zeros((sz.depth - last, sz.full), f32)
        for place, i, j, count in sz.runs(cell):
            for at in range(j, j + count):
                if (x0 + i, y0 + at) not in ready:
                    prepare(x0 + i, y0 + at)
                    ready.add((x0 + i, y0 + at))
        z1 = z0 + sz.p
        wrap = z1 % sz.gz
        for b in range(sz.blocks):
            lanes = slice(b * width, (b + 1) * width)
            for place, i, j, count in sz.runs(cell):
                row = sz.base + place * sz.p
                rhs_ref[slot, row : row + count * sz.p, lanes] = u_ref[
                    b, x0 + i, y0 + j : y0 + j + count, z0:z1
                ].reshape(count * sz.p, width)
        for b in range(sz.blocks):
            lanes = slice(b * width, (b + 1) * width)
            for place, i, j, count in sz.runs(cell):
                start = b * flat + ((x0 + i) * sz.gy + y0 + j) * sz.gz + wrap
                rhs_ref[slot, sz.tail + place : sz.tail + place + count, lanes] = u_flat[
                    pl.ds(start, count, stride=sz.gz)
                ]
        out_ref[cell] = jnp.dot(
            matrices[cell][...], rhs_ref[slot].astype(bf16), preferred_element_type=f32
        )


def corner_products(sz, u_corner, prod_ref, mat_refs, small_ref, tail_ref, acc_ref):
    width = sz.width
    flat = sz.gx * sz.gy * sz.gz
    acc_flat = acc_ref.reshape(sz.blocks * flat, width)
    matrices = [ref.at[c] for ref in mat_refs for c in range(ref.shape[0])]
    small_ref[...] = jnp.zeros_like(small_ref)
    touched = set()
    for cell, (x0, y0, z0) in enumerate(sz.origins):
        z1 = z0 + sz.p
        wrap = z1 % sz.gz
        corners = sz.cell_corners(cell)
        for rank, (i, j) in enumerate(corners):
            value = u_corner[sz.corner(x0 + i, y0 + j)]
            last = len(corners) * sz.p + rank
            for b in range(sz.blocks):
                lanes = slice(b * width, (b + 1) * width)
                small_ref[rank * sz.p : (rank + 1) * sz.p, lanes] = value[b, z0:z1]
                small_ref[last : last + 1, lanes] = value[b, wrap : wrap + 1]
        total = prod_ref[cell] + jnp.dot(
            matrices[cell][:, : small_ref.shape[0]], small_ref[...].astype(bf16),
            preferred_element_type=f32,
        )
        tail_ref[cell, : sz.base] = total[: sz.base]
        tail_ref[cell, sz.base :] = total[sz.tail :]
        spans = [(rank * sz.p, i, j, 1) for rank, (i, j) in enumerate(corners)]
        spans += [(sz.base + place * sz.p, i, j, count) for place, i, j, count in sz.runs(cell)]
        for row, i, j, count in spans:
            for at in range(count):
                part = total[row + at * sz.p : row + (at + 1) * sz.p]
                key = (x0 + i, y0 + j + at, z0)
                for b in range(sz.blocks):
                    value = part[:, b * width : (b + 1) * width]
                    if key in touched:
                        value = acc_ref[b, key[0], key[1], z0:z1] + value
                    acc_ref[b, key[0], key[1], z0:z1] = value
                touched.add(key)
    for cell, (x0, y0, z0) in enumerate(sz.origins):
        wrap = (z0 + sz.p) % sz.gz
        corners = sz.cell_corners(cell)
        spans = [(len(corners) * sz.p + rank, i, j, 1) for rank, (i, j) in enumerate(corners)]
        spans += [(sz.base + place, i, j, count) for place, i, j, count in sz.runs(cell)]
        for row, i, j, count in spans:
            for b in range(sz.blocks):
                start = b * flat + ((x0 + i) * sz.gy + y0 + j) * sz.gz + wrap
                rows = pl.ds(start, count, stride=sz.gz) if count > 1 else pl.ds(start, 1)
                lanes = slice(b * width, (b + 1) * width)
                acc_flat[rows] = acc_flat[rows] + tail_ref[cell, row : row + count, lanes]


def write_messages(sz, even, acc_ref, face, near, far):
    at_near = jnp.where(even, sz.ey, 0)
    for b in range(sz.blocks):
        face[0, b] = acc_ref[b, 0].astype(bf16)
        face[1, b] = acc_ref[b, sz.ex].astype(bf16)
        near[b] = acc_ref[b, :, at_near].astype(bf16)
        far[b] = acc_ref[b, :, sz.ey - at_near].astype(bf16)


def corner_pack_kernel(sz, near, far, out_ref):
    for side, i in enumerate((0, sz.ex)):
        for slot, ref in enumerate((near, far)):
            out_ref[side, slot] = ref[:, i]


def first_main(sz, n_mat, vec, from_x, from_y, own_inv, own_pot, *refs):
    mats = refs[:n_mat]
    prod_ref, ghost_x, ghost_y, u_ref, rhs_ref = refs[n_mat:]
    for j in range(sz.ey):
        ghost_x[0, j], ghost_x[1, j] = fields_of(from_x[j, :, sz.res + sz.full :])
    for i in range(sz.ex):
        ghost_y[0, i], ghost_y[1, i] = fields_of(from_y[i, :, sz.res + sz.full :])
    nodes = Nodes(sz, vec, from_x, from_y, own_inv, own_pot, ghost_x, ghost_y)

    def prepare(i, j):
        u_ref[:, i, j] = nodes.x(i, j) * nodes.inv(i, j)

    main_products(sz, prepare, u_ref, mats, rhs_ref, prod_ref)


def first_corner(sz, n_mat, even_ref, vec, from_x, from_y, corner, own_inv, own_pot, ghost_x, ghost_y,
                 prod_ref, *refs):
    mats = refs[:n_mat]
    acc_ref, face, near, far, last_x, last_field, small_ref, tail_ref = refs[n_mat:]
    last_field[0], last_field[1] = fields_of(corner[0, :, sz.res + sz.full :])
    last_x[...] = vectors_of(sz, corner[0])
    nodes = Nodes(sz, vec, from_x, from_y, own_inv, own_pot, ghost_x, ghost_y, last_field)
    u_corner = []
    for i, j in corner_edges(sz):
        x = last_x[...] if (i, j) == (sz.ex, sz.ey) else nodes.x(i, j)
        u_corner.append(x * nodes.inv(i, j))
    corner_products(sz, u_corner, prod_ref, mats, small_ref, tail_ref, acc_ref)
    write_messages(sz, even_ref[0] == 0, acc_ref, face, near, far)


def second_main(sz, n_mat, even_ref, vec, from_x, from_y, own_inv, own_pot, ghost_x, ghost_y,
                acc_in, face_in, near_in, far_in, *refs):
    mats = refs[:n_mat]
    prod_ref, y_ref, u_ref, rhs_ref = refs[n_mat:]
    nodes = Nodes(sz, vec, from_x, from_y, own_inv, own_pot, ghost_x, ghost_y)
    sums = Sums(sz, even_ref[0] == 0, acc_in, face_in, near_in, far_in)

    def prepare(i, j):
        old, inv = nodes.x(i, j), nodes.inv(i, j)
        image = inv * sums.at(i, j) + nodes.pot(i, j) * old
        new = (image - center_shift * old) / half_width
        y_ref[:, i, j] = new
        u_ref[:, i, j] = inv * new

    main_products(sz, prepare, u_ref, mats, rhs_ref, prod_ref)


def second_corner(sz, n_mat, even_ref, vec, from_x, from_y, own_inv, own_pot, ghost_x, ghost_y, last_x,
                  last_field, acc_in, face_in, near_in, far_in, corner_in, prod_ref, *refs):
    mats = refs[:n_mat]
    acc_ref, face, near, far, y_corner, small_ref, tail_ref = refs[n_mat:]
    even = even_ref[0] == 0
    nodes = Nodes(sz, vec, from_x, from_y, own_inv, own_pot, ghost_x, ghost_y, last_field)
    sums = Sums(sz, even, acc_in, face_in, near_in, far_in, corner_in)
    u_corner = []
    for at, (i, j) in enumerate(corner_edges(sz)):
        old = last_x[...] if (i, j) == (sz.ex, sz.ey) else nodes.x(i, j)
        inv = nodes.inv(i, j)
        image = inv * sums.at(i, j) + nodes.pot(i, j) * old
        new = (image - center_shift * old) / half_width
        y_corner[at] = new
        u_corner.append(inv * new)
    corner_products(sz, u_corner, prod_ref, mats, small_ref, tail_ref, acc_ref)
    write_messages(sz, even, acc_ref, face, near, far)


def third_main(sz, n_mat, even_ref, vec, from_x, from_y, own_inv, own_pot, ghost_x, ghost_y,
               acc_in, face_in, near_in, far_in, y_ref, *refs):
    mats = refs[:n_mat]
    prod_ref, new_ref, u_ref, rhs_ref = refs[n_mat:]
    nodes = Nodes(sz, vec, from_x, from_y, own_inv, own_pot, ghost_x, ghost_y)
    sums = Sums(sz, even_ref[0] == 0, acc_in, face_in, near_in, far_in)

    def prepare(i, j):
        old, inv = y_ref[:, i, j], nodes.inv(i, j)
        image = inv * sums.at(i, j) + nodes.pot(i, j) * old
        new = 2.0 * (image - center_shift * old) / half_width - nodes.x(i, j)
        new_ref[:, i, j] = new
        u_ref[:, i, j] = inv * new

    main_products(sz, prepare, u_ref, mats, rhs_ref, prod_ref)


def third_corner(sz, n_mat, norm_scale, even_ref, vec, from_x, from_y, own_inv, own_pot, ghost_x, ghost_y,
                 last_x, last_field, acc_in, face_in, near_in, far_in, corner_in, prod_ref, y_ref,
                 y_corner, new_ref, turned, *refs):
    mats = refs[:n_mat]
    out_hbm, face, side, corner, margin = refs[n_mat : n_mat + 5]
    part_ref, sem, acc_ref, rows_ref, small_ref, tail_ref = refs[n_mat + 5 :]
    nodes = Nodes(sz, vec, from_x, from_y, own_inv, own_pot, ghost_x, ghost_y, last_field)
    sums = Sums(sz, even_ref[0] == 0, acc_in, face_in, near_in, far_in, corner_in)
    u_corner, new_corner = [], []
    for at, (i, j) in enumerate(corner_edges(sz)):
        x = last_x[...] if (i, j) == (sz.ex, sz.ey) else nodes.x(i, j)
        old, inv = y_corner[at], nodes.inv(i, j)
        image = inv * sums.at(i, j) + nodes.pot(i, j) * old
        new_corner.append(2.0 * (image - center_shift * old) / half_width - x)
        u_corner.append(inv * new_corner[-1])
    corner_products(sz, u_corner, prod_ref, mats, small_ref, tail_ref, acc_ref)

    def put_row(at, value):
        for b in range(sz.blocks):
            rows_ref[at, :, b * sz.width : (b + 1) * sz.width] = value[b]

    copies = []
    for i in range(sz.gx):
        for j in range(sz.gy):
            acc, inv = acc_ref[:, i, j], nodes.inv(i, j)
            if i == sz.ex or j == sz.ey:
                value = gain * (inv * acc)
                rounded = value.astype(bf16)
                if j < sz.ey:
                    face[:, j] = rounded
                elif i < sz.ex:
                    side[:, i] = value
                else:
                    corner[...] = rounded
                put_row(sz.own_edges + (j if j < sz.ey else sz.ey + i), rounded)
                continue
            at = sz.corner(i, j)
            old = y_ref[:, i, j] if at is None else y_corner[at]
            new = new_ref[:, i, j] if at is None else new_corner[at]
            image = inv * acc + nodes.pot(i, j) * new
            value = 2.0 * (image - center_shift * new) / half_width - old
            part_ref[:, i, j] = value
            put_row(i * sz.ey + j, value.astype(bf16))
        if i < sz.ex:
            copies.append(pltpu.make_async_copy(part_ref.at[:, i], out_hbm.at[:, i], sem.at[i]))
            copies[-1].start()
    for at in range(sz.own_edges + sz.ey + sz.gx, sz.edges):
        rows_ref[at] = jnp.zeros((sz.ez, sz.full), bf16)
    local = jnp.dot(
        turned[...], rows_ref[...].reshape(sz.edges * sz.ez, sz.full), preferred_element_type=f32
    )
    margin[...] = (local * norm_scale).astype(bf16)
    for copy in copies:
        copy.wait()


def last_side_kernel(sz, side_ref, corner_ref, face_in, out_ref, face_out):
    del face_in, face_out
    for i in range(sz.ex):
        value = side_ref[:, i]
        if i == 0:
            value = value + corner_ref[...].astype(f32)
        out_ref[:, i] = value.astype(out_ref.dtype)


def last_kernel(sz, old_hbm, face, side, out_hbm, at_x, at_y, sems):
    del old_hbm
    pairs = [(at_x, out_hbm.at[:, 0]), (at_y, out_hbm.at[:, pl.ds(1, sz.ex - 1), 0])]
    loads = [pltpu.make_async_copy(b, a, sems.at[k]) for k, (a, b) in enumerate(pairs)]
    stores = [pltpu.make_async_copy(a, b, sems.at[k]) for k, (a, b) in enumerate(pairs)]
    for copy in loads:
        copy.start()
    for copy in loads:
        copy.wait()
    at_x[:, 0] += side[:, 0].astype(f32)
    for j in range(sz.ey):
        at_x[:, j] += face[:, j].astype(f32)
    for i in range(1, sz.ex):
        at_y[:, i - 1] += side[:, i].astype(f32)
    for copy in stores:
        copy.start()
    for copy in stores:
        copy.wait()


def like(shape, dtype):
    return jax.ShapeDtypeStruct(shape, dtype)


def call(kernel, name, flops, out_shape, scratch, operands, hbm=0, scalar_first=False, aliases=None,
         out_hbm=0):
    out_shape = [like(s.shape, s.dtype) for s in out_shape]
    size = sum(math.prod(s.shape) * jnp.dtype(s.dtype).itemsize for s in (*operands, *out_shape))
    whole = pl.BlockSpec(memory_space=pltpu.VMEM)
    specs = [pl.BlockSpec(memory_space=pltpu.HBM)] * hbm + [whole] * (len(operands) - hbm)
    if scalar_first:
        specs[0] = pl.BlockSpec(memory_space=pltpu.SMEM)
    out_specs = [pl.BlockSpec(memory_space=pltpu.HBM)] * out_hbm + [whole] * (len(out_shape) - out_hbm)
    for source, target in (aliases or {}).items():
        if source >= hbm:
            specs[source] = out_specs[target] = pl.BlockSpec(memory_space=pl.ANY)
    out_shape = [pltpu.HBM(s.shape, s.dtype) for s in out_shape[:out_hbm]] + out_shape[out_hbm:]
    operands = [pltpu.with_memory_space_constraint(a, pltpu.HBM) for a in operands[:hbm]] + list(
        operands[hbm:]
    )
    return pl.pallas_call(
        kernel,
        in_specs=specs,
        out_specs=out_specs,
        out_shape=out_shape,
        scratch_shapes=scratch,
        input_output_aliases=aliases or {},
        compiler_params=pltpu.CompilerParams(vmem_limit_bytes=VMEM_LIMIT),
        cost_estimate=pl.CostEstimate(flops=flops, bytes_accessed=size, transcendentals=0),
        name=name,
    )(*operands)


def body(vectors, resident, inv_mass, potential, cell_matrix, connectivity):
    sz = Sizes(vectors, resident, inv_mass, connectivity)
    nx, ny = lax.axis_size("dx"), lax.axis_size("dy")
    norm_scale = 1.0 / math.sqrt(sz.ex * sz.ey * sz.ez * nx * ny)
    blocks, ez, width, full = sz.blocks, sz.ez, sz.width, sz.full
    res_count = resident.shape[-1]
    tile = (ez, width)

    conn = connectivity.reshape(sz.cells, sz.nodes)
    to_x, to_y, conn = call(
        functools.partial(pack_kernel, sz), "pack", 0,
        [like((sz.ey, ez, sz.wide), bf16), like((sz.ex, ez, sz.wide), bf16), conn],
        [
            pltpu.VMEM((2, sz.ey, ez), f32), pltpu.VMEM((2, sz.ex, ez), f32),
            pltpu.SemaphoreType.DMA((7 + 2 * blocks,)),
        ],
        [vectors, resident, inv_mass, potential, conn], hbm=5,
    )
    from_x = send(to_x, -1, 0)
    from_y = send(to_y, 0, -1)

    halves = 2 if sz.cells % 2 == 0 else 1
    step = sz.cells // halves
    mats = []
    for at in range(0, sz.cells, step):
        mats += call(
            functools.partial(order_kernel, sz, at), "order_cells", 0,
            [like((step, sz.rows, sz.depth), bf16)],
            [], [cell_matrix, conn],
        )
    own_inv = jnp.broadcast_to(inv_mass[..., None], inv_mass.shape + (width,))
    own_pot = jnp.broadcast_to(potential[..., None], inv_mass.shape + (width,))
    parity = jnp.reshape(lax.axis_index("dy") % 2, (1,)).astype(jnp.int32)
    ghost_corner = send(from_y[:1], -1, 0)

    grid = (blocks, sz.gx, sz.gy) + tile
    own = (blocks, sz.ex, sz.ey) + tile
    products = like((sz.cells, sz.rows, full), f32)
    state_grid = like(grid, f32)
    messages = [
        like((2, blocks, sz.gy) + tile, bf16),
        like((blocks, sz.gx) + tile, bf16),
        like((blocks, sz.gx) + tile, bf16),
    ]
    main_scratch = [pltpu.VMEM(grid, f32), pltpu.VMEM((2, sz.depth, full), f32)]
    corner_scratch = [
        pltpu.VMEM((LANES, full), f32),
        pltpu.VMEM((sz.cells, sz.base + sz.rows - sz.tail, full), f32),
    ]
    n_mat = len(mats)
    flops = 2 * sz.cells * sz.rows * sz.depth * full
    small_flops = 2 * sz.cells * sz.rows * LANES * full

    def exchange(face, near, far):
        face = swap_x(face)
        near, far = swap_y(near, far)
        (corner,) = call(
            functools.partial(corner_pack_kernel, sz), "corner_pack", 0,
            [like((2, 2) + sz.edge, bf16)], [], [near, far],
        )
        return [face, near, far], swap_x(corner)

    prod, ghost_x, ghost_y = call(
        functools.partial(first_main, sz, n_mat), "first_main", flops,
        [products, like((2, sz.ey) + tile, f32), like((2, sz.ex) + tile, f32)], main_scratch,
        [vectors, from_x, from_y, own_inv, own_pot, *mats],
    )
    acc, face, near, far, last_x, last_field = call(
        functools.partial(first_corner, sz, n_mat), "first_corner", small_flops,
        [state_grid, *messages, like(sz.edge, f32), like((2,) + tile, f32)], corner_scratch,
        [
            parity, vectors, from_x, from_y, ghost_corner, own_inv, own_pot, ghost_x, ghost_y, prod, *mats,
        ],
        scalar_first=True,
    )
    (turned,) = call(
        functools.partial(turn_kernel, sz), "turn_residents", flops // 2,
        [like((res_count, sz.edges * ez), bf16)], [],
        [resident.reshape(-1, res_count), from_x, from_y, ghost_corner],
    )
    got, corner = exchange(face, near, far)
    state = [vectors, from_x, from_y, own_inv, own_pot, ghost_x, ghost_y]
    ends = [last_x, last_field]
    prod, y1 = call(
        functools.partial(second_main, sz, n_mat), "second_main", flops,
        [products, state_grid], main_scratch,
        [parity, *state, acc, *got, *mats], scalar_first=True,
    )
    acc, face, near, far, y1_corner = call(
        functools.partial(second_corner, sz, n_mat), "second_corner", small_flops,
        [state_grid, *messages, like((4,) + sz.edge, f32)], corner_scratch,
        [parity, *state, *ends, acc, *got, corner, prod, *mats], scalar_first=True,
    )
    got, corner = exchange(face, near, far)
    prod, y2 = call(
        functools.partial(third_main, sz, n_mat), "third_main", flops,
        [products, state_grid], main_scratch,
        [parity, *state, acc, *got, y1, *mats], scalar_first=True,
    )
    filtered, face, side, corner, local = call(
        functools.partial(third_corner, sz, n_mat, norm_scale), "third_corner",
        small_flops + 2 * res_count * sz.edges * ez * full,
        [
            like(own, f32),
            like((blocks, sz.ey) + tile, bf16), like((blocks, sz.ex) + tile, f32), like(sz.edge, bf16),
            like((res_count, full), bf16),
        ],
        [pltpu.VMEM(own, f32), pltpu.SemaphoreType.DMA((sz.ex,)), pltpu.VMEM(grid, f32), pltpu.VMEM((sz.edges, ez, full), bf16)] + corner_scratch,
        [parity, *state, *ends, acc, *got, corner, prod, y1, y1_corner, y2, turned, *mats],
        scalar_first=True, out_hbm=1,
    )

    pieces = lax.all_to_all(local.reshape(ny, -1, full), "dy", 0, 0)
    mine = jnp.sum(pieces.astype(f32), axis=0)
    margin = mine
    for steps in range(1, nx):
        margin = margin + send(mine, steps, 0)

    corner = send(corner, 1, 0)
    side, face = call(
        functools.partial(last_side_kernel, sz), "last_side", 0,
        [like((blocks, sz.ex) + tile, bf16), face], [], [side, corner, face], aliases={2: 1},
    )
    face = send(face, 1, 0)
    side = send(side, 0, 1)
    (filtered,) = call(
        functools.partial(last_kernel, sz), "last", 0, [like(own, f32)],
        [
            pltpu.VMEM((blocks, sz.ey) + tile, f32), pltpu.VMEM((blocks, sz.ex - 1) + tile, f32),
            pltpu.SemaphoreType.DMA((2,)),
        ],
        [filtered, face, side], hbm=1, out_hbm=1, aliases={0: 0},
    )
    return (filtered, margin)


def solution(mesh):
    return jax.shard_map(
        body,
        mesh=mesh,
        in_specs=(
            P(None, "dx", "dy", None, None),
            P("dx", "dy", None, None),
            P("dx", "dy", None),
            P("dx", "dy", None),
            P(),
            P("dx", "dy", None, None),
        ),
        out_specs=(P(None, "dx", "dy", None, None), P("dy", None)),
        check_vma=False,
    )
```

```python
import functools
import math

import jax
import jax.numpy as jnp
from jax import lax
from jax.experimental import pallas as pl
from jax.experimental.pallas import tpu as pltpu
from jax.sharding import PartitionSpec as P

LANES = 128
TILE = 256
SUB = 16
VMEM_LIMIT = 16 * 1024 * 1024

center_shift = 1.2
half_width = 2.0
gain = 2.0 / half_width

f32, bf16 = jnp.float32, jnp.bfloat16


def round_up(value, step):
    return -(-value // step) * step


class Sizes:
    def __init__(self, vectors, resident, inv_mass, connectivity):
        self.blocks = vectors.shape[0]
        self.width = vectors.shape[-1]
        self.full = self.blocks * self.width
        self.res = resident.shape[-1]
        self.wide = self.res + self.full + self.width
        self.ex, self.ey, self.ez = inv_mass.shape
        self.cells, self.nodes = connectivity.shape[2:]
        self.n1 = round(self.nodes ** (1.0 / 3.0))
        self.p = self.n1 - 1
        self.cx, self.cy, self.cz = self.ex // self.p, self.ey // self.p, self.ez // self.p
        self.gx, self.gy, self.gz = self.ex + 1, self.ey + 1, self.ez
        self.edge = (self.blocks, self.ez, self.width)
        self.origins = [
            (a * self.p, b * self.p, c * self.p)
            for a in range(self.cx)
            for b in range(self.cy)
            for c in range(self.cz)
        ]
        self.most = max(len(self.cell_corners(cell)) for cell in range(self.cells))
        self.base = round_up(self.most * self.n1, 8)
        plain = self.n1 * self.n1 - min(len(self.cell_corners(cell)) for cell in range(self.cells))
        self.tail = self.base + plain * self.p
        self.rows = round_up(self.tail + plain, SUB)
        self.depth = round_up(self.rows, LANES)
        self.own_edges = self.ex * self.ey
        self.edges = round_up(self.own_edges + self.ey + self.gx, LANES // self.ez)

    def corner(self, i, j):
        if i in (0, self.ex) and j in (0, self.ey):
            return 2 * (i // self.ex) + j // self.ey
        return None

    def cell_corners(self, cell):
        x0, y0, _ = self.origins[cell]
        return [
            (i, j)
            for i in range(self.n1)
            for j in range(self.n1)
            if self.corner(x0 + i, y0 + j) is not None
        ]

    def runs(self, cell):
        corners = self.cell_corners(cell)
        place = 0
        for i in range(self.n1):
            js = [j for j in range(self.n1) if (i, j) not in corners]
            while js:
                count = 1
                while count < len(js) and js[count] == js[0] + count:
                    count += 1
                yield place, i, js[0], count
                place += count
                js = js[count:]


def send(value, steps_x, steps_y):
    nx, ny = lax.axis_size("dx"), lax.axis_size("dy")
    pairs = [
        (a * ny + b, ((a + steps_x) % nx) * ny + (b + steps_y) % ny)
        for a in range(nx)
        for b in range(ny)
    ]
    return lax.ppermute(value, ("dx", "dy"), pairs)


def swap_x(value):
    if lax.axis_size("dx") == 2:
        return send(value, 1, 0)
    return jnp.stack([send(value[0], -1, 0), send(value[1], 1, 0)])


def send_near(value):
    pairs = [(b, b + 1 if b % 2 == 0 else b - 1) for b in range(lax.axis_size("dy"))]
    return lax.ppermute(value, "dy", pairs)


def swap_y(near, far):
    ny = lax.axis_size("dy")
    far_pairs = [(b, (b - 1 if b % 2 == 0 else b + 1) % ny) for b in range(ny)]
    far = lax.ppermute(far, "dy", far_pairs)
    return send_near(near), far


def order_kernel(sz, first, matrix_ref, conn_ref, out_ref):
    for slot in range(out_ref.shape[0]):
        cell = first + slot
        x0, y0, z0 = sz.origins[cell]
        conn = conn_ref[cell : cell + 1, :].astype(f32)
        li = jnp.floor((conn + 0.5) * (1.0 / (sz.gy * sz.gz)))
        rest = conn - li * (sz.gy * sz.gz)
        lj = jnp.floor((rest + 0.5) * (1.0 / sz.gz))
        lk = rest - lj * sz.gz - z0
        lk = jnp.where(lk < 0, lk + sz.gz, lk)
        column = (li - x0) * sz.n1 + (lj - y0)
        corners = [i * sz.n1 + j for i, j in sz.cell_corners(cell)]
        place = column
        for at in corners:
            place = place - jnp.where(column > at, 1.0, 0.0)
        index = jnp.where(lk < sz.p, sz.base + place * sz.p + lk, sz.tail + place)
        for rank, at in enumerate(corners):
            special = jnp.where(lk < sz.p, rank * sz.p + lk, len(corners) * sz.p + rank)
            index = jnp.where(column == at, special, index)
        index = index.astype(jnp.int32)
        row = lax.broadcasted_iota(jnp.int32, (sz.depth, sz.nodes), 0)
        pick = (row == index).astype(f32).astype(bf16)
        half = jnp.dot(pick[: sz.rows], matrix_ref[...], preferred_element_type=f32)
        half = half.astype(bf16)
        cuts = list(range(0, sz.depth, TILE)) + [sz.depth]
        for r0, r1 in zip(cuts[:-1], cuts[1:]):
            r1 = min(r1, sz.rows)
            block = lax.dot_general(
                half[r0:r1], pick[r0:], (((1,), (1,)), ((), ())), preferred_element_type=f32
            ).astype(bf16)
            out_ref[slot, r0:r1, r0:] = block
            for c0, c1 in zip(cuts[:-1], cuts[1:]):
                if c0 > r0:
                    mirror = block[:, c0 - r0 : c1 - r0].T
                    c1 = min(c1, sz.rows)
                    out_ref[slot, c0:c1, r0:r1] = mirror[: c1 - c0]


def field_row(inv, pot):
    lane = lax.broadcasted_iota(jnp.int32, inv.shape, inv.ndim - 1)
    row = jnp.zeros_like(inv)
    for at, rest in enumerate((inv, pot)):
        for k in range(3):
            part = rest.astype(bf16).astype(f32)
            rest = rest - part
            row = jnp.where(lane == 3 * at + k, part, row)
    return row.astype(bf16)


def field_rows(sz, inv, pot, count):
    inv, pot = inv.T, pot.T
    shape = (sz.ez, sz.width)
    for at in range(count):
        yield at, field_row(
            jnp.broadcast_to(inv[:, at : at + 1], shape), jnp.broadcast_to(pot[:, at : at + 1], shape)
        )


def fields_of(row):
    row = row.astype(f32)
    return [
        jnp.broadcast_to(sum(row[:, 3 * at + k : 3 * at + k + 1] for k in range(3)), row.shape)
        for at in range(2)
    ]


def pack_kernel(
    sz, vec_hbm, res_hbm, inv_hbm, pot_hbm, conn_hbm, to_x, to_y, conn_ref, at_x, at_y, sems
):
    pairs = [
        (inv_hbm.at[0], at_x.at[0]), (pot_hbm.at[0], at_x.at[1]),
        (inv_hbm.at[:, 0], at_y.at[0]), (pot_hbm.at[:, 0], at_y.at[1]),
        (res_hbm.at[0], to_x.at[:, :, pl.ds(0, sz.res)]),
        (res_hbm.at[:, 0], to_y.at[:, :, pl.ds(0, sz.res)]),
    ]
    for b in range(sz.blocks):
        lanes = pl.ds(sz.res + b * sz.width, sz.width)
        pairs.append((vec_hbm.at[b, 0], to_x.at[:, :, lanes]))
        pairs.append((vec_hbm.at[b, :, 0], to_y.at[:, :, lanes]))
    pairs.append((conn_hbm, conn_ref))
    copies = [pltpu.make_async_copy(a, b, sems.at[k]) for k, (a, b) in enumerate(pairs)]
    for copy in copies:
        copy.start()
    for copy in copies[:4]:
        copy.wait()
    for j, row in field_rows(sz, at_x[0], at_x[1], sz.ey):
        to_x[j, :, sz.res + sz.full :] = row
    for i, row in field_rows(sz, at_y[0], at_y[1], sz.ex):
        to_y[i, :, sz.res + sz.full :] = row
    for copy in copies[4:]:
        copy.wait()


def turn_kernel(sz, res_ref, from_x, from_y, corner, out_ref):
    own = sz.own_edges * sz.ez
    for g in range(0, sz.res, LANES):
        lanes = slice(g, g + LANES)
        out_ref[lanes, :own] = res_ref[:, lanes].T
        rest = sz.edges - sz.own_edges - sz.ey - sz.gx
        parts = [from_x[:, :, lanes], from_y[:, :, lanes], corner[:, :, lanes]]
        if rest:
            parts.append(jnp.zeros((rest, sz.ez, LANES), bf16))
        ghosts = jnp.concatenate(parts, axis=0)
        out_ref[lanes, own:] = ghosts.reshape(-1, LANES).T


def vectors_of(sz, edge):
    lanes = [slice(sz.res + b * sz.width, sz.res + (b + 1) * sz.width) for b in range(sz.blocks)]
    return jnp.stack([edge[:, at] for at in lanes]).astype(f32)


class Nodes:
    def __init__(self, sz, vec, from_x, from_y, own_inv, own_pot, ghost_x, ghost_y, corners=None):
        self.sz, self.vec, self.from_x, self.from_y = sz, vec, from_x, from_y
        self.own, self.ghost_x, self.ghost_y, self.corners = (own_inv, own_pot), ghost_x, ghost_y, corners

    def x(self, i, j):
        sz = self.sz
        if i < sz.ex and j < sz.ey:
            return self.vec[:, i, j].astype(f32)
        return vectors_of(sz, self.from_x[j] if i == sz.ex else self.from_y[i])

    def field(self, at, i, j):
        sz = self.sz
        if i < sz.ex and j < sz.ey:
            return self.own[at][i, j]
        if i < sz.ex:
            return self.ghost_y[at, i]
        if j < sz.ey:
            return self.ghost_x[at, j]
        return self.corners[at]

    def inv(self, i, j):
        return self.field(0, i, j)

    def pot(self, i, j):
        return self.field(1, i, j)


class Sums:
    def __init__(self, sz, even, acc, face, near, far, corner=None):
        self.sz, self.even, self.acc, self.face = sz, even, acc, face
        self.near, self.far, self.corner = near, far, corner

    def at(self, i, j):
        sz = self.sz
        total = self.acc[:, i, j]
        side = 1 if i == 0 else 0 if i == sz.ex else None
        if side is not None:
            total = total + self.face[side, :, j].astype(f32)
        if j in (0, sz.ey):
            is_near = self.even if j == sz.ey else jnp.logical_not(self.even)
            total = total + jnp.where(is_near, self.near[:, i].astype(f32), self.far[:, i].astype(f32))
            if side is not None:
                total = total + jnp.where(
                    is_near, self.corner[side, 0].astype(f32), self.corner[side, 1].astype(f32)
                )
        return total


def corner_edges(sz):
    return [(i, j) for i in (0, sz.ex) for j in (0, sz.ey)]


def main_products(sz, prepare, u_ref, mat_refs, rhs_ref, out_ref):
    width = sz.width
    flat = sz.gx * sz.gy * sz.gz
    u_flat = u_ref.reshape(sz.blocks * flat, width)
    matrices = [ref.at[c] for ref in mat_refs for c in range(ref.shape[0])]
    last = sz.nodes // 8 * 8
    ready = set()
    for cell, (x0, y0, z0) in enumerate(sz.origins):
        slot = cell % 2
        if cell < 2:
            rhs_ref[slot, : sz.base] = jnp.zeros((sz.base, sz.full), f32)
            rhs_ref[slot, last:] = jnp.zeros((sz.depth - last, sz.full), f32)
        for place, i, j, count in sz.runs(cell):
            for at in range(j, j + count):
                if (x0 + i, y0 + at) not in ready:
                    prepare(x0 + i, y0 + at)
                    ready.add((x0 + i, y0 + at))
        z1 = z0 + sz.p
        wrap = z1 % sz.gz
        for b in range(sz.blocks):
            lanes = slice(b * width, (b + 1) * width)
            for place, i, j, count in sz.runs(cell):
                row = sz.base + place * sz.p
                rhs_ref[slot, row : row + count * sz.p, lanes] = u_ref[
                    b, x0 + i, y0 + j : y0 + j + count, z0:z1
                ].reshape(count * sz.p, width)
        for b in range(sz.blocks):
            lanes = slice(b * width, (b + 1) * width)
            for place, i, j, count in sz.runs(cell):
                start = b * flat + ((x0 + i) * sz.gy + y0 + j) * sz.gz + wrap
                rhs_ref[slot, sz.tail + place : sz.tail + place + count, lanes] = u_flat[
                    pl.ds(start, count, stride=sz.gz)
                ]
        out_ref[cell] = jnp.dot(
            matrices[cell][...], rhs_ref[slot].astype(bf16), preferred_element_type=f32
        )


def corner_products(sz, u_corner, prod_ref, mat_refs, small_ref, tail_ref, acc_ref):
    width = sz.width
    flat = sz.gx * sz.gy * sz.gz
    acc_flat = acc_ref.reshape(sz.blocks * flat, width)
    matrices = [ref.at[c] for ref in mat_refs for c in range(ref.shape[0])]
    small_ref[...] = jnp.zeros_like(small_ref)
    touched = set()
    for cell, (x0, y0, z0) in enumerate(sz.origins):
        z1 = z0 + sz.p
        wrap = z1 % sz.gz
        corners = sz.cell_corners(cell)
        for rank, (i, j) in enumerate(corners):
            value = u_corner[sz.corner(x0 + i, y0 + j)]
            last = len(corners) * sz.p + rank
            for b in range(sz.blocks):
                lanes = slice(b * width, (b + 1) * width)
                small_ref[rank * sz.p : (rank + 1) * sz.p, lanes] = value[b, z0:z1]
                small_ref[last : last + 1, lanes] = value[b, wrap : wrap + 1]
        total = prod_ref[cell] + jnp.dot(
            matrices[cell][:, : small_ref.shape[0]], small_ref[...].astype(bf16),
            preferred_element_type=f32,
        )
        tail_ref[cell, : sz.base] = total[: sz.base]
        tail_ref[cell, sz.base :] = total[sz.tail :]
        spans = [(rank * sz.p, i, j, 1) for rank, (i, j) in enumerate(corners)]
        spans += [(sz.base + place * sz.p, i, j, count) for place, i, j, count in sz.runs(cell)]
        for row, i, j, count in spans:
            for at in range(count):
                part = total[row + at * sz.p : row + (at + 1) * sz.p]
                key = (x0 + i, y0 + j + at, z0)
                for b in range(sz.blocks):
                    value = part[:, b * width : (b + 1) * width]
                    if key in touched:
                        value = acc_ref[b, key[0], key[1], z0:z1] + value
                    acc_ref[b, key[0], key[1], z0:z1] = value
                touched.add(key)
    for cell, (x0, y0, z0) in enumerate(sz.origins):
        wrap = (z0 + sz.p) % sz.gz
        corners = sz.cell_corners(cell)
        spans = [(len(corners) * sz.p + rank, i, j, 1) for rank, (i, j) in enumerate(corners)]
        spans += [(sz.base + place, i, j, count) for place, i, j, count in sz.runs(cell)]
        for row, i, j, count in spans:
            for b in range(sz.blocks):
                start = b * flat + ((x0 + i) * sz.gy + y0 + j) * sz.gz + wrap
                rows = pl.ds(start, count, stride=sz.gz) if count > 1 else pl.ds(start, 1)
                lanes = slice(b * width, (b + 1) * width)
                acc_flat[rows] = acc_flat[rows] + tail_ref[cell, row : row + count, lanes]


def write_messages(sz, even, acc_ref, face, near, far):
    at_near = jnp.where(even, sz.ey, 0)
    for b in range(sz.blocks):
        face[0, b] = acc_ref[b, 0].astype(bf16)
        face[1, b] = acc_ref[b, sz.ex].astype(bf16)
        near[b] = acc_ref[b, :, at_near].astype(bf16)
        far[b] = acc_ref[b, :, sz.ey - at_near].astype(bf16)


def corner_pack_kernel(sz, near, far, out_ref):
    for side, i in enumerate((0, sz.ex)):
        for slot, ref in enumerate((near, far)):
            out_ref[side, slot] = ref[:, i]


def first_main(sz, n_mat, vec, from_x, from_y, own_inv, own_pot, *refs):
    mats = refs[:n_mat]
    prod_ref, ghost_x, ghost_y, u_ref, rhs_ref = refs[n_mat:]
    for j in range(sz.ey):
        ghost_x[0, j], ghost_x[1, j] = fields_of(from_x[j, :, sz.res + sz.full :])
    for i in range(sz.ex):
        ghost_y[0, i], ghost_y[1, i] = fields_of(from_y[i, :, sz.res + sz.full :])
    nodes = Nodes(sz, vec, from_x, from_y, own_inv, own_pot, ghost_x, ghost_y)

    def prepare(i, j):
        u_ref[:, i, j] = nodes.x(i, j) * nodes.inv(i, j)

    main_products(sz, prepare, u_ref, mats, rhs_ref, prod_ref)


def first_corner(sz, n_mat, even_ref, vec, from_x, from_y, corner, own_inv, own_pot, ghost_x, ghost_y,
                 prod_ref, *refs):
    mats = refs[:n_mat]
    acc_ref, face, near, far, last_x, last_field, small_ref, tail_ref = refs[n_mat:]
    last_field[0], last_field[1] = fields_of(corner[0, :, sz.res + sz.full :])
    last_x[...] = vectors_of(sz, corner[0])
    nodes = Nodes(sz, vec, from_x, from_y, own_inv, own_pot, ghost_x, ghost_y, last_field)
    u_corner = []
    for i, j in corner_edges(sz):
        x = last_x[...] if (i, j) == (sz.ex, sz.ey) else nodes.x(i, j)
        u_corner.append(x * nodes.inv(i, j))
    corner_products(sz, u_corner, prod_ref, mats, small_ref, tail_ref, acc_ref)
    write_messages(sz, even_ref[0] == 0, acc_ref, face, near, far)


def second_main(sz, n_mat, even_ref, vec, from_x, from_y, own_inv, own_pot, ghost_x, ghost_y,
                acc_in, face_in, near_in, far_in, *refs):
    mats = refs[:n_mat]
    prod_ref, y_ref, u_ref, rhs_ref = refs[n_mat:]
    nodes = Nodes(sz, vec, from_x, from_y, own_inv, own_pot, ghost_x, ghost_y)
    sums = Sums(sz, even_ref[0] == 0, acc_in, face_in, near_in, far_in)

    def prepare(i, j):
        old, inv = nodes.x(i, j), nodes.inv(i, j)
        image = inv * sums.at(i, j) + nodes.pot(i, j) * old
        new = (image - center_shift * old) / half_width
        y_ref[:, i, j] = new
        u_ref[:, i, j] = inv * new

    main_products(sz, prepare, u_ref, mats, rhs_ref, prod_ref)


def second_corner(sz, n_mat, even_ref, vec, from_x, from_y, own_inv, own_pot, ghost_x, ghost_y, last_x,
                  last_field, acc_in, face_in, near_in, far_in, corner_in, prod_ref, *refs):
    mats = refs[:n_mat]
    acc_ref, face, near, far, y_corner, small_ref, tail_ref = refs[n_mat:]
    even = even_ref[0] == 0
    nodes = Nodes(sz, vec, from_x, from_y, own_inv, own_pot, ghost_x, ghost_y, last_field)
    sums = Sums(sz, even, acc_in, face_in, near_in, far_in, corner_in)
    u_corner = []
    for at, (i, j) in enumerate(corner_edges(sz)):
        old = last_x[...] if (i, j) == (sz.ex, sz.ey) else nodes.x(i, j)
        inv = nodes.inv(i, j)
        image = inv * sums.at(i, j) + nodes.pot(i, j) * old
        new = (image - center_shift * old) / half_width
        y_corner[at] = new
        u_corner.append(inv * new)
    corner_products(sz, u_corner, prod_ref, mats, small_ref, tail_ref, acc_ref)
    write_messages(sz, even, acc_ref, face, near, far)


def third_main(sz, n_mat, even_ref, vec, from_x, from_y, own_inv, own_pot, ghost_x, ghost_y,
               acc_in, face_in, near_in, far_in, y_ref, *refs):
    mats = refs[:n_mat]
    prod_ref, new_ref, u_ref, rhs_ref = refs[n_mat:]
    nodes = Nodes(sz, vec, from_x, from_y, own_inv, own_pot, ghost_x, ghost_y)
    sums = Sums(sz, even_ref[0] == 0, acc_in, face_in, near_in, far_in)

    def prepare(i, j):
        old, inv = y_ref[:, i, j], nodes.inv(i, j)
        image = inv * sums.at(i, j) + nodes.pot(i, j) * old
        new = 2.0 * (image - center_shift * old) / half_width - nodes.x(i, j)
        new_ref[:, i, j] = new
        u_ref[:, i, j] = inv * new

    main_products(sz, prepare, u_ref, mats, rhs_ref, prod_ref)


def third_corner(sz, n_mat, norm_scale, even_ref, vec, from_x, from_y, own_inv, own_pot, ghost_x, ghost_y,
                 last_x, last_field, acc_in, face_in, near_in, far_in, corner_in, prod_ref, y_ref,
                 y_corner, new_ref, turned, *refs):
    mats = refs[:n_mat]
    out_hbm, margin_hbm, face, side, corner = refs[n_mat : n_mat + 5]
    part_ref, margin, sem, acc_ref, rows_ref, small_ref, tail_ref = refs[n_mat + 5 :]
    nodes = Nodes(sz, vec, from_x, from_y, own_inv, own_pot, ghost_x, ghost_y, last_field)
    sums = Sums(sz, even_ref[0] == 0, acc_in, face_in, near_in, far_in, corner_in)
    u_corner, new_corner = [], []
    for at, (i, j) in enumerate(corner_edges(sz)):
        x = last_x[...] if (i, j) == (sz.ex, sz.ey) else nodes.x(i, j)
        old, inv = y_corner[at], nodes.inv(i, j)
        image = inv * sums.at(i, j) + nodes.pot(i, j) * old
        new_corner.append(2.0 * (image - center_shift * old) / half_width - x)
        u_corner.append(inv * new_corner[-1])
    corner_products(sz, u_corner, prod_ref, mats, small_ref, tail_ref, acc_ref)

    def put_row(at, value):
        for b in range(sz.blocks):
            rows_ref[at, :, b * sz.width : (b + 1) * sz.width] = value[b]

    copies = []
    for i in range(sz.gx):
        for j in range(sz.gy):
            acc, inv = acc_ref[:, i, j], nodes.inv(i, j)
            if i == sz.ex or j == sz.ey:
                value = gain * (inv * acc)
                rounded = value.astype(bf16)
                if j < sz.ey:
                    face[:, j] = rounded
                elif i < sz.ex:
                    side[:, i] = value
                else:
                    corner[...] = rounded
                put_row(sz.own_edges + (j if j < sz.ey else sz.ey + i), rounded)
                continue
            at = sz.corner(i, j)
            old = y_ref[:, i, j] if at is None else y_corner[at]
            new = new_ref[:, i, j] if at is None else new_corner[at]
            image = inv * acc + nodes.pot(i, j) * new
            value = 2.0 * (image - center_shift * new) / half_width - old
            part_ref[:, i, j] = value
            put_row(i * sz.ey + j, value.astype(bf16))
        if i < sz.ex:
            copies.append(pltpu.make_async_copy(part_ref.at[:, i], out_hbm.at[:, i], sem.at[i]))
            copies[-1].start()
    for at in range(sz.own_edges + sz.ey + sz.gx, sz.edges):
        rows_ref[at] = jnp.zeros((sz.ez, sz.full), bf16)
    rows = rows_ref[...].reshape(sz.edges * sz.ez, sz.full)
    half = sz.res // 2
    for at in range(2):
        span = slice(at * half, (at + 1) * half)
        local = jnp.dot(turned[span], rows, preferred_element_type=f32)
        margin[span] = (local * norm_scale).astype(bf16)
        span = pl.ds(at * half, half)
        copies.append(pltpu.make_async_copy(margin.at[span], margin_hbm.at[span], sem.at[sz.ex + at]))
        copies[-1].start()
    for copy in copies:
        copy.wait()


def last_side_kernel(sz, side_ref, corner_ref, face_in, out_ref, face_out):
    del face_in, face_out
    for i in range(sz.ex):
        value = side_ref[:, i]
        if i == 0:
            value = value + corner_ref[...].astype(f32)
        out_ref[:, i] = value.astype(out_ref.dtype)


def last_kernel(sz, old_hbm, face, side, out_hbm, at_x, at_y, sems):
    del old_hbm
    pairs = [(at_x, out_hbm.at[:, 0]), (at_y, out_hbm.at[:, pl.ds(1, sz.ex - 1), 0])]
    loads = [pltpu.make_async_copy(b, a, sems.at[k]) for k, (a, b) in enumerate(pairs)]
    stores = [pltpu.make_async_copy(a, b, sems.at[k]) for k, (a, b) in enumerate(pairs)]
    for copy in loads:
        copy.start()
    for copy in loads:
        copy.wait()
    at_x[:, 0] += side[:, 0].astype(f32)
    for j in range(sz.ey):
        at_x[:, j] += face[:, j].astype(f32)
    for i in range(1, sz.ex):
        at_y[:, i - 1] += side[:, i].astype(f32)
    for copy in stores:
        copy.start()
    for copy in stores:
        copy.wait()


def like(shape, dtype):
    return jax.ShapeDtypeStruct(shape, dtype)


def call(kernel, name, flops, out_shape, scratch, operands, hbm=0, scalar_first=False, aliases=None,
         out_hbm=0):
    out_shape = [like(s.shape, s.dtype) for s in out_shape]
    size = sum(math.prod(s.shape) * jnp.dtype(s.dtype).itemsize for s in (*operands, *out_shape))
    whole = pl.BlockSpec(memory_space=pltpu.VMEM)
    specs = [pl.BlockSpec(memory_space=pltpu.HBM)] * hbm + [whole] * (len(operands) - hbm)
    if scalar_first:
        specs[0] = pl.BlockSpec(memory_space=pltpu.SMEM)
    out_specs = [pl.BlockSpec(memory_space=pltpu.HBM)] * out_hbm + [whole] * (len(out_shape) - out_hbm)
    for source, target in (aliases or {}).items():
        if source >= hbm:
            specs[source] = out_specs[target] = pl.BlockSpec(memory_space=pl.ANY)
    out_shape = [pltpu.HBM(s.shape, s.dtype) for s in out_shape[:out_hbm]] + out_shape[out_hbm:]
    operands = [pltpu.with_memory_space_constraint(a, pltpu.HBM) for a in operands[:hbm]] + list(
        operands[hbm:]
    )
    return pl.pallas_call(
        kernel,
        in_specs=specs,
        out_specs=out_specs,
        out_shape=out_shape,
        scratch_shapes=scratch,
        input_output_aliases=aliases or {},
        compiler_params=pltpu.CompilerParams(vmem_limit_bytes=VMEM_LIMIT),
        cost_estimate=pl.CostEstimate(flops=flops, bytes_accessed=size, transcendentals=0),
        name=name,
    )(*operands)


def body(vectors, resident, inv_mass, potential, cell_matrix, connectivity):
    sz = Sizes(vectors, resident, inv_mass, connectivity)
    nx, ny = lax.axis_size("dx"), lax.axis_size("dy")
    norm_scale = 1.0 / math.sqrt(sz.ex * sz.ey * sz.ez * nx * ny)
    blocks, ez, width, full = sz.blocks, sz.ez, sz.width, sz.full
    res_count = resident.shape[-1]
    tile = (ez, width)

    conn = connectivity.reshape(sz.cells, sz.nodes)
    to_x, to_y, conn = call(
        functools.partial(pack_kernel, sz), "pack", 0,
        [like((sz.ey, ez, sz.wide), bf16), like((sz.ex, ez, sz.wide), bf16), conn],
        [
            pltpu.VMEM((2, sz.ey, ez), f32), pltpu.VMEM((2, sz.ex, ez), f32),
            pltpu.SemaphoreType.DMA((7 + 2 * blocks,)),
        ],
        [vectors, resident, inv_mass, potential, conn], hbm=5,
    )
    from_x = send(to_x, -1, 0)
    from_y = send(to_y, 0, -1)

    halves = 2 if sz.cells % 2 == 0 else 1
    step = sz.cells // halves
    mats = []
    for at in range(0, sz.cells, step):
        mats += call(
            functools.partial(order_kernel, sz, at), "order_cells", 4 * step * sz.depth**3,
            [like((step, sz.rows, sz.depth), bf16)],
            [], [cell_matrix, conn],
        )
    own_inv = jnp.broadcast_to(inv_mass[..., None], inv_mass.shape + (width,))
    own_pot = jnp.broadcast_to(potential[..., None], inv_mass.shape + (width,))
    parity = jnp.reshape(lax.axis_index("dy") % 2, (1,)).astype(jnp.int32)
    ghost_corner = send(from_y[:1], -1, 0)

    grid = (blocks, sz.gx, sz.gy) + tile
    own = (blocks, sz.ex, sz.ey) + tile
    products = like((sz.cells, sz.rows, full), f32)
    state_grid = like(grid, f32)
    messages = [
        like((2, blocks, sz.gy) + tile, bf16),
        like((blocks, sz.gx) + tile, bf16),
        like((blocks, sz.gx) + tile, bf16),
    ]
    main_scratch = [pltpu.VMEM(grid, f32), pltpu.VMEM((2, sz.depth, full), f32)]
    corner_scratch = [
        pltpu.VMEM((LANES, full), f32),
        pltpu.VMEM((sz.cells, sz.base + sz.rows - sz.tail, full), f32),
    ]
    n_mat = len(mats)
    flops = 2 * sz.cells * sz.rows * sz.depth * full
    small_flops = 2 * sz.cells * sz.rows * LANES * full

    def exchange(face, near, far):
        face = swap_x(face)
        near, far = swap_y(near, far)
        (corner,) = call(
            functools.partial(corner_pack_kernel, sz), "corner_pack", 0,
            [like((2, 2) + sz.edge, bf16)], [], [near, far],
        )
        return [face, near, far], swap_x(corner)

    prod, ghost_x, ghost_y = call(
        functools.partial(first_main, sz, n_mat), "first_main", flops,
        [products, like((2, sz.ey) + tile, f32), like((2, sz.ex) + tile, f32)], main_scratch,
        [vectors, from_x, from_y, own_inv, own_pot, *mats],
    )
    acc, face, near, far, last_x, last_field = call(
        functools.partial(first_corner, sz, n_mat), "first_corner", small_flops,
        [state_grid, *messages, like(sz.edge, f32), like((2,) + tile, f32)], corner_scratch,
        [
            parity, vectors, from_x, from_y, ghost_corner, own_inv, own_pot, ghost_x, ghost_y, prod, *mats,
        ],
        scalar_first=True,
    )
    (turned,) = call(
        functools.partial(turn_kernel, sz), "turn_residents", flops // 2,
        [like((res_count, sz.edges * ez), bf16)], [],
        [resident.reshape(-1, res_count), from_x, from_y, ghost_corner],
    )
    got, corner = exchange(face, near, far)
    state = [vectors, from_x, from_y, own_inv, own_pot, ghost_x, ghost_y]
    ends = [last_x, last_field]
    prod, y1 = call(
        functools.partial(second_main, sz, n_mat), "second_main", flops,
        [products, state_grid], main_scratch,
        [parity, *state, acc, *got, *mats], scalar_first=True,
    )
    acc, face, near, far, y1_corner = call(
        functools.partial(second_corner, sz, n_mat), "second_corner", small_flops,
        [state_grid, *messages, like((4,) + sz.edge, f32)], corner_scratch,
        [parity, *state, *ends, acc, *got, corner, prod, *mats], scalar_first=True,
    )
    got, corner = exchange(face, near, far)
    prod, y2 = call(
        functools.partial(third_main, sz, n_mat), "third_main", flops,
        [products, state_grid], main_scratch,
        [parity, *state, acc, *got, y1, *mats], scalar_first=True,
    )
    filtered, local, face, side, corner = call(
        functools.partial(third_corner, sz, n_mat, norm_scale), "third_corner",
        small_flops + 2 * res_count * sz.edges * ez * full,
        [
            like(own, f32), like((res_count, full), bf16), like((blocks, sz.ey) + tile, bf16),
            like((blocks, sz.ex) + tile, f32), like(sz.edge, bf16),
        ],
        [pltpu.VMEM(own, f32), pltpu.VMEM((res_count, full), bf16), pltpu.SemaphoreType.DMA((sz.ex + 2,)), pltpu.VMEM(grid, f32), pltpu.VMEM((sz.edges, ez, full), bf16)] + corner_scratch,
        [parity, *state, *ends, acc, *got, corner, prod, y1, y1_corner, y2, turned, *mats],
        scalar_first=True, out_hbm=2,
    )

    pieces = lax.all_to_all(local.reshape(ny, -1, full), "dy", 0, 0)
    mine = jnp.sum(pieces.astype(f32), axis=0)
    margin = mine
    for steps in range(1, nx):
        margin = margin + send(mine, steps, 0)

    corner = send(corner, 1, 0)
    side, face = call(
        functools.partial(last_side_kernel, sz), "last_side", 0,
        [like((blocks, sz.ex) + tile, bf16), face], [], [side, corner, face], aliases={2: 1},
    )
    face = send(face, 1, 0)
    side = send(side, 0, 1)
    (filtered,) = call(
        functools.partial(last_kernel, sz), "last", 0, [like(own, f32)],
        [
            pltpu.VMEM((blocks, sz.ey) + tile, f32), pltpu.VMEM((blocks, sz.ex - 1) + tile, f32),
            pltpu.SemaphoreType.DMA((2,)),
        ],
        [filtered, face, side], hbm=1, out_hbm=1, aliases={0: 0},
    )
    return (filtered, margin)


def solution(mesh):
    return jax.shard_map(
        body,
        mesh=mesh,
        in_specs=(
            P(None, "dx", "dy", None, None),
            P("dx", "dy", None, None),
            P("dx", "dy", None),
            P("dx", "dy", None),
            P(),
            P("dx", "dy", None, None),
        ),
        out_specs=(P(None, "dx", "dy", None, None), P("dy", None)),
        check_vma=False,
    )
```
